32 devices in a mesh: grp: 4 (over y, x), wide: 8 (over z, core).
Axes of the slice: x: 2, y: 2, z: 4, core: 2. Of those that a mesh axis runs over, the one named last changes fastest.
Arguments:
- tiles: bfloat16 [1536, 256, 256], P(('grp', 'wide')), may hold values from -0.59765625 to 0.59765625
- contraction: int32 [1536], P(('grp', 'wide')), may hold values from 0 to 15
- row_tile: int32 [1536], P(('grp', 'wide')), may hold values from 0 to 31, as said below
- owner_map: int32 [32], replicated, may hold values from 0 to 31, as said below
- panel: bfloat16 [4096, 768], P('grp'), may hold values from -0.5390625 to 0.5390625
Outputs:
- column_block: float32 [8192, 768], P('wide')
The draws below stay inside these ranges and needn't reach their ends.
Inputs may be any that keep to these rules, and one draw needn't show every extreme that they name: `row_tile`: every row tile's owner is owner_map // 4; among the 48 contributions of one device at most 16 have row tiles of one owner, and on every device some owner gets exactly 16. `owner_map`: A permutation of the row tiles.
All inputs are finite; a program needn't handle non-finite values.
Results may differ from the reference program's by a relative error of at most 0.0003.
Values may be sent and summed in bfloat16 or wider, within the bound.
No kernel may reach another device: no remote copies, remote signals or barrier semaphores. Data moves between devices by JAX's collectives and lax.ppermute only.
A program may use at most 192 MiB of HBM per device.

```python
import jax
import jax.numpy as jnp
from jax import lax

TILE = 256
COL_TILES = 3
K_TILES = 16
OUT_DEV = 4
TILE_DEV = 48
MOST = 16
SLOTS = 128
ROW_TILES = 32
CONTRIBS = 1536
N_WIDE = 8


def owner_helper(key):
    base = jax.random.fold_in(key, 5)
    permuted = jax.random.permutation(jax.random.fold_in(base, 1), ROW_TILES).astype(jnp.int32)
    inverse = jnp.zeros((ROW_TILES,), jnp.int32).at[permuted].set(jnp.arange(ROW_TILES, dtype=jnp.int32))
    hotness = jax.random.randint(jax.random.fold_in(base, 2), (N_WIDE,), 0, 4)
    block_count = CONTRIBS // TILE_DEV
    block_keys = jax.random.split(jax.random.fold_in(base, 3), block_count)

    def one_block(block_key):
        first_key, second_key, third_key = jax.random.split(block_key, 3)
        slot_ids = jnp.arange(SLOTS, dtype=jnp.int32)
        owners = slot_ids // MOST
        forced = jax.random.randint(first_key, (), 0, N_WIDE)
        noise = jax.random.randint(second_key, (SLOTS,), 0, 65536)
        scores = noise + hotness[owners] * 16384 + (owners == forced).astype(jnp.int32) * 1048576
        scores = scores * SLOTS + slot_ids
        picked = lax.top_k(scores, TILE_DEV)[1]
        target = picked // MOST
        local_row = jax.random.randint(third_key, (TILE_DEV,), 0, OUT_DEV)
        return inverse[target * OUT_DEV + local_row]
    rows = jax.vmap(one_block)(block_keys).reshape(CONTRIBS).astype(jnp.int32)
    return (permuted, rows)


def draw_row_tile(key, part):
    return owner_helper(key)[1]


def draw_owner_map(key, part):
    return owner_helper(key)[0]


def with_ends(array, stream_key, low, largest):
    longest = array.shape.index(max(array.shape))
    spots = []
    for shift in (0, 1):
        where = [jax.random.randint(jax.random.fold_in(stream_key, axis), (), 0, length) for axis, length in enumerate(array.shape)]
        where[longest] = (where[longest] + shift) % array.shape[longest]
        spots.append(tuple(where))
    return array.at[spots[0]].set(low).at[spots[1]].set(largest)


def block_scale(stream_key, extent, cuts, least, largest):
    level, own = 1.0, jax.random.fold_in(stream_key, 6)
    for dim, blocks in cuts:
        draws = jnp.exp(jax.random.uniform(jax.random.fold_in(own, dim), (blocks,), jnp.float32, least / len(cuts), largest / len(cuts)))
        level = level * jnp.repeat(draws, extent[dim] // blocks).reshape([-1 if axis == dim else 1 for axis in range(len(extent))])
    return level


def centred(rng, shape, spread, reach, cuts=(), kind=jnp.bfloat16):
    result = jax.random.normal(rng, shape, jnp.float32) * spread
    if len(cuts) > 0:
        result = block_scale(rng, shape, cuts, -0.22, 0.18) * result
    return jnp.clip(result, min=-reach, max=reach).astype(kind)


def setup_inputs(seed: int = 0) -> dict:
    splits = jax.random.split(jax.random.key(seed), 6)
    return {
        "tiles": centred(splits[0], (CONTRIBS, TILE, TILE), 0.1, 0.59765625, ((0, 32),)),
        "contraction": with_ends(jax.random.randint(splits[1], (CONTRIBS,), 0, K_TILES), jax.random.fold_in(splits[1], 1), 0, K_TILES - 1).astype(jnp.int32),
        "row_tile": draw_row_tile(jax.random.fold_in(splits[5], 71), 0),
        "owner_map": draw_owner_map(jax.random.fold_in(splits[5], 71), 0),
        "panel": centred(splits[4], (K_TILES * TILE, COL_TILES * TILE), 0.09, 0.5390625, ((0, 4),)),
    }


def reference(tiles, contraction, row_tile, owner_map, panel):
    columns = panel.shape[1]
    panel_tiles = panel.reshape(K_TILES, TILE, columns)
    position = owner_map[row_tile].astype(jnp.int32)
    groups = CONTRIBS // TILE_DEV

    def step(summed, item):
        block_tiles, block_k, block_pos = item
        chosen = panel_tiles[block_k].astype(jnp.float32)
        products = jnp.einsum("sab,sbc->sac", block_tiles.astype(jnp.float32), chosen, precision=lax.Precision.HIGHEST)
        return summed.at[block_pos].add(products), None

    start = jnp.zeros((ROW_TILES, TILE, columns), jnp.float32)
    summed, unused = lax.scan(step, start, (tiles.reshape(groups, TILE_DEV, TILE, TILE), contraction.reshape(groups, TILE_DEV), position.reshape(groups, TILE_DEV)))
    return summed.reshape(ROW_TILES * TILE, columns)
```

```python
import functools
import math

import jax
import jax.numpy as jnp
from jax import lax
from jax.experimental import pallas as pl
from jax.experimental.pallas import tpu as pltpu
from jax.sharding import PartitionSpec as P

MIB = 1024 * 1024
CODE_ROWS = 16
CODE_STEPS = 256.0
TOP = 32000.0
CHUNK = 256
UNROLL = 2
LOG2 = math.log(2.0)


def place_slots(row_ids, owner_map, out_dev):
    table_ids = jnp.arange(owner_map.shape[0], dtype=jnp.int32)
    position = jnp.sum(jnp.where(row_ids[..., None] == table_ids, owner_map, 0), axis=-1)
    target = position // out_dev
    serial = jnp.arange(row_ids.shape[-1], dtype=jnp.int32)
    earlier = (target[..., :, None] == target[..., None, :]) & (serial[:, None] > serial[None, :])
    ranking = jnp.sum(earlier.astype(jnp.int32), axis=-1)
    return (position % out_dev, target, ranking)


def add_products(summed, arrived, slot_labels, panel_tiles):
    slot_count = arrived.shape[0]
    block_rows = math.gcd(slot_count, 32)
    out_dev = summed.shape[0]
    local_ids = jnp.arange(out_dev, dtype=jnp.int32)

    def one_block(which_block, running, source_tiles, source_labels):
        part_tiles = lax.dynamic_slice_in_dim(source_tiles, which_block * block_rows, block_rows, 0)
        part_labels = lax.dynamic_slice_in_dim(
            source_labels, which_block * block_rows, block_rows, 0
        )
        chosen = jnp.take(panel_tiles, part_labels[:, 1], axis=0)
        products = jnp.einsum(
            "sab,sbc->sac", part_tiles, chosen, preferred_element_type=jnp.float32
        )
        row_hits = (part_labels[:, 0][:, None] == local_ids[None, :]).astype(jnp.float32)
        return running + jnp.einsum(
            "sr,sac->rac", row_hits, products, precision=lax.Precision.HIGHEST
        )

    return lax.fori_loop(
        0,
        slot_count // block_rows,
        lambda which_block, running: one_block(which_block, running, arrived, slot_labels),
        summed,
    )


def slots_plan(tiles, contraction, row_tile, owner_map, panel):
    wide_count = lax.axis_size("wide")
    tile_dev = tiles.shape[0]
    tile_side = tiles.shape[1]
    out_dev = owner_map.shape[0] // wide_count
    most_slots = tile_dev * 8 // (3 * wide_count)
    slot_total = wide_count * most_slots
    local_row, target, ranking = place_slots(row_tile, owner_map, out_dev)
    slot_index = target * most_slots + ranking
    outgoing = jnp.zeros((slot_total, tile_side, tile_side), tiles.dtype).at[slot_index].set(tiles)
    all_rows, all_contraction = (
        lax.all_gather(row_tile, "wide", axis=0, tiled=True),
        lax.all_gather(contraction, "wide", axis=0, tiled=True),
    )
    all_rows = all_rows.reshape(wide_count, tile_dev)
    all_contraction = all_contraction.reshape(wide_count, tile_dev)
    source_local, source_target, source_rank = place_slots(all_rows, owner_map, out_dev)
    source_ids = jnp.arange(wide_count, dtype=jnp.int32)
    mine = source_target == lax.axis_index("wide")
    arrive_index = jnp.where(mine, source_ids[:, None] * most_slots + source_rank, slot_total)
    label_pairs = jnp.stack([source_local, all_contraction], axis=-1).reshape(
        wide_count * tile_dev, 2
    )
    vacant_label = jnp.stack(
        [jnp.full((slot_total,), out_dev, jnp.int32), jnp.zeros((slot_total,), jnp.int32)], axis=1
    )
    arrived_labels = vacant_label.at[arrive_index.reshape(-1)].set(label_pairs, mode="drop")
    gathered = lax.all_gather(panel, "grp", axis=0, tiled=True)
    panel_tiles = gathered.reshape(gathered.shape[0] // tile_side, tile_side, gathered.shape[1])
    summed = jnp.zeros((out_dev, tile_side, gathered.shape[1]), jnp.float32)
    arrived = lax.all_to_all(outgoing, "wide", split_axis=0, concat_axis=0, tiled=True)
    summed = add_products(summed, arrived, arrived_labels, panel_tiles)
    summed = lax.psum(summed, "grp")
    return summed.reshape(out_dev * tile_side, gathered.shape[1])


def encode(value):
    largest = jnp.max(jnp.abs(value), axis=0, keepdims=True)
    code = jnp.ceil(jnp.log(jnp.maximum(largest, 1e-30)) * (CODE_STEPS / LOG2))
    scale = jnp.exp(code * (-LOG2 / CODE_STEPS)) * TOP
    whole = jnp.round(value * scale).astype(jnp.int32).astype(jnp.int16)
    return whole, code.astype(jnp.int32)


def code_slab(code):
    return jnp.broadcast_to(code, (CODE_ROWS, code.shape[1])).astype(jnp.int16)


def column_scale(slab):
    code = slab.astype(jnp.int32).astype(jnp.float32)[:1]
    return jnp.exp(code * (LOG2 / CODE_STEPS)) * (1.0 / TOP)


def decode(whole, scale):
    return whole.astype(jnp.int32).astype(jnp.float32) * scale


def products_kernel(
    nz, count_ref, source_ref, slot_ref, label_ref,
    own_tiles, sib_tiles, own_panel, d1, d2, d3, s1, s2, s3,
    send_a, send_b, keep, stack, acc,
):
    side = own_tiles.shape[1]
    shard = own_panel.shape[0] // side
    half = shard // 2
    for t in range(shard):
        stack[t] = own_panel[pl.ds(t * side, side), :]
    for d, (near, far) in enumerate(((d1, s1), (d2, s2), (d3, s3)), 1):
        for t in range(half):
            stack[d * shard + t] = near[pl.ds(t * side, side), :]
            stack[d * shard + half + t] = far[pl.ds(t * side, side), :]

    @pl.loop(0, acc.shape[0])
    def _(i):
        acc[i] = jnp.zeros(acc.shape[1:], jnp.float32)

    for which, tiles in enumerate((own_tiles, sib_tiles)):

        @pl.loop(0, (count_ref[which] + UNROLL - 1) // UNROLL)
        def _(i, which=which, tiles=tiles):
            found = []
            for u in range(UNROLL):
                at = i * UNROLL + u
                found.append(
                    jnp.dot(
                        tiles[source_ref[which, at]],
                        stack[label_ref[which, at]],
                        preferred_element_type=jnp.float32,
                    )
                )
            for u in range(UNROLL):
                at = i * UNROLL + u
                acc[slot_ref[which, at]] += found[u]

    for first, send in ((0, send_a), (nz, send_b)):

        @pl.loop(0, nz)
        def _(i, first=first, send=send):
            whole, code = encode(acc[first + i])
            send[i, pl.ds(0, side), :] = whole
            send[i, pl.ds(side, CODE_ROWS), :] = code_slab(code)

    @pl.loop(0, 2 * nz)
    def _(i):
        keep[i] = acc[2 * nz + i]


def plane_kernel(nz, spot_ref, recv_a, recv_b, keep, send_a, send_b, kept):
    side = keep.shape[1]
    part = side // 2
    for first, axis, recv, send in ((0, 1, recv_a, send_a), (nz, 0, recv_b, send_b)):
        bit = spot_ref[axis]
        mine = pl.multiple_of(bit * part, part)
        other = pl.multiple_of((1 - bit) * part, part)

        @pl.loop(0, nz)
        def _(i, first=first, recv=recv, send=send, mine=mine, other=other):
            scale = column_scale(recv[i, pl.ds(side, CODE_ROWS), :])
            whole, code = encode(
                keep[first + i, pl.ds(other, part), :]
                + decode(recv[i, pl.ds(other, part), :], scale)
            )
            send[i, pl.ds(0, part), :] = whole
            send[i, pl.ds(part, CODE_ROWS), :] = code_slab(code)
            kept[first + i] = keep[first + i, pl.ds(mine, part), :] + decode(
                recv[i, pl.ds(mine, part), :], scale
            )


def line_kernel(nz, spot_ref, recv_a, recv_b, kept, *outs):
    part = kept.shape[1]
    here = spot_ref[2]

    def total(z):
        parts = []
        for first, recv in ((0, recv_a), (nz, recv_b)):
            scale = column_scale(recv[z, pl.ds(part, CODE_ROWS), :])
            parts.append(kept[first + z] + decode(recv[z, pl.ds(0, part), :], scale))
        return jnp.concatenate(parts, axis=0)

    for d in range(1, nz):
        whole, code = encode(total(lax.rem(here + d, nz)))
        outs[d - 1][pl.ds(0, 2 * part), :] = whole
        outs[d - 1][pl.ds(2 * part, CODE_ROWS), :] = code_slab(code)
    outs[nz - 1][...] = total(here)


def finish_kernel(nz, *refs):
    recvs, own, out = refs[: nz - 1], refs[nz - 1], refs[nz]
    side = own.shape[0]
    value = own[...]
    for recv in recvs:
        value += decode(recv[pl.ds(0, side), :], column_scale(recv[pl.ds(side, CODE_ROWS), :]))
    whole, code = encode(value)
    out[pl.ds(0, side), :] = whole
    out[pl.ds(side, CODE_ROWS), :] = code_slab(code)


def spread_kernel(spot_ref, *refs):
    blocks, out = refs[:4], refs[-1]
    side = blocks[0].shape[0] - CODE_ROWS
    part = side // 2
    for d, block in enumerate(blocks):
        x = spot_ref[0] if d % 2 == 0 else 1 - spot_ref[0]
        y = spot_ref[1] if d // 2 == 0 else 1 - spot_ref[1]
        scale = column_scale(block[pl.ds(side, CODE_ROWS), :])
        at_a = pl.multiple_of(x * side + y * part, part)
        at_b = pl.multiple_of((2 + y) * side + x * part, part)
        out[pl.ds(at_a, part), :] = decode(block[pl.ds(0, part), :], scale)
        out[pl.ds(at_b, part), :] = decode(block[pl.ds(part, part), :], scale)


def in_vmem(count):
    return [pl.BlockSpec(memory_space=pltpu.VMEM)] * count


def in_smem(count):
    return [pl.BlockSpec(memory_space=pltpu.SMEM)] * count


def shape(dims, kind):
    return jax.ShapeDtypeStruct(dims, kind)


def params(mib):
    return pltpu.CompilerParams(vmem_limit_bytes=mib * MIB)


def cost(flops, moved):
    return pl.CostEstimate(flops=flops, bytes_accessed=moved, transcendentals=0)


def compact(match, values):
    count = match.shape[-1]
    rank = jnp.cumsum(match.astype(jnp.int32), axis=-1) - 1
    at = jnp.arange(count + UNROLL, dtype=jnp.int32)
    hit = match[:, None, :] & (rank[:, None, :] == at[None, :, None])
    filled = jnp.any(hit, axis=-1)
    return filled, [jnp.sum(jnp.where(hit, v[:, None, :], 0), axis=-1) for v in values]


def sums_plan(tiles, contraction, row_tile, owner_map, panel):
    wide_count = lax.axis_size("wide")
    nz = wide_count // 2
    tile_dev, side = tiles.shape[0], tiles.shape[1]
    out_dev = owner_map.shape[0] // wide_count
    rows, columns = panel.shape
    shard = rows // side
    chunks = columns // CHUNK
    part = side // 2
    g, w = lax.axis_index("grp"), lax.axis_index("wide")
    x, y, z, core = g % 2, g // 2, w // 2, w % 2
    spot = jnp.stack([x, y, z]).astype(jnp.int32)

    def to_core(v):
        return lax.ppermute(v, "wide", [(i, i ^ 1) for i in range(wide_count)])

    def to_grp(v, d):
        return lax.ppermute(v, "grp", [(i, i ^ d) for i in range(4)])

    def to_line(v, d):
        return lax.ppermute(
            v, "wide", [(i, (i + 2 * d) % wide_count) for i in range(wide_count)]
        )

    near, far = [], []
    for j in range(chunks):
        mine = lax.dynamic_slice(panel, (core * (rows // 2), j * CHUNK), (rows // 2, CHUNK))
        near.append([to_grp(mine, d) for d in (1, 2, 3)])

    labels = jnp.stack([row_tile, contraction])
    both = jnp.stack([labels, to_core(labels)])
    sib_tiles = to_core(tiles)
    for j in range(chunks):
        far.append([to_core(v) for v in near[j]])

    table_ids = jnp.arange(owner_map.shape[0], dtype=jnp.int32)
    position = jnp.sum(jnp.where(both[:, 0, :, None] == table_ids, owner_map, 0), axis=-1)
    owner, local = position // out_dev, position % out_dev
    is_b, bit = local // 2, local % 2
    kept_here = bit == jnp.where(is_b == 1, y, x)
    slot = jnp.where(kept_here, 2 * nz, 0) + is_b * nz + owner // 2
    k = both[:, 1]
    apart, inner = (k // shard) ^ g, k % shard
    half = shard // 2
    crossed = jnp.where(inner // half == core, 0, half) + inner % half
    label = jnp.where(apart == 0, inner, apart * shard + crossed)
    match = owner % 2 == core
    serial = jnp.broadcast_to(jnp.arange(tile_dev, dtype=jnp.int32), match.shape)
    filled, (source, slot, label) = compact(match, [serial, slot, label])
    slot = jnp.where(filled, slot, 4 * nz)
    count = jnp.sum(match.astype(jnp.int32), axis=-1)

    result = None
    for j in range(chunks):
        send_a, send_b, keep = pl.pallas_call(
            functools.partial(products_kernel, nz),
            grid=(1,),
            in_specs=in_smem(4)
            + in_vmem(2)
            + [pl.BlockSpec((rows, CHUNK), lambda i, j=j: (0, j))]
            + in_vmem(6),
            out_specs=in_vmem(3),
            out_shape=[
                shape((nz, side + CODE_ROWS, CHUNK), jnp.int16),
                shape((nz, side + CODE_ROWS, CHUNK), jnp.int16),
                shape((2 * nz, side, CHUNK), jnp.float32),
            ],
            scratch_shapes=[
                pltpu.VMEM((4 * shard, side, CHUNK), panel.dtype),
                pltpu.VMEM((4 * nz + 1, side, CHUNK), jnp.float32),
            ],
            compiler_params=params(48),
            cost_estimate=cost(
                2 * tile_dev * side * side * CHUNK, 4 * tile_dev * side * side
            ),
            name="products",
        )(count, source, slot, label, tiles, sib_tiles, panel, *near[j], *far[j])

        send_a, send_b, kept = pl.pallas_call(
            functools.partial(plane_kernel, nz),
            in_specs=in_smem(1) + in_vmem(3),
            out_specs=in_vmem(3),
            out_shape=[
                shape((nz, part + CODE_ROWS, CHUNK), jnp.int16),
                shape((nz, part + CODE_ROWS, CHUNK), jnp.int16),
                shape((2 * nz, part, CHUNK), jnp.float32),
            ],
            compiler_params=params(16),
            cost_estimate=cost(10 * 2 * nz * side * CHUNK, 8 * 2 * nz * side * CHUNK),
            name="plane",
        )(spot, to_grp(send_a, 1), to_grp(send_b, 2), keep)

        *sends, own = pl.pallas_call(
            functools.partial(line_kernel, nz),
            in_specs=in_smem(1) + in_vmem(3),
            out_specs=in_vmem(nz),
            out_shape=[shape((side + CODE_ROWS, CHUNK), jnp.int16)] * (nz - 1)
            + [shape((side, CHUNK), jnp.float32)],
            compiler_params=params(16),
            cost_estimate=cost(10 * nz * side * CHUNK, 8 * nz * side * CHUNK),
            name="line",
        )(spot, to_grp(send_a, 2), to_grp(send_b, 1), kept)

        done = pl.pallas_call(
            functools.partial(finish_kernel, nz),
            in_specs=in_vmem(nz),
            out_specs=pl.BlockSpec(memory_space=pltpu.VMEM),
            out_shape=shape((side + CODE_ROWS, CHUNK), jnp.int16),
            compiler_params=params(16),
            cost_estimate=cost(10 * nz * side * CHUNK, 4 * nz * side * CHUNK),
            name="finish",
        )(*[to_line(v, d) for d, v in enumerate(sends, 1)], own)

        blocks = [done] + [to_grp(done, d) for d in (1, 2, 3)]
        earlier = [] if result is None else [result]
        result = pl.pallas_call(
            spread_kernel,
            grid=(1,),
            in_specs=in_smem(1) + in_vmem(4) + [pl.BlockSpec(memory_space=pl.ANY)] * len(earlier),
            out_specs=pl.BlockSpec((out_dev * side, CHUNK), lambda i, j=j: (0, j)),
            out_shape=shape((out_dev * side, columns), jnp.float32),
            input_output_aliases={5: 0} if earlier else {},
            compiler_params=params(16),
            cost_estimate=cost(4 * out_dev * side * CHUNK, 6 * out_dev * side * CHUNK),
            name="spread",
        )(spot, *blocks, *earlier)
    return result


def per_device(tiles, contraction, row_tile, owner_map, panel):
    dense = owner_map.shape[0] <= tiles.shape[0]
    fits = lax.axis_size("grp") == 4 and lax.axis_size("wide") % 2 == 0
    out_dev = owner_map.shape[0] // lax.axis_size("wide")
    if dense and fits and out_dev == 4 and panel.shape[1] % CHUNK == 0:
        return sums_plan(tiles, contraction, row_tile, owner_map, panel)
    return slots_plan(tiles, contraction, row_tile, owner_map, panel)


def solution(mesh):
    return jax.shard_map(
        per_device,
        mesh=mesh,
        in_specs=(
            P(("grp", "wide"), None, None),
            P(("grp", "wide")),
            P(("grp", "wide")),
            P(),
            P("grp", None),
        ),
        out_specs=P("wide", None),
        check_vma=False,
    )
```

```python
import functools
import math

import jax
import jax.numpy as jnp
from jax import lax
from jax.experimental import pallas as pl
from jax.experimental.pallas import tpu as pltpu
from jax.sharding import PartitionSpec as P

MIB = 1024 * 1024
CODE_ROWS = 16
CODE_STEPS = 256.0
TOP = 32000.0
CHUNK = 256
UNROLL = 4
LOG2 = math.log(2.0)


def place_slots(row_ids, owner_map, out_dev):
    table_ids = jnp.arange(owner_map.shape[0], dtype=jnp.int32)
    position = jnp.sum(jnp.where(row_ids[..., None] == table_ids, owner_map, 0), axis=-1)
    target = position // out_dev
    serial = jnp.arange(row_ids.shape[-1], dtype=jnp.int32)
    earlier = (target[..., :, None] == target[..., None, :]) & (serial[:, None] > serial[None, :])
    ranking = jnp.sum(earlier.astype(jnp.int32), axis=-1)
    return (position % out_dev, target, ranking)


def add_products(summed, arrived, slot_labels, panel_tiles):
    slot_count = arrived.shape[0]
    block_rows = math.gcd(slot_count, 32)
    out_dev = summed.shape[0]
    local_ids = jnp.arange(out_dev, dtype=jnp.int32)

    def one_block(which_block, running, source_tiles, source_labels):
        part_tiles = lax.dynamic_slice_in_dim(source_tiles, which_block * block_rows, block_rows, 0)
        part_labels = lax.dynamic_slice_in_dim(
            source_labels, which_block * block_rows, block_rows, 0
        )
        chosen = jnp.take(panel_tiles, part_labels[:, 1], axis=0)
        products = jnp.einsum(
            "sab,sbc->sac", part_tiles, chosen, preferred_element_type=jnp.float32
        )
        row_hits = (part_labels[:, 0][:, None] == local_ids[None, :]).astype(jnp.float32)
        return running + jnp.einsum(
            "sr,sac->rac", row_hits, products, precision=lax.Precision.HIGHEST
        )

    return lax.fori_loop(
        0,
        slot_count // block_rows,
        lambda which_block, running: one_block(which_block, running, arrived, slot_labels),
        summed,
    )


def slots_plan(tiles, contraction, row_tile, owner_map, panel):
    wide_count = lax.axis_size("wide")
    tile_dev = tiles.shape[0]
    tile_side = tiles.shape[1]
    out_dev = owner_map.shape[0] // wide_count
    most_slots = tile_dev * 8 // (3 * wide_count)
    slot_total = wide_count * most_slots
    local_row, target, ranking = place_slots(row_tile, owner_map, out_dev)
    slot_index = target * most_slots + ranking
    outgoing = jnp.zeros((slot_total, tile_side, tile_side), tiles.dtype).at[slot_index].set(tiles)
    all_rows, all_contraction = (
        lax.all_gather(row_tile, "wide", axis=0, tiled=True),
        lax.all_gather(contraction, "wide", axis=0, tiled=True),
    )
    all_rows = all_rows.reshape(wide_count, tile_dev)
    all_contraction = all_contraction.reshape(wide_count, tile_dev)
    source_local, source_target, source_rank = place_slots(all_rows, owner_map, out_dev)
    source_ids = jnp.arange(wide_count, dtype=jnp.int32)
    mine = source_target == lax.axis_index("wide")
    arrive_index = jnp.where(mine, source_ids[:, None] * most_slots + source_rank, slot_total)
    label_pairs = jnp.stack([source_local, all_contraction], axis=-1).reshape(
        wide_count * tile_dev, 2
    )
    vacant_label = jnp.stack(
        [jnp.full((slot_total,), out_dev, jnp.int32), jnp.zeros((slot_total,), jnp.int32)], axis=1
    )
    arrived_labels = vacant_label.at[arrive_index.reshape(-1)].set(label_pairs, mode="drop")
    gathered = lax.all_gather(panel, "grp", axis=0, tiled=True)
    panel_tiles = gathered.reshape(gathered.shape[0] // tile_side, tile_side, gathered.shape[1])
    summed = jnp.zeros((out_dev, tile_side, gathered.shape[1]), jnp.float32)
    arrived = lax.all_to_all(outgoing, "wide", split_axis=0, concat_axis=0, tiled=True)
    summed = add_products(summed, arrived, arrived_labels, panel_tiles)
    summed = lax.psum(summed, "grp")
    return summed.reshape(out_dev * tile_side, gathered.shape[1])


def encode(value):
    largest = jnp.max(jnp.abs(value), axis=0, keepdims=True)
    code = jnp.ceil(jnp.log(jnp.maximum(largest, 1e-30)) * (CODE_STEPS / LOG2))
    scale = jnp.exp(code * (-LOG2 / CODE_STEPS)) * TOP
    whole = jnp.round(value * scale).astype(jnp.int32).astype(jnp.int16)
    return whole, code.astype(jnp.int32)


def put_encoded(ref, value):
    side = value.shape[0]
    whole, code = encode(value)
    ref[pl.ds(0, side), :] = whole
    ref[pl.ds(side, CODE_ROWS), :] = jnp.broadcast_to(
        code, (CODE_ROWS, code.shape[1])
    ).astype(jnp.int16)


def get_decoded(ref, side):
    code = ref[pl.ds(side, CODE_ROWS), :].astype(jnp.int32).astype(jnp.float32)[:1]
    scale = jnp.exp(code * (LOG2 / CODE_STEPS)) * (1.0 / TOP)
    return ref[pl.ds(0, side), :].astype(jnp.int32).astype(jnp.float32) * scale


def products_kernel(
    pieces, ends_ref, source_ref, slot_ref, label_ref,
    own_tiles, sib_tiles, own_panel, d1, d2, d3, s1, s2, s3,
    send, keep, held, stack, acc, sems,
):
    tile_dev, side = held.shape[1], held.shape[2]
    shard = own_panel.shape[0] // side
    half = shard // 2
    outs = send.shape[0]
    copies = []
    for q, (which, first, count) in enumerate(pieces):
        tiles = (own_tiles, sib_tiles)[which]
        copies.append(
            pltpu.make_async_copy(
                tiles.at[pl.ds(first, count)], held.at[which, pl.ds(first, count)], sems.at[q]
            )
        )
        copies[-1].start()
    for t in range(shard):
        stack[t] = own_panel[pl.ds(t * side, side), :]
    for d, (near, far) in enumerate(((d1, s1), (d2, s2), (d3, s3)), 1):
        for t in range(half):
            stack[d * shard + t] = near[pl.ds(t * side, side), :]
            stack[d * shard + half + t] = far[pl.ds(t * side, side), :]

    @pl.loop(0, acc.shape[0])
    def _(i):
        acc[i] = jnp.zeros(acc.shape[1:], jnp.float32)

    def some(which, at, count):
        found = [
            jnp.dot(
                held[which, source_ref[which, at + u]],
                stack[label_ref[which, at + u]],
                preferred_element_type=jnp.float32,
            )
            for u in range(count)
        ]
        for u in range(count):
            acc[slot_ref[which, at + u]] += found[u]

    for q, (which, first, count) in enumerate(pieces):
        copies[q].wait()
        begin = 0 if first == 0 else ends_ref[q - 1]
        end = ends_ref[q]
        rounds = (end - begin) // UNROLL

        @pl.loop(0, rounds)
        def _(i, which=which, begin=begin):
            some(which, begin + i * UNROLL, UNROLL)

        @pl.loop(begin + rounds * UNROLL, end)
        def _(i, which=which):
            some(which, i, 1)

    @pl.loop(0, outs)
    def _(i):
        put_encoded(send.at[i], acc[i])

    @pl.loop(0, outs)
    def _(i):
        keep[i] = acc[outs + i]


def stage_kernel(low, bit_ref, recv, kept, send, keep):
    side = kept.shape[1]
    bit = bit_ref[0]

    @pl.loop(0, send.shape[0])
    def _(i):
        base = (i // low) * (2 * low) + i % low
        other, mine = base + (1 - bit) * low, base + bit * low
        put_encoded(send.at[i], kept[other] + get_decoded(recv.at[other], side))
        keep[i] = kept[mine] + get_decoded(recv.at[mine], side)


def finish_kernel(recv, kept, out):
    put_encoded(out, kept[0] + get_decoded(recv.at[0], kept.shape[1]))


def spread_kernel(*refs):
    blocks, out = refs[0], refs[-1]
    side = blocks.shape[1] - CODE_ROWS
    for i in range(blocks.shape[0]):
        out[pl.ds(i * side, side), :] = get_decoded(blocks.at[i], side)


def in_vmem(count):
    return [pl.BlockSpec(memory_space=pltpu.VMEM)] * count


def in_smem(count):
    return [pl.BlockSpec(memory_space=pltpu.SMEM)] * count


def in_any(count):
    return [pl.BlockSpec(memory_space=pl.ANY)] * count


def shape(dims, kind):
    return jax.ShapeDtypeStruct(dims, kind)


def params(mib):
    return pltpu.CompilerParams(vmem_limit_bytes=mib * MIB)


def cost(flops, moved):
    return pl.CostEstimate(flops=flops, bytes_accessed=moved, transcendentals=0)


def compact(match, values):
    count = match.shape[-1]
    rank = jnp.cumsum(match.astype(jnp.int32), axis=-1) - 1
    at = jnp.arange(count, dtype=jnp.int32)
    hit = match[:, None, :] & (rank[:, None, :] == at[None, :, None])
    return [jnp.sum(jnp.where(hit, v[:, None, :], 0), axis=-1) for v in values]


def sums_plan(tiles, contraction, row_tile, owner_map, panel):
    wide_count = lax.axis_size("wide")
    tile_dev, side = tiles.shape[0], tiles.shape[1]
    out_dev = owner_map.shape[0] // wide_count
    rows, columns = panel.shape
    shard = rows // side
    chunks = columns // CHUNK
    sums = owner_map.shape[0] // 2
    g, w = lax.axis_index("grp"), lax.axis_index("wide")
    core = w % 2

    def to_core(v):
        return lax.ppermute(v, "wide", [(i, i ^ 1) for i in range(wide_count)])

    def to_grp(v, d):
        return lax.ppermute(v, "grp", [(i, i ^ d) for i in range(4)])

    dims = {
        "x": (0, g % 2, lambda v: to_grp(v, 1)),
        "y": (1, g // 2, lambda v: to_grp(v, 2)),
    }
    for b in range((wide_count // 2).bit_length() - 1):
        pairs = [(i, i ^ (2 << b)) for i in range(wide_count)]
        dims["z%d" % b] = (
            2 + b,
            (w // (2 << b)) % 2,
            lambda v, pairs=pairs: lax.ppermute(v, "wide", pairs),
        )
    rest = [name for name in dims if name not in ("x", "y", "z0")]
    orders = [["x", "y", "z0"] + rest, ["y", "x", "z0"] + rest, ["z0", "y", "x"] + rest]

    labels = jnp.stack([row_tile, contraction])
    both = jnp.stack([labels, to_core(labels)])
    sib_tiles = to_core(tiles)

    near, far = [], []
    for j in range(chunks):
        mine = lax.dynamic_slice(panel, (core * (rows // 2), j * CHUNK), (rows // 2, CHUNK))
        if j > 0:
            mine, *near[j - 1] = lax.optimization_barrier((mine, *near[j - 1]))
        near.append([to_grp(mine, d) for d in (1, 2, 3)])
    for j in range(chunks):
        far.append([to_core(v) for v in near[j]])

    table_ids = jnp.arange(owner_map.shape[0], dtype=jnp.int32)
    position = jnp.sum(jnp.where(both[:, 0, :, None] == table_ids, owner_map, 0), axis=-1)
    owner, local = position // out_dev, position % out_dev
    index = (owner // 2) * out_dev + local
    k = both[:, 1]
    apart, inner = (k // shard) ^ g, k % shard
    half = shard // 2
    crossed = jnp.where(inner // half == core, 0, half) + inner % half
    label = jnp.where(apart == 0, inner, apart * shard + crossed)
    match = owner % 2 == core
    serial = jnp.broadcast_to(jnp.arange(tile_dev, dtype=jnp.int32), match.shape)
    source, index, label = compact(match, [serial, index, label])
    cut = tile_dev // 4
    pieces = ((0, 0, cut), (0, cut, tile_dev - cut), (1, 0, tile_dev))
    ends = jnp.stack(
        [
            jnp.sum((match[which] & (serial[which] < first + count)).astype(jnp.int32))
            for which, first, count in pieces
        ]
    )

    result = None
    for j in range(chunks):
        order = orders[j % len(orders)]
        left = ["z%d" % b for b in reversed(range(len(dims) - 2))] + ["y", "x"]
        bit, own_bit, move = dims[order[0]]
        low = 1 << bit
        kept_here = (index // low) % 2 == own_bit
        slot = (index // (2 * low)) * low + index % low + jnp.where(kept_here, sums // 2, 0)
        left.remove(order[0])
        send, keep = pl.pallas_call(
            functools.partial(products_kernel, pieces),
            grid=(1,),
            in_specs=in_smem(4)
            + in_any(2)
            + [pl.BlockSpec((rows, CHUNK), lambda i, j=j: (0, j))]
            + in_vmem(6),
            out_specs=in_vmem(2),
            out_shape=[
                shape((sums // 2, side + CODE_ROWS, CHUNK), jnp.int16),
                shape((sums // 2, side, CHUNK), jnp.float32),
            ],
            scratch_shapes=[
                pltpu.VMEM((2, tile_dev, side, side), tiles.dtype),
                pltpu.VMEM((4 * shard, side, CHUNK), panel.dtype),
                pltpu.VMEM((sums, side, CHUNK), jnp.float32),
                pltpu.SemaphoreType.DMA((len(pieces),)),
            ],
            compiler_params=params(40),
            cost_estimate=cost(
                2 * tile_dev * side * side * CHUNK, 4 * tile_dev * side * side
            ),
            name="products",
        )(ends, source, slot, label, tiles, sib_tiles, panel, *near[j], *far[j])

        for name in order[1:]:
            recv = move(send)
            _, own_bit, move = dims[name]
            low = 1 << (len(left) - 1 - left.index(name))
            left.remove(name)
            count = keep.shape[0] // 2
            send, keep = pl.pallas_call(
                functools.partial(stage_kernel, low),
                in_specs=in_smem(1) + in_vmem(2),
                out_specs=in_vmem(2),
                out_shape=[
                    shape((count, side + CODE_ROWS, CHUNK), jnp.int16),
                    shape((count, side, CHUNK), jnp.float32),
                ],
                compiler_params=params(16),
                cost_estimate=cost(20 * count * side * CHUNK, 18 * count * side * CHUNK),
                name="stage",
            )(own_bit.astype(jnp.int32)[None], recv, keep)

        done = pl.pallas_call(
            finish_kernel,
            in_specs=in_vmem(2),
            out_specs=pl.BlockSpec(memory_space=pltpu.VMEM),
            out_shape=shape((side + CODE_ROWS, CHUNK), jnp.int16),
            compiler_params=params(16),
            cost_estimate=cost(20 * side * CHUNK, 8 * side * CHUNK),
            name="finish",
        )(move(send), keep)

        blocks = lax.all_gather(done, "grp", axis=0)
        earlier = [] if result is None else [result]
        result = pl.pallas_call(
            spread_kernel,
            grid=(1,),
            in_specs=in_vmem(1) + in_any(len(earlier)),
            out_specs=pl.BlockSpec((out_dev * side, CHUNK), lambda i, j=j: (0, j)),
            out_shape=shape((out_dev * side, columns), jnp.float32),
            input_output_aliases={1: 0} if earlier else {},
            compiler_params=params(16),
            cost_estimate=cost(4 * out_dev * side * CHUNK, 6 * out_dev * side * CHUNK),
            name="spread",
        )(blocks, *earlier)
    return result


def per_device(tiles, contraction, row_tile, owner_map, panel):
    dense = owner_map.shape[0] <= tiles.shape[0]
    wide_count = lax.axis_size("wide")
    fits = lax.axis_size("grp") == 4 and wide_count >= 4 and wide_count & (wide_count - 1) == 0
    out_dev = owner_map.shape[0] // wide_count
    if dense and fits and out_dev == 4 and panel.shape[1] % CHUNK == 0:
        return sums_plan(tiles, contraction, row_tile, owner_map, panel)
    return slots_plan(tiles, contraction, row_tile, owner_map, panel)


def solution(mesh):
    return jax.shard_map(
        per_device,
        mesh=mesh,
        in_specs=(
            P(("grp", "wide"), None, None),
            P(("grp", "wide")),
            P(("grp", "wide")),
            P(),
            P("grp", None),
        ),
        out_specs=P("wide", None),
        check_vma=False,
    )
```

```python
import functools
import math

import jax
import jax.numpy as jnp
from jax import lax
from jax.experimental import pallas as pl
from jax.experimental.pallas import tpu as pltpu
from jax.sharding import PartitionSpec as P

MIB = 1024 * 1024
CODE_ROWS = 16
CODE_STEPS = 256.0
TOP = 32000.0
CHUNK = 256
UNROLL = 4
LOG2 = math.log(2.0)


def place_slots(row_ids, owner_map, out_dev):
    table_ids = jnp.arange(owner_map.shape[0], dtype=jnp.int32)
    position = jnp.sum(jnp.where(row_ids[..., None] == table_ids, owner_map, 0), axis=-1)
    target = position // out_dev
    serial = jnp.arange(row_ids.shape[-1], dtype=jnp.int32)
    earlier = (target[..., :, None] == target[..., None, :]) & (serial[:, None] > serial[None, :])
    ranking = jnp.sum(earlier.astype(jnp.int32), axis=-1)
    return (position % out_dev, target, ranking)


def add_products(summed, arrived, slot_labels, panel_tiles):
    slot_count = arrived.shape[0]
    block_rows = math.gcd(slot_count, 32)
    out_dev = summed.shape[0]
    local_ids = jnp.arange(out_dev, dtype=jnp.int32)

    def one_block(which_block, running, source_tiles, source_labels):
        part_tiles = lax.dynamic_slice_in_dim(source_tiles, which_block * block_rows, block_rows, 0)
        part_labels = lax.dynamic_slice_in_dim(
            source_labels, which_block * block_rows, block_rows, 0
        )
        chosen = jnp.take(panel_tiles, part_labels[:, 1], axis=0)
        products = jnp.einsum(
            "sab,sbc->sac", part_tiles, chosen, preferred_element_type=jnp.float32
        )
        row_hits = (part_labels[:, 0][:, None] == local_ids[None, :]).astype(jnp.float32)
        return running + jnp.einsum(
            "sr,sac->rac", row_hits, products, precision=lax.Precision.HIGHEST
        )

    return lax.fori_loop(
        0,
        slot_count // block_rows,
        lambda which_block, running: one_block(which_block, running, arrived, slot_labels),
        summed,
    )


def slots_plan(tiles, contraction, row_tile, owner_map, panel):
    wide_count = lax.axis_size("wide")
    tile_dev = tiles.shape[0]
    tile_side = tiles.shape[1]
    out_dev = owner_map.shape[0] // wide_count
    most_slots = tile_dev * 8 // (3 * wide_count)
    slot_total = wide_count * most_slots
    local_row, target, ranking = place_slots(row_tile, owner_map, out_dev)
    slot_index = target * most_slots + ranking
    outgoing = jnp.zeros((slot_total, tile_side, tile_side), tiles.dtype).at[slot_index].set(tiles)
    all_rows, all_contraction = (
        lax.all_gather(row_tile, "wide", axis=0, tiled=True),
        lax.all_gather(contraction, "wide", axis=0, tiled=True),
    )
    all_rows = all_rows.reshape(wide_count, tile_dev)
    all_contraction = all_contraction.reshape(wide_count, tile_dev)
    source_local, source_target, source_rank = place_slots(all_rows, owner_map, out_dev)
    source_ids = jnp.arange(wide_count, dtype=jnp.int32)
    mine = source_target == lax.axis_index("wide")
    arrive_index = jnp.where(mine, source_ids[:, None] * most_slots + source_rank, slot_total)
    label_pairs = jnp.stack([source_local, all_contraction], axis=-1).reshape(
        wide_count * tile_dev, 2
    )
    vacant_label = jnp.stack(
        [jnp.full((slot_total,), out_dev, jnp.int32), jnp.zeros((slot_total,), jnp.int32)], axis=1
    )
    arrived_labels = vacant_label.at[arrive_index.reshape(-1)].set(label_pairs, mode="drop")
    gathered = lax.all_gather(panel, "grp", axis=0, tiled=True)
    panel_tiles = gathered.reshape(gathered.shape[0] // tile_side, tile_side, gathered.shape[1])
    summed = jnp.zeros((out_dev, tile_side, gathered.shape[1]), jnp.float32)
    arrived = lax.all_to_all(outgoing, "wide", split_axis=0, concat_axis=0, tiled=True)
    summed = add_products(summed, arrived, arrived_labels, panel_tiles)
    summed = lax.psum(summed, "grp")
    return summed.reshape(out_dev * tile_side, gathered.shape[1])


def encode(value):
    largest = jnp.max(jnp.abs(value), axis=0, keepdims=True)
    code = jnp.ceil(jnp.log(jnp.maximum(largest, 1e-30)) * (CODE_STEPS / LOG2))
    scale = jnp.exp(code * (-LOG2 / CODE_STEPS)) * TOP
    whole = jnp.round(value * scale).astype(jnp.int32).astype(jnp.int16)
    return whole, code.astype(jnp.int32)


def put_encoded(ref, value):
    side = value.shape[0]
    whole, code = encode(value)
    ref[pl.ds(0, side), :] = whole
    ref[pl.ds(side, CODE_ROWS), :] = jnp.broadcast_to(
        code, (CODE_ROWS, code.shape[1])
    ).astype(jnp.int16)


def get_decoded(ref, side):
    code = ref[pl.ds(side, CODE_ROWS), :].astype(jnp.int32).astype(jnp.float32)[:1]
    scale = jnp.exp(code * (LOG2 / CODE_STEPS)) * (1.0 / TOP)
    return ref[pl.ds(0, side), :].astype(jnp.int32).astype(jnp.float32) * scale


def products_kernel(
    pieces, ends_ref, source_ref, slot_ref, label_ref,
    own_tiles, sib_tiles, own_panel, d1, d2, d3, s1, s2, s3,
    send_a, send_b, keep, held, stack, acc, sems,
):
    tile_dev, side = held.shape[1], held.shape[2]
    shard = own_panel.shape[0] // side
    half = shard // 2
    outs = send_a.shape[0]
    copies = []
    for q, (which, first, count) in enumerate(pieces):
        tiles = (own_tiles, sib_tiles)[which]
        copies.append(
            pltpu.make_async_copy(
                tiles.at[pl.ds(first, count)], held.at[which, pl.ds(first, count)], sems.at[q]
            )
        )
        copies[-1].start()
    for t in range(shard):
        stack[t] = own_panel[pl.ds(t * side, side), :]
    for d, (near, far) in enumerate(((d1, s1), (d2, s2), (d3, s3)), 1):
        for t in range(half):
            stack[d * shard + t] = near[pl.ds(t * side, side), :]
            stack[d * shard + half + t] = far[pl.ds(t * side, side), :]

    @pl.loop(0, acc.shape[0])
    def _(i):
        acc[i] = jnp.zeros(acc.shape[1:], jnp.float32)

    def some(which, at, count):
        found = [
            jnp.dot(
                held[which, source_ref[which, at + u]],
                stack[label_ref[which, at + u]],
                preferred_element_type=jnp.float32,
            )
            for u in range(count)
        ]
        for u in range(count):
            acc[slot_ref[which, at + u]] += found[u]

    for q, (which, first, count) in enumerate(pieces):
        copies[q].wait()
        begin = 0 if first == 0 else ends_ref[q - 1]
        end = ends_ref[q]
        rounds = (end - begin) // UNROLL

        @pl.loop(0, rounds)
        def _(i, which=which, begin=begin):
            some(which, begin + i * UNROLL, UNROLL)

        @pl.loop(begin + rounds * UNROLL, end)
        def _(i, which=which):
            some(which, i, 1)

    @pl.loop(0, outs)
    def _(i):
        put_encoded(send_a.at[i], acc[i])
        put_encoded(send_b.at[i], acc[outs + i])

    @pl.loop(0, 2 * outs)
    def _(i):
        keep[i] = acc[2 * outs + i]


def plane_kernel(bits_ref, recv_a, recv_b, kept, send_a, send_b, keep):
    side, half = kept.shape[1], send_a.shape[0]
    for first, bit, recv, send in ((0, bits_ref[1], recv_a, send_a), (1, bits_ref[0], recv_b, send_b)):

        @pl.loop(0, half)
        def _(i, first=first, bit=bit, recv=recv, send=send):
            other, mine = 2 * i + 1 - bit, 2 * i + bit
            base = first * 2 * half
            put_encoded(send.at[i], kept[base + other] + get_decoded(recv.at[other], side))
            keep[first * half + i] = kept[base + mine] + get_decoded(recv.at[mine], side)


def owner_kernel(bits_ref, recv_a, recv_b, kept, send, keep):
    side, half = kept.shape[1], send.shape[0]
    odd = bits_ref[2]

    @pl.loop(0, half)
    def _(i):
        value_a = kept[i] + get_decoded(recv_a.at[i], side)
        value_b = kept[half + i] + get_decoded(recv_b.at[i], side)
        put_encoded(send.at[i], jnp.where(odd == 1, value_a, value_b))
        keep[i] = jnp.where(odd == 1, value_b, value_a)


def line_kernel(bits_ref, recv, kept, send, keep, *, which):
    side, half = kept.shape[1], send.shape[0]
    bit = bits_ref[which]

    @pl.loop(0, half)
    def _(i):
        other, mine = 2 * i + 1 - bit, 2 * i + bit
        put_encoded(send.at[i], kept[other] + get_decoded(recv.at[other], side))
        keep[i] = kept[mine] + get_decoded(recv.at[mine], side)


def finish_kernel(recv, kept, out):
    put_encoded(out, kept[0] + get_decoded(recv.at[0], kept.shape[1]))


def spread_kernel(grp_ref, *refs):
    blocks, out = refs[:4], refs[-1]
    side = blocks[0].shape[0] - CODE_ROWS
    for d, block in enumerate(blocks):
        at = pl.multiple_of((grp_ref[0] ^ d) * side, side)
        out[pl.ds(at, side), :] = get_decoded(block, side)


def in_vmem(count):
    return [pl.BlockSpec(memory_space=pltpu.VMEM)] * count


def in_smem(count):
    return [pl.BlockSpec(memory_space=pltpu.SMEM)] * count


def in_any(count):
    return [pl.BlockSpec(memory_space=pl.ANY)] * count


def shape(dims, kind):
    return jax.ShapeDtypeStruct(dims, kind)


def params(mib):
    return pltpu.CompilerParams(vmem_limit_bytes=mib * MIB)


def cost(flops, moved):
    return pl.CostEstimate(flops=flops, bytes_accessed=moved, transcendentals=0)


def compact(match, values):
    count = match.shape[-1]
    rank = jnp.cumsum(match.astype(jnp.int32), axis=-1) - 1
    at = jnp.arange(count, dtype=jnp.int32)
    hit = match[:, None, :] & (rank[:, None, :] == at[None, :, None])
    return [jnp.sum(jnp.where(hit, v[:, None, :], 0), axis=-1) for v in values]


def sums_plan(tiles, contraction, row_tile, owner_map, panel):
    wide_count = lax.axis_size("wide")
    tile_dev, side = tiles.shape[0], tiles.shape[1]
    out_dev = owner_map.shape[0] // wide_count
    rows, columns = panel.shape
    shard = rows // side
    chunks = columns // CHUNK
    sums = owner_map.shape[0] // 2
    g, w = lax.axis_index("grp"), lax.axis_index("wide")
    core = w % 2

    def to_core(v):
        return lax.ppermute(v, "wide", [(i, i ^ 1) for i in range(wide_count)])

    def to_grp(v, d):
        return lax.ppermute(v, "grp", [(i, i ^ d) for i in range(4)])

    def to_line(v, b):
        return lax.ppermute(v, "wide", [(i, i ^ (2 << b)) for i in range(wide_count)])

    x, y, z = g % 2, g // 2, w // 2
    z_bits = (wide_count // 2).bit_length() - 1
    bits = jnp.stack([x, y] + [(z >> b) & 1 for b in range(z_bits)]).astype(jnp.int32)
    spot = g.astype(jnp.int32)[None]

    labels = jnp.stack([row_tile, contraction])
    both = jnp.stack([labels, to_core(labels)])
    sib_tiles = to_core(tiles)

    mines = []
    for j in range(chunks):
        mine = lax.dynamic_slice(panel, (core * (rows // 2), j * CHUNK), (rows // 2, CHUNK))
        mines.append(mine)

    table_ids = jnp.arange(owner_map.shape[0], dtype=jnp.int32)
    position = jnp.sum(jnp.where(both[:, 0, :, None] == table_ids, owner_map, 0), axis=-1)
    owner, local = position // out_dev, position % out_dev
    to_z, odd = owner // 4, (owner // 2) % 2
    bit_x, bit_y = local % 2, local // 2
    first = jnp.where(odd == 1, bit_y == y, bit_x == x)
    second = jnp.where(odd == 1, bit_x, bit_y)
    index = jnp.where(first, sums // 2, 0) + odd * (sums // 4) + 2 * to_z + second
    k = both[:, 1]
    apart, inner = (k // shard) ^ g, k % shard
    half = shard // 2
    crossed = jnp.where(inner // half == core, 0, half) + inner % half
    label = jnp.where(apart == 0, inner, apart * shard + crossed)
    match = owner % 2 == core
    serial = jnp.broadcast_to(jnp.arange(tile_dev, dtype=jnp.int32), match.shape)
    source, slot, label = compact(match, [serial, index, label])
    cut = tile_dev // 4
    pieces = ((0, 0, cut), (0, cut, tile_dev - cut), (1, 0, tile_dev))
    ends = jnp.stack(
        [
            jnp.sum((match[which] & (serial[which] < first + count)).astype(jnp.int32))
            for which, first, count in pieces
        ]
    )

    result, near = None, [to_grp(mines[0], d) for d in (1, 2, 3)]
    first_send = None
    for j in range(chunks):
        if first_send is not None:
            first_send, *near = lax.optimization_barrier((first_send, *near))
        far = [to_core(v) for v in near]
        here = near
        if j + 1 < chunks:
            after = [mines[j + 1], far[0], *near]
            if first_send is not None:
                after.append(first_send)
            mine, far[0], *here = lax.optimization_barrier(tuple(after))[: 2 + len(near)]
            near = [to_grp(mine, d) for d in (1, 2, 3)]
        quarter = sums // 4
        send_a, send_b, keep = pl.pallas_call(
            functools.partial(products_kernel, pieces),
            grid=(1,),
            in_specs=in_smem(4)
            + [pl.BlockSpec(memory_space=pltpu.HBM)] * 2
            + [pl.BlockSpec((rows, CHUNK), lambda i, j=j: (0, j))]
            + in_vmem(6),
            out_specs=in_vmem(3),
            out_shape=[
                shape((quarter, side + CODE_ROWS, CHUNK), jnp.int16),
                shape((quarter, side + CODE_ROWS, CHUNK), jnp.int16),
                shape((2 * quarter, side, CHUNK), jnp.float32),
            ],
            scratch_shapes=[
                pltpu.VMEM((2, tile_dev, side, side), tiles.dtype),
                pltpu.VMEM((4 * shard, side, CHUNK), panel.dtype),
                pltpu.VMEM((sums, side, CHUNK), jnp.float32),
                pltpu.SemaphoreType.DMA((len(pieces),)),
            ],
            compiler_params=params(40),
            cost_estimate=cost(
                2 * tile_dev * side * side * CHUNK, 4 * tile_dev * side * side
            ),
            name="products",
        )(ends, source, slot, label, tiles, sib_tiles, panel, *here, *far)
        first_send = send_a

        count = quarter // 2
        send_a, send_b, keep = pl.pallas_call(
            plane_kernel,
            in_specs=in_smem(1) + in_vmem(3),
            out_specs=in_vmem(3),
            out_shape=[
                shape((count, side + CODE_ROWS, CHUNK), jnp.int16),
                shape((count, side + CODE_ROWS, CHUNK), jnp.int16),
                shape((2 * count, side, CHUNK), jnp.float32),
            ],
            compiler_params=params(16),
            cost_estimate=cost(40 * count * side * CHUNK, 36 * count * side * CHUNK),
            name="plane",
        )(bits, to_grp(send_a, 1), to_grp(send_b, 2), keep)

        send, keep = pl.pallas_call(
            owner_kernel,
            in_specs=in_smem(1) + in_vmem(3),
            out_specs=in_vmem(2),
            out_shape=[
                shape((count, side + CODE_ROWS, CHUNK), jnp.int16),
                shape((count, side, CHUNK), jnp.float32),
            ],
            compiler_params=params(16),
            cost_estimate=cost(20 * count * side * CHUNK, 18 * count * side * CHUNK),
            name="owner",
        )(bits, to_grp(send_a, 2), to_grp(send_b, 1), keep)

        for b in range(1, z_bits):
            count = keep.shape[0] // 2
            send, keep = pl.pallas_call(
                functools.partial(line_kernel, which=2 + b),
                in_specs=in_smem(1) + in_vmem(2),
                out_specs=in_vmem(2),
                out_shape=[
                    shape((count, side + CODE_ROWS, CHUNK), jnp.int16),
                    shape((count, side, CHUNK), jnp.float32),
                ],
                compiler_params=params(16),
                cost_estimate=cost(20 * count * side * CHUNK, 18 * count * side * CHUNK),
                name="line",
            )(bits, to_line(send, b - 1), keep)

        done = pl.pallas_call(
            finish_kernel,
            in_specs=in_vmem(2),
            out_specs=pl.BlockSpec(memory_space=pltpu.VMEM),
            out_shape=shape((side + CODE_ROWS, CHUNK), jnp.int16),
            compiler_params=params(16),
            cost_estimate=cost(20 * side * CHUNK, 8 * side * CHUNK),
            name="finish",
        )(to_line(send, z_bits - 1), keep)

        blocks = [done] + [to_grp(done, d) for d in (1, 2, 3)]
        earlier = [] if result is None else [result]
        result = pl.pallas_call(
            spread_kernel,
            grid=(1,),
            in_specs=in_smem(1) + in_vmem(4) + in_any(len(earlier)),
            out_specs=pl.BlockSpec((out_dev * side, CHUNK), lambda i, j=j: (0, j)),
            out_shape=shape((out_dev * side, columns), jnp.float32),
            input_output_aliases={5: 0} if earlier else {},
            compiler_params=params(16),
            cost_estimate=cost(4 * out_dev * side * CHUNK, 6 * out_dev * side * CHUNK),
            name="spread",
        )(spot, *blocks, *earlier)
    return result


def per_device(tiles, contraction, row_tile, owner_map, panel):
    dense = owner_map.shape[0] <= tiles.shape[0]
    wide_count = lax.axis_size("wide")
    fits = lax.axis_size("grp") == 4 and wide_count >= 4 and wide_count & (wide_count - 1) == 0
    out_dev = owner_map.shape[0] // wide_count
    if dense and fits and out_dev == 4 and panel.shape[1] % CHUNK == 0:
        return sums_plan(tiles, contraction, row_tile, owner_map, panel)
    return slots_plan(tiles, contraction, row_tile, owner_map, panel)


def solution(mesh):
    return jax.shard_map(
        per_device,
        mesh=mesh,
        in_specs=(
            P(("grp", "wide"), None, None),
            P(("grp", "wide")),
            P(("grp", "wide")),
            P(),
            P("grp", None),
        ),
        out_specs=P("wide", None),
        check_vma=False,
    )
```

```python
import functools
import math

import jax
import jax.numpy as jnp
from jax import lax
from jax.experimental import pallas as pl
from jax.experimental.pallas import tpu as pltpu
from jax.sharding import PartitionSpec as P

MIB = 1024 * 1024
CODE_ROWS = 16
CODE_STEPS = 256.0
TOP = 32000.0
CHUNK = 256
UNROLL = 4
LOG2 = math.log(2.0)


def place_slots(row_ids, owner_map, out_dev):
    table_ids = jnp.arange(owner_map.shape[0], dtype=jnp.int32)
    position = jnp.sum(jnp.where(row_ids[..., None] == table_ids, owner_map, 0), axis=-1)
    target = position // out_dev
    serial = jnp.arange(row_ids.shape[-1], dtype=jnp.int32)
    earlier = (target[..., :, None] == target[..., None, :]) & (serial[:, None] > serial[None, :])
    ranking = jnp.sum(earlier.astype(jnp.int32), axis=-1)
    return (position % out_dev, target, ranking)


def add_products(summed, arrived, slot_labels, panel_tiles):
    slot_count = arrived.shape[0]
    block_rows = math.gcd(slot_count, 32)
    out_dev = summed.shape[0]
    local_ids = jnp.arange(out_dev, dtype=jnp.int32)

    def one_block(which_block, running, source_tiles, source_labels):
        part_tiles = lax.dynamic_slice_in_dim(source_tiles, which_block * block_rows, block_rows, 0)
        part_labels = lax.dynamic_slice_in_dim(
            source_labels, which_block * block_rows, block_rows, 0
        )
        chosen = jnp.take(panel_tiles, part_labels[:, 1], axis=0)
        products = jnp.einsum(
            "sab,sbc->sac", part_tiles, chosen, preferred_element_type=jnp.float32
        )
        row_hits = (part_labels[:, 0][:, None] == local_ids[None, :]).astype(jnp.float32)
        return running + jnp.einsum(
            "sr,sac->rac", row_hits, products, precision=lax.Precision.HIGHEST
        )

    return lax.fori_loop(
        0,
        slot_count // block_rows,
        lambda which_block, running: one_block(which_block, running, arrived, slot_labels),
        summed,
    )


def slots_plan(tiles, contraction, row_tile, owner_map, panel):
    wide_count = lax.axis_size("wide")
    tile_dev = tiles.shape[0]
    tile_side = tiles.shape[1]
    out_dev = owner_map.shape[0] // wide_count
    most_slots = tile_dev * 8 // (3 * wide_count)
    slot_total = wide_count * most_slots
    local_row, target, ranking = place_slots(row_tile, owner_map, out_dev)
    slot_index = target * most_slots + ranking
    outgoing = jnp.zeros((slot_total, tile_side, tile_side), tiles.dtype).at[slot_index].set(tiles)
    all_rows, all_contraction = (
        lax.all_gather(row_tile, "wide", axis=0, tiled=True),
        lax.all_gather(contraction, "wide", axis=0, tiled=True),
    )
    all_rows = all_rows.reshape(wide_count, tile_dev)
    all_contraction = all_contraction.reshape(wide_count, tile_dev)
    source_local, source_target, source_rank = place_slots(all_rows, owner_map, out_dev)
    source_ids = jnp.arange(wide_count, dtype=jnp.int32)
    mine = source_target == lax.axis_index("wide")
    arrive_index = jnp.where(mine, source_ids[:, None] * most_slots + source_rank, slot_total)
    label_pairs = jnp.stack([source_local, all_contraction], axis=-1).reshape(
        wide_count * tile_dev, 2
    )
    vacant_label = jnp.stack(
        [jnp.full((slot_total,), out_dev, jnp.int32), jnp.zeros((slot_total,), jnp.int32)], axis=1
    )
    arrived_labels = vacant_label.at[arrive_index.reshape(-1)].set(label_pairs, mode="drop")
    gathered = lax.all_gather(panel, "grp", axis=0, tiled=True)
    panel_tiles = gathered.reshape(gathered.shape[0] // tile_side, tile_side, gathered.shape[1])
    summed = jnp.zeros((out_dev, tile_side, gathered.shape[1]), jnp.float32)
    arrived = lax.all_to_all(outgoing, "wide", split_axis=0, concat_axis=0, tiled=True)
    summed = add_products(summed, arrived, arrived_labels, panel_tiles)
    summed = lax.psum(summed, "grp")
    return summed.reshape(out_dev * tile_side, gathered.shape[1])


def encode(value):
    largest = jnp.max(jnp.abs(value), axis=0, keepdims=True)
    code = jnp.ceil(jnp.log(jnp.maximum(largest, 1e-30)) * (CODE_STEPS / LOG2))
    scale = jnp.exp(code * (-LOG2 / CODE_STEPS)) * TOP
    whole = jnp.round(value * scale).astype(jnp.int32).astype(jnp.int16)
    return whole, code.astype(jnp.int32)


def put_encoded(ref, value):
    side = value.shape[0]
    whole, code = encode(value)
    ref[pl.ds(0, side), :] = whole
    ref[pl.ds(side, CODE_ROWS), :] = jnp.broadcast_to(
        code, (CODE_ROWS, code.shape[1])
    ).astype(jnp.int16)


def get_decoded(ref, side):
    code = ref[pl.ds(side, CODE_ROWS), :].astype(jnp.int32).astype(jnp.float32)[:1]
    scale = jnp.exp(code * (LOG2 / CODE_STEPS)) * (1.0 / TOP)
    return ref[pl.ds(0, side), :].astype(jnp.int32).astype(jnp.float32) * scale


def products_kernel(
    pieces, slot_ref, label_ref, own_tiles, sib_tiles, p0, p1, p2, p3, *refs
):
    *outs, held, stack, acc, sems = refs
    side = held.shape[2]
    copies = []
    for q, (which, first, count) in enumerate(pieces):
        tiles = (own_tiles, sib_tiles)[which]
        copies.append(
            pltpu.make_async_copy(
                tiles.at[pl.ds(first, count)], held.at[which, pl.ds(first, count)], sems.at[q]
            )
        )
        copies[-1].start()
    shard = p0.shape[0] // side
    for d, panel in enumerate((p0, p1, p2, p3)):
        for t in range(shard):
            stack[d * shard + t] = panel[pl.ds(t * side, side), :]

    @pl.loop(0, acc.shape[0])
    def _(i):
        acc[i] = jnp.zeros(acc.shape[1:], jnp.float32)

    for q, (which, first, count) in enumerate(pieces):
        copies[q].wait()

        @pl.loop(0, count // UNROLL)
        def _(i, which=which, first=first):
            at = first + i * UNROLL
            found = [
                jnp.dot(
                    held[which, at + u],
                    stack[label_ref[which, at + u]],
                    preferred_element_type=jnp.float32,
                )
                for u in range(UNROLL)
            ]
            for u in range(UNROLL):
                acc[slot_ref[which, at + u]] += found[u]

    sent = 0
    for out in outs:
        if out.dtype == jnp.int16:

            @pl.loop(0, out.shape[0])
            def _(i, out=out, sent=sent):
                put_encoded(out.at[i], acc[sent + i])
        else:

            @pl.loop(0, out.shape[0])
            def _(i, out=out, sent=sent):
                out[i] = acc[sent + i]

        sent += out.shape[0]


def plane_kernel(bits_ref, recv_a, recv_b, kept, send_a, send_b, keep):
    side, half = kept.shape[1], send_a.shape[0]
    for first, bit, recv, send in ((0, bits_ref[1], recv_a, send_a), (1, bits_ref[0], recv_b, send_b)):

        @pl.loop(0, half)
        def _(i, first=first, bit=bit, recv=recv, send=send):
            other, mine = 2 * i + 1 - bit, 2 * i + bit
            base = first * 2 * half
            put_encoded(send.at[i], kept[base + other] + get_decoded(recv.at[other], side))
            keep[first * half + i] = kept[base + mine] + get_decoded(recv.at[mine], side)


def owner_kernel(recv_a, recv_b, kept, out):
    side, half = kept.shape[1], recv_a.shape[0]

    @pl.loop(0, half)
    def _(i):
        put_encoded(out.at[2 * i], kept[i] + get_decoded(recv_a.at[i], side))
        put_encoded(out.at[2 * i + 1], kept[half + i] + get_decoded(recv_b.at[i], side))


def over_line(recv, side, step, at):
    halves = []
    for core in range(2):
        value = get_decoded(recv.at[core * step + at], side)
        for z in range(1, recv.shape[0] // (2 * step)):
            value += get_decoded(recv.at[(2 * z + core) * step + at], side)
        halves.append(value)
    return jnp.concatenate(halves, axis=1)


def finish_kernel(recv, out):
    put_encoded(out, over_line(recv, out.shape[0] - CODE_ROWS, 1, 0))


def line_kernel(grp_ref, recv, send_1, send_2, send_3, keep):
    side, rows = keep.shape[0], 4
    for d, send in enumerate((send_1, send_2, send_3), 1):
        put_encoded(send, over_line(recv, side, rows, grp_ref[0] ^ d))
    keep[...] = over_line(recv, side, rows, grp_ref[0])


def finish_plane_kernel(recv_1, recv_2, recv_3, kept, out):
    value = kept[...]
    for recv in (recv_1, recv_2, recv_3):
        value += get_decoded(recv, kept.shape[0])
    put_encoded(out, value)


def spread_kernel(grp_ref, *refs):
    blocks, out = refs[:4], refs[-1]
    side = blocks[0].shape[0] - CODE_ROWS
    for d, block in enumerate(blocks):
        at = pl.multiple_of((grp_ref[0] ^ d) * side, side)
        out[pl.ds(at, side), :] = get_decoded(block, side)


def in_vmem(count):
    return [pl.BlockSpec(memory_space=pltpu.VMEM)] * count


def in_smem(count):
    return [pl.BlockSpec(memory_space=pltpu.SMEM)] * count


def in_any(count):
    return [pl.BlockSpec(memory_space=pl.ANY)] * count


def shape(dims, kind):
    return jax.ShapeDtypeStruct(dims, kind)


def params(mib):
    return pltpu.CompilerParams(vmem_limit_bytes=mib * MIB)


def cost(flops, moved):
    return pl.CostEstimate(flops=flops, bytes_accessed=moved, transcendentals=0)


def sums_plan(tiles, contraction, row_tile, owner_map, panel):
    wide_count = lax.axis_size("wide")
    nz = wide_count // 2
    tile_dev, side = tiles.shape[0], tiles.shape[1]
    out_dev = owner_map.shape[0] // wide_count
    rows, columns = panel.shape
    shard = rows // side
    chunks = columns // CHUNK
    width = CHUNK // 2
    sums = owner_map.shape[0]
    coded = side + CODE_ROWS
    g, w = lax.axis_index("grp"), lax.axis_index("wide")
    x, y, core = g % 2, g // 2, w % 2
    bits = jnp.stack([x, y]).astype(jnp.int32)
    spot = g.astype(jnp.int32)[None]

    def to_core(v):
        return lax.ppermute(v, "wide", [(i, i ^ 1) for i in range(wide_count)])

    def to_grp(v, d):
        return lax.ppermute(v, "grp", [(i, i ^ d) for i in range(4)])

    def over_wide(v):
        return lax.all_to_all(v, "wide", split_axis=0, concat_axis=0, tiled=True)

    def kernel(body, name, ins, outs, moved, smem=0):
        one = len(outs) == 1
        return pl.pallas_call(
            body,
            in_specs=in_smem(smem) + in_vmem(ins),
            out_specs=in_vmem(1)[0] if one else in_vmem(len(outs)),
            out_shape=outs[0] if one else outs,
            compiler_params=params(16),
            cost_estimate=cost(4 * moved, moved),
            name=name,
        )

    sib_tiles = to_core(tiles)
    mines = [
        lax.dynamic_slice(panel, (0, j * CHUNK + core * width), (rows, width))
        for j in range(chunks)
    ]
    near = [to_grp(mines[0], d) for d in (1, 2, 3)]

    labels = jnp.stack([row_tile, contraction])
    both = jnp.stack([labels, to_core(labels)])
    table_ids = jnp.arange(sums, dtype=jnp.int32)
    position = jnp.sum(jnp.where(both[:, 0, :, None] == table_ids, owner_map, 0), axis=-1)
    owner, local = position // out_dev, position % out_dev
    to_z, second_half = owner // 2, owner % 2
    bit_x, bit_y = local % 2, local // 2
    first = jnp.where(second_half == 1, bit_y == y, bit_x == x)
    second = jnp.where(second_half == 1, bit_x, bit_y)
    quarter = sums // 4
    in_plane = jnp.where(first, 2 * quarter, 0) + second_half * quarter + 2 * to_z + second
    k = both[:, 1]
    label = ((k // shard) ^ g) * shard + k % shard
    cut = tile_dev // 4
    pieces = ((0, 0, cut), (0, cut, tile_dev - cut), (1, 0, tile_dev))

    def products(slot, parts, outs):
        return pl.pallas_call(
            functools.partial(products_kernel, pieces),
            in_specs=in_smem(2) + [pl.BlockSpec(memory_space=pltpu.HBM)] * 2 + in_vmem(4),
            out_specs=in_vmem(len(outs)),
            out_shape=outs,
            scratch_shapes=[
                pltpu.VMEM((2, tile_dev, side, side), tiles.dtype),
                pltpu.VMEM((4 * shard, side, width), panel.dtype),
                pltpu.VMEM((sums, side, width), jnp.float32),
                pltpu.SemaphoreType.DMA((len(pieces),)),
            ],
            compiler_params=params(59),
            cost_estimate=cost(4 * tile_dev * side * side * width, 4 * tile_dev * side * side),
            name="products",
        )(slot, label, tiles, sib_tiles, *parts)

    result, first_sums = None, None
    for j in range(chunks):
        parts = [mines[j], *near]
        if j + 1 < chunks:
            after = [mines[j + 1], *near]
            if first_sums is not None:
                after.append(first_sums)
            mine = lax.optimization_barrier(tuple(after))[0]
            near = [to_grp(mine, d) for d in (1, 2, 3)]

        if j == 0:
            (first_sums,) = products(position, parts, [shape((sums, coded, width), jnp.int16)])
            tile = shape((coded, CHUNK), jnp.int16)
            *sends, keep = kernel(
                line_kernel,
                "line",
                1,
                [tile] * 3 + [shape((side, CHUNK), jnp.float32)],
                2 * sums * side * width,
                smem=1,
            )(spot, over_wide(first_sums))
            done = kernel(finish_plane_kernel, "finish_plane", 4, [tile], 16 * side * CHUNK)(
                *[to_grp(v, d) for d, v in enumerate(sends, 1)], keep
            )
        else:
            send_a, send_b, keep = products(
                in_plane,
                parts,
                [shape((quarter, coded, width), jnp.int16)] * 2
                + [shape((2 * quarter, side, width), jnp.float32)],
            )
            count = quarter // 2
            send_a, send_b, keep = kernel(
                plane_kernel,
                "plane",
                3,
                [shape((count, coded, width), jnp.int16)] * 2
                + [shape((2 * count, side, width), jnp.float32)],
                36 * count * side * width,
                smem=1,
            )(bits, to_grp(send_a, 1), to_grp(send_b, 2), keep)
            sent = kernel(
                owner_kernel,
                "owner",
                3,
                [shape((2 * count, coded, width), jnp.int16)],
                20 * count * side * width,
            )(to_grp(send_a, 2), to_grp(send_b, 1), keep)
            done = kernel(finish_kernel, "finish", 1, [tile], 16 * side * CHUNK)(over_wide(sent))

        blocks = [done] + [to_grp(done, d) for d in (1, 2, 3)]
        earlier = [] if result is None else [result]
        result = pl.pallas_call(
            spread_kernel,
            grid=(1,),
            in_specs=in_smem(1) + in_vmem(4) + in_any(len(earlier)),
            out_specs=pl.BlockSpec((out_dev * side, CHUNK), lambda i, j=j: (0, j)),
            out_shape=shape((out_dev * side, columns), jnp.float32),
            input_output_aliases={5: 0} if earlier else {},
            compiler_params=params(16),
            cost_estimate=cost(4 * out_dev * side * CHUNK, 6 * out_dev * side * CHUNK),
            name="spread",
        )(spot, *blocks, *earlier)
    return result


def per_device(tiles, contraction, row_tile, owner_map, panel):
    dense = owner_map.shape[0] <= tiles.shape[0]
    wide_count = lax.axis_size("wide")
    fits = lax.axis_size("grp") == 4 and wide_count % 2 == 0 and tiles.shape[0] % 16 == 0
    out_dev = owner_map.shape[0] // wide_count
    if dense and fits and out_dev == 4 and panel.shape[1] % CHUNK == 0:
        return sums_plan(tiles, contraction, row_tile, owner_map, panel)
    return slots_plan(tiles, contraction, row_tile, owner_map, panel)


def solution(mesh):
    return jax.shard_map(
        per_device,
        mesh=mesh,
        in_specs=(
            P(("grp", "wide"), None, None),
            P(("grp", "wide")),
            P(("grp", "wide")),
            P(),
            P("grp", None),
        ),
        out_specs=P("wide", None),
        check_vma=False,
    )
```

```python
import functools
import math

import jax
import jax.numpy as jnp
from jax import lax
from jax.experimental import pallas as pl
from jax.experimental.pallas import tpu as pltpu
from jax.sharding import PartitionSpec as P

MIB = 1024 * 1024
CODE_ROWS = 16
CODE_STEPS = 256.0
TOP = 32000.0
CHUNK = 256
UNROLL = 4
LOG2 = math.log(2.0)


def place_slots(row_ids, owner_map, out_dev):
    table_ids = jnp.arange(owner_map.shape[0], dtype=jnp.int32)
    position = jnp.sum(jnp.where(row_ids[..., None] == table_ids, owner_map, 0), axis=-1)
    target = position // out_dev
    serial = jnp.arange(row_ids.shape[-1], dtype=jnp.int32)
    earlier = (target[..., :, None] == target[..., None, :]) & (serial[:, None] > serial[None, :])
    ranking = jnp.sum(earlier.astype(jnp.int32), axis=-1)
    return (position % out_dev, target, ranking)


def add_products(summed, arrived, slot_labels, panel_tiles):
    slot_count = arrived.shape[0]
    block_rows = math.gcd(slot_count, 32)
    out_dev = summed.shape[0]
    local_ids = jnp.arange(out_dev, dtype=jnp.int32)

    def one_block(which_block, running, source_tiles, source_labels):
        part_tiles = lax.dynamic_slice_in_dim(source_tiles, which_block * block_rows, block_rows, 0)
        part_labels = lax.dynamic_slice_in_dim(
            source_labels, which_block * block_rows, block_rows, 0
        )
        chosen = jnp.take(panel_tiles, part_labels[:, 1], axis=0)
        products = jnp.einsum(
            "sab,sbc->sac", part_tiles, chosen, preferred_element_type=jnp.float32
        )
        row_hits = (part_labels[:, 0][:, None] == local_ids[None, :]).astype(jnp.float32)
        return running + jnp.einsum(
            "sr,sac->rac", row_hits, products, precision=lax.Precision.HIGHEST
        )

    return lax.fori_loop(
        0,
        slot_count // block_rows,
        lambda which_block, running: one_block(which_block, running, arrived, slot_labels),
        summed,
    )


def slots_plan(tiles, contraction, row_tile, owner_map, panel):
    wide_count = lax.axis_size("wide")
    tile_dev = tiles.shape[0]
    tile_side = tiles.shape[1]
    out_dev = owner_map.shape[0] // wide_count
    most_slots = tile_dev * 8 // (3 * wide_count)
    slot_total = wide_count * most_slots
    local_row, target, ranking = place_slots(row_tile, owner_map, out_dev)
    slot_index = target * most_slots + ranking
    outgoing = jnp.zeros((slot_total, tile_side, tile_side), tiles.dtype).at[slot_index].set(tiles)
    all_rows, all_contraction = (
        lax.all_gather(row_tile, "wide", axis=0, tiled=True),
        lax.all_gather(contraction, "wide", axis=0, tiled=True),
    )
    all_rows = all_rows.reshape(wide_count, tile_dev)
    all_contraction = all_contraction.reshape(wide_count, tile_dev)
    source_local, source_target, source_rank = place_slots(all_rows, owner_map, out_dev)
    source_ids = jnp.arange(wide_count, dtype=jnp.int32)
    mine = source_target == lax.axis_index("wide")
    arrive_index = jnp.where(mine, source_ids[:, None] * most_slots + source_rank, slot_total)
    label_pairs = jnp.stack([source_local, all_contraction], axis=-1).reshape(
        wide_count * tile_dev, 2
    )
    vacant_label = jnp.stack(
        [jnp.full((slot_total,), out_dev, jnp.int32), jnp.zeros((slot_total,), jnp.int32)], axis=1
    )
    arrived_labels = vacant_label.at[arrive_index.reshape(-1)].set(label_pairs, mode="drop")
    gathered = lax.all_gather(panel, "grp", axis=0, tiled=True)
    panel_tiles = gathered.reshape(gathered.shape[0] // tile_side, tile_side, gathered.shape[1])
    summed = jnp.zeros((out_dev, tile_side, gathered.shape[1]), jnp.float32)
    arrived = lax.all_to_all(outgoing, "wide", split_axis=0, concat_axis=0, tiled=True)
    summed = add_products(summed, arrived, arrived_labels, panel_tiles)
    summed = lax.psum(summed, "grp")
    return summed.reshape(out_dev * tile_side, gathered.shape[1])


def encode(value):
    largest = jnp.max(jnp.abs(value), axis=0, keepdims=True)
    code = jnp.ceil(jnp.log(jnp.maximum(largest, 1e-30)) * (CODE_STEPS / LOG2))
    scale = jnp.exp(code * (-LOG2 / CODE_STEPS)) * TOP
    whole = jnp.round(value * scale).astype(jnp.int32).astype(jnp.int16)
    return whole, code.astype(jnp.int32)


def put_encoded(ref, value):
    side = value.shape[0]
    whole, code = encode(value)
    ref[pl.ds(0, side), :] = whole
    ref[pl.ds(side, CODE_ROWS), :] = jnp.broadcast_to(
        code, (CODE_ROWS, code.shape[1])
    ).astype(jnp.int16)


def get_decoded(ref, side):
    code = ref[pl.ds(side, CODE_ROWS), :].astype(jnp.int32).astype(jnp.float32)[:1]
    scale = jnp.exp(code * (LOG2 / CODE_STEPS)) * (1.0 / TOP)
    return ref[pl.ds(0, side), :].astype(jnp.int32).astype(jnp.float32) * scale


def join_kernel(order_ref, *refs):
    *parts, out = refs
    rows = parts[0].shape[0]
    for i, part in enumerate(parts):
        out[pl.ds(i * rows, rows), :] = part[...]


def products_kernel(
    pieces, ends_ref, source_ref, slot_ref, label_ref, own_tiles, sib_tiles, *refs
):
    own_panel, near, far, *outs, held, stack, acc, sems = refs
    tile_dev, side = held.shape[1], held.shape[2]
    shard = own_panel.shape[0] // side
    half = shard // 2
    copies = []
    for q, (which, first, count) in enumerate(pieces):
        tiles = (own_tiles, sib_tiles)[which]
        copies.append(
            pltpu.make_async_copy(
                tiles.at[pl.ds(first, count)], held.at[which, pl.ds(first, count)], sems.at[q]
            )
        )
        copies[-1].start()
    for t in range(shard):
        stack[t] = own_panel[pl.ds(t * side, side), :]
    for i in range(3 * half):
        at = shard + (i // half) * shard + i % half
        stack[at] = near[pl.ds(i * side, side), :]
        stack[at + half] = far[pl.ds(i * side, side), :]

    @pl.loop(0, acc.shape[0])
    def _(i):
        acc[i] = jnp.zeros(acc.shape[1:], jnp.float32)

    def some(which, at, count):
        found = [
            jnp.dot(
                held[which, source_ref[which, at + u]],
                stack[label_ref[which, at + u]],
                preferred_element_type=jnp.float32,
            )
            for u in range(count)
        ]
        for u in range(count):
            acc[slot_ref[which, at + u]] += found[u]

    for q, (which, first, count) in enumerate(pieces):
        copies[q].wait()
        begin = 0 if first == 0 else ends_ref[q - 1]
        end = ends_ref[q]
        rounds = (end - begin) // UNROLL

        @pl.loop(0, rounds)
        def _(i, which=which, begin=begin):
            some(which, begin + i * UNROLL, UNROLL)

        @pl.loop(begin + rounds * UNROLL, end)
        def _(i, which=which):
            some(which, i, 1)

    sent = 0
    for out in outs:

        @pl.loop(0, out.shape[0])
        def _(i, out=out, sent=sent):
            if out.dtype == jnp.int16:
                put_encoded(out.at[i], acc[sent + i])
            else:
                out[i] = acc[sent + i]

        sent += out.shape[0]


def plane_kernel(bits_ref, recv_a, recv_b, kept, send_a, send_b, keep):
    side, half = kept.shape[1], send_a.shape[0]
    for first, bit, recv, send in ((0, bits_ref[1], recv_a, send_a), (1, bits_ref[0], recv_b, send_b)):

        @pl.loop(0, half)
        def _(i, first=first, bit=bit, recv=recv, send=send):
            other, mine = 2 * i + 1 - bit, 2 * i + bit
            base = first * 2 * half
            put_encoded(send.at[i], kept[base + other] + get_decoded(recv.at[other], side))
            keep[first * half + i] = kept[base + mine] + get_decoded(recv.at[mine], side)


def owner_kernel(bits_ref, recv_a, recv_b, kept, send, keep):
    side, half = kept.shape[1], send.shape[0]
    odd = bits_ref[2]

    @pl.loop(0, half)
    def _(i):
        value_a = kept[i] + get_decoded(recv_a.at[i], side)
        value_b = kept[half + i] + get_decoded(recv_b.at[i], side)
        put_encoded(send.at[i], jnp.where(odd == 1, value_a, value_b))
        keep[i] = jnp.where(odd == 1, value_b, value_a)


def line_kernel(bits_ref, recv, kept, send, keep):
    side, half = kept.shape[1], send.shape[0]
    bit = bits_ref[3]

    @pl.loop(0, half)
    def _(i):
        other, mine = (1 - bit) * half + i, bit * half + i
        put_encoded(send.at[i], kept[other] + get_decoded(recv.at[other], side))
        keep[i] = kept[mine] + get_decoded(recv.at[mine], side)


def rows_kernel(bits_ref, recv, kept, send_1, send_2, send_3, keep):
    side = kept.shape[1]
    row = bits_ref[1] * 2 + bits_ref[0]
    for d, send in enumerate((send_1, send_2, send_3), 1):
        put_encoded(send, kept[row ^ d] + get_decoded(recv.at[row ^ d], side))
    keep[...] = kept[row] + get_decoded(recv.at[row], side)


def finish_kernel(bits_ref, *refs):
    *recvs, kept, out = refs
    value = kept[...]
    for recv in recvs:
        value += get_decoded(recv, kept.shape[0])
    put_encoded(out, value)


def spread_kernel(bits_ref, *refs):
    blocks, out = refs[:4], refs[-1]
    side = blocks[0].shape[0] - CODE_ROWS
    row = bits_ref[1] * 2 + bits_ref[0]
    for d, block in enumerate(blocks):
        at = pl.multiple_of((row ^ d) * side, side)
        out[pl.ds(at, side), :] = get_decoded(block, side)


def in_vmem(count):
    return [pl.BlockSpec(memory_space=pltpu.VMEM)] * count


def in_smem(count):
    return [pl.BlockSpec(memory_space=pltpu.SMEM)] * count


def in_any(count):
    return [pl.BlockSpec(memory_space=pl.ANY)] * count


def shape(dims, kind):
    return jax.ShapeDtypeStruct(dims, kind)


def params(mib):
    return pltpu.CompilerParams(vmem_limit_bytes=mib * MIB)


def cost(flops, moved):
    return pl.CostEstimate(flops=flops, bytes_accessed=moved, transcendentals=0)


def compact(match, values):
    count = match.shape[-1]
    rank = jnp.cumsum(match.astype(jnp.int32), axis=-1) - 1
    at = jnp.arange(count, dtype=jnp.int32)
    hit = match[:, None, :] & (rank[:, None, :] == at[None, :, None])
    return [jnp.sum(jnp.where(hit, v[:, None, :], 0), axis=-1) for v in values]


def sums_plan(tiles, contraction, row_tile, owner_map, panel):
    wide_count = lax.axis_size("wide")
    tile_dev, side = tiles.shape[0], tiles.shape[1]
    out_dev = owner_map.shape[0] // wide_count
    rows, columns = panel.shape
    shard = rows // side
    chunks = columns // CHUNK
    sums = owner_map.shape[0] // 2
    g, w = lax.axis_index("grp"), lax.axis_index("wide")
    core = w % 2

    def to_core(v):
        return lax.ppermute(v, "wide", [(i, i ^ 1) for i in range(wide_count)])

    def to_grp(v, d):
        return lax.ppermute(v, "grp", [(i, i ^ d) for i in range(4)])

    def to_line(v, b):
        return lax.ppermute(v, "wide", [(i, i ^ (2 << b)) for i in range(wide_count)])

    x, y, z = g % 2, g // 2, w // 2
    bits = jnp.stack([x, y, z % 2, z // 2]).astype(jnp.int32)

    labels = jnp.stack([row_tile, contraction])
    both = jnp.stack([labels, to_core(labels)])
    sib_tiles = to_core(tiles)

    mines = [
        lax.dynamic_slice(panel, (core * (rows // 2), j * CHUNK), (rows // 2, CHUNK))
        for j in range(chunks)
    ]
    near = [[to_grp(mines[0], d) for d in (1, 2, 3)]]
    for mine in mines[1:]:
        mine = lax.optimization_barrier((mine, *near[-1]))[0]
        near.append([to_grp(mine, d) for d in (1, 2, 3)])

    table_ids = jnp.arange(owner_map.shape[0], dtype=jnp.int32)
    position = jnp.sum(jnp.where(both[:, 0, :, None] == table_ids, owner_map, 0), axis=-1)
    owner, local = position // out_dev, position % out_dev
    to_z, odd = owner // 4, (owner // 2) % 2
    bit_x, bit_y = local % 2, local // 2
    first = jnp.where(odd == 1, bit_y == y, bit_x == x)
    second = jnp.where(odd == 1, bit_x, bit_y)
    in_plane = jnp.where(first, sums // 2, 0) + odd * (sums // 4) + 2 * to_z + second
    in_line = jnp.where(odd == z % 2, sums // 2, 0) + to_z * out_dev + local
    k = both[:, 1]
    apart, inner = (k // shard) ^ g, k % shard
    half = shard // 2
    crossed = jnp.where(inner // half == core, 0, half) + inner % half
    label = jnp.where(apart == 0, inner, apart * shard + crossed)
    match = owner % 2 == core
    serial = jnp.broadcast_to(jnp.arange(tile_dev, dtype=jnp.int32), match.shape)
    source, in_plane, in_line, label = compact(match, [serial, in_plane, in_line, label])
    cut = tile_dev // 4
    pieces = ((0, 0, cut), (0, cut, tile_dev - cut), (1, 0, tile_dev))
    ends = jnp.stack(
        [
            jnp.sum((match[which] & (serial[which] < first + count)).astype(jnp.int32))
            for which, first, count in pieces
        ]
    )

    half, quarter = sums // 2, sums // 4
    coded = shape((side + CODE_ROWS, CHUNK), jnp.int16)
    plain = shape((side, CHUNK), jnp.float32)

    def stack_of(count, one):
        return shape((count, *one.shape), one.dtype)

    last = None

    def in_order(small):
        return small if last is None else lax.optimization_barrier((small, last))[0]

    def call(body, name, outs, *args):
        nonlocal last
        done = pl.pallas_call(
            body,
            in_specs=in_smem(1) + in_vmem(len(args)),
            out_specs=in_vmem(len(outs)),
            out_shape=outs,
            compiler_params=params(16),
            cost_estimate=cost(0, sum(math.prod(a.shape) * a.dtype.itemsize for a in args)),
            name=name,
        )(in_order(bits), *args)
        last = done[0]
        return done

    def join(j):
        (joined,) = call(join_kernel, "join", [shape((3 * rows // 2, CHUNK), panel.dtype)], *near[j])
        return joined, to_core(joined)

    def products(j, slot, outs, joined, crossed):
        nonlocal last
        done = pl.pallas_call(
            functools.partial(products_kernel, pieces),
            grid=(1,),
            in_specs=in_smem(4)
            + [pl.BlockSpec(memory_space=pltpu.HBM)] * 2
            + [pl.BlockSpec((rows, CHUNK), lambda i: (0, j))]
            + in_vmem(2),
            out_specs=in_vmem(len(outs)),
            out_shape=outs,
            scratch_shapes=[
                pltpu.VMEM((2, tile_dev, side, side), tiles.dtype),
                pltpu.VMEM((4 * shard, side, CHUNK), panel.dtype),
                pltpu.VMEM((sums, side, CHUNK), jnp.float32),
                pltpu.SemaphoreType.DMA((len(pieces),)),
            ],
            compiler_params=params(54),
            cost_estimate=cost(0, 4 * tile_dev * side * side),
            name="products",
        )(in_order(ends), source, slot, label, tiles, sib_tiles, panel, joined, crossed)
        last = done[0]
        return done

    def spread(j, done, result):
        nonlocal last
        blocks = [done] + [to_grp(done, d) for d in (1, 2, 3)]
        earlier = [] if result is None else [result]
        last = pl.pallas_call(
            spread_kernel,
            grid=(1,),
            in_specs=in_smem(1) + in_vmem(4) + in_any(len(earlier)),
            out_specs=pl.BlockSpec((out_dev * side, CHUNK), lambda i: (0, j)),
            out_shape=shape((out_dev * side, columns), jnp.float32),
            input_output_aliases={5: 0} if earlier else {},
            compiler_params=params(16),
            cost_estimate=cost(0, 6 * out_dev * side * CHUNK),
            name="spread",
        )(in_order(bits), *blocks, *earlier)
        return last

    def line_first(j):
        joined, crossed = join(j)
        yield
        send, keep = products(
            j, in_line, [stack_of(half, coded), stack_of(half, plain)], joined, crossed
        )
        yield
        recv = to_line(send, 0)
        send, keep = call(
            line_kernel, "line", [stack_of(quarter, coded), stack_of(quarter, plain)], recv, keep
        )
        yield
        *sends, keep = call(rows_kernel, "rows", [coded] * 3 + [plain], to_line(send, 1), keep)
        yield
        recvs = [to_grp(v, d) for d, v in enumerate(sends, 1)]
        (done,) = call(finish_kernel, "finish", [coded], *recvs, keep)
        yield
        yield done

    def plane_first(j):
        joined, crossed = join(j)
        yield
        send_a, send_b, keep = products(
            j, in_plane, [stack_of(quarter, coded)] * 2 + [stack_of(half, plain)], joined, crossed
        )
        yield
        send_a, send_b, keep = call(
            plane_kernel,
            "plane",
            [stack_of(quarter // 2, coded)] * 2 + [stack_of(quarter, plain)],
            to_grp(send_a, 1),
            to_grp(send_b, 2),
            keep,
        )
        yield
        send, keep = call(
            owner_kernel,
            "owner",
            [stack_of(quarter // 2, coded), stack_of(quarter // 2, plain)],
            to_grp(send_a, 2),
            to_grp(send_b, 1),
            keep,
        )
        yield
        send, keep = call(
            line_kernel,
            "line",
            [stack_of(quarter // 4, coded), stack_of(quarter // 4, plain)],
            to_line(send, 0),
            keep,
        )
        yield
        recv = to_line(send, 1)
        (done,) = call(finish_kernel, "finish", [coded], recv[0], keep[0])
        yield
        yield done

    steps, lengths = [0] * chunks, [5] + [6] * (chunks - 1)
    work = [(line_first if j == 0 else plane_first)(j) for j in range(chunks)]
    dones, result = {}, None
    for j in (0, 0, 1, 1, 2, 2, 0, 1, 2, 1, 0, 2, 1, 0, 1, 2, 0, 2, 1, 2):
        if j in dones:
            result = spread(j, dones[j], result)
            continue
        next(work[j])
        steps[j] += 1
        if steps[j] == lengths[j]:
            dones[j] = next(work[j])
    return result


def per_device(tiles, contraction, row_tile, owner_map, panel):
    dense = owner_map.shape[0] <= tiles.shape[0]
    wide_count = lax.axis_size("wide")
    fits = lax.axis_size("grp") == 4 and wide_count >= 4 and wide_count & (wide_count - 1) == 0
    out_dev = owner_map.shape[0] // wide_count
    if dense and fits and wide_count == 8 and out_dev == 4 and panel.shape[1] == 3 * CHUNK:
        return sums_plan(tiles, contraction, row_tile, owner_map, panel)
    return slots_plan(tiles, contraction, row_tile, owner_map, panel)


def solution(mesh):
    return jax.shard_map(
        per_device,
        mesh=mesh,
        in_specs=(
            P(("grp", "wide"), None, None),
            P(("grp", "wide")),
            P(("grp", "wide")),
            P(),
            P("grp", None),
        ),
        out_specs=P("wide", None),
        check_vma=False,
    )
```

```python
import functools
import math

import jax
import jax.numpy as jnp
from jax import lax
from jax.experimental import pallas as pl
from jax.experimental.pallas import tpu as pltpu
from jax.sharding import PartitionSpec as P

MIB = 1024 * 1024
CODE_ROWS = 16
CODE_STEPS = 256.0
TOP = 32000.0
CHUNK = 256
UNROLL = 4
LOG2 = math.log(2.0)


def place_slots(row_ids, owner_map, out_dev):
    table_ids = jnp.arange(owner_map.shape[0], dtype=jnp.int32)
    position = jnp.sum(jnp.where(row_ids[..., None] == table_ids, owner_map, 0), axis=-1)
    target = position // out_dev
    serial = jnp.arange(row_ids.shape[-1], dtype=jnp.int32)
    earlier = (target[..., :, None] == target[..., None, :]) & (serial[:, None] > serial[None, :])
    ranking = jnp.sum(earlier.astype(jnp.int32), axis=-1)
    return (position % out_dev, target, ranking)


def add_products(summed, arrived, slot_labels, panel_tiles):
    slot_count = arrived.shape[0]
    block_rows = math.gcd(slot_count, 32)
    out_dev = summed.shape[0]
    local_ids = jnp.arange(out_dev, dtype=jnp.int32)

    def one_block(which_block, running, source_tiles, source_labels):
        part_tiles = lax.dynamic_slice_in_dim(source_tiles, which_block * block_rows, block_rows, 0)
        part_labels = lax.dynamic_slice_in_dim(
            source_labels, which_block * block_rows, block_rows, 0
        )
        chosen = jnp.take(panel_tiles, part_labels[:, 1], axis=0)
        products = jnp.einsum(
            "sab,sbc->sac", part_tiles, chosen, preferred_element_type=jnp.float32
        )
        row_hits = (part_labels[:, 0][:, None] == local_ids[None, :]).astype(jnp.float32)
        return running + jnp.einsum(
            "sr,sac->rac", row_hits, products, precision=lax.Precision.HIGHEST
        )

    return lax.fori_loop(
        0,
        slot_count // block_rows,
        lambda which_block, running: one_block(which_block, running, arrived, slot_labels),
        summed,
    )


def slots_plan(tiles, contraction, row_tile, owner_map, panel):
    wide_count = lax.axis_size("wide")
    tile_dev = tiles.shape[0]
    tile_side = tiles.shape[1]
    out_dev = owner_map.shape[0] // wide_count
    most_slots = tile_dev * 8 // (3 * wide_count)
    slot_total = wide_count * most_slots
    local_row, target, ranking = place_slots(row_tile, owner_map, out_dev)
    slot_index = target * most_slots + ranking
    outgoing = jnp.zeros((slot_total, tile_side, tile_side), tiles.dtype).at[slot_index].set(tiles)
    all_rows, all_contraction = (
        lax.all_gather(row_tile, "wide", axis=0, tiled=True),
        lax.all_gather(contraction, "wide", axis=0, tiled=True),
    )
    all_rows = all_rows.reshape(wide_count, tile_dev)
    all_contraction = all_contraction.reshape(wide_count, tile_dev)
    source_local, source_target, source_rank = place_slots(all_rows, owner_map, out_dev)
    source_ids = jnp.arange(wide_count, dtype=jnp.int32)
    mine = source_target == lax.axis_index("wide")
    arrive_index = jnp.where(mine, source_ids[:, None] * most_slots + source_rank, slot_total)
    label_pairs = jnp.stack([source_local, all_contraction], axis=-1).reshape(
        wide_count * tile_dev, 2
    )
    vacant_label = jnp.stack(
        [jnp.full((slot_total,), out_dev, jnp.int32), jnp.zeros((slot_total,), jnp.int32)], axis=1
    )
    arrived_labels = vacant_label.at[arrive_index.reshape(-1)].set(label_pairs, mode="drop")
    gathered = lax.all_gather(panel, "grp", axis=0, tiled=True)
    panel_tiles = gathered.reshape(gathered.shape[0] // tile_side, tile_side, gathered.shape[1])
    summed = jnp.zeros((out_dev, tile_side, gathered.shape[1]), jnp.float32)
    arrived = lax.all_to_all(outgoing, "wide", split_axis=0, concat_axis=0, tiled=True)
    summed = add_products(summed, arrived, arrived_labels, panel_tiles)
    summed = lax.psum(summed, "grp")
    return summed.reshape(out_dev * tile_side, gathered.shape[1])


def encode(value):
    largest = jnp.max(jnp.abs(value), axis=0, keepdims=True)
    code = jnp.ceil(jnp.log(jnp.maximum(largest, 1e-30)) * (CODE_STEPS / LOG2))
    scale = jnp.exp(code * (-LOG2 / CODE_STEPS)) * TOP
    whole = jnp.round(value * scale).astype(jnp.int32).astype(jnp.int16)
    return whole, code.astype(jnp.int32)


def put_encoded(ref, value):
    side = value.shape[0]
    whole, code = encode(value)
    ref[pl.ds(0, side), :] = whole
    ref[pl.ds(side, CODE_ROWS), :] = jnp.broadcast_to(
        code, (CODE_ROWS, code.shape[1])
    ).astype(jnp.int16)


def get_decoded(ref, side):
    code = ref[pl.ds(side, CODE_ROWS), :].astype(jnp.int32).astype(jnp.float32)[:1]
    scale = jnp.exp(code * (LOG2 / CODE_STEPS)) * (1.0 / TOP)
    return ref[pl.ds(0, side), :].astype(jnp.int32).astype(jnp.float32) * scale


def hold_kernel(order_ref, tiles, out, sem):
    copy = pltpu.make_async_copy(tiles, out, sem)
    copy.start()
    copy.wait()


def join_kernel(order_ref, *refs):
    *parts, out = refs
    rows = parts[0].shape[0]
    for i, part in enumerate(parts):
        out[pl.ds(i * rows, rows), :] = part[...]


def products_kernel(
    count_ref, source_ref, slot_ref, label_ref, own_tiles, sib_tiles, *refs
):
    own_panel, near, far, *outs, stack, acc = refs
    side = own_tiles.shape[1]
    shard = own_panel.shape[0] // side
    half = shard // 2
    for t in range(shard):
        stack[t] = own_panel[pl.ds(t * side, side), :]
    for i in range(3 * half):
        at = shard + (i // half) * shard + i % half
        stack[at] = near[pl.ds(i * side, side), :]
        stack[at + half] = far[pl.ds(i * side, side), :]

    @pl.loop(0, acc.shape[0])
    def _(i):
        acc[i] = jnp.zeros(acc.shape[1:], jnp.float32)

    for which, tiles in enumerate((own_tiles, sib_tiles)):

        def some(at, count, which=which, tiles=tiles):
            found = [
                jnp.dot(
                    tiles[source_ref[which, at + u]],
                    stack[label_ref[which, at + u]],
                    preferred_element_type=jnp.float32,
                )
                for u in range(count)
            ]
            for u in range(count):
                acc[slot_ref[which, at + u]] += found[u]

        count = count_ref[which]
        rounds = count // UNROLL

        @pl.loop(0, rounds)
        def _(i, some=some):
            some(i * UNROLL, UNROLL)

        @pl.loop(rounds * UNROLL, count)
        def _(i, some=some):
            some(i, 1)

    sent = 0
    for out in outs:

        @pl.loop(0, out.shape[0])
        def _(i, out=out, sent=sent):
            if out.dtype == jnp.int16:
                put_encoded(out.at[i], acc[sent + i])
            else:
                out[i] = acc[sent + i]

        sent += out.shape[0]


def plane_kernel(bits_ref, recv_a, recv_b, kept, send_a, send_b, keep):
    side, half = kept.shape[1], send_a.shape[0]
    for first, bit, recv, send in ((0, bits_ref[1], recv_a, send_a), (1, bits_ref[0], recv_b, send_b)):

        @pl.loop(0, half)
        def _(i, first=first, bit=bit, recv=recv, send=send):
            other, mine = 2 * i + 1 - bit, 2 * i + bit
            base = first * 2 * half
            put_encoded(send.at[i], kept[base + other] + get_decoded(recv.at[other], side))
            keep[first * half + i] = kept[base + mine] + get_decoded(recv.at[mine], side)


def owner_kernel(bits_ref, recv_a, recv_b, kept, send, keep):
    side, half = kept.shape[1], send.shape[0]
    odd = bits_ref[2]

    @pl.loop(0, half)
    def _(i):
        value_a = kept[i] + get_decoded(recv_a.at[i], side)
        value_b = kept[half + i] + get_decoded(recv_b.at[i], side)
        put_encoded(send.at[i], jnp.where(odd == 1, value_a, value_b))
        keep[i] = jnp.where(odd == 1, value_b, value_a)


def line_kernel(bits_ref, recv, kept, send, keep):
    side, half = kept.shape[1], send.shape[0]
    bit = bits_ref[3]

    @pl.loop(0, half)
    def _(i):
        other, mine = (1 - bit) * half + i, bit * half + i
        put_encoded(send.at[i], kept[other] + get_decoded(recv.at[other], side))
        keep[i] = kept[mine] + get_decoded(recv.at[mine], side)


def rows_kernel(bits_ref, recv, kept, send_1, send_2, send_3, keep):
    side = kept.shape[1]
    row = bits_ref[1] * 2 + bits_ref[0]
    for d, send in enumerate((send_1, send_2, send_3), 1):
        put_encoded(send, kept[row ^ d] + get_decoded(recv.at[row ^ d], side))
    keep[...] = kept[row] + get_decoded(recv.at[row], side)


def finish_kernel(bits_ref, *refs):
    *recvs, kept, out = refs
    value = kept[...]
    for recv in recvs:
        value += get_decoded(recv, kept.shape[0])
    put_encoded(out, value)


def spread_kernel(bits_ref, *refs):
    blocks, out = refs[:4], refs[-1]
    side = blocks[0].shape[0] - CODE_ROWS
    row = bits_ref[1] * 2 + bits_ref[0]
    for d, block in enumerate(blocks):
        at = pl.multiple_of((row ^ d) * side, side)
        out[pl.ds(at, side), :] = get_decoded(block, side)


def in_vmem(count):
    return [pl.BlockSpec(memory_space=pltpu.VMEM)] * count


def in_smem(count):
    return [pl.BlockSpec(memory_space=pltpu.SMEM)] * count


def in_any(count):
    return [pl.BlockSpec(memory_space=pl.ANY)] * count


def shape(dims, kind):
    return jax.ShapeDtypeStruct(dims, kind)


def params(mib):
    return pltpu.CompilerParams(vmem_limit_bytes=mib * MIB)


def cost(flops, moved):
    return pl.CostEstimate(flops=flops, bytes_accessed=moved, transcendentals=0)


def compact(match, values):
    count = match.shape[-1]
    rank = jnp.cumsum(match.astype(jnp.int32), axis=-1) - 1
    at = jnp.arange(count, dtype=jnp.int32)
    hit = match[:, None, :] & (rank[:, None, :] == at[None, :, None])
    return [jnp.sum(jnp.where(hit, v[:, None, :], 0), axis=-1) for v in values]


def sums_plan(tiles, contraction, row_tile, owner_map, panel):
    wide_count = lax.axis_size("wide")
    tile_dev, side = tiles.shape[0], tiles.shape[1]
    out_dev = owner_map.shape[0] // wide_count
    rows, columns = panel.shape
    shard = rows // side
    chunks = columns // CHUNK
    sums = owner_map.shape[0] // 2
    g, w = lax.axis_index("grp"), lax.axis_index("wide")
    core = w % 2

    def to_core(v):
        return lax.ppermute(v, "wide", [(i, i ^ 1) for i in range(wide_count)])

    def to_grp(v, d):
        return lax.ppermute(v, "grp", [(i, i ^ d) for i in range(4)])

    def to_line(v, b):
        return lax.ppermute(v, "wide", [(i, i ^ (2 << b)) for i in range(wide_count)])

    x, y, z = g % 2, g // 2, w // 2
    bits = jnp.stack([x, y, z % 2, z // 2]).astype(jnp.int32)

    labels = jnp.stack([row_tile, contraction])
    both = jnp.stack([labels, to_core(labels)])
    sib_tiles = to_core(tiles)

    mines = [
        lax.dynamic_slice(panel, (core * (rows // 2), j * CHUNK), (rows // 2, CHUNK))
        for j in range(chunks)
    ]
    near = [[to_grp(mines[0], d) for d in (1, 2, 3)]]
    for mine in mines[1:]:
        mine = lax.optimization_barrier((mine, *near[-1]))[0]
        near.append([to_grp(mine, d) for d in (1, 2, 3)])

    table_ids = jnp.arange(owner_map.shape[0], dtype=jnp.int32)
    position = jnp.sum(jnp.where(both[:, 0, :, None] == table_ids, owner_map, 0), axis=-1)
    owner, local = position // out_dev, position % out_dev
    to_z, odd = owner // 4, (owner // 2) % 2
    bit_x, bit_y = local % 2, local // 2
    first = jnp.where(odd == 1, bit_y == y, bit_x == x)
    second = jnp.where(odd == 1, bit_x, bit_y)
    in_plane = jnp.where(first, sums // 2, 0) + odd * (sums // 4) + 2 * to_z + second
    in_line = jnp.where(odd == z % 2, sums // 2, 0) + to_z * out_dev + local
    k = both[:, 1]
    apart, inner = (k // shard) ^ g, k % shard
    half = shard // 2
    crossed = jnp.where(inner // half == core, 0, half) + inner % half
    label = jnp.where(apart == 0, inner, apart * shard + crossed)
    match = owner % 2 == core
    serial = jnp.broadcast_to(jnp.arange(tile_dev, dtype=jnp.int32), match.shape)
    source, in_plane, in_line, label = compact(match, [serial, in_plane, in_line, label])
    found = jnp.sum(match.astype(jnp.int32), axis=-1)

    half, quarter = sums // 2, sums // 4
    coded = shape((side + CODE_ROWS, CHUNK), jnp.int16)
    plain = shape((side, CHUNK), jnp.float32)

    def stack_of(count, one):
        return shape((count, *one.shape), one.dtype)

    last = None

    def in_order(small):
        return small if last is None else lax.optimization_barrier((small, last))[0]

    def call(body, name, outs, *args):
        nonlocal last
        done = pl.pallas_call(
            body,
            in_specs=in_smem(1) + in_vmem(len(args)),
            out_specs=in_vmem(len(outs)),
            out_shape=outs,
            compiler_params=params(16),
            cost_estimate=cost(0, sum(math.prod(a.shape) * a.dtype.itemsize for a in args)),
            name=name,
        )(in_order(bits), *args)
        last = done[0]
        return done

    own_tiles = pl.pallas_call(
        hold_kernel,
        in_specs=in_smem(1) + in_any(1),
        out_specs=in_vmem(1)[0],
        out_shape=shape(tiles.shape, tiles.dtype),
        scratch_shapes=[pltpu.SemaphoreType.DMA],
        compiler_params=params(54),
        cost_estimate=cost(0, 2 * tile_dev * side * side),
        name="hold",
    )(lax.optimization_barrier((bits, both))[0], tiles)
    last = own_tiles

    def join(j):
        (joined,) = call(join_kernel, "join", [shape((3 * rows // 2, CHUNK), panel.dtype)], *near[j])
        return joined, to_core(joined)

    def products(j, slot, outs, joined, crossed):
        nonlocal last
        done = pl.pallas_call(
            products_kernel,
            grid=(1,),
            in_specs=in_smem(4)
            + in_vmem(2)
            + [pl.BlockSpec((rows, CHUNK), lambda i: (0, j))]
            + in_vmem(2),
            out_specs=in_vmem(len(outs)),
            out_shape=outs,
            scratch_shapes=[
                pltpu.VMEM((4 * shard, side, CHUNK), panel.dtype),
                pltpu.VMEM((sums, side, CHUNK), jnp.float32),
            ],
            compiler_params=params(32),
            cost_estimate=cost(0, 4 * tile_dev * side * side),
            name="products",
        )(in_order(found), source, slot, label, own_tiles, sib_tiles, panel, joined, crossed)
        last = done[0]
        return done

    def spread(j, done, result):
        nonlocal last
        blocks = [done] + [to_grp(done, d) for d in (1, 2, 3)]
        earlier = [] if result is None else [result]
        last = pl.pallas_call(
            spread_kernel,
            grid=(1,),
            in_specs=in_smem(1) + in_vmem(4) + in_any(len(earlier)),
            out_specs=pl.BlockSpec((out_dev * side, CHUNK), lambda i: (0, j)),
            out_shape=shape((out_dev * side, columns), jnp.float32),
            input_output_aliases={5: 0} if earlier else {},
            compiler_params=params(16),
            cost_estimate=cost(0, 6 * out_dev * side * CHUNK),
            name="spread",
        )(in_order(bits), *blocks, *earlier)
        return last

    def line_first(j):
        joined, crossed = join(j)
        yield
        send, keep = products(
            j, in_line, [stack_of(half, coded), stack_of(half, plain)], joined, crossed
        )
        yield
        recv = to_line(send, 0)
        send, keep = call(
            line_kernel, "line", [stack_of(quarter, coded), stack_of(quarter, plain)], recv, keep
        )
        yield
        *sends, keep = call(rows_kernel, "rows", [coded] * 3 + [plain], to_line(send, 1), keep)
        yield
        recvs = [to_grp(v, d) for d, v in enumerate(sends, 1)]
        (done,) = call(finish_kernel, "finish", [coded], *recvs, keep)
        yield
        yield done

    def plane_first(j):
        joined, crossed = join(j)
        yield
        send_a, send_b, keep = products(
            j, in_plane, [stack_of(quarter, coded)] * 2 + [stack_of(half, plain)], joined, crossed
        )
        yield
        send_a, send_b, keep = call(
            plane_kernel,
            "plane",
            [stack_of(quarter // 2, coded)] * 2 + [stack_of(quarter, plain)],
            to_grp(send_a, 1),
            to_grp(send_b, 2),
            keep,
        )
        yield
        send, keep = call(
            owner_kernel,
            "owner",
            [stack_of(quarter // 2, coded), stack_of(quarter // 2, plain)],
            to_grp(send_a, 2),
            to_grp(send_b, 1),
            keep,
        )
        yield
        send, keep = call(
            line_kernel,
            "line",
            [stack_of(quarter // 4, coded), stack_of(quarter // 4, plain)],
            to_line(send, 0),
            keep,
        )
        yield
        recv = to_line(send, 1)
        (done,) = call(finish_kernel, "finish", [coded], recv[0], keep[0])
        yield
        yield done

    steps, lengths = [0] * chunks, [5] + [6] * (chunks - 1)
    work = [(line_first if j == 0 else plane_first)(j) for j in range(chunks)]
    dones, result = {}, None
    for j in (0, 0, 1, 1, 2, 2, 0, 1, 2, 1, 0, 2, 1, 0, 1, 2, 0, 2, 1, 2):
        if j in dones:
            result = spread(j, dones[j], result)
            continue
        next(work[j])
        steps[j] += 1
        if steps[j] == lengths[j]:
            dones[j] = next(work[j])
    return result


def per_device(tiles, contraction, row_tile, owner_map, panel):
    dense = owner_map.shape[0] <= tiles.shape[0]
    wide_count = lax.axis_size("wide")
    fits = lax.axis_size("grp") == 4 and wide_count >= 4 and wide_count & (wide_count - 1) == 0
    out_dev = owner_map.shape[0] // wide_count
    if dense and fits and wide_count == 8 and out_dev == 4 and panel.shape[1] == 3 * CHUNK:
        return sums_plan(tiles, contraction, row_tile, owner_map, panel)
    return slots_plan(tiles, contraction, row_tile, owner_map, panel)


def solution(mesh):
    return jax.shard_map(
        per_device,
        mesh=mesh,
        in_specs=(
            P(("grp", "wide"), None, None),
            P(("grp", "wide")),
            P(("grp", "wide")),
            P(),
            P("grp", None),
        ),
        out_specs=P("wide", None),
        check_vma=False,
    )
```

```python
import functools
import math

import jax
import jax.numpy as jnp
from jax import lax
from jax.experimental import pallas as pl
from jax.experimental.pallas import tpu as pltpu
from jax.sharding import PartitionSpec as P

MIB = 1024 * 1024
CODE_ROWS = 16
CODE_STEPS = 256.0
TOP = 32000.0
CHUNK = 256
UNROLL = 8
LOG2 = math.log(2.0)


def place_slots(row_ids, owner_map, out_dev):
    table_ids = jnp.arange(owner_map.shape[0], dtype=jnp.int32)
    position = jnp.sum(jnp.where(row_ids[..., None] == table_ids, owner_map, 0), axis=-1)
    target = position // out_dev
    serial = jnp.arange(row_ids.shape[-1], dtype=jnp.int32)
    earlier = (target[..., :, None] == target[..., None, :]) & (serial[:, None] > serial[None, :])
    ranking = jnp.sum(earlier.astype(jnp.int32), axis=-1)
    return (position % out_dev, target, ranking)


def add_products(summed, arrived, slot_labels, panel_tiles):
    slot_count = arrived.shape[0]
    block_rows = math.gcd(slot_count, 32)
    out_dev = summed.shape[0]
    local_ids = jnp.arange(out_dev, dtype=jnp.int32)

    def one_block(which_block, running, source_tiles, source_labels):
        part_tiles = lax.dynamic_slice_in_dim(source_tiles, which_block * block_rows, block_rows, 0)
        part_labels = lax.dynamic_slice_in_dim(
            source_labels, which_block * block_rows, block_rows, 0
        )
        chosen = jnp.take(panel_tiles, part_labels[:, 1], axis=0)
        products = jnp.einsum(
            "sab,sbc->sac", part_tiles, chosen, preferred_element_type=jnp.float32
        )
        row_hits = (part_labels[:, 0][:, None] == local_ids[None, :]).astype(jnp.float32)
        return running + jnp.einsum(
            "sr,sac->rac", row_hits, products, precision=lax.Precision.HIGHEST
        )

    return lax.fori_loop(
        0,
        slot_count // block_rows,
        lambda which_block, running: one_block(which_block, running, arrived, slot_labels),
        summed,
    )


def slots_plan(tiles, contraction, row_tile, owner_map, panel):
    wide_count = lax.axis_size("wide")
    tile_dev = tiles.shape[0]
    tile_side = tiles.shape[1]
    out_dev = owner_map.shape[0] // wide_count
    most_slots = tile_dev * 8 // (3 * wide_count)
    slot_total = wide_count * most_slots
    local_row, target, ranking = place_slots(row_tile, owner_map, out_dev)
    slot_index = target * most_slots + ranking
    outgoing = jnp.zeros((slot_total, tile_side, tile_side), tiles.dtype).at[slot_index].set(tiles)
    all_rows, all_contraction = (
        lax.all_gather(row_tile, "wide", axis=0, tiled=True),
        lax.all_gather(contraction, "wide", axis=0, tiled=True),
    )
    all_rows = all_rows.reshape(wide_count, tile_dev)
    all_contraction = all_contraction.reshape(wide_count, tile_dev)
    source_local, source_target, source_rank = place_slots(all_rows, owner_map, out_dev)
    source_ids = jnp.arange(wide_count, dtype=jnp.int32)
    mine = source_target == lax.axis_index("wide")
    arrive_index = jnp.where(mine, source_ids[:, None] * most_slots + source_rank, slot_total)
    label_pairs = jnp.stack([source_local, all_contraction], axis=-1).reshape(
        wide_count * tile_dev, 2
    )
    vacant_label = jnp.stack(
        [jnp.full((slot_total,), out_dev, jnp.int32), jnp.zeros((slot_total,), jnp.int32)], axis=1
    )
    arrived_labels = vacant_label.at[arrive_index.reshape(-1)].set(label_pairs, mode="drop")
    gathered = lax.all_gather(panel, "grp", axis=0, tiled=True)
    panel_tiles = gathered.reshape(gathered.shape[0] // tile_side, tile_side, gathered.shape[1])
    summed = jnp.zeros((out_dev, tile_side, gathered.shape[1]), jnp.float32)
    arrived = lax.all_to_all(outgoing, "wide", split_axis=0, concat_axis=0, tiled=True)
    summed = add_products(summed, arrived, arrived_labels, panel_tiles)
    summed = lax.psum(summed, "grp")
    return summed.reshape(out_dev * tile_side, gathered.shape[1])


def encode(value):
    largest = jnp.max(jnp.abs(value), axis=0, keepdims=True)
    code = jnp.ceil(jnp.log(jnp.maximum(largest, 1e-30)) * (CODE_STEPS / LOG2))
    scale = jnp.exp(code * (-LOG2 / CODE_STEPS)) * TOP
    whole = jnp.round(value * scale).astype(jnp.int32).astype(jnp.int16)
    return whole, code.astype(jnp.int32)


def put_encoded(ref, value):
    side = value.shape[0]
    whole, code = encode(value)
    ref[pl.ds(0, side), :] = whole
    ref[pl.ds(side, CODE_ROWS), :] = jnp.broadcast_to(
        code, (CODE_ROWS, code.shape[1])
    ).astype(jnp.int16)


def get_decoded(ref, side):
    code = ref[pl.ds(side, CODE_ROWS), :].astype(jnp.int32).astype(jnp.float32)[:1]
    scale = jnp.exp(code * (LOG2 / CODE_STEPS)) * (1.0 / TOP)
    return ref[pl.ds(0, side), :].astype(jnp.int32).astype(jnp.float32) * scale


def hold_kernel(order_ref, tiles, out, sem):
    copy = pltpu.make_async_copy(tiles, out, sem)
    copy.start()
    copy.wait()


def join_kernel(order_ref, *refs):
    *parts, out = refs
    rows = parts[0].shape[0]
    for i, part in enumerate(parts):
        out[pl.ds(i * rows, rows), :] = part[...]


def products_kernel(
    fill, rounds_ref, source_ref, slot_ref, label_ref, own_tiles, sib_tiles, own_panel, *refs
):
    parts = refs[: 1 + max(which for which, _, _ in fill)]
    *outs, stack, acc = refs[len(parts) :]
    side = own_tiles.shape[1]
    for t in range(own_panel.shape[0] // side):
        stack[t] = own_panel[pl.ds(t * side, side), :]
    for which, t, at in fill:
        stack[at] = parts[which][pl.ds(t * side, side), :]

    @pl.loop(0, acc.shape[0])
    def _(i):
        acc[i] = jnp.zeros(acc.shape[1:], jnp.float32)

    for which, tiles in enumerate((own_tiles, sib_tiles)):

        @pl.loop(0, rounds_ref[which])
        def _(i, which=which, tiles=tiles):
            found = [
                jnp.dot(
                    tiles[source_ref[which, i * UNROLL + u]],
                    stack[label_ref[which, i * UNROLL + u]],
                    preferred_element_type=jnp.float32,
                )
                for u in range(UNROLL)
            ]
            for u in range(UNROLL):
                acc[slot_ref[which, i * UNROLL + u]] += found[u]

    sent = 0
    for out in outs:

        @pl.loop(0, out.shape[0])
        def _(i, out=out, sent=sent):
            if out.dtype == jnp.int16:
                put_encoded(out.at[i], acc[sent + i])
            else:
                out[i] = acc[sent + i]

        sent += out.shape[0]


def plane_kernel(bits_ref, recv_a, recv_b, kept, send_a, send_b, keep):
    side, half = kept.shape[1], send_a.shape[0]
    for first, bit, recv, send in ((0, bits_ref[1], recv_a, send_a), (1, bits_ref[0], recv_b, send_b)):

        @pl.loop(0, half)
        def _(i, first=first, bit=bit, recv=recv, send=send):
            other, mine = 2 * i + 1 - bit, 2 * i + bit
            base = first * 2 * half
            put_encoded(send.at[i], kept[base + other] + get_decoded(recv.at[other], side))
            keep[first * half + i] = kept[base + mine] + get_decoded(recv.at[mine], side)


def owner_kernel(bits_ref, recv_a, recv_b, kept, send, keep):
    side, half = kept.shape[1], send.shape[0]
    odd = bits_ref[2]

    @pl.loop(0, half)
    def _(i):
        value_a = kept[i] + get_decoded(recv_a.at[i], side)
        value_b = kept[half + i] + get_decoded(recv_b.at[i], side)
        put_encoded(send.at[i], jnp.where(odd == 1, value_a, value_b))
        keep[i] = jnp.where(odd == 1, value_b, value_a)


def line_kernel(bits_ref, recv, kept, send, keep):
    side, half = kept.shape[1], send.shape[0]
    bit = bits_ref[3]

    @pl.loop(0, half)
    def _(i):
        other, mine = (1 - bit) * half + i, bit * half + i
        put_encoded(send.at[i], kept[other] + get_decoded(recv.at[other], side))
        keep[i] = kept[mine] + get_decoded(recv.at[mine], side)


def rows_kernel(bits_ref, recv, kept, send_1, send_2, send_3, keep):
    side = kept.shape[1]
    row = bits_ref[1] * 2 + bits_ref[0]
    for d, send in enumerate((send_1, send_2, send_3), 1):
        put_encoded(send, kept[row ^ d] + get_decoded(recv.at[row ^ d], side))
    keep[...] = kept[row] + get_decoded(recv.at[row], side)


def finish_kernel(bits_ref, *refs):
    *recvs, kept, out = refs
    value = kept[...]
    for recv in recvs:
        value += get_decoded(recv, kept.shape[0])
    put_encoded(out, value)


def spread_kernel(bits_ref, *refs):
    blocks, out = refs[:4], refs[-1]
    side = blocks[0].shape[0] - CODE_ROWS
    row = bits_ref[1] * 2 + bits_ref[0]
    for d, block in enumerate(blocks):
        at = pl.multiple_of((row ^ d) * side, side)
        out[pl.ds(at, side), :] = get_decoded(block, side)


def in_vmem(count):
    return [pl.BlockSpec(memory_space=pltpu.VMEM)] * count


def in_smem(count):
    return [pl.BlockSpec(memory_space=pltpu.SMEM)] * count


def in_any(count):
    return [pl.BlockSpec(memory_space=pl.ANY)] * count


def shape(dims, kind):
    return jax.ShapeDtypeStruct(dims, kind)


def params(mib):
    return pltpu.CompilerParams(vmem_limit_bytes=mib * MIB)


def cost(flops, moved):
    return pl.CostEstimate(flops=flops, bytes_accessed=moved, transcendentals=0)


def compact(match, values):
    count = -(-match.shape[-1] // UNROLL) * UNROLL
    rank = jnp.cumsum(match.astype(jnp.int32), axis=-1) - 1
    at = jnp.arange(count, dtype=jnp.int32)
    hit = match[:, None, :] & (rank[:, None, :] == at[None, :, None])
    return [jnp.sum(jnp.where(hit, v[:, None, :], 0), axis=-1) for v in values]


def sums_plan(tiles, contraction, row_tile, owner_map, panel):
    wide_count = lax.axis_size("wide")
    tile_dev, side = tiles.shape[0], tiles.shape[1]
    out_dev = owner_map.shape[0] // wide_count
    rows, columns = panel.shape
    shard = rows // side
    chunks = columns // CHUNK
    sums = owner_map.shape[0] // 2
    g, w = lax.axis_index("grp"), lax.axis_index("wide")
    core = w % 2

    def to_core(v):
        return lax.ppermute(v, "wide", [(i, i ^ 1) for i in range(wide_count)])

    def to_grp(v, d):
        return lax.ppermute(v, "grp", [(i, i ^ d) for i in range(4)])

    def to_line(v, b):
        return lax.ppermute(v, "wide", [(i, i ^ (2 << b)) for i in range(wide_count)])

    x, y, z = g % 2, g // 2, w // 2
    bits = jnp.stack([x, y, z % 2, z // 2]).astype(jnp.int32)

    labels = jnp.stack([row_tile, contraction])
    both = jnp.stack([labels, to_core(labels)])
    sib_tiles = to_core(tiles)

    def own_half(source, j):
        return lax.dynamic_slice(source, (core * (rows // 2), j * CHUNK), (rows // 2, CHUNK))

    mine = own_half(panel, 0)
    near = [to_grp(mine, d) for d in (1, 2, 3)]
    later = lax.optimization_barrier((panel, *near))[0]
    ways = [None, (1, 2), (2, 1)]
    mines = [mine] + [own_half(later, j) for j in range(1, chunks)]
    firsts = [None] + [to_grp(mines[j], ways[j][0]) for j in range(1, chunks)]

    table_ids = jnp.arange(owner_map.shape[0], dtype=jnp.int32)
    position = jnp.sum(jnp.where(both[:, 0, :, None] == table_ids, owner_map, 0), axis=-1)
    owner, local = position // out_dev, position % out_dev
    to_z, odd = owner // 4, (owner // 2) % 2
    bit_x, bit_y = local % 2, local // 2
    first = jnp.where(odd == 1, bit_y == y, bit_x == x)
    second = jnp.where(odd == 1, bit_x, bit_y)
    in_plane = jnp.where(first, sums // 2, 0) + odd * (sums // 4) + 2 * to_z + second
    in_line = jnp.where(odd == z % 2, sums // 2, 0) + to_z * out_dev + local
    k = both[:, 1]
    apart, inner = (k // shard) ^ g, k % shard
    half = shard // 2
    crossed = jnp.where(inner // half == core, 0, half) + inner % half
    label = jnp.where(apart == 0, inner, apart * shard + crossed)
    match = owner % 2 == core
    serial = jnp.broadcast_to(jnp.arange(tile_dev, dtype=jnp.int32), match.shape)
    source, in_plane, in_line, label = compact(match, [serial, in_plane, in_line, label])
    found = jnp.sum(match.astype(jnp.int32), axis=-1)
    rounds = (found + UNROLL - 1) // UNROLL
    beyond = jnp.arange(source.shape[-1], dtype=jnp.int32) >= found[:, None]
    in_plane = jnp.where(beyond, sums, in_plane)
    in_line = jnp.where(beyond, sums, in_line)

    half, quarter = sums // 2, sums // 4
    coded = shape((side + CODE_ROWS, CHUNK), jnp.int16)
    plain = shape((side, CHUNK), jnp.float32)

    def stack_of(count, one):
        return shape((count, *one.shape), one.dtype)

    last = None

    def in_order(small):
        return small if last is None else lax.optimization_barrier((small, last))[0]

    def call(body, name, outs, *args):
        nonlocal last
        done = pl.pallas_call(
            body,
            in_specs=in_smem(1) + in_vmem(len(args)),
            out_specs=in_vmem(len(outs)),
            out_shape=outs,
            compiler_params=params(16),
            cost_estimate=cost(0, sum(math.prod(a.shape) * a.dtype.itemsize for a in args)),
            name=name,
        )(in_order(bits), *args)
        last = done[0]
        return done

    own_tiles = pl.pallas_call(
        hold_kernel,
        in_specs=in_smem(1) + in_any(1),
        out_specs=in_vmem(1)[0],
        out_shape=shape(tiles.shape, tiles.dtype),
        scratch_shapes=[pltpu.SemaphoreType.DMA],
        compiler_params=params(16),
        cost_estimate=cost(0, 2 * tile_dev * side * side),
        name="hold",
    )(lax.optimization_barrier((bits, both))[0], tiles)
    last = own_tiles

    def places(operand, tiles_of, first):
        return [
            (operand, t, d * shard + first + i % part)
            for i, (t, d) in enumerate((t, d) for d, ts in tiles_of for t in ts)
        ]

    part = shard // 2

    def join(j):
        (joined,) = call(join_kernel, "join", [shape((3 * rows // 2, CHUNK), panel.dtype)], *near)
        tiles_of = [(d, range((d - 1) * part, d * part)) for d in (1, 2, 3)]
        fill = places(0, tiles_of, 0) + places(1, tiles_of, part)
        return fill, [joined, to_core(joined)]

    def pair(j):
        way, other = ways[j]
        (joined,) = call(
            join_kernel, "join", [shape((rows, CHUNK), panel.dtype)], mines[j], firsts[j]
        )
        second = to_grp(joined, other)
        in_first = [(way, range(part, 2 * part))]
        in_second = [(other, range(part)), (way ^ other, range(part, 2 * part))]
        fill = (
            places(0, in_first, 0)
            + places(1, in_first, part)
            + places(2, in_second, 0)
            + places(3, in_second, part)
        )
        return fill, [joined, to_core(joined), second, to_core(second)]

    def products(j, slot, outs, fill, parts):
        nonlocal last
        done = pl.pallas_call(
            functools.partial(products_kernel, tuple(fill)),
            grid=(1,),
            in_specs=in_smem(4)
            + in_vmem(2)
            + [pl.BlockSpec((rows, CHUNK), lambda i: (0, j))]
            + in_vmem(len(parts)),
            out_specs=in_vmem(len(outs)),
            out_shape=outs,
            scratch_shapes=[
                pltpu.VMEM((4 * shard, side, CHUNK), panel.dtype),
                pltpu.VMEM((sums + 1, side, CHUNK), jnp.float32),
            ],
            compiler_params=params(32),
            cost_estimate=cost(0, 4 * tile_dev * side * side),
            name="products",
        )(in_order(rounds), source, slot, label, own_tiles, sib_tiles, panel, *parts)
        last = done[0]
        return done

    def spread(j, done, result):
        nonlocal last
        blocks = [done] + [to_grp(done, d) for d in (1, 2, 3)]
        earlier = [] if result is None else [result]
        last = pl.pallas_call(
            spread_kernel,
            grid=(1,),
            in_specs=in_smem(1) + in_vmem(4) + in_any(len(earlier)),
            out_specs=pl.BlockSpec((out_dev * side, CHUNK), lambda i: (0, j)),
            out_shape=shape((out_dev * side, columns), jnp.float32),
            input_output_aliases={5: 0} if earlier else {},
            compiler_params=params(16),
            cost_estimate=cost(0, 6 * out_dev * side * CHUNK),
            name="spread",
        )(in_order(bits), *blocks, *earlier)
        return last

    def line_first(j):
        panel_of = join(j)
        yield
        send, keep = products(
            j, in_line, [stack_of(half, coded), stack_of(half, plain)], *panel_of
        )
        yield
        recv = to_line(send, 0)
        send, keep = call(
            line_kernel, "line", [stack_of(quarter, coded), stack_of(quarter, plain)], recv, keep
        )
        yield
        *sends, keep = call(rows_kernel, "rows", [coded] * 3 + [plain], to_line(send, 1), keep)
        yield
        recvs = [to_grp(v, d) for d, v in enumerate(sends, 1)]
        (done,) = call(finish_kernel, "finish", [coded], *recvs, keep)
        yield
        yield done

    def plane_first(j):
        panel_of = pair(j)
        yield
        send_a, send_b, keep = products(
            j, in_plane, [stack_of(quarter, coded)] * 2 + [stack_of(half, plain)], *panel_of
        )
        yield
        send_a, send_b, keep = call(
            plane_kernel,
            "plane",
            [stack_of(quarter // 2, coded)] * 2 + [stack_of(quarter, plain)],
            to_grp(send_a, 1),
            to_grp(send_b, 2),
            keep,
        )
        yield
        send, keep = call(
            owner_kernel,
            "owner",
            [stack_of(quarter // 2, coded), stack_of(quarter // 2, plain)],
            to_grp(send_a, 2),
            to_grp(send_b, 1),
            keep,
        )
        yield
        send, keep = call(
            line_kernel,
            "line",
            [stack_of(quarter // 4, coded), stack_of(quarter // 4, plain)],
            to_line(send, 0),
            keep,
        )
        yield
        recv = to_line(send, 1)
        (done,) = call(finish_kernel, "finish", [coded], recv[0], keep[0])
        yield
        yield done

    steps, lengths = [0] * chunks, [5] + [6] * (chunks - 1)
    work = [(line_first if j == 0 else plane_first)(j) for j in range(chunks)]
    dones, result = {}, None
    for j in (0, 0, 1, 2, 1, 2, 0, 1, 2, 1, 0, 2, 1, 0, 1, 2, 0, 2, 1, 2):
        if j in dones:
            result = spread(j, dones[j], result)
            continue
        next(work[j])
        steps[j] += 1
        if steps[j] == lengths[j]:
            dones[j] = next(work[j])
    return result


def per_device(tiles, contraction, row_tile, owner_map, panel):
    dense = owner_map.shape[0] <= tiles.shape[0]
    wide_count = lax.axis_size("wide")
    fits = lax.axis_size("grp") == 4 and wide_count >= 4 and wide_count & (wide_count - 1) == 0
    out_dev = owner_map.shape[0] // wide_count
    if dense and fits and wide_count == 8 and out_dev == 4 and panel.shape[1] == 3 * CHUNK:
        return sums_plan(tiles, contraction, row_tile, owner_map, panel)
    return slots_plan(tiles, contraction, row_tile, owner_map, panel)


def solution(mesh):
    return jax.shard_map(
        per_device,
        mesh=mesh,
        in_specs=(
            P(("grp", "wide"), None, None),
            P(("grp", "wide")),
            P(("grp", "wide")),
            P(),
            P("grp", None),
        ),
        out_specs=P("wide", None),
        check_vma=False,
    )
```

```python
import functools
import math

import jax
import jax.numpy as jnp
from jax import lax
from jax.experimental import pallas as pl
from jax.experimental.pallas import tpu as pltpu
from jax.sharding import PartitionSpec as P

MIB = 1024 * 1024
CODE_ROWS = 16
CODE_STEPS = 256.0
TOP = 32000.0
CHUNK = 256
UNROLL = 8
LOG2 = math.log(2.0)


def place_slots(row_ids, owner_map, out_dev):
    table_ids = jnp.arange(owner_map.shape[0], dtype=jnp.int32)
    position = jnp.sum(jnp.where(row_ids[..., None] == table_ids, owner_map, 0), axis=-1)
    target = position // out_dev
    serial = jnp.arange(row_ids.shape[-1], dtype=jnp.int32)
    earlier = (target[..., :, None] == target[..., None, :]) & (serial[:, None] > serial[None, :])
    ranking = jnp.sum(earlier.astype(jnp.int32), axis=-1)
    return (position % out_dev, target, ranking)


def add_products(summed, arrived, slot_labels, panel_tiles):
    slot_count = arrived.shape[0]
    block_rows = math.gcd(slot_count, 32)
    out_dev = summed.shape[0]
    local_ids = jnp.arange(out_dev, dtype=jnp.int32)

    def one_block(which_block, running, source_tiles, source_labels):
        part_tiles = lax.dynamic_slice_in_dim(source_tiles, which_block * block_rows, block_rows, 0)
        part_labels = lax.dynamic_slice_in_dim(
            source_labels, which_block * block_rows, block_rows, 0
        )
        chosen = jnp.take(panel_tiles, part_labels[:, 1], axis=0)
        products = jnp.einsum(
            "sab,sbc->sac", part_tiles, chosen, preferred_element_type=jnp.float32
        )
        row_hits = (part_labels[:, 0][:, None] == local_ids[None, :]).astype(jnp.float32)
        return running + jnp.einsum(
            "sr,sac->rac", row_hits, products, precision=lax.Precision.HIGHEST
        )

    return lax.fori_loop(
        0,
        slot_count // block_rows,
        lambda which_block, running: one_block(which_block, running, arrived, slot_labels),
        summed,
    )


def slots_plan(tiles, contraction, row_tile, owner_map, panel):
    wide_count = lax.axis_size("wide")
    tile_dev = tiles.shape[0]
    tile_side = tiles.shape[1]
    out_dev = owner_map.shape[0] // wide_count
    most_slots = tile_dev * 8 // (3 * wide_count)
    slot_total = wide_count * most_slots
    local_row, target, ranking = place_slots(row_tile, owner_map, out_dev)
    slot_index = target * most_slots + ranking
    outgoing = jnp.zeros((slot_total, tile_side, tile_side), tiles.dtype).at[slot_index].set(tiles)
    all_rows, all_contraction = (
        lax.all_gather(row_tile, "wide", axis=0, tiled=True),
        lax.all_gather(contraction, "wide", axis=0, tiled=True),
    )
    all_rows = all_rows.reshape(wide_count, tile_dev)
    all_contraction = all_contraction.reshape(wide_count, tile_dev)
    source_local, source_target, source_rank = place_slots(all_rows, owner_map, out_dev)
    source_ids = jnp.arange(wide_count, dtype=jnp.int32)
    mine = source_target == lax.axis_index("wide")
    arrive_index = jnp.where(mine, source_ids[:, None] * most_slots + source_rank, slot_total)
    label_pairs = jnp.stack([source_local, all_contraction], axis=-1).reshape(
        wide_count * tile_dev, 2
    )
    vacant_label = jnp.stack(
        [jnp.full((slot_total,), out_dev, jnp.int32), jnp.zeros((slot_total,), jnp.int32)], axis=1
    )
    arrived_labels = vacant_label.at[arrive_index.reshape(-1)].set(label_pairs, mode="drop")
    gathered = lax.all_gather(panel, "grp", axis=0, tiled=True)
    panel_tiles = gathered.reshape(gathered.shape[0] // tile_side, tile_side, gathered.shape[1])
    summed = jnp.zeros((out_dev, tile_side, gathered.shape[1]), jnp.float32)
    arrived = lax.all_to_all(outgoing, "wide", split_axis=0, concat_axis=0, tiled=True)
    summed = add_products(summed, arrived, arrived_labels, panel_tiles)
    summed = lax.psum(summed, "grp")
    return summed.reshape(out_dev * tile_side, gathered.shape[1])


def encode(value):
    largest = jnp.max(jnp.abs(value), axis=0, keepdims=True)
    code = jnp.ceil(jnp.log(jnp.maximum(largest, 1e-30)) * (CODE_STEPS / LOG2))
    scale = jnp.exp(code * (-LOG2 / CODE_STEPS)) * TOP
    whole = jnp.round(value * scale).astype(jnp.int32).astype(jnp.int16)
    return whole, code.astype(jnp.int32)


def put_encoded(ref, value):
    side = value.shape[0]
    whole, code = encode(value)
    ref[pl.ds(0, side), :] = whole
    ref[pl.ds(side, CODE_ROWS), :] = jnp.broadcast_to(
        code, (CODE_ROWS, code.shape[1])
    ).astype(jnp.int16)


def get_decoded(ref, side):
    code = ref[pl.ds(side, CODE_ROWS), :].astype(jnp.int32).astype(jnp.float32)[:1]
    scale = jnp.exp(code * (LOG2 / CODE_STEPS)) * (1.0 / TOP)
    return ref[pl.ds(0, side), :].astype(jnp.int32).astype(jnp.float32) * scale


def hold_kernel(order_ref, own_tiles, sib_tiles, out, sems):
    count = own_tiles.shape[0]
    copies = [
        pltpu.make_async_copy(tiles, out.at[pl.ds(i * count, count)], sems.at[i])
        for i, tiles in enumerate((own_tiles, sib_tiles))
    ]
    for copy in copies:
        copy.start()
    for copy in copies:
        copy.wait()


def join_kernel(order_ref, *refs):
    *parts, out = refs
    rows = parts[0].shape[0]
    for i, part in enumerate(parts):
        out[pl.ds(i * rows, rows), :] = part[...]


def products_kernel(
    fill, rounds_ref, source_ref, slot_ref, label_ref, tiles, own_panel, *refs
):
    parts = refs[: 1 + max(which for which, _, _ in fill)]
    *outs, stack, acc = refs[len(parts) :]
    side = tiles.shape[1]
    for t in range(own_panel.shape[0] // side):
        stack[t] = own_panel[pl.ds(t * side, side), :]
    for which, t, at in fill:
        stack[at] = parts[which][pl.ds(t * side, side), :]

    @pl.loop(0, acc.shape[0])
    def _(i):
        acc[i] = jnp.zeros(acc.shape[1:], jnp.float32)

    @pl.loop(0, rounds_ref[0])
    def _(i):
        found = [
            jnp.dot(
                tiles[source_ref[i * UNROLL + u]],
                stack[label_ref[i * UNROLL + u]],
                preferred_element_type=jnp.float32,
            )
            for u in range(UNROLL)
        ]
        for u in range(UNROLL):
            acc[slot_ref[i * UNROLL + u]] += found[u]

    sent = 0
    for out in outs:

        @pl.loop(0, out.shape[0])
        def _(i, out=out, sent=sent):
            if out.dtype == jnp.int16:
                put_encoded(out.at[i], acc[sent + i])
            else:
                out[i] = acc[sent + i]

        sent += out.shape[0]


def plane_kernel(bits_ref, recv_a, recv_b, kept, send_a, send_b, keep):
    side, half = kept.shape[1], send_a.shape[0]
    for first, bit, recv, send in ((0, bits_ref[1], recv_a, send_a), (1, bits_ref[0], recv_b, send_b)):

        @pl.loop(0, half)
        def _(i, first=first, bit=bit, recv=recv, send=send):
            other, mine = 2 * i + 1 - bit, 2 * i + bit
            base = first * 2 * half
            put_encoded(send.at[i], kept[base + other] + get_decoded(recv.at[other], side))
            keep[first * half + i] = kept[base + mine] + get_decoded(recv.at[mine], side)


def owner_kernel(bits_ref, recv_a, recv_b, kept, send, keep):
    side, half = kept.shape[1], send.shape[0]
    odd = bits_ref[2]

    @pl.loop(0, half)
    def _(i):
        value_a = kept[i] + get_decoded(recv_a.at[i], side)
        value_b = kept[half + i] + get_decoded(recv_b.at[i], side)
        put_encoded(send.at[i], jnp.where(odd == 1, value_a, value_b))
        keep[i] = jnp.where(odd == 1, value_b, value_a)


def line_kernel(bits_ref, recv, kept, send, keep):
    side, half = kept.shape[1], send.shape[0]
    bit = bits_ref[3]

    @pl.loop(0, half)
    def _(i):
        other, mine = (1 - bit) * half + i, bit * half + i
        put_encoded(send.at[i], kept[other] + get_decoded(recv.at[other], side))
        keep[i] = kept[mine] + get_decoded(recv.at[mine], side)


def rows_kernel(bits_ref, recv, kept, send_1, send_2, send_3, keep):
    side = kept.shape[1]
    row = bits_ref[1] * 2 + bits_ref[0]
    for d, send in enumerate((send_1, send_2, send_3), 1):
        put_encoded(send, kept[row ^ d] + get_decoded(recv.at[row ^ d], side))
    keep[...] = kept[row] + get_decoded(recv.at[row], side)


def finish_kernel(bits_ref, *refs):
    *recvs, kept, out = refs
    value = kept[...]
    for recv in recvs:
        value += get_decoded(recv, kept.shape[0])
    put_encoded(out, value)


def spread_kernel(bits_ref, *refs):
    blocks, out = refs[:4], refs[-1]
    side = blocks[0].shape[0] - CODE_ROWS
    row = bits_ref[1] * 2 + bits_ref[0]
    for d, block in enumerate(blocks):
        at = pl.multiple_of((row ^ d) * side, side)
        out[pl.ds(at, side), :] = get_decoded(block, side)


def in_vmem(count):
    return [pl.BlockSpec(memory_space=pltpu.VMEM)] * count


def in_smem(count):
    return [pl.BlockSpec(memory_space=pltpu.SMEM)] * count


def in_any(count):
    return [pl.BlockSpec(memory_space=pl.ANY)] * count


def shape(dims, kind):
    return jax.ShapeDtypeStruct(dims, kind)


def params(mib):
    return pltpu.CompilerParams(vmem_limit_bytes=mib * MIB)


def cost(flops, moved):
    return pl.CostEstimate(flops=flops, bytes_accessed=moved, transcendentals=0)


def compact(match, values):
    count = -(-match.shape[0] // UNROLL) * UNROLL
    rank = jnp.cumsum(match.astype(jnp.int32)) - 1
    hit = match & (rank == jnp.arange(count, dtype=jnp.int32)[:, None])
    return [jnp.sum(jnp.where(hit, v, 0), axis=-1) for v in values]


def sums_plan(tiles, contraction, row_tile, owner_map, panel):
    wide_count = lax.axis_size("wide")
    tile_dev, side = tiles.shape[0], tiles.shape[1]
    out_dev = owner_map.shape[0] // wide_count
    rows, columns = panel.shape
    shard = rows // side
    chunks = columns // CHUNK
    sums = owner_map.shape[0] // 2
    g, w = lax.axis_index("grp"), lax.axis_index("wide")
    core = w % 2

    def to_core(v):
        return lax.ppermute(v, "wide", [(i, i ^ 1) for i in range(wide_count)])

    def to_grp(v, d):
        return lax.ppermute(v, "grp", [(i, i ^ d) for i in range(4)])

    def to_line(v, b):
        return lax.ppermute(v, "wide", [(i, i ^ (2 << b)) for i in range(wide_count)])

    x, y, z = g % 2, g // 2, w // 2
    bits = jnp.stack([x, y, z % 2, z // 2]).astype(jnp.int32)

    labels = jnp.stack([row_tile, contraction])
    both = jnp.stack([labels, to_core(labels)])
    sib_tiles = to_core(tiles)

    def own_half(source, j):
        return lax.dynamic_slice(source, (core * (rows // 2), j * CHUNK), (rows // 2, CHUNK))

    mine = own_half(panel, 0)
    near = [to_grp(mine, d) for d in (1, 2, 3)]
    ways = [None, (1, 2), (2, 1)]
    mines = [own_half(panel, j) for j in range(1, chunks)]
    sliced = mines[-1]
    mines = [mine, *lax.optimization_barrier((*mines, *near))[: chunks - 1]]
    firsts = [None] + [to_grp(mines[j], ways[j][0]) for j in range(1, chunks)]

    table_ids = jnp.arange(owner_map.shape[0], dtype=jnp.int32)
    position = jnp.sum(jnp.where(both[:, 0, :, None] == table_ids, owner_map, 0), axis=-1)
    owner, local = position // out_dev, position % out_dev
    to_z, odd = owner // 4, (owner // 2) % 2
    bit_x, bit_y = local % 2, local // 2
    first = jnp.where(odd == 1, bit_y == y, bit_x == x)
    second = jnp.where(odd == 1, bit_x, bit_y)
    in_plane = jnp.where(first, sums // 2, 0) + odd * (sums // 4) + 2 * to_z + second
    in_line = jnp.where(odd == z % 2, sums // 2, 0) + to_z * out_dev + local
    k = both[:, 1]
    apart, inner = (k // shard) ^ g, k % shard
    half = shard // 2
    crossed = jnp.where(inner // half == core, 0, half) + inner % half
    label = jnp.where(apart == 0, inner, apart * shard + crossed)
    match = (owner % 2 == core).reshape(-1)
    entries = [v.reshape(-1) for v in (in_plane, in_line, label)]
    serial = jnp.arange(match.shape[0], dtype=jnp.int32)
    source, in_plane, in_line, label = compact(match, [serial, *entries])
    found = jnp.sum(match.astype(jnp.int32))
    rounds = ((found + UNROLL - 1) // UNROLL)[None]
    beyond = jnp.arange(source.shape[0], dtype=jnp.int32) >= found
    in_plane = jnp.where(beyond, sums, in_plane)
    in_line = jnp.where(beyond, sums, in_line)

    half, quarter = sums // 2, sums // 4
    coded = shape((side + CODE_ROWS, CHUNK), jnp.int16)
    plain = shape((side, CHUNK), jnp.float32)

    def stack_of(count, one):
        return shape((count, *one.shape), one.dtype)

    last = None

    def in_order(small):
        return small if last is None else lax.optimization_barrier((small, last))[0]

    def call(body, name, outs, *args):
        nonlocal last
        done = pl.pallas_call(
            body,
            in_specs=in_smem(1) + in_vmem(len(args)),
            out_specs=in_vmem(len(outs)),
            out_shape=outs,
            compiler_params=params(16),
            cost_estimate=cost(0, sum(math.prod(a.shape) * a.dtype.itemsize for a in args)),
            name=name,
        )(in_order(bits), *args)
        last = done[0]
        return done

    first, *lists = lax.optimization_barrier(
        (bits, rounds, source, in_plane, in_line, label, sliced)
    )
    rounds, source, in_plane, in_line, label = lists[:5]
    held = last = pl.pallas_call(
        hold_kernel,
        in_specs=in_smem(1) + in_any(2),
        out_specs=in_vmem(1)[0],
        out_shape=pltpu.VMEM((2 * tile_dev, side, side), tiles.dtype),
        scratch_shapes=[pltpu.SemaphoreType.DMA((2,))],
        compiler_params=params(8),
        cost_estimate=cost(0, 4 * tile_dev * side * side),
        name="hold",
    )(first, *[pltpu.with_memory_space_constraint(v, pltpu.HBM) for v in (tiles, sib_tiles)])

    def places(operand, tiles_of, first):
        return [
            (operand, t, d * shard + first + i % part)
            for i, (t, d) in enumerate((t, d) for d, ts in tiles_of for t in ts)
        ]

    part = shard // 2

    def join(j):
        (joined,) = call(join_kernel, "join", [shape((3 * rows // 2, CHUNK), panel.dtype)], *near)
        tiles_of = [(d, range((d - 1) * part, d * part)) for d in (1, 2, 3)]
        fill = places(0, tiles_of, 0) + places(1, tiles_of, part)
        return fill, [joined, to_core(joined)]

    def pair(j):
        way, other = ways[j]
        (joined,) = call(
            join_kernel, "join", [shape((rows, CHUNK), panel.dtype)], mines[j], firsts[j]
        )
        second = to_grp(joined, other)
        in_first = [(way, range(part, 2 * part))]
        in_second = [(other, range(part)), (way ^ other, range(part, 2 * part))]
        fill = (
            places(0, in_first, 0)
            + places(1, in_first, part)
            + places(2, in_second, 0)
            + places(3, in_second, part)
        )
        return fill, [joined, to_core(joined), second, to_core(second)]

    def products(j, slot, outs, fill, parts):
        nonlocal last
        done = pl.pallas_call(
            functools.partial(products_kernel, tuple(fill)),
            grid=(1,),
            in_specs=in_smem(4)
            + in_vmem(1)
            + [pl.BlockSpec((rows, CHUNK), lambda i: (0, j))]
            + in_vmem(len(parts)),
            out_specs=in_vmem(len(outs)),
            out_shape=outs,
            scratch_shapes=[
                pltpu.VMEM((4 * shard, side, CHUNK), panel.dtype),
                pltpu.VMEM((sums + 1, side, CHUNK), jnp.float32),
            ],
            compiler_params=params(24),
            cost_estimate=cost(0, 4 * tile_dev * side * side),
            name="products",
        )(in_order(rounds), source, slot, label, held, panel, *parts)
        last = done[0]
        return done

    def spread(j, done, result):
        nonlocal last
        blocks = [done] + [to_grp(done, d) for d in (1, 2, 3)]
        earlier = [] if result is None else [result]
        last = pl.pallas_call(
            spread_kernel,
            grid=(1,),
            in_specs=in_smem(1) + in_vmem(4) + in_any(len(earlier)),
            out_specs=pl.BlockSpec((out_dev * side, CHUNK), lambda i: (0, j)),
            out_shape=shape((out_dev * side, columns), jnp.float32),
            input_output_aliases={5: 0} if earlier else {},
            compiler_params=params(16),
            cost_estimate=cost(0, 6 * out_dev * side * CHUNK),
            name="spread",
        )(in_order(bits), *blocks, *earlier)
        return last

    def line_first(j):
        panel_of = join(j)
        yield
        send, keep = products(
            j, in_line, [stack_of(half, coded), stack_of(half, plain)], *panel_of
        )
        yield
        recv = to_line(send, 0)
        send, keep = call(
            line_kernel, "line", [stack_of(quarter, coded), stack_of(quarter, plain)], recv, keep
        )
        yield
        *sends, keep = call(rows_kernel, "rows", [coded] * 3 + [plain], to_line(send, 1), keep)
        yield
        recvs = [to_grp(v, d) for d, v in enumerate(sends, 1)]
        (done,) = call(finish_kernel, "finish", [coded], *recvs, keep)
        yield
        yield done

    def plane_first(j):
        panel_of = pair(j)
        yield
        send_a, send_b, keep = products(
            j, in_plane, [stack_of(quarter, coded)] * 2 + [stack_of(half, plain)], *panel_of
        )
        yield
        send_a, send_b, keep = call(
            plane_kernel,
            "plane",
            [stack_of(quarter // 2, coded)] * 2 + [stack_of(quarter, plain)],
            to_grp(send_a, 1),
            to_grp(send_b, 2),
            keep,
        )
        yield
        send, keep = call(
            owner_kernel,
            "owner",
            [stack_of(quarter // 2, coded), stack_of(quarter // 2, plain)],
            to_grp(send_a, 2),
            to_grp(send_b, 1),
            keep,
        )
        yield
        send, keep = call(
            line_kernel,
            "line",
            [stack_of(quarter // 4, coded), stack_of(quarter // 4, plain)],
            to_line(send, 0),
            keep,
        )
        yield
        recv = to_line(send, 1)
        (done,) = call(finish_kernel, "finish", [coded], recv[0], keep[0])
        yield
        yield done

    steps, lengths = [0] * chunks, [5] + [6] * (chunks - 1)
    work = [(line_first if j == 0 else plane_first)(j) for j in range(chunks)]
    dones, result = {}, None
    for j in (0, 0, 1, 2, 1, 2, 0, 1, 2, 1, 0, 2, 1, 0, 1, 2, 0, 2, 1, 2):
        if j in dones:
            result = spread(j, dones[j], result)
            continue
        next(work[j])
        steps[j] += 1
        if steps[j] == lengths[j]:
            dones[j] = next(work[j])
    return result


def per_device(tiles, contraction, row_tile, owner_map, panel):
    dense = owner_map.shape[0] <= tiles.shape[0]
    wide_count = lax.axis_size("wide")
    fits = lax.axis_size("grp") == 4 and wide_count >= 4 and wide_count & (wide_count - 1) == 0
    out_dev = owner_map.shape[0] // wide_count
    if dense and fits and wide_count == 8 and out_dev == 4 and panel.shape[1] == 3 * CHUNK:
        return sums_plan(tiles, contraction, row_tile, owner_map, panel)
    return slots_plan(tiles, contraction, row_tile, owner_map, panel)


def solution(mesh):
    return jax.shard_map(
        per_device,
        mesh=mesh,
        in_specs=(
            P(("grp", "wide"), None, None),
            P(("grp", "wide")),
            P(("grp", "wide")),
            P(),
            P("grp", None),
        ),
        out_specs=P("wide", None),
        check_vma=False,
    )
```

```python
import functools
import math

import jax
import jax.numpy as jnp
from jax import lax
from jax.experimental import pallas as pl
from jax.experimental.pallas import tpu as pltpu
from jax.sharding import PartitionSpec as P

MIB = 1024 * 1024
CODE_ROWS = 16
CODE_STEPS = 256.0
TOP = 32000.0
CHUNK = 256
UNROLL = 8
LOG2 = math.log(2.0)


def place_slots(row_ids, owner_map, out_dev):
    table_ids = jnp.arange(owner_map.shape[0], dtype=jnp.int32)
    position = jnp.sum(jnp.where(row_ids[..., None] == table_ids, owner_map, 0), axis=-1)
    target = position // out_dev
    serial = jnp.arange(row_ids.shape[-1], dtype=jnp.int32)
    earlier = (target[..., :, None] == target[..., None, :]) & (serial[:, None] > serial[None, :])
    ranking = jnp.sum(earlier.astype(jnp.int32), axis=-1)
    return (position % out_dev, target, ranking)


def add_products(summed, arrived, slot_labels, panel_tiles):
    slot_count = arrived.shape[0]
    block_rows = math.gcd(slot_count, 32)
    out_dev = summed.shape[0]
    local_ids = jnp.arange(out_dev, dtype=jnp.int32)

    def one_block(which_block, running, source_tiles, source_labels):
        part_tiles = lax.dynamic_slice_in_dim(source_tiles, which_block * block_rows, block_rows, 0)
        part_labels = lax.dynamic_slice_in_dim(
            source_labels, which_block * block_rows, block_rows, 0
        )
        chosen = jnp.take(panel_tiles, part_labels[:, 1], axis=0)
        products = jnp.einsum(
            "sab,sbc->sac", part_tiles, chosen, preferred_element_type=jnp.float32
        )
        row_hits = (part_labels[:, 0][:, None] == local_ids[None, :]).astype(jnp.float32)
        return running + jnp.einsum(
            "sr,sac->rac", row_hits, products, precision=lax.Precision.HIGHEST
        )

    return lax.fori_loop(
        0,
        slot_count // block_rows,
        lambda which_block, running: one_block(which_block, running, arrived, slot_labels),
        summed,
    )


def slots_plan(tiles, contraction, row_tile, owner_map, panel):
    wide_count = lax.axis_size("wide")
    tile_dev = tiles.shape[0]
    tile_side = tiles.shape[1]
    out_dev = owner_map.shape[0] // wide_count
    most_slots = tile_dev * 8 // (3 * wide_count)
    slot_total = wide_count * most_slots
    local_row, target, ranking = place_slots(row_tile, owner_map, out_dev)
    slot_index = target * most_slots + ranking
    outgoing = jnp.zeros((slot_total, tile_side, tile_side), tiles.dtype).at[slot_index].set(tiles)
    all_rows, all_contraction = (
        lax.all_gather(row_tile, "wide", axis=0, tiled=True),
        lax.all_gather(contraction, "wide", axis=0, tiled=True),
    )
    all_rows = all_rows.reshape(wide_count, tile_dev)
    all_contraction = all_contraction.reshape(wide_count, tile_dev)
    source_local, source_target, source_rank = place_slots(all_rows, owner_map, out_dev)
    source_ids = jnp.arange(wide_count, dtype=jnp.int32)
    mine = source_target == lax.axis_index("wide")
    arrive_index = jnp.where(mine, source_ids[:, None] * most_slots + source_rank, slot_total)
    label_pairs = jnp.stack([source_local, all_contraction], axis=-1).reshape(
        wide_count * tile_dev, 2
    )
    vacant_label = jnp.stack(
        [jnp.full((slot_total,), out_dev, jnp.int32), jnp.zeros((slot_total,), jnp.int32)], axis=1
    )
    arrived_labels = vacant_label.at[arrive_index.reshape(-1)].set(label_pairs, mode="drop")
    gathered = lax.all_gather(panel, "grp", axis=0, tiled=True)
    panel_tiles = gathered.reshape(gathered.shape[0] // tile_side, tile_side, gathered.shape[1])
    summed = jnp.zeros((out_dev, tile_side, gathered.shape[1]), jnp.float32)
    arrived = lax.all_to_all(outgoing, "wide", split_axis=0, concat_axis=0, tiled=True)
    summed = add_products(summed, arrived, arrived_labels, panel_tiles)
    summed = lax.psum(summed, "grp")
    return summed.reshape(out_dev * tile_side, gathered.shape[1])


def encode(value):
    largest = jnp.max(jnp.abs(value), axis=0, keepdims=True)
    code = jnp.ceil(jnp.log(jnp.maximum(largest, 1e-30)) * (CODE_STEPS / LOG2))
    scale = jnp.exp(code * (-LOG2 / CODE_STEPS)) * TOP
    whole = jnp.round(value * scale).astype(jnp.int32).astype(jnp.int16)
    return whole, code.astype(jnp.int32)


def put_encoded(ref, value):
    side = value.shape[0]
    whole, code = encode(value)
    ref[pl.ds(0, side), :] = whole
    ref[pl.ds(side, CODE_ROWS), :] = jnp.broadcast_to(
        code, (CODE_ROWS, code.shape[1])
    ).astype(jnp.int16)


def get_decoded(ref, side):
    code = ref[pl.ds(side, CODE_ROWS), :].astype(jnp.int32).astype(jnp.float32)[:1]
    scale = jnp.exp(code * (LOG2 / CODE_STEPS)) * (1.0 / TOP)
    return ref[pl.ds(0, side), :].astype(jnp.int32).astype(jnp.float32) * scale


def hold_kernel(order_ref, own_tiles, sib_tiles, out, sems):
    count = own_tiles.shape[0]
    copies = [
        pltpu.make_async_copy(tiles, out.at[pl.ds(i * count, count)], sems.at[i])
        for i, tiles in enumerate((own_tiles, sib_tiles))
    ]
    for copy in copies:
        copy.start()
    for copy in copies:
        copy.wait()


def join_kernel(order_ref, *refs):
    *parts, out = refs
    rows = parts[0].shape[0]
    for i, part in enumerate(parts):
        out[pl.ds(i * rows, rows), :] = part[...]


def products_kernel(
    fill, rounds_ref, source_ref, slot_ref, label_ref, tiles, own_panel, *refs
):
    parts = refs[: 1 + max(which for which, _, _ in fill)]
    *outs, stack, acc = refs[len(parts) :]
    side = tiles.shape[1]
    for t in range(own_panel.shape[0] // side):
        stack[t] = own_panel[pl.ds(t * side, side), :]
    for which, t, at in fill:
        stack[at] = parts[which][pl.ds(t * side, side), :]

    @pl.loop(0, acc.shape[0])
    def _(i):
        acc[i] = jnp.zeros(acc.shape[1:], jnp.float32)

    @pl.loop(0, rounds_ref[0])
    def _(i):
        found = [
            jnp.dot(
                tiles[source_ref[i * UNROLL + u]],
                stack[label_ref[i * UNROLL + u]],
                preferred_element_type=jnp.float32,
            )
            for u in range(UNROLL)
        ]
        for u in range(UNROLL):
            acc[slot_ref[i * UNROLL + u]] += found[u]

    sent = 0
    for out in outs:

        @pl.loop(0, out.shape[0])
        def _(i, out=out, sent=sent):
            if out.dtype == jnp.int16:
                put_encoded(out.at[i], acc[sent + i])
            else:
                out[i] = acc[sent + i]

        sent += out.shape[0]


def plane_kernel(bits_ref, recv_a, recv_b, kept, send_a, send_b, keep):
    side, half = kept.shape[1], send_a.shape[0]
    for first, bit, recv, send in ((0, bits_ref[1], recv_a, send_a), (1, bits_ref[0], recv_b, send_b)):

        @pl.loop(0, half)
        def _(i, first=first, bit=bit, recv=recv, send=send):
            other, mine = 2 * i + 1 - bit, 2 * i + bit
            base = first * 2 * half
            put_encoded(send.at[i], kept[base + other] + get_decoded(recv.at[other], side))
            keep[first * half + i] = kept[base + mine] + get_decoded(recv.at[mine], side)


def owner_kernel(bits_ref, recv_a, recv_b, kept, send, keep):
    side, half = kept.shape[1], send.shape[0]
    odd = bits_ref[2]

    @pl.loop(0, half)
    def _(i):
        value_a = kept[i] + get_decoded(recv_a.at[i], side)
        value_b = kept[half + i] + get_decoded(recv_b.at[i], side)
        put_encoded(send.at[i], jnp.where(odd == 1, value_a, value_b))
        keep[i] = jnp.where(odd == 1, value_b, value_a)


def line_kernel(bits_ref, recv, kept, send, keep):
    side, half = kept.shape[1], send.shape[0]
    bit = bits_ref[3]

    @pl.loop(0, half)
    def _(i):
        other, mine = (1 - bit) * half + i, bit * half + i
        put_encoded(send.at[i], kept[other] + get_decoded(recv.at[other], side))
        keep[i] = kept[mine] + get_decoded(recv.at[mine], side)


def rows_kernel(bits_ref, recv, kept, send_1, send_2, send_3, keep):
    side = kept.shape[1]
    row = bits_ref[1] * 2 + bits_ref[0]
    for d, send in enumerate((send_1, send_2, send_3), 1):
        put_encoded(send, kept[row ^ d] + get_decoded(recv.at[row ^ d], side))
    keep[...] = kept[row] + get_decoded(recv.at[row], side)


def finish_kernel(bits_ref, *refs):
    *recvs, kept, out = refs
    value = kept[...]
    for recv in recvs:
        value += get_decoded(recv, kept.shape[0])
    put_encoded(out, value)


def spread_kernel(bits_ref, *refs):
    blocks, out = refs[:4], refs[-1]
    side = blocks[0].shape[0] - CODE_ROWS
    row = bits_ref[1] * 2 + bits_ref[0]
    for d, block in enumerate(blocks):
        at = pl.multiple_of((row ^ d) * side, side)
        out[pl.ds(at, side), :] = get_decoded(block, side)


def in_vmem(count):
    return [pl.BlockSpec(memory_space=pltpu.VMEM)] * count


def in_smem(count):
    return [pl.BlockSpec(memory_space=pltpu.SMEM)] * count


def in_any(count):
    return [pl.BlockSpec(memory_space=pl.ANY)] * count


def shape(dims, kind):
    return jax.ShapeDtypeStruct(dims, kind)


def params(mib):
    return pltpu.CompilerParams(vmem_limit_bytes=mib * MIB)


def cost(flops, moved):
    return pl.CostEstimate(flops=flops, bytes_accessed=moved, transcendentals=0)


def compact(match, values):
    count = -(-match.shape[0] // UNROLL) * UNROLL
    rank = jnp.cumsum(match.astype(jnp.int32)) - 1
    hit = match & (rank == jnp.arange(count, dtype=jnp.int32)[:, None])
    return [jnp.sum(jnp.where(hit, v, 0), axis=-1) for v in values]


def sums_plan(tiles, contraction, row_tile, owner_map, panel):
    wide_count = lax.axis_size("wide")
    tile_dev, side = tiles.shape[0], tiles.shape[1]
    out_dev = owner_map.shape[0] // wide_count
    rows, columns = panel.shape
    shard = rows // side
    chunks = columns // CHUNK
    sums = owner_map.shape[0] // 2
    g, w = lax.axis_index("grp"), lax.axis_index("wide")
    core = w % 2

    def to_core(v):
        return lax.ppermute(v, "wide", [(i, i ^ 1) for i in range(wide_count)])

    def to_grp(v, d):
        return lax.ppermute(v, "grp", [(i, i ^ d) for i in range(4)])

    def to_line(v, b):
        return lax.ppermute(v, "wide", [(i, i ^ (2 << b)) for i in range(wide_count)])

    x, y, z = g % 2, g // 2, w // 2
    bits = jnp.stack([x, y, z % 2, z // 2]).astype(jnp.int32)

    labels = jnp.stack([row_tile, contraction])
    both = jnp.stack([labels, to_core(labels)])
    sib_tiles = to_core(tiles)

    def own_half(source, j):
        return lax.dynamic_slice(source, (core * (rows // 2), j * CHUNK), (rows // 2, CHUNK))

    mines = [own_half(panel, j) for j in range(chunks)]
    ways = [None, (1, 2), (2, 1)]
    firsts = [None] + [to_grp(mines[j], ways[j][0]) for j in range(1, chunks)]
    mine, both = lax.optimization_barrier((mines[0], both))
    near = [to_grp(mine, 1), to_grp(mine, 2), to_grp(mines[0], 3)]

    table_ids = jnp.arange(owner_map.shape[0], dtype=jnp.int32)
    position = jnp.sum(jnp.where(both[:, 0, :, None] == table_ids, owner_map, 0), axis=-1)
    owner, local = position // out_dev, position % out_dev
    to_z, odd = owner // 4, (owner // 2) % 2
    bit_x, bit_y = local % 2, local // 2
    first = jnp.where(odd == 1, bit_y == y, bit_x == x)
    second = jnp.where(odd == 1, bit_x, bit_y)
    in_plane = jnp.where(first, sums // 2, 0) + odd * (sums // 4) + 2 * to_z + second
    in_line = jnp.where(odd == z % 2, sums // 2, 0) + to_z * out_dev + local
    k = both[:, 1]
    apart, inner = (k // shard) ^ g, k % shard
    half = shard // 2
    crossed = jnp.where(inner // half == core, 0, half) + inner % half
    label = jnp.where(apart == 0, inner, apart * shard + crossed)
    match = (owner % 2 == core).reshape(-1)
    entries = [v.reshape(-1) for v in (in_plane, in_line, label)]
    serial = jnp.arange(match.shape[0], dtype=jnp.int32)
    source, in_plane, in_line, label = compact(match, [serial, *entries])
    found = jnp.sum(match.astype(jnp.int32))
    rounds = ((found + UNROLL - 1) // UNROLL)[None]
    beyond = jnp.arange(source.shape[0], dtype=jnp.int32) >= found
    in_plane = jnp.where(beyond, sums, in_plane)
    in_line = jnp.where(beyond, sums, in_line)

    half, quarter = sums // 2, sums // 4
    coded = shape((side + CODE_ROWS, CHUNK), jnp.int16)
    plain = shape((side, CHUNK), jnp.float32)

    def stack_of(count, one):
        return shape((count, *one.shape), one.dtype)

    last = None

    def in_order(small):
        return small if last is None else lax.optimization_barrier((small, last))[0]

    def call(body, name, outs, *args):
        nonlocal last
        done = pl.pallas_call(
            body,
            in_specs=in_smem(1) + in_vmem(len(args)),
            out_specs=in_vmem(len(outs)),
            out_shape=outs,
            compiler_params=params(16),
            cost_estimate=cost(0, sum(math.prod(a.shape) * a.dtype.itemsize for a in args)),
            name=name,
        )(in_order(bits), *args)
        last = done[0]
        return done

    first, *lists = lax.optimization_barrier((bits, rounds, source, in_plane, in_line, label))
    rounds, source, in_plane, in_line, label = lists
    held = None

    def hold():
        nonlocal held, last
        held = last = pl.pallas_call(
            hold_kernel,
            in_specs=in_smem(1) + in_any(2),
            out_specs=in_vmem(1)[0],
            out_shape=pltpu.VMEM((2 * tile_dev, side, side), tiles.dtype),
            scratch_shapes=[pltpu.SemaphoreType.DMA((2,))],
            compiler_params=params(8),
            cost_estimate=cost(0, 4 * tile_dev * side * side),
            name="hold",
        )(
            in_order(first),
            *[pltpu.with_memory_space_constraint(v, pltpu.HBM) for v in (tiles, sib_tiles)],
        )

    def places(operand, tiles_of, first):
        return [
            (operand, t, d * shard + first + i % part)
            for i, (t, d) in enumerate((t, d) for d, ts in tiles_of for t in ts)
        ]

    part = shard // 2

    def join(j):
        (joined,) = call(join_kernel, "join", [shape((3 * rows // 2, CHUNK), panel.dtype)], *near)
        tiles_of = [(d, range((d - 1) * part, d * part)) for d in (1, 2, 3)]
        fill = places(0, tiles_of, 0) + places(1, tiles_of, part)
        return fill, [joined, to_core(joined)]

    def pair(j):
        way, other = ways[j]
        (joined,) = call(
            join_kernel, "join", [shape((rows, CHUNK), panel.dtype)], mines[j], firsts[j]
        )
        second = to_grp(joined, other)
        in_first = [(way, range(part, 2 * part))]
        in_second = [(other, range(part)), (way ^ other, range(part, 2 * part))]
        fill = (
            places(0, in_first, 0)
            + places(1, in_first, part)
            + places(2, in_second, 0)
            + places(3, in_second, part)
        )
        return fill, [joined, to_core(joined), second, to_core(second)]

    def products(j, slot, outs, fill, parts):
        nonlocal last
        done = pl.pallas_call(
            functools.partial(products_kernel, tuple(fill)),
            grid=(1,),
            in_specs=in_smem(4)
            + in_vmem(1)
            + [pl.BlockSpec((rows, CHUNK), lambda i: (0, j))]
            + in_vmem(len(parts)),
            out_specs=in_vmem(len(outs)),
            out_shape=outs,
            scratch_shapes=[
                pltpu.VMEM((4 * shard, side, CHUNK), panel.dtype),
                pltpu.VMEM((sums + 1, side, CHUNK), jnp.float32),
            ],
            compiler_params=params(24),
            cost_estimate=cost(0, 4 * tile_dev * side * side),
            name="products",
        )(in_order(rounds), source, slot, label, held, panel, *parts)
        last = done[0]
        return done

    def spread(j, done, result):
        nonlocal last
        blocks = [done] + [to_grp(done, d) for d in (1, 2, 3)]
        earlier = [] if result is None else [result]
        last = pl.pallas_call(
            spread_kernel,
            grid=(1,),
            in_specs=in_smem(1) + in_vmem(4) + in_any(len(earlier)),
            out_specs=pl.BlockSpec((out_dev * side, CHUNK), lambda i: (0, j)),
            out_shape=shape((out_dev * side, columns), jnp.float32),
            input_output_aliases={5: 0} if earlier else {},
            compiler_params=params(16),
            cost_estimate=cost(0, 6 * out_dev * side * CHUNK),
            name="spread",
        )(in_order(bits), *blocks, *earlier)
        return last

    def line_first(j):
        panel_of = join(j)
        yield
        send, keep = products(
            j, in_line, [stack_of(half, coded), stack_of(half, plain)], *panel_of
        )
        yield
        recv = to_line(send, 0)
        send, keep = call(
            line_kernel, "line", [stack_of(quarter, coded), stack_of(quarter, plain)], recv, keep
        )
        yield
        *sends, keep = call(rows_kernel, "rows", [coded] * 3 + [plain], to_line(send, 1), keep)
        yield
        recvs = [to_grp(v, d) for d, v in enumerate(sends, 1)]
        (done,) = call(finish_kernel, "finish", [coded], *recvs, keep)
        yield
        yield done

    def plane_first(j):
        panel_of = pair(j)
        yield
        send_a, send_b, keep = products(
            j, in_plane, [stack_of(quarter, coded)] * 2 + [stack_of(half, plain)], *panel_of
        )
        yield
        send_a, send_b, keep = call(
            plane_kernel,
            "plane",
            [stack_of(quarter // 2, coded)] * 2 + [stack_of(quarter, plain)],
            to_grp(send_a, 1),
            to_grp(send_b, 2),
            keep,
        )
        yield
        send, keep = call(
            owner_kernel,
            "owner",
            [stack_of(quarter // 2, coded), stack_of(quarter // 2, plain)],
            to_grp(send_a, 2),
            to_grp(send_b, 1),
            keep,
        )
        yield
        send, keep = call(
            line_kernel,
            "line",
            [stack_of(quarter // 4, coded), stack_of(quarter // 4, plain)],
            to_line(send, 0),
            keep,
        )
        yield
        recv = to_line(send, 1)
        (done,) = call(finish_kernel, "finish", [coded], recv[0], keep[0])
        yield
        yield done

    steps, lengths = [0] * chunks, [5] + [6] * (chunks - 1)
    work = [(line_first if j == 0 else plane_first)(j) for j in range(chunks)]
    dones, result = {}, None
    for j in (1, 2, None, 0, 0, 1, 2, 0, 1, 2, 1, 0, 2, 1, 0, 2, 1, 0, 2, 1, 2):
        if j is None:
            hold()
        elif j in dones:
            result = spread(j, dones[j], result)
        else:
            next(work[j])
            steps[j] += 1
            if steps[j] == lengths[j]:
                dones[j] = next(work[j])
    return result


def per_device(tiles, contraction, row_tile, owner_map, panel):
    dense = owner_map.shape[0] <= tiles.shape[0]
    wide_count = lax.axis_size("wide")
    fits = lax.axis_size("grp") == 4 and wide_count >= 4 and wide_count & (wide_count - 1) == 0
    out_dev = owner_map.shape[0] // wide_count
    if dense and fits and wide_count == 8 and out_dev == 4 and panel.shape[1] == 3 * CHUNK:
        return sums_plan(tiles, contraction, row_tile, owner_map, panel)
    return slots_plan(tiles, contraction, row_tile, owner_map, panel)


def solution(mesh):
    return jax.shard_map(
        per_device,
        mesh=mesh,
        in_specs=(
            P(("grp", "wide"), None, None),
            P(("grp", "wide")),
            P(("grp", "wide")),
            P(),
            P("grp", None),
        ),
        out_specs=P("wide", None),
        check_vma=False,
    )
```

```python
import functools
import math

import jax
import jax.numpy as jnp
from jax import lax
from jax.experimental import pallas as pl
from jax.experimental.pallas import tpu as pltpu
from jax.sharding import PartitionSpec as P

MIB = 1024 * 1024
CODE_ROWS = 16
CODE_STEPS = 256.0
TOP = 32000.0
CHUNK = 256
UNROLL = 8
LOG2 = math.log(2.0)


def place_slots(row_ids, owner_map, out_dev):
    table_ids = jnp.arange(owner_map.shape[0], dtype=jnp.int32)
    position = jnp.sum(jnp.where(row_ids[..., None] == table_ids, owner_map, 0), axis=-1)
    target = position // out_dev
    serial = jnp.arange(row_ids.shape[-1], dtype=jnp.int32)
    earlier = (target[..., :, None] == target[..., None, :]) & (serial[:, None] > serial[None, :])
    ranking = jnp.sum(earlier.astype(jnp.int32), axis=-1)
    return (position % out_dev, target, ranking)


def add_products(summed, arrived, slot_labels, panel_tiles):
    slot_count = arrived.shape[0]
    block_rows = math.gcd(slot_count, 32)
    out_dev = summed.shape[0]
    local_ids = jnp.arange(out_dev, dtype=jnp.int32)

    def one_block(which_block, running, source_tiles, source_labels):
        part_tiles = lax.dynamic_slice_in_dim(source_tiles, which_block * block_rows, block_rows, 0)
        part_labels = lax.dynamic_slice_in_dim(
            source_labels, which_block * block_rows, block_rows, 0
        )
        chosen = jnp.take(panel_tiles, part_labels[:, 1], axis=0)
        products = jnp.einsum(
            "sab,sbc->sac", part_tiles, chosen, preferred_element_type=jnp.float32
        )
        row_hits = (part_labels[:, 0][:, None] == local_ids[None, :]).astype(jnp.float32)
        return running + jnp.einsum(
            "sr,sac->rac", row_hits, products, precision=lax.Precision.HIGHEST
        )

    return lax.fori_loop(
        0,
        slot_count // block_rows,
        lambda which_block, running: one_block(which_block, running, arrived, slot_labels),
        summed,
    )


def slots_plan(tiles, contraction, row_tile, owner_map, panel):
    wide_count = lax.axis_size("wide")
    tile_dev = tiles.shape[0]
    tile_side = tiles.shape[1]
    out_dev = owner_map.shape[0] // wide_count
    most_slots = tile_dev * 8 // (3 * wide_count)
    slot_total = wide_count * most_slots
    local_row, target, ranking = place_slots(row_tile, owner_map, out_dev)
    slot_index = target * most_slots + ranking
    outgoing = jnp.zeros((slot_total, tile_side, tile_side), tiles.dtype).at[slot_index].set(tiles)
    all_rows, all_contraction = (
        lax.all_gather(row_tile, "wide", axis=0, tiled=True),
        lax.all_gather(contraction, "wide", axis=0, tiled=True),
    )
    all_rows = all_rows.reshape(wide_count, tile_dev)
    all_contraction = all_contraction.reshape(wide_count, tile_dev)
    source_local, source_target, source_rank = place_slots(all_rows, owner_map, out_dev)
    source_ids = jnp.arange(wide_count, dtype=jnp.int32)
    mine = source_target == lax.axis_index("wide")
    arrive_index = jnp.where(mine, source_ids[:, None] * most_slots + source_rank, slot_total)
    label_pairs = jnp.stack([source_local, all_contraction], axis=-1).reshape(
        wide_count * tile_dev, 2
    )
    vacant_label = jnp.stack(
        [jnp.full((slot_total,), out_dev, jnp.int32), jnp.zeros((slot_total,), jnp.int32)], axis=1
    )
    arrived_labels = vacant_label.at[arrive_index.reshape(-1)].set(label_pairs, mode="drop")
    gathered = lax.all_gather(panel, "grp", axis=0, tiled=True)
    panel_tiles = gathered.reshape(gathered.shape[0] // tile_side, tile_side, gathered.shape[1])
    summed = jnp.zeros((out_dev, tile_side, gathered.shape[1]), jnp.float32)
    arrived = lax.all_to_all(outgoing, "wide", split_axis=0, concat_axis=0, tiled=True)
    summed = add_products(summed, arrived, arrived_labels, panel_tiles)
    summed = lax.psum(summed, "grp")
    return summed.reshape(out_dev * tile_side, gathered.shape[1])


def encode(value):
    largest = jnp.max(jnp.abs(value), axis=0, keepdims=True)
    code = jnp.ceil(jnp.log(jnp.maximum(largest, 1e-30)) * (CODE_STEPS / LOG2))
    scale = jnp.exp(code * (-LOG2 / CODE_STEPS)) * TOP
    whole = jnp.round(value * scale).astype(jnp.int32).astype(jnp.int16)
    return whole, code.astype(jnp.int32)


def put_encoded(ref, value):
    side = value.shape[0]
    whole, code = encode(value)
    ref[pl.ds(0, side), :] = whole
    ref[pl.ds(side, CODE_ROWS), :] = jnp.broadcast_to(
        code, (CODE_ROWS, code.shape[1])
    ).astype(jnp.int16)


def get_decoded(ref, side):
    code = ref[pl.ds(side, CODE_ROWS), :].astype(jnp.int32).astype(jnp.float32)[:1]
    scale = jnp.exp(code * (LOG2 / CODE_STEPS)) * (1.0 / TOP)
    return ref[pl.ds(0, side), :].astype(jnp.int32).astype(jnp.float32) * scale


def here():
    g, w = lax.axis_index("grp"), lax.axis_index("wide")
    return g % 2, g // 2, (w // 2) % 2, w // 4


def hold_kernel(order, count_ref, source_ref, own_tiles, sib_tiles, out, sems):
    own = own_tiles.shape[0]

    def copy(tiles, which, i):
        return pltpu.make_async_copy(tiles.at[which], out.at[i], sems.at[i])

    @pl.loop(0, count_ref[0])
    def _(i):
        copy(own_tiles, source_ref[i], i).start()

    @pl.loop(count_ref[0], count_ref[1])
    def _(i):
        copy(sib_tiles, source_ref[i] - own, i).start()

    @pl.loop(0, count_ref[1])
    def _(i):
        copy(own_tiles, 0, i).wait()


def join_kernel(order, *refs):
    *parts, out = refs
    rows = parts[0].shape[0]
    for i, part in enumerate(parts):
        out[pl.ds(i * rows, rows), :] = part[...]


def products_kernel(fill, order, count_ref, slot_ref, label_ref, tiles, own_panel, *refs):
    parts = refs[: 1 + max(which for which, _, _ in fill)]
    *sends, sums, stack = refs[len(parts) :]
    side = tiles.shape[1]
    for t in range(own_panel.shape[0] // side):
        stack[t] = own_panel[pl.ds(t * side, side), :]
    for which, t, at in fill:
        stack[at] = parts[which][pl.ds(t * side, side), :]

    @pl.loop(0, sums.shape[0])
    def _(i):
        sums[i] = jnp.zeros(sums.shape[1:], jnp.float32)

    @pl.loop(0, (count_ref[1] + UNROLL - 1) // UNROLL)
    def _(i):
        found = [
            jnp.dot(
                tiles[i * UNROLL + u],
                stack[label_ref[i * UNROLL + u]],
                preferred_element_type=jnp.float32,
            )
            for u in range(UNROLL)
        ]
        for u in range(UNROLL):
            sums[slot_ref[i * UNROLL + u]] += found[u]

    sent = sums.shape[0] // 2
    for send in sends:

        @pl.loop(0, send.shape[0])
        def _(i, send=send, sent=sent):
            put_encoded(send.at[i], sums[sent + i])

        sent += send.shape[0]


def plane_kernel(order, recv_a, recv_b, kept, send_a, send_b, keep):
    side, half = kept.shape[1], send_a.shape[0]
    x, y, _, _ = here()
    for base, bit, recv, send in ((0, y, recv_a, send_a), (1, x, recv_b, send_b)):

        @pl.loop(0, half)
        def _(i, base=base, bit=bit, recv=recv, send=send):
            other, mine = 2 * i + 1 - bit, 2 * i + bit
            at = base * 2 * half
            put_encoded(send.at[i], kept[at + other] + get_decoded(recv.at[other], side))
            keep[base * half + i] = kept[at + mine] + get_decoded(recv.at[mine], side)


def owner_kernel(order, recv_a, recv_b, kept, send, keep):
    side, half = kept.shape[1], send.shape[0]
    odd = here()[2]

    @pl.loop(0, half)
    def _(i):
        value_a = kept[i] + get_decoded(recv_a.at[i], side)
        value_b = kept[half + i] + get_decoded(recv_b.at[i], side)
        put_encoded(send.at[i], jnp.where(odd == 1, value_a, value_b))
        keep[i] = jnp.where(odd == 1, value_b, value_a)


def rows_kernel(order, recv, kept, send_1, send_2, send_3, keep):
    side = kept.shape[1]
    x, y, _, _ = here()
    row = 2 * y + x
    for d, send in enumerate((send_1, send_2, send_3), 1):
        put_encoded(send, kept[row ^ d] + get_decoded(recv.at[row ^ d], side))
    keep[...] = kept[row] + get_decoded(recv.at[row], side)


def finish_rows_kernel(order, *refs):
    *recvs, kept, out = refs
    value = kept[...]
    for recv in recvs:
        value += get_decoded(recv, kept.shape[0])
    put_encoded(out, value)


def line_kernel(order, recv, kept, send, keep):
    side, half = kept.shape[1], send.shape[0]
    bit = here()[3]

    @pl.loop(0, half)
    def _(i):
        other, mine = (1 - bit) * half + i, bit * half + i
        put_encoded(send.at[i], kept[other] + get_decoded(recv.at[other], side))
        keep[i] = kept[mine] + get_decoded(recv.at[mine], side)


def finish_kernel(order, recv, kept, out):
    put_encoded(out, kept[0] + get_decoded(recv.at[0], kept.shape[1]))


def spread_kernel(chunk, order, *refs):
    blocks, (out, rows, sems) = refs[:4], refs[-3:]
    side, width = rows.shape[1:]
    x, y, _, _ = here()
    copies = []
    for d, block in enumerate(blocks):
        rows[d] = get_decoded(block, side)
        at = pl.multiple_of(((2 * y + x) ^ d) * side, side)
        copies.append(
            pltpu.make_async_copy(
                rows.at[d], out.at[pl.ds(at, side), pl.ds(chunk * width, width)], sems.at[d]
            )
        )
        copies[-1].start()
    for copy in copies:
        copy.wait()


def in_vmem(count):
    return [pl.BlockSpec(memory_space=pltpu.VMEM)] * count


def in_smem(count):
    return [pl.BlockSpec(memory_space=pltpu.SMEM)] * count


def in_any(count):
    return [pl.BlockSpec(memory_space=pl.ANY)] * count


def shape(dims, kind):
    return jax.ShapeDtypeStruct(dims, kind)


def params(mib):
    return pltpu.CompilerParams(vmem_limit_bytes=mib * MIB)


def cost(flops, moved):
    return pl.CostEstimate(flops=flops, bytes_accessed=moved, transcendentals=0)


def compact(match, values):
    count = -(-match.shape[0] // UNROLL) * UNROLL
    rank = jnp.cumsum(match.astype(jnp.int32)) - 1
    hit = match & (rank == jnp.arange(count, dtype=jnp.int32)[:, None])
    return [jnp.sum(jnp.where(hit, v, 0), axis=-1) for v in values]


def sums_plan(tiles, contraction, row_tile, owner_map, panel):
    wide_count = lax.axis_size("wide")
    tile_dev, side = tiles.shape[0], tiles.shape[1]
    out_dev = owner_map.shape[0] // wide_count
    rows, columns = panel.shape
    shard = rows // side
    chunks = columns // CHUNK
    sums = owner_map.shape[0] // 2
    g, w = lax.axis_index("grp"), lax.axis_index("wide")
    core = w % 2

    def to_core(v):
        return lax.ppermute(v, "wide", [(i, i ^ 1) for i in range(wide_count)])

    def to_grp(v, d):
        return lax.ppermute(v, "grp", [(i, i ^ d) for i in range(4)])

    def to_line(v, b):
        return lax.ppermute(v, "wide", [(i, i ^ (2 << b)) for i in range(wide_count)])

    x, y, z = g % 2, g // 2, w // 2

    labels = jnp.stack([row_tile, contraction])
    both = jnp.stack([labels, to_core(labels)])
    sib_tiles = to_core(tiles)

    def own_half(source, j):
        return lax.dynamic_slice(source, (core * (rows // 2), j * CHUNK), (rows // 2, CHUNK))

    mines = [own_half(panel, j) for j in range(chunks)]
    ways = [None, (1, 2), (2, 1)]
    firsts = [None] + [to_grp(mines[j], ways[j][0]) for j in range(1, chunks)]
    mine, both = lax.optimization_barrier((mines[0], both))
    near = [to_grp(mine, 1), to_grp(mine, 2), to_grp(mines[0], 3)]

    table_ids = jnp.arange(owner_map.shape[0], dtype=jnp.int32)
    position = jnp.sum(jnp.where(both[:, 0, :, None] == table_ids, owner_map, 0), axis=-1)
    owner, local = position // out_dev, position % out_dev
    to_z, odd = owner // 4, (owner // 2) % 2
    bit_x, bit_y = local % 2, local // 2
    first = jnp.where(odd == 1, bit_y == y, bit_x == x)
    second = jnp.where(odd == 1, bit_x, bit_y)
    in_plane = jnp.where(first, 0, sums // 2) + odd * (sums // 4) + 2 * to_z + second
    in_line = jnp.where(odd == z % 2, 0, sums // 2) + to_z * out_dev + local
    k = both[:, 1]
    apart, inner = (k // shard) ^ g, k % shard
    half = shard // 2
    crossed = jnp.where(inner // half == core, 0, half) + inner % half
    label = jnp.where(apart == 0, inner, apart * shard + crossed)
    match = (owner % 2 == core).reshape(-1)
    entries = [v.reshape(-1) for v in (in_plane, in_line, label)]
    serial = jnp.arange(match.shape[0], dtype=jnp.int32)
    source, in_plane, in_line, label = compact(match, [serial, *entries])
    counts = jnp.stack([jnp.sum(match[:tile_dev]), jnp.sum(match)]).astype(jnp.int32)
    beyond = jnp.arange(source.shape[0], dtype=jnp.int32) >= counts[1]
    in_plane = jnp.where(beyond, sums, in_plane)
    in_line = jnp.where(beyond, sums, in_line)

    half, quarter = sums // 2, sums // 4
    coded = shape((side + CODE_ROWS, CHUNK), jnp.int16)
    plain = shape((side, CHUNK), jnp.float32)

    def stack_of(count, one):
        return shape((count, *one.shape), one.dtype)

    order = jnp.zeros((1,), jnp.int32)
    last = None

    def in_order():
        return order if last is None else lax.optimization_barrier((order, last))[0]

    def call(body, name, outs, *args, smem=0, mib=16, extra=(), **more):
        nonlocal last
        done = pl.pallas_call(
            body,
            in_specs=more.pop("in_specs", in_any(1) + in_smem(smem) + in_vmem(len(args) - smem)),
            out_specs=more.pop("out_specs", in_vmem(len(outs))),
            out_shape=outs,
            scratch_shapes=list(extra),
            compiler_params=params(mib),
            cost_estimate=cost(0, sum(math.prod(a.shape) * a.dtype.itemsize for a in args)),
            name=name,
            **more,
        )(in_order(), *args)
        last = done[0]
        return done

    counts, source, in_plane, in_line, label = lax.optimization_barrier(
        (counts, source, in_plane, in_line, label)
    )

    def places(operand, tiles_of, first):
        return [
            (operand, t, d * shard + first + i % part)
            for i, (t, d) in enumerate((t, d) for d, ts in tiles_of for t in ts)
        ]

    part = shard // 2

    def join(j):
        (joined,) = call(join_kernel, "join", [shape((3 * rows // 2, CHUNK), panel.dtype)], *near)
        tiles_of = [(d, range((d - 1) * part, d * part)) for d in (1, 2, 3)]
        fill = places(0, tiles_of, 0) + places(1, tiles_of, part)
        return fill, [joined, to_core(joined)]

    def pair(j):
        way, other = ways[j]
        (joined,) = call(
            join_kernel, "join", [shape((rows, CHUNK), panel.dtype)], mines[j], firsts[j]
        )
        second = to_grp(joined, other)
        in_first = [(way, range(part, 2 * part))]
        in_second = [(other, range(part)), (way ^ other, range(part, 2 * part))]
        fill = (
            places(0, in_first, 0)
            + places(1, in_first, part)
            + places(2, in_second, 0)
            + places(3, in_second, part)
        )
        return fill, [joined, to_core(joined), second, to_core(second)]

    def products(j, slot, sends, fill, parts):
        *sends, kept = call(
            functools.partial(products_kernel, tuple(fill)),
            "products",
            [*sends, stack_of(sums + 1, plain)],
            counts,
            slot,
            label,
            held,
            panel,
            *parts,
            grid=(1,),
            in_specs=in_any(1)
            + in_smem(3)
            + in_vmem(1)
            + [pl.BlockSpec((rows, CHUNK), lambda i: (0, j))]
            + in_vmem(len(parts)),
            extra=[pltpu.VMEM((4 * shard, side, CHUNK), panel.dtype)],
            mib=24,
        )
        return *sends, kept

    def gathered(done):
        return [done] + [to_grp(done, d) for d in (1, 2, 3)]

    def spread(j, blocks, result):
        earlier = [] if result is None else [result]
        return call(
            functools.partial(spread_kernel, j),
            "spread",
            [shape((out_dev * side, columns), jnp.float32)],
            *blocks,
            *earlier,
            in_specs=in_any(1) + in_vmem(4) + in_any(len(earlier)),
            out_specs=in_any(1),
            input_output_aliases={5: 0} if earlier else {},
            extra=[pltpu.VMEM((4, side, CHUNK), jnp.float32), pltpu.SemaphoreType.DMA((4,))],
        )[0]

    eighth = quarter // 2
    pairs = {j: pair(j) for j in (1, 2)}
    (held,) = call(
        hold_kernel,
        "hold",
        [pltpu.VMEM((2 * tile_dev, side, side), tiles.dtype)],
        counts,
        source,
        *[pltpu.with_memory_space_constraint(v, pltpu.HBM) for v in (tiles, sib_tiles)],
        in_specs=in_any(1) + in_smem(2) + in_any(2),
        extra=[pltpu.SemaphoreType.DMA((2 * tile_dev,))],
        mib=8,
    )

    send, keep_0 = products(0, in_line, [stack_of(half, coded)], *join(0))
    sent_0 = send
    sent, keep = {}, {}
    for j in (1, 2):
        send_a, send_b, keep[j] = products(j, in_plane, [stack_of(quarter, coded)] * 2, *pairs[j])
        sent[j] = send_a, send_b

    sent_0, keep_0 = call(
        line_kernel,
        "line",
        [stack_of(quarter, coded), stack_of(quarter, plain)],
        to_line(sent_0, 0),
        keep_0,
    )

    def plane(j):
        return call(
            plane_kernel,
            "plane",
            [stack_of(eighth, coded)] * 2 + [stack_of(quarter, plain)],
            to_grp(sent[j][0], 1),
            to_grp(sent[j][1], 2),
            keep[j],
        )

    def owner(j):
        return call(
            owner_kernel,
            "owner",
            [stack_of(eighth, coded), stack_of(eighth, plain)],
            to_grp(sent[j][0], 2),
            to_grp(sent[j][1], 1),
            keep[j],
        )

    *sent[1], keep[1] = plane(1)
    *sent[2], keep[2] = plane(2)
    sent[1], keep[1] = owner(1)
    *sends, keep_0 = call(
        rows_kernel, "rows", [coded] * 3 + [plain], to_line(sent_0, 1), keep_0
    )
    sent[2], keep[2] = owner(2)
    (done_0,) = call(
        finish_rows_kernel,
        "finish_rows",
        [coded],
        *[to_grp(v, d) for d, v in enumerate(sends, 1)],
        keep_0,
    )

    for j in (1, 2):
        sent[j], keep[j] = call(
            line_kernel,
            "line",
            [stack_of(1, coded), stack_of(1, plain)],
            to_line(sent[j], 0),
            keep[j],
        )
    (done_1,) = call(finish_kernel, "finish", [coded], to_line(sent[1], 1), keep[1])
    result = spread(0, gathered(done_0), None)
    (done_2,) = call(finish_kernel, "finish", [coded], to_line(sent[2], 1), keep[2])
    result = spread(1, gathered(done_1), result)
    return spread(2, gathered(done_2), result)


def per_device(tiles, contraction, row_tile, owner_map, panel):
    dense = owner_map.shape[0] <= tiles.shape[0]
    wide_count = lax.axis_size("wide")
    fits = lax.axis_size("grp") == 4 and wide_count >= 4 and wide_count & (wide_count - 1) == 0
    out_dev = owner_map.shape[0] // wide_count
    if dense and fits and wide_count == 8 and out_dev == 4 and panel.shape[1] == 3 * CHUNK:
        return sums_plan(tiles, contraction, row_tile, owner_map, panel)
    return slots_plan(tiles, contraction, row_tile, owner_map, panel)


def solution(mesh):
    return jax.shard_map(
        per_device,
        mesh=mesh,
        in_specs=(
            P(("grp", "wide"), None, None),
            P(("grp", "wide")),
            P(("grp", "wide")),
            P(),
            P("grp", None),
        ),
        out_specs=P("wide", None),
        check_vma=False,
    )
```

```python
import functools
import math

import jax
import jax.numpy as jnp
from jax import lax
from jax.experimental import pallas as pl
from jax.experimental.pallas import tpu as pltpu
from jax.sharding import PartitionSpec as P

MIB = 1024 * 1024
CODE_ROWS = 16
CODE_STEPS = 256.0
TOP = 32000.0
CHUNK = 256
UNROLL = 8
LOG2 = math.log(2.0)


def place_slots(row_ids, owner_map, out_dev):
    table_ids = jnp.arange(owner_map.shape[0], dtype=jnp.int32)
    position = jnp.sum(jnp.where(row_ids[..., None] == table_ids, owner_map, 0), axis=-1)
    target = position // out_dev
    serial = jnp.arange(row_ids.shape[-1], dtype=jnp.int32)
    earlier = (target[..., :, None] == target[..., None, :]) & (serial[:, None] > serial[None, :])
    ranking = jnp.sum(earlier.astype(jnp.int32), axis=-1)
    return (position % out_dev, target, ranking)


def add_products(summed, arrived, slot_labels, panel_tiles):
    slot_count = arrived.shape[0]
    block_rows = math.gcd(slot_count, 32)
    out_dev = summed.shape[0]
    local_ids = jnp.arange(out_dev, dtype=jnp.int32)

    def one_block(which_block, running, source_tiles, source_labels):
        part_tiles = lax.dynamic_slice_in_dim(source_tiles, which_block * block_rows, block_rows, 0)
        part_labels = lax.dynamic_slice_in_dim(
            source_labels, which_block * block_rows, block_rows, 0
        )
        chosen = jnp.take(panel_tiles, part_labels[:, 1], axis=0)
        products = jnp.einsum(
            "sab,sbc->sac", part_tiles, chosen, preferred_element_type=jnp.float32
        )
        row_hits = (part_labels[:, 0][:, None] == local_ids[None, :]).astype(jnp.float32)
        return running + jnp.einsum(
            "sr,sac->rac", row_hits, products, precision=lax.Precision.HIGHEST
        )

    return lax.fori_loop(
        0,
        slot_count // block_rows,
        lambda which_block, running: one_block(which_block, running, arrived, slot_labels),
        summed,
    )


def slots_plan(tiles, contraction, row_tile, owner_map, panel):
    wide_count = lax.axis_size("wide")
    tile_dev = tiles.shape[0]
    tile_side = tiles.shape[1]
    out_dev = owner_map.shape[0] // wide_count
    most_slots = tile_dev * 8 // (3 * wide_count)
    slot_total = wide_count * most_slots
    local_row, target, ranking = place_slots(row_tile, owner_map, out_dev)
    slot_index = target * most_slots + ranking
    outgoing = jnp.zeros((slot_total, tile_side, tile_side), tiles.dtype).at[slot_index].set(tiles)
    all_rows, all_contraction = (
        lax.all_gather(row_tile, "wide", axis=0, tiled=True),
        lax.all_gather(contraction, "wide", axis=0, tiled=True),
    )
    all_rows = all_rows.reshape(wide_count, tile_dev)
    all_contraction = all_contraction.reshape(wide_count, tile_dev)
    source_local, source_target, source_rank = place_slots(all_rows, owner_map, out_dev)
    source_ids = jnp.arange(wide_count, dtype=jnp.int32)
    mine = source_target == lax.axis_index("wide")
    arrive_index = jnp.where(mine, source_ids[:, None] * most_slots + source_rank, slot_total)
    label_pairs = jnp.stack([source_local, all_contraction], axis=-1).reshape(
        wide_count * tile_dev, 2
    )
    vacant_label = jnp.stack(
        [jnp.full((slot_total,), out_dev, jnp.int32), jnp.zeros((slot_total,), jnp.int32)], axis=1
    )
    arrived_labels = vacant_label.at[arrive_index.reshape(-1)].set(label_pairs, mode="drop")
    gathered = lax.all_gather(panel, "grp", axis=0, tiled=True)
    panel_tiles = gathered.reshape(gathered.shape[0] // tile_side, tile_side, gathered.shape[1])
    summed = jnp.zeros((out_dev, tile_side, gathered.shape[1]), jnp.float32)
    arrived = lax.all_to_all(outgoing, "wide", split_axis=0, concat_axis=0, tiled=True)
    summed = add_products(summed, arrived, arrived_labels, panel_tiles)
    summed = lax.psum(summed, "grp")
    return summed.reshape(out_dev * tile_side, gathered.shape[1])


def encode(value):
    largest = jnp.max(jnp.abs(value), axis=0, keepdims=True)
    code = jnp.ceil(jnp.log(jnp.maximum(largest, 1e-30)) * (CODE_STEPS / LOG2))
    scale = jnp.exp(code * (-LOG2 / CODE_STEPS)) * TOP
    whole = jnp.round(value * scale).astype(jnp.int32).astype(jnp.int16)
    return whole, code.astype(jnp.int32)


def put_encoded(ref, value):
    side = value.shape[0]
    whole, code = encode(value)
    ref[pl.ds(0, side), :] = whole
    ref[pl.ds(side, CODE_ROWS), :] = jnp.broadcast_to(
        code, (CODE_ROWS, code.shape[1])
    ).astype(jnp.int16)


def get_decoded(ref, side):
    code = ref[pl.ds(side, CODE_ROWS), :].astype(jnp.int32).astype(jnp.float32)[:1]
    scale = jnp.exp(code * (LOG2 / CODE_STEPS)) * (1.0 / TOP)
    return ref[pl.ds(0, side), :].astype(jnp.int32).astype(jnp.float32) * scale


def here():
    g, w = lax.axis_index("grp"), lax.axis_index("wide")
    return g % 2, g // 2, (w // 2) % 2, w // 4


def hold_kernel(
    order, row_ref, k_ref, sib_ref, owner_ref, own_tiles, sib_tiles,
    count_ref, plane_ref, line_ref, label_ref, out, sems,
):
    tile_dev = own_tiles.shape[0]
    sums = owner_ref.shape[0] // 2
    shard, out_dev = 4, 4
    x, y, z_low, _ = here()
    g, core = lax.axis_index("grp"), lax.axis_index("wide") % 2

    def copy(tiles, which, at):
        return pltpu.make_async_copy(tiles.at[which], out.at[at], sems.at[at])

    def scan(tiles, row, k, count):
        def one(i, count):
            position = owner_ref[row(i)]
            owner, local = lax.div(position, out_dev), lax.rem(position, out_dev)
            match = lax.rem(owner, 2) == core

            @pl.when(match)
            def _():
                copy(tiles, i, count).start()
                odd, to_z = lax.rem(lax.div(owner, 2), 2), lax.div(owner, 4)
                bit_x, bit_y = lax.rem(local, 2), lax.div(local, 2)
                first = jnp.where(odd == 1, bit_y == y, bit_x == x)
                second = jnp.where(odd == 1, bit_x, bit_y)
                plane_ref[count] = (
                    jnp.where(first, 0, sums // 2) + odd * (sums // 4) + 2 * to_z + second
                )
                line_ref[count] = (
                    jnp.where(odd == z_low, 0, sums // 2) + to_z * out_dev + local
                )
                apart, inner = lax.div(k(i), shard) ^ g, lax.rem(k(i), shard)
                half = shard // 2
                crossed = jnp.where(lax.div(inner, half) == core, 0, half) + lax.rem(inner, half)
                label_ref[count] = jnp.where(apart == 0, inner, apart * shard + crossed)

            return count + match.astype(jnp.int32)

        return lax.fori_loop(0, tile_dev, one, count)

    count = scan(own_tiles, lambda i: row_ref[i], lambda i: k_ref[i], 0)
    count = scan(sib_tiles, lambda i: sib_ref[0, i], lambda i: sib_ref[1, i], count)
    count_ref[0] = count
    for i in range(UNROLL):
        plane_ref[count + i] = sums
        line_ref[count + i] = sums
        label_ref[count + i] = 0

    @pl.loop(0, count)
    def _(i):
        copy(own_tiles, 0, i).wait()


def join_kernel(order, *refs):
    *parts, out = refs
    rows = parts[0].shape[0]
    for i, part in enumerate(parts):
        out[pl.ds(i * rows, rows), :] = part[...]


def products_kernel(fill, order, count_ref, slot_ref, label_ref, tiles, own_panel, *refs):
    parts = refs[: 1 + max(which for which, _, _ in fill)]
    *sends, sums, stack = refs[len(parts) :]
    side = tiles.shape[1]
    for t in range(own_panel.shape[0] // side):
        stack[t] = own_panel[pl.ds(t * side, side), :]
    for which, t, at in fill:
        stack[at] = parts[which][pl.ds(t * side, side), :]

    @pl.loop(0, sums.shape[0])
    def _(i):
        sums[i] = jnp.zeros(sums.shape[1:], jnp.float32)

    @pl.loop(0, lax.div(count_ref[0] + UNROLL - 1, UNROLL))
    def _(i):
        found = [
            jnp.dot(
                tiles[i * UNROLL + u],
                stack[label_ref[i * UNROLL + u]],
                preferred_element_type=jnp.float32,
            )
            for u in range(UNROLL)
        ]
        for u in range(UNROLL):
            sums[slot_ref[i * UNROLL + u]] += found[u]

    sent = sums.shape[0] // 2
    for send in sends:

        @pl.loop(0, send.shape[0])
        def _(i, send=send, sent=sent):
            put_encoded(send.at[i], sums[sent + i])

        sent += send.shape[0]


def plane_kernel(order, recv_a, recv_b, kept, send_a, send_b, keep):
    side, half = kept.shape[1], send_a.shape[0]
    x, y, _, _ = here()
    for base, bit, recv, send in ((0, y, recv_a, send_a), (1, x, recv_b, send_b)):

        @pl.loop(0, half)
        def _(i, base=base, bit=bit, recv=recv, send=send):
            other, mine = 2 * i + 1 - bit, 2 * i + bit
            at = base * 2 * half
            put_encoded(send.at[i], kept[at + other] + get_decoded(recv.at[other], side))
            keep[base * half + i] = kept[at + mine] + get_decoded(recv.at[mine], side)


def owner_kernel(order, recv_a, recv_b, kept, send, keep):
    side, half = kept.shape[1], send.shape[0]
    odd = here()[2]

    @pl.loop(0, half)
    def _(i):
        value_a = kept[i] + get_decoded(recv_a.at[i], side)
        value_b = kept[half + i] + get_decoded(recv_b.at[i], side)
        put_encoded(send.at[i], jnp.where(odd == 1, value_a, value_b))
        keep[i] = jnp.where(odd == 1, value_b, value_a)


def rows_kernel(order, recv, kept, send_1, send_2, send_3, keep):
    side = kept.shape[1]
    x, y, _, _ = here()
    row = 2 * y + x
    for d, send in enumerate((send_1, send_2, send_3), 1):
        put_encoded(send, kept[row ^ d] + get_decoded(recv.at[row ^ d], side))
    keep[...] = kept[row] + get_decoded(recv.at[row], side)


def finish_rows_kernel(order, *refs):
    *recvs, kept, out = refs
    value = kept[...]
    for recv in recvs:
        value += get_decoded(recv, kept.shape[0])
    put_encoded(out, value)


def line_kernel(order, recv, kept, send, keep):
    side, half = kept.shape[1], send.shape[0]
    bit = here()[3]

    @pl.loop(0, half)
    def _(i):
        other, mine = (1 - bit) * half + i, bit * half + i
        put_encoded(send.at[i], kept[other] + get_decoded(recv.at[other], side))
        keep[i] = kept[mine] + get_decoded(recv.at[mine], side)


def finish_kernel(order, recv, kept, out):
    put_encoded(out, kept[0] + get_decoded(recv.at[0], kept.shape[1]))


def spread_kernel(chunk, order, *refs):
    blocks, (out, rows, sems) = refs[:4], refs[-3:]
    side, width = rows.shape[1:]
    x, y, _, _ = here()
    copies = []
    for d, block in enumerate(blocks):
        rows[d] = get_decoded(block, side)
        at = pl.multiple_of(((2 * y + x) ^ d) * side, side)
        copies.append(
            pltpu.make_async_copy(
                rows.at[d], out.at[pl.ds(at, side), pl.ds(chunk * width, width)], sems.at[d]
            )
        )
        copies[-1].start()
    for copy in copies:
        copy.wait()


def in_vmem(count):
    return [pl.BlockSpec(memory_space=pltpu.VMEM)] * count


def in_smem(count):
    return [pl.BlockSpec(memory_space=pltpu.SMEM)] * count


def in_any(count):
    return [pl.BlockSpec(memory_space=pl.ANY)] * count


def shape(dims, kind):
    return jax.ShapeDtypeStruct(dims, kind)


def params(mib):
    return pltpu.CompilerParams(vmem_limit_bytes=mib * MIB)


def cost(flops, moved):
    return pl.CostEstimate(flops=flops, bytes_accessed=moved, transcendentals=0)


def sums_plan(tiles, contraction, row_tile, owner_map, panel):
    wide_count = lax.axis_size("wide")
    tile_dev, side = tiles.shape[0], tiles.shape[1]
    out_dev = owner_map.shape[0] // wide_count
    rows, columns = panel.shape
    shard = rows // side
    chunks = columns // CHUNK
    sums = owner_map.shape[0] // 2
    core = lax.axis_index("wide") % 2

    def to_core(v):
        return lax.ppermute(v, "wide", [(i, i ^ 1) for i in range(wide_count)])

    def to_grp(v, d):
        return lax.ppermute(v, "grp", [(i, i ^ d) for i in range(4)])

    def to_line(v, b):
        return lax.ppermute(v, "wide", [(i, i ^ (2 << b)) for i in range(wide_count)])


    sib_labels = to_core(jnp.stack([row_tile, contraction]))
    sib_tiles = to_core(tiles)

    def own_half(source, j):
        return lax.dynamic_slice(source, (core * (rows // 2), j * CHUNK), (rows // 2, CHUNK))

    mines = [own_half(panel, j) for j in range(chunks)]
    ways = [None, (1, 2), (2, 1)]
    firsts = [None] + [to_grp(mines[j], ways[j][0]) for j in range(1, chunks)]
    mine, sib_labels = lax.optimization_barrier((mines[0], sib_labels))
    near = [to_grp(mine, 1), to_grp(mine, 2), to_grp(mines[0], 3)]

    half, quarter = sums // 2, sums // 4
    coded = shape((side + CODE_ROWS, CHUNK), jnp.int16)
    plain = shape((side, CHUNK), jnp.float32)

    def stack_of(count, one):
        return shape((count, *one.shape), one.dtype)

    order = jnp.zeros((1,), jnp.int32)
    last = None

    def in_order():
        return order if last is None else lax.optimization_barrier((order, last))[0]

    def call(body, name, outs, *args, smem=0, mib=16, extra=(), **more):
        nonlocal last
        done = pl.pallas_call(
            body,
            in_specs=more.pop("in_specs", in_any(1) + in_smem(smem) + in_vmem(len(args) - smem)),
            out_specs=more.pop("out_specs", in_vmem(len(outs))),
            out_shape=outs,
            scratch_shapes=list(extra),
            compiler_params=params(mib),
            cost_estimate=cost(0, sum(math.prod(a.shape) * a.dtype.itemsize for a in args)),
            name=name,
            **more,
        )(in_order(), *args)
        last = done[0]
        return done

    def places(operand, tiles_of, first):
        return [
            (operand, t, d * shard + first + i % part)
            for i, (t, d) in enumerate((t, d) for d, ts in tiles_of for t in ts)
        ]

    part = shard // 2

    def join(j):
        (joined,) = call(join_kernel, "join", [shape((3 * rows // 2, CHUNK), panel.dtype)], *near)
        tiles_of = [(d, range((d - 1) * part, d * part)) for d in (1, 2, 3)]
        fill = places(0, tiles_of, 0) + places(1, tiles_of, part)
        return fill, [joined, to_core(joined)]

    def pair(j):
        way, other = ways[j]
        (joined,) = call(
            join_kernel, "join", [shape((rows, CHUNK), panel.dtype)], mines[j], firsts[j]
        )
        second = to_grp(joined, other)
        in_first = [(way, range(part, 2 * part))]
        in_second = [(other, range(part)), (way ^ other, range(part, 2 * part))]
        fill = (
            places(0, in_first, 0)
            + places(1, in_first, part)
            + places(2, in_second, 0)
            + places(3, in_second, part)
        )
        return fill, [joined, to_core(joined), second, to_core(second)]

    def products(j, slot, sends, fill, parts):
        *sends, kept = call(
            functools.partial(products_kernel, tuple(fill)),
            "products",
            [*sends, stack_of(sums + 1, plain)],
            counts,
            slot,
            label,
            held,
            panel,
            *parts,
            grid=(1,),
            in_specs=in_any(1)
            + in_smem(3)
            + in_vmem(1)
            + [pl.BlockSpec((rows, CHUNK), lambda i: (0, j))]
            + in_vmem(len(parts)),
            extra=[pltpu.VMEM((4 * shard, side, CHUNK), panel.dtype)],
            mib=24,
        )
        return *sends, kept

    def gathered(done):
        return [done] + [to_grp(done, d) for d in (1, 2, 3)]

    def spread(j, blocks, result):
        earlier = [] if result is None else [result]
        return call(
            functools.partial(spread_kernel, j),
            "spread",
            [shape((out_dev * side, columns), jnp.float32)],
            *blocks,
            *earlier,
            in_specs=in_any(1) + in_vmem(4) + in_any(len(earlier)),
            out_specs=in_any(1),
            input_output_aliases={5: 0} if earlier else {},
            extra=[pltpu.VMEM((4, side, CHUNK), jnp.float32), pltpu.SemaphoreType.DMA((4,))],
        )[0]

    eighth = quarter // 2
    entries = shape((2 * tile_dev + UNROLL,), jnp.int32)
    counts, in_plane, in_line, label, held = call(
        hold_kernel,
        "hold",
        [shape((1,), jnp.int32)]
        + [entries] * 3
        + [pltpu.VMEM((2 * tile_dev + UNROLL, side, side), tiles.dtype)],
        row_tile,
        contraction,
        sib_labels,
        owner_map,
        *[pltpu.with_memory_space_constraint(v, pltpu.HBM) for v in (tiles, sib_tiles)],
        in_specs=in_any(1) + in_smem(4) + in_any(2),
        out_specs=in_smem(4) + in_vmem(1),
        extra=[pltpu.SemaphoreType.DMA((2 * tile_dev,))],
        mib=8,
    )
    last = held
    pairs = {j: pair(j) for j in (1, 2)}

    send, keep_0 = products(0, in_line, [stack_of(half, coded)], *join(0))
    sent_0 = send
    sent, keep = {}, {}
    for j in (1, 2):
        send_a, send_b, keep[j] = products(j, in_plane, [stack_of(quarter, coded)] * 2, *pairs[j])
        sent[j] = send_a, send_b

    sent_0, keep_0 = call(
        line_kernel,
        "line",
        [stack_of(quarter, coded), stack_of(quarter, plain)],
        to_line(sent_0, 0),
        keep_0,
    )

    def plane(j):
        return call(
            plane_kernel,
            "plane",
            [stack_of(eighth, coded)] * 2 + [stack_of(quarter, plain)],
            to_grp(sent[j][0], 1),
            to_grp(sent[j][1], 2),
            keep[j],
        )

    def owner(j):
        return call(
            owner_kernel,
            "owner",
            [stack_of(eighth, coded), stack_of(eighth, plain)],
            to_grp(sent[j][0], 2),
            to_grp(sent[j][1], 1),
            keep[j],
        )

    *sent[1], keep[1] = plane(1)
    *sent[2], keep[2] = plane(2)
    sent[1], keep[1] = owner(1)
    sent[2], keep[2] = owner(2)
    *sends, keep_0 = call(
        rows_kernel, "rows", [coded] * 3 + [plain], to_line(sent_0, 1), keep_0
    )
    (done_0,) = call(
        finish_rows_kernel,
        "finish_rows",
        [coded],
        *[to_grp(v, d) for d, v in enumerate(sends, 1)],
        keep_0,
    )

    for j in (1, 2):
        sent[j], keep[j] = call(
            line_kernel,
            "line",
            [stack_of(1, coded), stack_of(1, plain)],
            to_line(sent[j], 0),
            keep[j],
        )
    (done_1,) = call(finish_kernel, "finish", [coded], to_line(sent[1], 1), keep[1])
    result = spread(0, gathered(done_0), None)
    (done_2,) = call(finish_kernel, "finish", [coded], to_line(sent[2], 1), keep[2])
    result = spread(1, gathered(done_1), result)
    return spread(2, gathered(done_2), result)


def per_device(tiles, contraction, row_tile, owner_map, panel):
    dense = owner_map.shape[0] <= tiles.shape[0]
    wide_count = lax.axis_size("wide")
    fits = lax.axis_size("grp") == 4 and wide_count >= 4 and wide_count & (wide_count - 1) == 0
    out_dev = owner_map.shape[0] // wide_count
    if dense and fits and wide_count == 8 and out_dev == 4 and panel.shape[1] == 3 * CHUNK:
        return sums_plan(tiles, contraction, row_tile, owner_map, panel)
    return slots_plan(tiles, contraction, row_tile, owner_map, panel)


def solution(mesh):
    return jax.shard_map(
        per_device,
        mesh=mesh,
        in_specs=(
            P(("grp", "wide"), None, None),
            P(("grp", "wide")),
            P(("grp", "wide")),
            P(),
            P("grp", None),
        ),
        out_specs=P("wide", None),
        check_vma=False,
    )
```

```python
import functools
import math

import jax
import jax.numpy as jnp
from jax import lax
from jax.experimental import pallas as pl
from jax.experimental.pallas import tpu as pltpu
from jax.sharding import PartitionSpec as P

MIB = 1024 * 1024
CODE_ROWS = 16
CODE_STEPS = 256.0
TOP = 32000.0
CHUNK = 256
UNROLL = 8
LOG2 = math.log(2.0)


def place_slots(row_ids, owner_map, out_dev):
    table_ids = jnp.arange(owner_map.shape[0], dtype=jnp.int32)
    position = jnp.sum(jnp.where(row_ids[..., None] == table_ids, owner_map, 0), axis=-1)
    target = position // out_dev
    serial = jnp.arange(row_ids.shape[-1], dtype=jnp.int32)
    earlier = (target[..., :, None] == target[..., None, :]) & (serial[:, None] > serial[None, :])
    ranking = jnp.sum(earlier.astype(jnp.int32), axis=-1)
    return (position % out_dev, target, ranking)


def add_products(summed, arrived, slot_labels, panel_tiles):
    slot_count = arrived.shape[0]
    block_rows = math.gcd(slot_count, 32)
    out_dev = summed.shape[0]
    local_ids = jnp.arange(out_dev, dtype=jnp.int32)

    def one_block(which_block, running, source_tiles, source_labels):
        part_tiles = lax.dynamic_slice_in_dim(source_tiles, which_block * block_rows, block_rows, 0)
        part_labels = lax.dynamic_slice_in_dim(
            source_labels, which_block * block_rows, block_rows, 0
        )
        chosen = jnp.take(panel_tiles, part_labels[:, 1], axis=0)
        products = jnp.einsum(
            "sab,sbc->sac", part_tiles, chosen, preferred_element_type=jnp.float32
        )
        row_hits = (part_labels[:, 0][:, None] == local_ids[None, :]).astype(jnp.float32)
        return running + jnp.einsum(
            "sr,sac->rac", row_hits, products, precision=lax.Precision.HIGHEST
        )

    return lax.fori_loop(
        0,
        slot_count // block_rows,
        lambda which_block, running: one_block(which_block, running, arrived, slot_labels),
        summed,
    )


def slots_plan(tiles, contraction, row_tile, owner_map, panel):
    wide_count = lax.axis_size("wide")
    tile_dev = tiles.shape[0]
    tile_side = tiles.shape[1]
    out_dev = owner_map.shape[0] // wide_count
    most_slots = tile_dev * 8 // (3 * wide_count)
    slot_total = wide_count * most_slots
    local_row, target, ranking = place_slots(row_tile, owner_map, out_dev)
    slot_index = target * most_slots + ranking
    outgoing = jnp.zeros((slot_total, tile_side, tile_side), tiles.dtype).at[slot_index].set(tiles)
    all_rows, all_contraction = (
        lax.all_gather(row_tile, "wide", axis=0, tiled=True),
        lax.all_gather(contraction, "wide", axis=0, tiled=True),
    )
    all_rows = all_rows.reshape(wide_count, tile_dev)
    all_contraction = all_contraction.reshape(wide_count, tile_dev)
    source_local, source_target, source_rank = place_slots(all_rows, owner_map, out_dev)
    source_ids = jnp.arange(wide_count, dtype=jnp.int32)
    mine = source_target == lax.axis_index("wide")
    arrive_index = jnp.where(mine, source_ids[:, None] * most_slots + source_rank, slot_total)
    label_pairs = jnp.stack([source_local, all_contraction], axis=-1).reshape(
        wide_count * tile_dev, 2
    )
    vacant_label = jnp.stack(
        [jnp.full((slot_total,), out_dev, jnp.int32), jnp.zeros((slot_total,), jnp.int32)], axis=1
    )
    arrived_labels = vacant_label.at[arrive_index.reshape(-1)].set(label_pairs, mode="drop")
    gathered = lax.all_gather(panel, "grp", axis=0, tiled=True)
    panel_tiles = gathered.reshape(gathered.shape[0] // tile_side, tile_side, gathered.shape[1])
    summed = jnp.zeros((out_dev, tile_side, gathered.shape[1]), jnp.float32)
    arrived = lax.all_to_all(outgoing, "wide", split_axis=0, concat_axis=0, tiled=True)
    summed = add_products(summed, arrived, arrived_labels, panel_tiles)
    summed = lax.psum(summed, "grp")
    return summed.reshape(out_dev * tile_side, gathered.shape[1])


def encode(value):
    largest = jnp.max(jnp.abs(value), axis=0, keepdims=True)
    code = jnp.ceil(jnp.log(jnp.maximum(largest, 1e-30)) * (CODE_STEPS / LOG2))
    scale = jnp.exp(code * (-LOG2 / CODE_STEPS)) * TOP
    whole = jnp.round(value * scale).astype(jnp.int32).astype(jnp.int16)
    return whole, code.astype(jnp.int32)


def put_encoded(ref, value):
    side = value.shape[0]
    whole, code = encode(value)
    ref[pl.ds(0, side), :] = whole
    ref[pl.ds(side, CODE_ROWS), :] = jnp.broadcast_to(
        code, (CODE_ROWS, code.shape[1])
    ).astype(jnp.int16)


def get_decoded(ref, side):
    code = ref[pl.ds(side, CODE_ROWS), :].astype(jnp.int32).astype(jnp.float32)[:1]
    scale = jnp.exp(code * (LOG2 / CODE_STEPS)) * (1.0 / TOP)
    return ref[pl.ds(0, side), :].astype(jnp.int32).astype(jnp.float32) * scale


def here():
    g, w = lax.axis_index("grp"), lax.axis_index("wide")
    return g % 2, g // 2, (w // 2) % 2, w // 4


def hold_kernel(
    order, own_ref, sib_ref, own_tiles, sib_tiles,
    count_ref, plane_ref, line_ref, label_ref, out, sems,
):
    tile_dev = own_tiles.shape[0]
    sums = (own_ref.shape[0] - 2 * tile_dev) // 2
    shard, out_dev = 4, 4
    x, y, z_low, _ = here()
    g, core = lax.axis_index("grp"), lax.axis_index("wide") % 2

    def copy(tiles, which, at):
        return pltpu.make_async_copy(tiles.at[which], out.at[at], sems.at[at])

    def scan(tiles, index_ref, count):
        def one(i, count):
            position = own_ref[2 * tile_dev + index_ref[i]]
            k = index_ref[tile_dev + i]
            owner, local = lax.div(position, out_dev), lax.rem(position, out_dev)
            match = lax.rem(owner, 2) == core

            @pl.when(match)
            def _():
                copy(tiles, i, count).start()
                odd, to_z = lax.rem(lax.div(owner, 2), 2), lax.div(owner, 4)
                bit_x, bit_y = lax.rem(local, 2), lax.div(local, 2)
                first = jnp.where(odd == 1, bit_y == y, bit_x == x)
                second = jnp.where(odd == 1, bit_x, bit_y)
                plane_ref[count] = (
                    jnp.where(first, 0, sums // 2) + odd * (sums // 4) + 2 * to_z + second
                )
                line_ref[count] = (
                    jnp.where(odd == z_low, 0, sums // 2) + to_z * out_dev + local
                )
                apart, inner = lax.div(k, shard) ^ g, lax.rem(k, shard)
                half = shard // 2
                crossed = jnp.where(lax.div(inner, half) == core, 0, half) + lax.rem(inner, half)
                label_ref[count] = jnp.where(apart == 0, inner, apart * shard + crossed)

            return count + match.astype(jnp.int32)

        return lax.fori_loop(0, tile_dev, one, count)

    count = scan(own_tiles, own_ref, 0)
    count = scan(sib_tiles, sib_ref, count)
    count_ref[0] = count
    for i in range(UNROLL):
        plane_ref[count + i] = sums
        line_ref[count + i] = sums
        label_ref[count + i] = 0

    @pl.loop(0, count)
    def _(i):
        copy(own_tiles, 0, i).wait()


def join_kernel(order, *refs):
    *parts, out = refs
    rows = parts[0].shape[0]
    for i, part in enumerate(parts):
        out[pl.ds(i * rows, rows), :] = part[...]


def products_kernel(
    fill, chunk, order, count_ref, slot_ref, label_ref, tiles, own_panel, *refs
):
    parts = refs[: 1 + max(which for which, _, _ in fill)]
    *sends, sums, stack = refs[len(parts) :]
    side, width = stack.shape[1:]
    for t in range(own_panel.shape[0] // side):
        stack[t] = own_panel[pl.ds(t * side, side), pl.ds(chunk * width, width)]
    for which, t, at in fill:
        stack[at] = parts[which][pl.ds(t * side, side), :]

    @pl.loop(0, sums.shape[0])
    def _(i):
        sums[i] = jnp.zeros(sums.shape[1:], jnp.float32)

    @pl.loop(0, lax.div(count_ref[0] + UNROLL - 1, UNROLL))
    def _(i):
        found = [
            jnp.dot(
                tiles[i * UNROLL + u],
                stack[label_ref[i * UNROLL + u]],
                preferred_element_type=jnp.float32,
            )
            for u in range(UNROLL)
        ]
        for u in range(UNROLL):
            sums[slot_ref[i * UNROLL + u]] += found[u]

    sent = sums.shape[0] // 2
    for send in sends:

        @pl.loop(0, send.shape[0])
        def _(i, send=send, sent=sent):
            put_encoded(send.at[i], sums[sent + i])

        sent += send.shape[0]


def plane_kernel(order, recv_a, recv_b, kept, send_a, send_b, keep):
    side, half = kept.shape[1], send_a.shape[0]
    x, y, _, _ = here()
    for base, bit, recv, send in ((0, y, recv_a, send_a), (1, x, recv_b, send_b)):

        @pl.loop(0, half)
        def _(i, base=base, bit=bit, recv=recv, send=send):
            other, mine = 2 * i + 1 - bit, 2 * i + bit
            at = base * 2 * half
            put_encoded(send.at[i], kept[at + other] + get_decoded(recv.at[other], side))
            keep[base * half + i] = kept[at + mine] + get_decoded(recv.at[mine], side)


def owner_kernel(order, recv_a, recv_b, kept, send, keep):
    side, half = kept.shape[1], send.shape[0]
    odd = here()[2]

    @pl.loop(0, half)
    def _(i):
        value_a = kept[i] + get_decoded(recv_a.at[i], side)
        value_b = kept[half + i] + get_decoded(recv_b.at[i], side)
        put_encoded(send.at[i], jnp.where(odd == 1, value_a, value_b))
        keep[i] = jnp.where(odd == 1, value_b, value_a)


def rows_kernel(order, recv, kept, send_1, send_2, send_3, keep):
    side = kept.shape[1]
    x, y, _, _ = here()
    row = 2 * y + x
    for d, send in enumerate((send_1, send_2, send_3), 1):
        put_encoded(send, kept[row ^ d] + get_decoded(recv.at[row ^ d], side))
    keep[...] = kept[row] + get_decoded(recv.at[row], side)


def finish_rows_kernel(order, *refs):
    *recvs, kept, out = refs
    value = kept[...]
    for recv in recvs:
        value += get_decoded(recv, kept.shape[0])
    put_encoded(out, value)


def line_kernel(order, recv, kept, send, keep):
    side, half = kept.shape[1], send.shape[0]
    bit = here()[3]

    @pl.loop(0, half)
    def _(i):
        other, mine = (1 - bit) * half + i, bit * half + i
        put_encoded(send.at[i], kept[other] + get_decoded(recv.at[other], side))
        keep[i] = kept[mine] + get_decoded(recv.at[mine], side)


def finish_kernel(order, recv, kept, out):
    put_encoded(out, kept[0] + get_decoded(recv.at[0], kept.shape[1]))


def spread_kernel(chunk, order, *refs):
    blocks, (out, rows, sems) = refs[:4], refs[-3:]
    side, width = rows.shape[1:]
    x, y, _, _ = here()
    copies = []
    for d, block in enumerate(blocks):
        rows[d] = get_decoded(block, side)
        at = pl.multiple_of(((2 * y + x) ^ d) * side, side)
        copies.append(
            pltpu.make_async_copy(
                rows.at[d], out.at[pl.ds(at, side), pl.ds(chunk * width, width)], sems.at[d]
            )
        )
        copies[-1].start()
    for copy in copies:
        copy.wait()


def in_vmem(count):
    return [pl.BlockSpec(memory_space=pltpu.VMEM)] * count


def in_smem(count):
    return [pl.BlockSpec(memory_space=pltpu.SMEM)] * count


def in_any(count):
    return [pl.BlockSpec(memory_space=pl.ANY)] * count


def shape(dims, kind):
    return jax.ShapeDtypeStruct(dims, kind)


def params(mib):
    return pltpu.CompilerParams(vmem_limit_bytes=mib * MIB)


def cost(flops, moved):
    return pl.CostEstimate(flops=flops, bytes_accessed=moved, transcendentals=0)


def sums_plan(tiles, contraction, row_tile, owner_map, panel):
    wide_count = lax.axis_size("wide")
    tile_dev, side = tiles.shape[0], tiles.shape[1]
    out_dev = owner_map.shape[0] // wide_count
    rows, columns = panel.shape
    shard = rows // side
    chunks = columns // CHUNK
    sums = owner_map.shape[0] // 2
    core = lax.axis_index("wide") % 2

    def to_core(v):
        return lax.ppermute(v, "wide", [(i, i ^ 1) for i in range(wide_count)])

    def to_grp(v, d):
        return lax.ppermute(v, "grp", [(i, i ^ d) for i in range(4)])

    def to_line(v, b):
        return lax.ppermute(v, "wide", [(i, i ^ (2 << b)) for i in range(wide_count)])


    own_index = jnp.concatenate([row_tile, contraction, owner_map])
    sib_index = to_core(own_index)
    sib_tiles = to_core(tiles)

    def own_half(source, j):
        return lax.dynamic_slice(source, (core * (rows // 2), j * CHUNK), (rows // 2, CHUNK))

    mines = [own_half(panel, j) for j in range(chunks)]
    ways = [None, (1, 2), (2, 1)]
    firsts = [None] + [to_grp(mines[j], ways[j][0]) for j in range(1, chunks)]
    mine, sib_index = lax.optimization_barrier((mines[0], sib_index))
    near = [to_grp(mine, 1), to_grp(mine, 2), to_grp(mines[0], 3)]

    half, quarter = sums // 2, sums // 4
    coded = shape((side + CODE_ROWS, CHUNK), jnp.int16)
    plain = shape((side, CHUNK), jnp.float32)

    def stack_of(count, one):
        return shape((count, *one.shape), one.dtype)

    order = jnp.zeros((1,), jnp.int32)
    last = None

    def in_order():
        return order if last is None else lax.optimization_barrier((order, last))[0]

    def call(body, name, outs, *args, smem=0, mib=16, extra=(), **more):
        nonlocal last
        done = pl.pallas_call(
            body,
            in_specs=more.pop("in_specs", in_any(1) + in_smem(smem) + in_vmem(len(args) - smem)),
            out_specs=more.pop("out_specs", in_vmem(len(outs))),
            out_shape=outs,
            scratch_shapes=list(extra),
            compiler_params=params(mib),
            cost_estimate=cost(0, sum(math.prod(a.shape) * a.dtype.itemsize for a in args)),
            name=name,
            **more,
        )(in_order(), *args)
        last = done[0]
        return done

    def places(operand, tiles_of, first):
        return [
            (operand, t, d * shard + first + i % part)
            for i, (t, d) in enumerate((t, d) for d, ts in tiles_of for t in ts)
        ]

    part = shard // 2

    def join(j):
        (joined,) = call(join_kernel, "join", [shape((3 * rows // 2, CHUNK), panel.dtype)], *near)
        tiles_of = [(d, range((d - 1) * part, d * part)) for d in (1, 2, 3)]
        fill = places(0, tiles_of, 0) + places(1, tiles_of, part)
        return fill, [joined, to_core(joined)]

    def pair(j):
        way, other = ways[j]
        (joined,) = call(
            join_kernel, "join", [shape((rows, CHUNK), panel.dtype)], mines[j], firsts[j]
        )
        second = to_grp(joined, other)
        in_first = [(way, range(part, 2 * part))]
        in_second = [(other, range(part)), (way ^ other, range(part, 2 * part))]
        fill = (
            places(0, in_first, 0)
            + places(1, in_first, part)
            + places(2, in_second, 0)
            + places(3, in_second, part)
        )
        return fill, [joined, to_core(joined), second, to_core(second)]

    def products(j, slot, sends, fill, parts):
        *sends, kept = call(
            functools.partial(products_kernel, tuple(fill), j),
            "products",
            [*sends, stack_of(sums + 1, plain)],
            counts,
            slot,
            label,
            held,
            panel,
            *parts,
            smem=3,
            extra=[pltpu.VMEM((4 * shard, side, CHUNK), panel.dtype)],
            mib=24,
        )
        return *sends, kept

    def gathered(done):
        return [done] + [to_grp(done, d) for d in (1, 2, 3)]

    def spread(j, blocks, result):
        earlier = [] if result is None else [result]
        return call(
            functools.partial(spread_kernel, j),
            "spread",
            [shape((out_dev * side, columns), jnp.float32)],
            *blocks,
            *earlier,
            in_specs=in_any(1) + in_vmem(4) + in_any(len(earlier)),
            out_specs=in_any(1),
            input_output_aliases={5: 0} if earlier else {},
            extra=[pltpu.VMEM((4, side, CHUNK), jnp.float32), pltpu.SemaphoreType.DMA((4,))],
        )[0]

    eighth = quarter // 2
    entries = shape((2 * tile_dev + UNROLL,), jnp.int32)
    counts, in_plane, in_line, label, held = call(
        hold_kernel,
        "hold",
        [shape((1,), jnp.int32)]
        + [entries] * 3
        + [pltpu.VMEM((2 * tile_dev + UNROLL, side, side), tiles.dtype)],
        own_index,
        sib_index,
        *[pltpu.with_memory_space_constraint(v, pltpu.HBM) for v in (tiles, sib_tiles)],
        in_specs=in_any(1) + in_smem(2) + in_any(2),
        out_specs=in_smem(4) + in_vmem(1),
        extra=[pltpu.SemaphoreType.DMA((2 * tile_dev,))],
        mib=8,
    )
    last = held
    pairs = {j: pair(j) for j in (1, 2)}

    send, keep_0 = products(0, in_line, [stack_of(half, coded)], *join(0))
    sent_0 = send
    sent, keep = {}, {}
    for j in (1, 2):
        send_a, send_b, keep[j] = products(j, in_plane, [stack_of(quarter, coded)] * 2, *pairs[j])
        sent[j] = send_a, send_b

    sent_0, keep_0 = call(
        line_kernel,
        "line",
        [stack_of(quarter, coded), stack_of(quarter, plain)],
        to_line(sent_0, 0),
        keep_0,
    )

    def plane(j):
        return call(
            plane_kernel,
            "plane",
            [stack_of(eighth, coded)] * 2 + [stack_of(quarter, plain)],
            to_grp(sent[j][0], 1),
            to_grp(sent[j][1], 2),
            keep[j],
        )

    def owner(j):
        return call(
            owner_kernel,
            "owner",
            [stack_of(eighth, coded), stack_of(eighth, plain)],
            to_grp(sent[j][0], 2),
            to_grp(sent[j][1], 1),
            keep[j],
        )

    *sent[1], keep[1] = plane(1)
    *sent[2], keep[2] = plane(2)
    sent[1], keep[1] = owner(1)
    sent[2], keep[2] = owner(2)
    *sends, keep_0 = call(
        rows_kernel, "rows", [coded] * 3 + [plain], to_line(sent_0, 1), keep_0
    )
    (done_0,) = call(
        finish_rows_kernel,
        "finish_rows",
        [coded],
        *[to_grp(v, d) for d, v in enumerate(sends, 1)],
        keep_0,
    )

    for j in (1, 2):
        sent[j], keep[j] = call(
            line_kernel,
            "line",
            [stack_of(1, coded), stack_of(1, plain)],
            to_line(sent[j], 0),
            keep[j],
        )
    (done_1,) = call(finish_kernel, "finish", [coded], to_line(sent[1], 1), keep[1])
    result = spread(0, gathered(done_0), None)
    (done_2,) = call(finish_kernel, "finish", [coded], to_line(sent[2], 1), keep[2])
    result = spread(1, gathered(done_1), result)
    return spread(2, gathered(done_2), result)


def per_device(tiles, contraction, row_tile, owner_map, panel):
    dense = owner_map.shape[0] <= tiles.shape[0]
    wide_count = lax.axis_size("wide")
    fits = lax.axis_size("grp") == 4 and wide_count >= 4 and wide_count & (wide_count - 1) == 0
    out_dev = owner_map.shape[0] // wide_count
    if dense and fits and wide_count == 8 and out_dev == 4 and panel.shape[1] == 3 * CHUNK:
        return sums_plan(tiles, contraction, row_tile, owner_map, panel)
    return slots_plan(tiles, contraction, row_tile, owner_map, panel)


def solution(mesh):
    return jax.shard_map(
        per_device,
        mesh=mesh,
        in_specs=(
            P(("grp", "wide"), None, None),
            P(("grp", "wide")),
            P(("grp", "wide")),
            P(),
            P("grp", None),
        ),
        out_specs=P("wide", None),
        check_vma=False,
    )
```

```python
import functools
import math

import jax
import jax.numpy as jnp
from jax import lax
from jax.experimental import pallas as pl
from jax.experimental.pallas import tpu as pltpu
from jax.sharding import PartitionSpec as P

MIB = 1024 * 1024
CODE_ROWS = 16
CODE_STEPS = 256.0
TOP = 32000.0
CHUNK = 256
UNROLL = 8
LOG2 = math.log(2.0)


def place_slots(row_ids, owner_map, out_dev):
    table_ids = jnp.arange(owner_map.shape[0], dtype=jnp.int32)
    position = jnp.sum(jnp.where(row_ids[..., None] == table_ids, owner_map, 0), axis=-1)
    target = position // out_dev
    serial = jnp.arange(row_ids.shape[-1], dtype=jnp.int32)
    earlier = (target[..., :, None] == target[..., None, :]) & (serial[:, None] > serial[None, :])
    ranking = jnp.sum(earlier.astype(jnp.int32), axis=-1)
    return (position % out_dev, target, ranking)


def add_products(summed, arrived, slot_labels, panel_tiles):
    slot_count = arrived.shape[0]
    block_rows = math.gcd(slot_count, 32)
    out_dev = summed.shape[0]
    local_ids = jnp.arange(out_dev, dtype=jnp.int32)

    def one_block(which_block, running, source_tiles, source_labels):
        part_tiles = lax.dynamic_slice_in_dim(source_tiles, which_block * block_rows, block_rows, 0)
        part_labels = lax.dynamic_slice_in_dim(
            source_labels, which_block * block_rows, block_rows, 0
        )
        chosen = jnp.take(panel_tiles, part_labels[:, 1], axis=0)
        products = jnp.einsum(
            "sab,sbc->sac", part_tiles, chosen, preferred_element_type=jnp.float32
        )
        row_hits = (part_labels[:, 0][:, None] == local_ids[None, :]).astype(jnp.float32)
        return running + jnp.einsum(
            "sr,sac->rac", row_hits, products, precision=lax.Precision.HIGHEST
        )

    return lax.fori_loop(
        0,
        slot_count // block_rows,
        lambda which_block, running: one_block(which_block, running, arrived, slot_labels),
        summed,
    )


def slots_plan(tiles, contraction, row_tile, owner_map, panel):
    wide_count = lax.axis_size("wide")
    tile_dev = tiles.shape[0]
    tile_side = tiles.shape[1]
    out_dev = owner_map.shape[0] // wide_count
    most_slots = tile_dev * 8 // (3 * wide_count)
    slot_total = wide_count * most_slots
    local_row, target, ranking = place_slots(row_tile, owner_map, out_dev)
    slot_index = target * most_slots + ranking
    outgoing = jnp.zeros((slot_total, tile_side, tile_side), tiles.dtype).at[slot_index].set(tiles)
    all_rows, all_contraction = (
        lax.all_gather(row_tile, "wide", axis=0, tiled=True),
        lax.all_gather(contraction, "wide", axis=0, tiled=True),
    )
    all_rows = all_rows.reshape(wide_count, tile_dev)
    all_contraction = all_contraction.reshape(wide_count, tile_dev)
    source_local, source_target, source_rank = place_slots(all_rows, owner_map, out_dev)
    source_ids = jnp.arange(wide_count, dtype=jnp.int32)
    mine = source_target == lax.axis_index("wide")
    arrive_index = jnp.where(mine, source_ids[:, None] * most_slots + source_rank, slot_total)
    label_pairs = jnp.stack([source_local, all_contraction], axis=-1).reshape(
        wide_count * tile_dev, 2
    )
    vacant_label = jnp.stack(
        [jnp.full((slot_total,), out_dev, jnp.int32), jnp.zeros((slot_total,), jnp.int32)], axis=1
    )
    arrived_labels = vacant_label.at[arrive_index.reshape(-1)].set(label_pairs, mode="drop")
    gathered = lax.all_gather(panel, "grp", axis=0, tiled=True)
    panel_tiles = gathered.reshape(gathered.shape[0] // tile_side, tile_side, gathered.shape[1])
    summed = jnp.zeros((out_dev, tile_side, gathered.shape[1]), jnp.float32)
    arrived = lax.all_to_all(outgoing, "wide", split_axis=0, concat_axis=0, tiled=True)
    summed = add_products(summed, arrived, arrived_labels, panel_tiles)
    summed = lax.psum(summed, "grp")
    return summed.reshape(out_dev * tile_side, gathered.shape[1])


def encode(value):
    largest = jnp.max(jnp.abs(value), axis=0, keepdims=True)
    code = jnp.ceil(jnp.log(jnp.maximum(largest, 1e-30)) * (CODE_STEPS / LOG2))
    scale = jnp.exp(code * (-LOG2 / CODE_STEPS)) * TOP
    whole = jnp.round(value * scale).astype(jnp.int32).astype(jnp.int16)
    return whole, code.astype(jnp.int32)


def put_encoded(ref, value):
    side = value.shape[0]
    whole, code = encode(value)
    ref[pl.ds(0, side), :] = whole
    ref[pl.ds(side, CODE_ROWS), :] = jnp.broadcast_to(
        code, (CODE_ROWS, code.shape[1])
    ).astype(jnp.int16)


def get_decoded(ref, side):
    code = ref[pl.ds(side, CODE_ROWS), :].astype(jnp.int32).astype(jnp.float32)[:1]
    scale = jnp.exp(code * (LOG2 / CODE_STEPS)) * (1.0 / TOP)
    return ref[pl.ds(0, side), :].astype(jnp.int32).astype(jnp.float32) * scale


def here():
    g, w = lax.axis_index("grp"), lax.axis_index("wide")
    return g % 2, g // 2, (w // 2) % 2, w // 4


def hold_kernel(
    order, own_ref, sib_ref, own_tiles, sib_tiles,
    count_ref, plane_ref, line_ref, label_ref, out, sems,
):
    tile_dev = own_tiles.shape[0]
    sums = (own_ref.shape[0] - 2 * tile_dev) // 2
    shard, out_dev = 4, 4
    x, y, z_low, _ = here()
    g, core = lax.axis_index("grp"), lax.axis_index("wide") % 2

    def copy(tiles, which, at):
        return pltpu.make_async_copy(tiles.at[which], out.at[at], sems.at[at])

    def scan(tiles, index_ref, count):
        def one(i, count):
            position = own_ref[2 * tile_dev + index_ref[i]]
            k = index_ref[tile_dev + i]
            owner, local = lax.div(position, out_dev), lax.rem(position, out_dev)
            match = lax.rem(owner, 2) == core

            @pl.when(match)
            def _():
                copy(tiles, i, count).start()
                odd, to_z = lax.rem(lax.div(owner, 2), 2), lax.div(owner, 4)
                bit_x, bit_y = lax.rem(local, 2), lax.div(local, 2)
                first = jnp.where(odd == 1, bit_y == y, bit_x == x)
                second = jnp.where(odd == 1, bit_x, bit_y)
                plane_ref[count] = (
                    jnp.where(first, 0, sums // 2) + odd * (sums // 4) + 2 * to_z + second
                )
                line_ref[count] = (
                    jnp.where(odd == z_low, 0, sums // 2) + to_z * out_dev + local
                )
                apart, inner = lax.div(k, shard) ^ g, lax.rem(k, shard)
                half = shard // 2
                crossed = jnp.where(lax.div(inner, half) == core, 0, half) + lax.rem(inner, half)
                label_ref[count] = jnp.where(apart == 0, inner, apart * shard + crossed)

            return count + match.astype(jnp.int32)

        return lax.fori_loop(0, tile_dev, one, count)

    count = scan(own_tiles, own_ref, 0)
    count = scan(sib_tiles, sib_ref, count)
    count_ref[0] = count
    for i in range(UNROLL):
        plane_ref[count + i] = sums
        line_ref[count + i] = sums
        label_ref[count + i] = 0

    @pl.loop(0, count)
    def _(i):
        copy(own_tiles, 0, i).wait()


def join_kernel(order, *refs):
    *parts, out = refs
    rows = parts[0].shape[0]
    for i, part in enumerate(parts):
        out[pl.ds(i * rows, rows), :] = part[...]


def products_kernel(
    fill, chunk, order, count_ref, slot_ref, label_ref, tiles, own_panel, *refs
):
    parts = refs[: 1 + max(which for which, _, _ in fill)]
    *sends, sums, stack = refs[len(parts) :]
    side, width = stack.shape[1:]
    for t in range(own_panel.shape[0] // side):
        stack[t] = own_panel[pl.ds(t * side, side), pl.ds(chunk * width, width)]
    for which, t, at in fill:
        stack[at] = parts[which][pl.ds(t * side, side), :]

    @pl.loop(0, sums.shape[0])
    def _(i):
        sums[i] = jnp.zeros(sums.shape[1:], jnp.float32)

    @pl.loop(0, lax.div(count_ref[0] + UNROLL - 1, UNROLL))
    def _(i):
        found = [
            jnp.dot(
                tiles[i * UNROLL + u],
                stack[label_ref[i * UNROLL + u]],
                preferred_element_type=jnp.float32,
            )
            for u in range(UNROLL)
        ]
        for u in range(UNROLL):
            sums[slot_ref[i * UNROLL + u]] += found[u]

    sent = sums.shape[0] // 2
    for send in sends:

        @pl.loop(0, send.shape[0])
        def _(i, send=send, sent=sent):
            put_encoded(send.at[i], sums[sent + i])

        sent += send.shape[0]


def plane_kernel(order, recv_a, recv_b, kept, send_a, send_b, keep):
    side, half = kept.shape[1], send_a.shape[0]
    x, y, _, _ = here()
    for base, bit, recv, send in ((0, y, recv_a, send_a), (1, x, recv_b, send_b)):

        @pl.loop(0, half)
        def _(i, base=base, bit=bit, recv=recv, send=send):
            other, mine = 2 * i + 1 - bit, 2 * i + bit
            at = base * 2 * half
            put_encoded(send.at[i], kept[at + other] + get_decoded(recv.at[other], side))
            keep[base * half + i] = kept[at + mine] + get_decoded(recv.at[mine], side)


def owner_kernel(order, recv_a, recv_b, kept, send, keep):
    side, half = kept.shape[1], send.shape[0]
    odd = here()[2]

    @pl.loop(0, half)
    def _(i):
        value_a = kept[i] + get_decoded(recv_a.at[i], side)
        value_b = kept[half + i] + get_decoded(recv_b.at[i], side)
        put_encoded(send.at[i], jnp.where(odd == 1, value_a, value_b))
        keep[i] = jnp.where(odd == 1, value_b, value_a)


def rows_kernel(order, recv, kept, send_a, send_b):
    side, half = kept.shape[1], send_a.shape[0]
    for i in range(2 * half):
        put_encoded(
            (send_a, send_b)[i // half].at[i % half], kept[i] + get_decoded(recv.at[i], side)
        )


def swap_kernel(order, own_a, own_b, recv_a, recv_b, send_a, send_b):
    side = own_a.shape[1] - CODE_ROWS
    for own, recv, send in ((own_a, recv_a, send_a), (own_b, recv_b, send_b)):
        for i in range(own.shape[0]):
            put_encoded(send.at[i], get_decoded(own.at[i], side) + get_decoded(recv.at[i], side))


def line_kernel(order, recv, kept, send, keep):
    side, half = kept.shape[1], send.shape[0]
    bit = here()[3]

    @pl.loop(0, half)
    def _(i):
        other, mine = (1 - bit) * half + i, bit * half + i
        put_encoded(send.at[i], kept[other] + get_decoded(recv.at[other], side))
        keep[i] = kept[mine] + get_decoded(recv.at[mine], side)


def finish_kernel(order, recv, kept, out):
    put_encoded(out, kept[0] + get_decoded(recv.at[0], kept.shape[1]))


def spread_kernel(chunk, order, *refs):
    blocks, (out, rows, sems) = refs[:4], refs[-3:]
    side, width = rows.shape[1:]
    x, y, _, _ = here()
    halves = len(blocks[0].shape) == 3
    copies = []
    for i in range(4):
        if halves:
            own, recv = blocks[i // 2].at[i % 2], blocks[2 + i // 2].at[i % 2]
            rows[i] = get_decoded(own, side) + get_decoded(recv, side)
            at = i * side
        else:
            rows[i] = get_decoded(blocks[i], side)
            at = pl.multiple_of(((2 * y + x) ^ i) * side, side)
        copies.append(
            pltpu.make_async_copy(
                rows.at[i], out.at[pl.ds(at, side), pl.ds(chunk * width, width)], sems.at[i]
            )
        )
        copies[-1].start()
    for copy in copies:
        copy.wait()


def in_vmem(count):
    return [pl.BlockSpec(memory_space=pltpu.VMEM)] * count


def in_smem(count):
    return [pl.BlockSpec(memory_space=pltpu.SMEM)] * count


def in_any(count):
    return [pl.BlockSpec(memory_space=pl.ANY)] * count


def shape(dims, kind):
    return jax.ShapeDtypeStruct(dims, kind)


def params(mib):
    return pltpu.CompilerParams(vmem_limit_bytes=mib * MIB)


def cost(flops, moved):
    return pl.CostEstimate(flops=flops, bytes_accessed=moved, transcendentals=0)


def sums_plan(tiles, contraction, row_tile, owner_map, panel):
    wide_count = lax.axis_size("wide")
    tile_dev, side = tiles.shape[0], tiles.shape[1]
    out_dev = owner_map.shape[0] // wide_count
    rows, columns = panel.shape
    shard = rows // side
    chunks = columns // CHUNK
    sums = owner_map.shape[0] // 2
    core = lax.axis_index("wide") % 2

    def to_core(v):
        return lax.ppermute(v, "wide", [(i, i ^ 1) for i in range(wide_count)])

    def to_grp(v, d):
        return lax.ppermute(v, "grp", [(i, i ^ d) for i in range(4)])

    def to_line(v, b):
        return lax.ppermute(v, "wide", [(i, i ^ (2 << b)) for i in range(wide_count)])


    own_index = jnp.concatenate([row_tile, contraction, owner_map])
    sib_index = to_core(own_index)
    sib_tiles = to_core(tiles)

    def own_half(source, j):
        return lax.dynamic_slice(source, (core * (rows // 2), j * CHUNK), (rows // 2, CHUNK))

    mines = [own_half(panel, j) for j in range(chunks)]
    ways = [None, (1, 2), (2, 1)]
    firsts = [None] + [to_grp(mines[j], ways[j][0]) for j in range(1, chunks)]
    mine, sib_index = lax.optimization_barrier((mines[0], sib_index))
    near = [to_grp(mine, 1), to_grp(mine, 2), to_grp(mines[0], 3)]

    half, quarter = sums // 2, sums // 4
    coded = shape((side + CODE_ROWS, CHUNK), jnp.int16)
    plain = shape((side, CHUNK), jnp.float32)

    def stack_of(count, one):
        return shape((count, *one.shape), one.dtype)

    order = jnp.zeros((1,), jnp.int32)
    last = None

    def in_order():
        return order if last is None else lax.optimization_barrier((order, last))[0]

    def call(body, name, outs, *args, smem=0, mib=16, extra=(), **more):
        nonlocal last
        done = pl.pallas_call(
            body,
            in_specs=more.pop("in_specs", in_any(1) + in_smem(smem) + in_vmem(len(args) - smem)),
            out_specs=more.pop("out_specs", in_vmem(len(outs))),
            out_shape=outs,
            scratch_shapes=list(extra),
            compiler_params=params(mib),
            cost_estimate=cost(0, sum(math.prod(a.shape) * a.dtype.itemsize for a in args)),
            name=name,
            **more,
        )(in_order(), *args)
        last = done[0]
        return done

    def places(operand, tiles_of, first):
        return [
            (operand, t, d * shard + first + i % part)
            for i, (t, d) in enumerate((t, d) for d, ts in tiles_of for t in ts)
        ]

    part = shard // 2

    def join(j):
        (joined,) = call(join_kernel, "join", [shape((3 * rows // 2, CHUNK), panel.dtype)], *near)
        tiles_of = [(d, range((d - 1) * part, d * part)) for d in (1, 2, 3)]
        fill = places(0, tiles_of, 0) + places(1, tiles_of, part)
        return fill, [joined, to_core(joined)]

    def pair(j):
        way, other = ways[j]
        (joined,) = call(
            join_kernel, "join", [shape((rows, CHUNK), panel.dtype)], mines[j], firsts[j]
        )
        second = to_grp(joined, other)
        in_first = [(way, range(part, 2 * part))]
        in_second = [(other, range(part)), (way ^ other, range(part, 2 * part))]
        fill = (
            places(0, in_first, 0)
            + places(1, in_first, part)
            + places(2, in_second, 0)
            + places(3, in_second, part)
        )
        return fill, [joined, to_core(joined), second, to_core(second)]

    def products(j, slot, sends, fill, parts):
        *sends, kept = call(
            functools.partial(products_kernel, tuple(fill), j),
            "products",
            [*sends, stack_of(sums + 1, plain)],
            counts,
            slot,
            label,
            held,
            panel,
            *parts,
            smem=3,
            extra=[pltpu.VMEM((4 * shard, side, CHUNK), panel.dtype)],
            mib=24,
        )
        return *sends, kept

    def gathered(done):
        return [done] + [to_grp(done, d) for d in (1, 2, 3)]

    def spread(j, blocks, result):
        earlier = [] if result is None else [result]
        return call(
            functools.partial(spread_kernel, j),
            "spread",
            [shape((out_dev * side, columns), jnp.float32)],
            *blocks,
            *earlier,
            in_specs=in_any(1) + in_vmem(4) + in_any(len(earlier)),
            out_specs=in_any(1),
            input_output_aliases={5: 0} if earlier else {},
            extra=[pltpu.VMEM((4, side, CHUNK), jnp.float32), pltpu.SemaphoreType.DMA((4,))],
        )[0]

    eighth = quarter // 2
    entries = shape((2 * tile_dev + UNROLL,), jnp.int32)
    counts, in_plane, in_line, label, held = call(
        hold_kernel,
        "hold",
        [shape((1,), jnp.int32)]
        + [entries] * 3
        + [pltpu.VMEM((2 * tile_dev + UNROLL, side, side), tiles.dtype)],
        own_index,
        sib_index,
        *[pltpu.with_memory_space_constraint(v, pltpu.HBM) for v in (tiles, sib_tiles)],
        in_specs=in_any(1) + in_smem(2) + in_any(2),
        out_specs=in_smem(4) + in_vmem(1),
        extra=[pltpu.SemaphoreType.DMA((2 * tile_dev,))],
        mib=8,
    )
    last = held
    pairs = {j: pair(j) for j in (1, 2)}

    send, keep_0 = products(0, in_line, [stack_of(half, coded)], *join(0))
    sent_0 = send
    sent, keep = {}, {}
    for j in (1, 2):
        send_a, send_b, keep[j] = products(j, in_plane, [stack_of(quarter, coded)] * 2, *pairs[j])
        sent[j] = send_a, send_b

    sent_0, keep_0 = call(
        line_kernel,
        "line",
        [stack_of(quarter, coded), stack_of(quarter, plain)],
        to_line(sent_0, 0),
        keep_0,
    )

    def plane(j):
        return call(
            plane_kernel,
            "plane",
            [stack_of(eighth, coded)] * 2 + [stack_of(quarter, plain)],
            to_grp(sent[j][0], 1),
            to_grp(sent[j][1], 2),
            keep[j],
        )

    def owner(j):
        return call(
            owner_kernel,
            "owner",
            [stack_of(eighth, coded), stack_of(eighth, plain)],
            to_grp(sent[j][0], 2),
            to_grp(sent[j][1], 1),
            keep[j],
        )

    *sent[1], keep[1] = plane(1)
    *sent[2], keep[2] = plane(2)
    sent[1], keep[1] = owner(1)
    sent[2], keep[2] = owner(2)
    pair_of = [stack_of(2, coded)] * 2
    own_a, own_b = call(rows_kernel, "rows", pair_of, to_line(sent_0, 1), keep_0)

    def line(j):
        return call(
            line_kernel,
            "line",
            [stack_of(1, coded), stack_of(1, plain)],
            to_line(sent[j], 0),
            keep[j],
        )

    sent[1], keep[1] = line(1)
    sent[2], keep[2] = line(2)
    own_a, own_b = call(
        swap_kernel, "swap", pair_of, own_a, own_b, to_grp(own_a, 1), to_grp(own_b, 2)
    )
    (done_1,) = call(finish_kernel, "finish", [coded], to_line(sent[1], 1), keep[1])
    (done_2,) = call(finish_kernel, "finish", [coded], to_line(sent[2], 1), keep[2])
    result = spread(0, [own_a, own_b, to_grp(own_a, 2), to_grp(own_b, 1)], None)
    result = spread(1, gathered(done_1), result)
    return spread(2, gathered(done_2), result)


def per_device(tiles, contraction, row_tile, owner_map, panel):
    dense = owner_map.shape[0] <= tiles.shape[0]
    wide_count = lax.axis_size("wide")
    fits = lax.axis_size("grp") == 4 and wide_count >= 4 and wide_count & (wide_count - 1) == 0
    out_dev = owner_map.shape[0] // wide_count
    if dense and fits and wide_count == 8 and out_dev == 4 and panel.shape[1] == 3 * CHUNK:
        return sums_plan(tiles, contraction, row_tile, owner_map, panel)
    return slots_plan(tiles, contraction, row_tile, owner_map, panel)


def solution(mesh):
    return jax.shard_map(
        per_device,
        mesh=mesh,
        in_specs=(
            P(("grp", "wide"), None, None),
            P(("grp", "wide")),
            P(("grp", "wide")),
            P(),
            P("grp", None),
        ),
        out_specs=P("wide", None),
        check_vma=False,
    )
```

```python
import functools
import math

import jax
import jax.numpy as jnp
from jax import lax
from jax.experimental import pallas as pl
from jax.experimental.pallas import tpu as pltpu
from jax.sharding import PartitionSpec as P

MIB = 1024 * 1024
CODE_ROWS = 16
CODE_STEPS = 256.0
TOP = 32000.0
CHUNK = 256
UNROLL = 8
LOG2 = math.log(2.0)


def place_slots(row_ids, owner_map, out_dev):
    table_ids = jnp.arange(owner_map.shape[0], dtype=jnp.int32)
    position = jnp.sum(jnp.where(row_ids[..., None] == table_ids, owner_map, 0), axis=-1)
    target = position // out_dev
    serial = jnp.arange(row_ids.shape[-1], dtype=jnp.int32)
    earlier = (target[..., :, None] == target[..., None, :]) & (serial[:, None] > serial[None, :])
    ranking = jnp.sum(earlier.astype(jnp.int32), axis=-1)
    return (position % out_dev, target, ranking)


def add_products(summed, arrived, slot_labels, panel_tiles):
    slot_count = arrived.shape[0]
    block_rows = math.gcd(slot_count, 32)
    out_dev = summed.shape[0]
    local_ids = jnp.arange(out_dev, dtype=jnp.int32)

    def one_block(which_block, running, source_tiles, source_labels):
        part_tiles = lax.dynamic_slice_in_dim(source_tiles, which_block * block_rows, block_rows, 0)
        part_labels = lax.dynamic_slice_in_dim(
            source_labels, which_block * block_rows, block_rows, 0
        )
        chosen = jnp.take(panel_tiles, part_labels[:, 1], axis=0)
        products = jnp.einsum(
            "sab,sbc->sac", part_tiles, chosen, preferred_element_type=jnp.float32
        )
        row_hits = (part_labels[:, 0][:, None] == local_ids[None, :]).astype(jnp.float32)
        return running + jnp.einsum(
            "sr,sac->rac", row_hits, products, precision=lax.Precision.HIGHEST
        )

    return lax.fori_loop(
        0,
        slot_count // block_rows,
        lambda which_block, running: one_block(which_block, running, arrived, slot_labels),
        summed,
    )


def slots_plan(tiles, contraction, row_tile, owner_map, panel):
    wide_count = lax.axis_size("wide")
    tile_dev = tiles.shape[0]
    tile_side = tiles.shape[1]
    out_dev = owner_map.shape[0] // wide_count
    most_slots = tile_dev * 8 // (3 * wide_count)
    slot_total = wide_count * most_slots
    local_row, target, ranking = place_slots(row_tile, owner_map, out_dev)
    slot_index = target * most_slots + ranking
    outgoing = jnp.zeros((slot_total, tile_side, tile_side), tiles.dtype).at[slot_index].set(tiles)
    all_rows, all_contraction = (
        lax.all_gather(row_tile, "wide", axis=0, tiled=True),
        lax.all_gather(contraction, "wide", axis=0, tiled=True),
    )
    all_rows = all_rows.reshape(wide_count, tile_dev)
    all_contraction = all_contraction.reshape(wide_count, tile_dev)
    source_local, source_target, source_rank = place_slots(all_rows, owner_map, out_dev)
    source_ids = jnp.arange(wide_count, dtype=jnp.int32)
    mine = source_target == lax.axis_index("wide")
    arrive_index = jnp.where(mine, source_ids[:, None] * most_slots + source_rank, slot_total)
    label_pairs = jnp.stack([source_local, all_contraction], axis=-1).reshape(
        wide_count * tile_dev, 2
    )
    vacant_label = jnp.stack(
        [jnp.full((slot_total,), out_dev, jnp.int32), jnp.zeros((slot_total,), jnp.int32)], axis=1
    )
    arrived_labels = vacant_label.at[arrive_index.reshape(-1)].set(label_pairs, mode="drop")
    gathered = lax.all_gather(panel, "grp", axis=0, tiled=True)
    panel_tiles = gathered.reshape(gathered.shape[0] // tile_side, tile_side, gathered.shape[1])
    summed = jnp.zeros((out_dev, tile_side, gathered.shape[1]), jnp.float32)
    arrived = lax.all_to_all(outgoing, "wide", split_axis=0, concat_axis=0, tiled=True)
    summed = add_products(summed, arrived, arrived_labels, panel_tiles)
    summed = lax.psum(summed, "grp")
    return summed.reshape(out_dev * tile_side, gathered.shape[1])


def encode(value):
    largest = jnp.max(jnp.abs(value), axis=0, keepdims=True)
    code = jnp.ceil(jnp.log(jnp.maximum(largest, 1e-30)) * (CODE_STEPS / LOG2))
    scale = jnp.exp(code * (-LOG2 / CODE_STEPS)) * TOP
    whole = jnp.round(value * scale).astype(jnp.int32).astype(jnp.int16)
    return whole, code.astype(jnp.int32)


def put_encoded(ref, value):
    side = value.shape[0]
    whole, code = encode(value)
    ref[pl.ds(0, side), :] = whole
    ref[pl.ds(side, CODE_ROWS), :] = jnp.broadcast_to(
        code, (CODE_ROWS, code.shape[1])
    ).astype(jnp.int16)


def get_decoded(ref, side):
    code = ref[pl.ds(side, CODE_ROWS), :].astype(jnp.int32).astype(jnp.float32)[:1]
    scale = jnp.exp(code * (LOG2 / CODE_STEPS)) * (1.0 / TOP)
    return ref[pl.ds(0, side), :].astype(jnp.int32).astype(jnp.float32) * scale


def here():
    g, w = lax.axis_index("grp"), lax.axis_index("wide")
    return g % 2, g // 2, (w // 2) % 2, w // 4


def hold_kernel(
    order, own_ref, sib_ref, own_tiles, sib_tiles,
    count_ref, plane_ref, line_ref, label_ref, out, sems,
):
    tile_dev = own_tiles.shape[0]
    sums = (own_ref.shape[0] - 2 * tile_dev) // 2
    shard, out_dev = 4, 4
    x, y, z_low, _ = here()
    g, core = lax.axis_index("grp"), lax.axis_index("wide") % 2

    def copy(tiles, which, at):
        return pltpu.make_async_copy(tiles.at[which], out.at[at], sems.at[at])

    def scan(tiles, index_ref, count):
        def one(i, count):
            position = own_ref[2 * tile_dev + index_ref[i]]
            k = index_ref[tile_dev + i]
            owner, local = lax.div(position, out_dev), lax.rem(position, out_dev)
            match = lax.rem(owner, 2) == core

            @pl.when(match)
            def _():
                copy(tiles, i, count).start()
                odd, to_z = lax.rem(lax.div(owner, 2), 2), lax.div(owner, 4)
                bit_x, bit_y = lax.rem(local, 2), lax.div(local, 2)
                first = jnp.where(odd == 1, bit_y == y, bit_x == x)
                second = jnp.where(odd == 1, bit_x, bit_y)
                plane_ref[count] = (
                    jnp.where(first, 0, sums // 2) + odd * (sums // 4) + 2 * to_z + second
                )
                line_ref[count] = (
                    jnp.where(odd == z_low, 0, sums // 2) + to_z * out_dev + local
                )
                apart, inner = lax.div(k, shard) ^ g, lax.rem(k, shard)
                half = shard // 2
                crossed = jnp.where(lax.div(inner, half) == core, 0, half) + lax.rem(inner, half)
                label_ref[count] = jnp.where(apart == 0, inner, apart * shard + crossed)

            return count + match.astype(jnp.int32)

        return lax.fori_loop(0, tile_dev, one, count)

    count = scan(own_tiles, own_ref, 0)
    count = scan(sib_tiles, sib_ref, count)
    count_ref[0] = count
    for i in range(UNROLL):
        plane_ref[count + i] = sums
        line_ref[count + i] = sums
        label_ref[count + i] = 0

    @pl.loop(0, count)
    def _(i):
        copy(own_tiles, 0, i).wait()


def join_kernel(order, *refs):
    *parts, out = refs
    rows = parts[0].shape[0]
    for i, part in enumerate(parts):
        out[pl.ds(i * rows, rows), :] = part[...]


def products_kernel(
    chunk, order, count_ref, slot_ref, label_ref, tiles, own_panel, near, far, *refs
):
    *sends, sums, stack = refs
    side, width = stack.shape[1:]
    shard = own_panel.shape[0] // side
    half = shard // 2
    for t in range(shard):
        stack[t] = own_panel[pl.ds(t * side, side), pl.ds(chunk * width, width)]
    if chunk == 0:
        for i in range(3 * half):
            at = shard + (i // half) * shard + i % half
            stack[at] = near[pl.ds(i * side, side), :]
            stack[at + half] = far[pl.ds(i * side, side), :]
    else:
        g = lax.axis_index("grp")
        columns = pl.ds((chunk - 1) * width, width)
        for d in range(1, 4):
            for t in range(half):
                rows = pl.ds(t * side, side)
                stack[d * shard + t] = near[g ^ d, rows, columns]
                stack[d * shard + half + t] = far[g ^ d, rows, columns]

    @pl.loop(0, sums.shape[0])
    def _(i):
        sums[i] = jnp.zeros(sums.shape[1:], jnp.float32)

    @pl.loop(0, lax.div(count_ref[0] + UNROLL - 1, UNROLL))
    def _(i):
        found = [
            jnp.dot(
                tiles[i * UNROLL + u],
                stack[label_ref[i * UNROLL + u]],
                preferred_element_type=jnp.float32,
            )
            for u in range(UNROLL)
        ]
        for u in range(UNROLL):
            sums[slot_ref[i * UNROLL + u]] += found[u]

    sent = sums.shape[0] // 2
    for send in sends:

        @pl.loop(0, send.shape[0])
        def _(i, send=send, sent=sent):
            put_encoded(send.at[i], sums[sent + i])

        sent += send.shape[0]


def plane_kernel(order, recv_a, recv_b, kept, send_a, send_b, keep):
    side, half = kept.shape[1], send_a.shape[0]
    x, y, _, _ = here()
    for base, bit, recv, send in ((0, y, recv_a, send_a), (1, x, recv_b, send_b)):

        @pl.loop(0, half)
        def _(i, base=base, bit=bit, recv=recv, send=send):
            other, mine = 2 * i + 1 - bit, 2 * i + bit
            at = base * 2 * half
            put_encoded(send.at[i], kept[at + other] + get_decoded(recv.at[other], side))
            keep[base * half + i] = kept[at + mine] + get_decoded(recv.at[mine], side)


def owner_kernel(order, recv_a, recv_b, kept, send, keep):
    side, half = kept.shape[1], send.shape[0]
    odd = here()[2]

    @pl.loop(0, half)
    def _(i):
        value_a = kept[i] + get_decoded(recv_a.at[i], side)
        value_b = kept[half + i] + get_decoded(recv_b.at[i], side)
        put_encoded(send.at[i], jnp.where(odd == 1, value_a, value_b))
        keep[i] = jnp.where(odd == 1, value_b, value_a)


def rows_kernel(order, recv, kept, send_a, send_b):
    side, half = kept.shape[1], send_a.shape[0]
    for i in range(2 * half):
        put_encoded(
            (send_a, send_b)[i // half].at[i % half], kept[i] + get_decoded(recv.at[i], side)
        )


def swap_kernel(order, own_a, own_b, recv_a, recv_b, send_a, send_b):
    side = own_a.shape[1] - CODE_ROWS
    for own, recv, send in ((own_a, recv_a, send_a), (own_b, recv_b, send_b)):
        for i in range(own.shape[0]):
            put_encoded(send.at[i], get_decoded(own.at[i], side) + get_decoded(recv.at[i], side))


def line_kernel(order, recv, kept, send, keep):
    side, half = kept.shape[1], send.shape[0]
    bit = here()[3]

    @pl.loop(0, half)
    def _(i):
        other, mine = (1 - bit) * half + i, bit * half + i
        put_encoded(send.at[i], kept[other] + get_decoded(recv.at[other], side))
        keep[i] = kept[mine] + get_decoded(recv.at[mine], side)


def finish_kernel(order, recv, kept, out):
    put_encoded(out, kept[0] + get_decoded(recv.at[0], kept.shape[1]))


def spread_kernel(chunk, order, *refs):
    blocks, (out, rows, sems) = refs[:4], refs[-3:]
    side, width = rows.shape[1:]
    x, y, _, _ = here()
    halves = len(blocks[0].shape) == 3
    copies = []
    for i in range(4):
        if halves:
            own, recv = blocks[i // 2].at[i % 2], blocks[2 + i // 2].at[i % 2]
            rows[i] = get_decoded(own, side) + get_decoded(recv, side)
            at = i * side
        else:
            rows[i] = get_decoded(blocks[i], side)
            at = pl.multiple_of(((2 * y + x) ^ i) * side, side)
        copies.append(
            pltpu.make_async_copy(
                rows.at[i], out.at[pl.ds(at, side), pl.ds(chunk * width, width)], sems.at[i]
            )
        )
        copies[-1].start()
    for copy in copies:
        copy.wait()


def in_vmem(count):
    return [pl.BlockSpec(memory_space=pltpu.VMEM)] * count


def in_smem(count):
    return [pl.BlockSpec(memory_space=pltpu.SMEM)] * count


def in_any(count):
    return [pl.BlockSpec(memory_space=pl.ANY)] * count


def shape(dims, kind):
    return jax.ShapeDtypeStruct(dims, kind)


def params(mib):
    return pltpu.CompilerParams(vmem_limit_bytes=mib * MIB)


def cost(flops, moved):
    return pl.CostEstimate(flops=flops, bytes_accessed=moved, transcendentals=0)


def sums_plan(tiles, contraction, row_tile, owner_map, panel):
    wide_count = lax.axis_size("wide")
    tile_dev, side = tiles.shape[0], tiles.shape[1]
    out_dev = owner_map.shape[0] // wide_count
    rows, columns = panel.shape
    shard = rows // side
    chunks = columns // CHUNK
    sums = owner_map.shape[0] // 2
    core = lax.axis_index("wide") % 2

    def to_core(v):
        return lax.ppermute(v, "wide", [(i, i ^ 1) for i in range(wide_count)])

    def to_grp(v, d):
        return lax.ppermute(v, "grp", [(i, i ^ d) for i in range(4)])

    def to_line(v, b):
        return lax.ppermute(v, "wide", [(i, i ^ (2 << b)) for i in range(wide_count)])


    own_index = jnp.concatenate([row_tile, contraction, owner_map])
    sib_index = to_core(own_index)
    sib_tiles = to_core(tiles)

    def own_half(first, count):
        return lax.dynamic_slice(
            panel, (core * (rows // 2), first * CHUNK), (rows // 2, count * CHUNK)
        )

    mine = own_half(0, 1)
    near_0 = [to_grp(mine, d) for d in (1, 2, 3)]
    near = lax.all_gather(own_half(1, chunks - 1), "grp", axis=0)

    half, quarter = sums // 2, sums // 4
    coded = shape((side + CODE_ROWS, CHUNK), jnp.int16)
    plain = shape((side, CHUNK), jnp.float32)

    def stack_of(count, one):
        return shape((count, *one.shape), one.dtype)

    order = jnp.zeros((1,), jnp.int32)
    last = None

    def in_order():
        return order if last is None else lax.optimization_barrier((order, last))[0]

    def call(body, name, outs, *args, smem=0, mib=16, extra=(), **more):
        nonlocal last
        done = pl.pallas_call(
            body,
            in_specs=more.pop("in_specs", in_any(1) + in_smem(smem) + in_vmem(len(args) - smem)),
            out_specs=more.pop("out_specs", in_vmem(len(outs))),
            out_shape=outs,
            scratch_shapes=list(extra),
            compiler_params=params(mib),
            cost_estimate=cost(0, sum(math.prod(a.shape) * a.dtype.itemsize for a in args)),
            name=name,
            **more,
        )(in_order(), *args)
        last = done[0]
        return done

    def products(j, slot, sends, *parts):
        *sends, kept = call(
            functools.partial(products_kernel, j),
            "products",
            [*sends, stack_of(sums + 1, plain)],
            counts,
            slot,
            label,
            held,
            panel,
            *parts,
            smem=3,
            extra=[pltpu.VMEM((4 * shard, side, CHUNK), panel.dtype)],
            mib=24,
        )
        return *sends, kept

    def gathered(done):
        return [done] + [to_grp(done, d) for d in (1, 2, 3)]

    def spread(j, blocks, result):
        earlier = [] if result is None else [result]
        return call(
            functools.partial(spread_kernel, j),
            "spread",
            [shape((out_dev * side, columns), jnp.float32)],
            *blocks,
            *earlier,
            in_specs=in_any(1) + in_vmem(4) + in_any(len(earlier)),
            out_specs=in_any(1),
            input_output_aliases={5: 0} if earlier else {},
            extra=[pltpu.VMEM((4, side, CHUNK), jnp.float32), pltpu.SemaphoreType.DMA((4,))],
        )[0]

    eighth = quarter // 2
    entries = shape((2 * tile_dev + UNROLL,), jnp.int32)
    counts, in_plane, in_line, label, held = call(
        hold_kernel,
        "hold",
        [shape((1,), jnp.int32)]
        + [entries] * 3
        + [pltpu.VMEM((2 * tile_dev + UNROLL, side, side), tiles.dtype)],
        own_index,
        sib_index,
        *[pltpu.with_memory_space_constraint(v, pltpu.HBM) for v in (tiles, sib_tiles)],
        in_specs=in_any(1) + in_smem(2) + in_any(2),
        out_specs=in_smem(4) + in_vmem(1),
        extra=[pltpu.SemaphoreType.DMA((2 * tile_dev,))],
        mib=8,
    )
    last = held

    (joined,) = call(join_kernel, "join", [shape((3 * rows // 2, CHUNK), panel.dtype)], *near_0)
    sent_0, keep_0 = products(0, in_line, [stack_of(half, coded)], joined, to_core(joined))
    sent, keep = {}, {}
    near = lax.optimization_barrier((near, sent_0))[0]
    far = to_core(near)
    for j in (1, 2):
        *sent[j], keep[j] = products(j, in_plane, [stack_of(quarter, coded)] * 2, near, far)

    sent_0, keep_0 = call(
        line_kernel,
        "line",
        [stack_of(quarter, coded), stack_of(quarter, plain)],
        to_line(sent_0, 0),
        keep_0,
    )

    def plane(j):
        return call(
            plane_kernel,
            "plane",
            [stack_of(eighth, coded)] * 2 + [stack_of(quarter, plain)],
            to_grp(sent[j][0], 1),
            to_grp(sent[j][1], 2),
            keep[j],
        )

    def owner(j):
        return call(
            owner_kernel,
            "owner",
            [stack_of(eighth, coded), stack_of(eighth, plain)],
            to_grp(sent[j][0], 2),
            to_grp(sent[j][1], 1),
            keep[j],
        )

    *sent[1], keep[1] = plane(1)
    *sent[2], keep[2] = plane(2)
    sent[1], keep[1] = owner(1)
    sent[2], keep[2] = owner(2)
    pair_of = [stack_of(2, coded)] * 2
    own_a, own_b = call(rows_kernel, "rows", pair_of, to_line(sent_0, 1), keep_0)

    def line(j):
        return call(
            line_kernel,
            "line",
            [stack_of(1, coded), stack_of(1, plain)],
            to_line(sent[j], 0),
            keep[j],
        )

    sent[1], keep[1] = line(1)
    sent[2], keep[2] = line(2)
    own_a, own_b = call(
        swap_kernel, "swap", pair_of, own_a, own_b, to_grp(own_a, 1), to_grp(own_b, 2)
    )
    (done_1,) = call(finish_kernel, "finish", [coded], to_line(sent[1], 1), keep[1])
    (done_2,) = call(finish_kernel, "finish", [coded], to_line(sent[2], 1), keep[2])
    result = spread(0, [own_a, own_b, to_grp(own_a, 2), to_grp(own_b, 1)], None)
    result = spread(1, gathered(done_1), result)
    return spread(2, gathered(done_2), result)


def per_device(tiles, contraction, row_tile, owner_map, panel):
    dense = owner_map.shape[0] <= tiles.shape[0]
    wide_count = lax.axis_size("wide")
    fits = lax.axis_size("grp") == 4 and wide_count >= 4 and wide_count & (wide_count - 1) == 0
    out_dev = owner_map.shape[0] // wide_count
    if dense and fits and wide_count == 8 and out_dev == 4 and panel.shape[1] == 3 * CHUNK:
        return sums_plan(tiles, contraction, row_tile, owner_map, panel)
    return slots_plan(tiles, contraction, row_tile, owner_map, panel)


def solution(mesh):
    return jax.shard_map(
        per_device,
        mesh=mesh,
        in_specs=(
            P(("grp", "wide"), None, None),
            P(("grp", "wide")),
            P(("grp", "wide")),
            P(),
            P("grp", None),
        ),
        out_specs=P("wide", None),
        check_vma=False,
    )
```

```python
import functools
import math

import jax
import jax.numpy as jnp
from jax import lax
from jax.experimental import pallas as pl
from jax.experimental.pallas import tpu as pltpu
from jax.sharding import PartitionSpec as P

MIB = 1024 * 1024
CODE_ROWS = 16
CODE_STEPS = 256.0
TOP = 32000.0
CHUNK = 256
UNROLL = 8
LOG2 = math.log(2.0)


def place_slots(row_ids, owner_map, out_dev):
    table_ids = jnp.arange(owner_map.shape[0], dtype=jnp.int32)
    position = jnp.sum(jnp.where(row_ids[..., None] == table_ids, owner_map, 0), axis=-1)
    target = position // out_dev
    serial = jnp.arange(row_ids.shape[-1], dtype=jnp.int32)
    earlier = (target[..., :, None] == target[..., None, :]) & (serial[:, None] > serial[None, :])
    ranking = jnp.sum(earlier.astype(jnp.int32), axis=-1)
    return (position % out_dev, target, ranking)


def add_products(summed, arrived, slot_labels, panel_tiles):
    slot_count = arrived.shape[0]
    block_rows = math.gcd(slot_count, 32)
    out_dev = summed.shape[0]
    local_ids = jnp.arange(out_dev, dtype=jnp.int32)

    def one_block(which_block, running, source_tiles, source_labels):
        part_tiles = lax.dynamic_slice_in_dim(source_tiles, which_block * block_rows, block_rows, 0)
        part_labels = lax.dynamic_slice_in_dim(
            source_labels, which_block * block_rows, block_rows, 0
        )
        chosen = jnp.take(panel_tiles, part_labels[:, 1], axis=0)
        products = jnp.einsum(
            "sab,sbc->sac", part_tiles, chosen, preferred_element_type=jnp.float32
        )
        row_hits = (part_labels[:, 0][:, None] == local_ids[None, :]).astype(jnp.float32)
        return running + jnp.einsum(
            "sr,sac->rac", row_hits, products, precision=lax.Precision.HIGHEST
        )

    return lax.fori_loop(
        0,
        slot_count // block_rows,
        lambda which_block, running: one_block(which_block, running, arrived, slot_labels),
        summed,
    )


def slots_plan(tiles, contraction, row_tile, owner_map, panel):
    wide_count = lax.axis_size("wide")
    tile_dev = tiles.shape[0]
    tile_side = tiles.shape[1]
    out_dev = owner_map.shape[0] // wide_count
    most_slots = tile_dev * 8 // (3 * wide_count)
    slot_total = wide_count * most_slots
    local_row, target, ranking = place_slots(row_tile, owner_map, out_dev)
    slot_index = target * most_slots + ranking
    outgoing = jnp.zeros((slot_total, tile_side, tile_side), tiles.dtype).at[slot_index].set(tiles)
    all_rows, all_contraction = (
        lax.all_gather(row_tile, "wide", axis=0, tiled=True),
        lax.all_gather(contraction, "wide", axis=0, tiled=True),
    )
    all_rows = all_rows.reshape(wide_count, tile_dev)
    all_contraction = all_contraction.reshape(wide_count, tile_dev)
    source_local, source_target, source_rank = place_slots(all_rows, owner_map, out_dev)
    source_ids = jnp.arange(wide_count, dtype=jnp.int32)
    mine = source_target == lax.axis_index("wide")
    arrive_index = jnp.where(mine, source_ids[:, None] * most_slots + source_rank, slot_total)
    label_pairs = jnp.stack([source_local, all_contraction], axis=-1).reshape(
        wide_count * tile_dev, 2
    )
    vacant_label = jnp.stack(
        [jnp.full((slot_total,), out_dev, jnp.int32), jnp.zeros((slot_total,), jnp.int32)], axis=1
    )
    arrived_labels = vacant_label.at[arrive_index.reshape(-1)].set(label_pairs, mode="drop")
    gathered = lax.all_gather(panel, "grp", axis=0, tiled=True)
    panel_tiles = gathered.reshape(gathered.shape[0] // tile_side, tile_side, gathered.shape[1])
    summed = jnp.zeros((out_dev, tile_side, gathered.shape[1]), jnp.float32)
    arrived = lax.all_to_all(outgoing, "wide", split_axis=0, concat_axis=0, tiled=True)
    summed = add_products(summed, arrived, arrived_labels, panel_tiles)
    summed = lax.psum(summed, "grp")
    return summed.reshape(out_dev * tile_side, gathered.shape[1])


def encode(value):
    largest = jnp.max(jnp.abs(value), axis=0, keepdims=True)
    code = jnp.ceil(jnp.log(jnp.maximum(largest, 1e-30)) * (CODE_STEPS / LOG2))
    scale = jnp.exp(code * (-LOG2 / CODE_STEPS)) * TOP
    whole = jnp.round(value * scale).astype(jnp.int32).astype(jnp.int16)
    return whole, code.astype(jnp.int32)


def put_encoded(ref, value):
    side = value.shape[0]
    whole, code = encode(value)
    ref[pl.ds(0, side), :] = whole
    ref[pl.ds(side, CODE_ROWS), :] = jnp.broadcast_to(
        code, (CODE_ROWS, code.shape[1])
    ).astype(jnp.int16)


def get_decoded(ref, side):
    code = ref[pl.ds(side, CODE_ROWS), :].astype(jnp.int32).astype(jnp.float32)[:1]
    scale = jnp.exp(code * (LOG2 / CODE_STEPS)) * (1.0 / TOP)
    return ref[pl.ds(0, side), :].astype(jnp.int32).astype(jnp.float32) * scale


def here():
    g, w = lax.axis_index("grp"), lax.axis_index("wide")
    return g % 2, g // 2, (w // 2) % 2, w // 4


def hold_kernel(
    order, own_ref, sib_ref, own_tiles, sib_tiles,
    count_ref, plane_ref, line_ref, label_ref, out, sems,
):
    tile_dev = own_tiles.shape[0]
    sums = (own_ref.shape[0] - 2 * tile_dev) // 2
    shard, out_dev = 4, 4
    x, y, z_low, _ = here()
    g, core = lax.axis_index("grp"), lax.axis_index("wide") % 2

    def copy(tiles, which, at):
        return pltpu.make_async_copy(tiles.at[which], out.at[at], sems.at[at])

    def scan(tiles, index_ref, count):
        def one(i, count):
            position = own_ref[2 * tile_dev + index_ref[i]]
            k = index_ref[tile_dev + i]
            owner, local = lax.div(position, out_dev), lax.rem(position, out_dev)
            match = lax.rem(owner, 2) == core

            @pl.when(match)
            def _():
                copy(tiles, i, count).start()
                odd, to_z = lax.rem(lax.div(owner, 2), 2), lax.div(owner, 4)
                bit_x, bit_y = lax.rem(local, 2), lax.div(local, 2)
                first = jnp.where(odd == 1, bit_y == y, bit_x == x)
                second = jnp.where(odd == 1, bit_x, bit_y)
                plane_ref[count] = (
                    jnp.where(first, 0, sums // 2) + odd * (sums // 4) + 2 * to_z + second
                )
                line_ref[count] = (
                    jnp.where(odd == z_low, 0, sums // 2) + to_z * out_dev + local
                )
                apart, inner = lax.div(k, shard) ^ g, lax.rem(k, shard)
                half = shard // 2
                crossed = jnp.where(lax.div(inner, half) == core, 0, half) + lax.rem(inner, half)
                label_ref[count] = jnp.where(apart == 0, inner, apart * shard + crossed)

            return count + match.astype(jnp.int32)

        return lax.fori_loop(0, tile_dev, one, count)

    count = scan(own_tiles, own_ref, 0)
    count = scan(sib_tiles, sib_ref, count)
    count_ref[0] = count
    for i in range(UNROLL):
        plane_ref[count + i] = sums
        line_ref[count + i] = sums
        label_ref[count + i] = 0

    @pl.loop(0, count)
    def _(i):
        copy(own_tiles, 0, i).wait()


def join_kernel(order, *refs):
    *parts, out = refs
    rows = parts[0].shape[0]
    for i, part in enumerate(parts):
        out[pl.ds(i * rows, rows), :] = part[...]


def products_kernel(
    fill, chunk, order, count_ref, slot_ref, label_ref, tiles, own_panel, *refs
):
    parts = refs[: 1 + max(which for which, _, _ in fill)]
    *sends, sums, stack = refs[len(parts) :]
    side, width = stack.shape[1:]
    for t in range(own_panel.shape[0] // side):
        stack[t] = own_panel[pl.ds(t * side, side), pl.ds(chunk * width, width)]
    for which, t, at in fill:
        stack[at] = parts[which][pl.ds(t * side, side), :]

    @pl.loop(0, sums.shape[0])
    def _(i):
        sums[i] = jnp.zeros(sums.shape[1:], jnp.float32)

    @pl.loop(0, lax.div(count_ref[0] + UNROLL - 1, UNROLL))
    def _(i):
        found = [
            jnp.dot(
                tiles[i * UNROLL + u],
                stack[label_ref[i * UNROLL + u]],
                preferred_element_type=jnp.float32,
            )
            for u in range(UNROLL)
        ]
        for u in range(UNROLL):
            sums[slot_ref[i * UNROLL + u]] += found[u]

    sent = sums.shape[0] // 2
    for send in sends:

        @pl.loop(0, send.shape[0])
        def _(i, send=send, sent=sent):
            put_encoded(send.at[i], sums[sent + i])

        sent += send.shape[0]


def plane_kernel(order, recv_a, recv_b, kept, send_a, send_b, keep):
    side, half = kept.shape[1], send_a.shape[0]
    x, y, _, _ = here()
    for base, bit, recv, send in ((0, y, recv_a, send_a), (1, x, recv_b, send_b)):

        @pl.loop(0, half)
        def _(i, base=base, bit=bit, recv=recv, send=send):
            other, mine = 2 * i + 1 - bit, 2 * i + bit
            at = base * 2 * half
            put_encoded(send.at[i], kept[at + other] + get_decoded(recv.at[other], side))
            keep[base * half + i] = kept[at + mine] + get_decoded(recv.at[mine], side)


def owner_kernel(order, recv_a, recv_b, kept, send, keep):
    side, half = kept.shape[1], send.shape[0]
    odd = here()[2]

    @pl.loop(0, half)
    def _(i):
        value_a = kept[i] + get_decoded(recv_a.at[i], side)
        value_b = kept[half + i] + get_decoded(recv_b.at[i], side)
        put_encoded(send.at[i], jnp.where(odd == 1, value_a, value_b))
        keep[i] = jnp.where(odd == 1, value_b, value_a)


def rows_kernel(order, recv, kept, send_a, send_b):
    side, half = kept.shape[1], send_a.shape[0]
    for i in range(2 * half):
        put_encoded(
            (send_a, send_b)[i // half].at[i % half], kept[i] + get_decoded(recv.at[i], side)
        )


def swap_kernel(order, own_a, own_b, recv_a, recv_b, send_a, send_b):
    side = own_a.shape[1] - CODE_ROWS
    for own, recv, send in ((own_a, recv_a, send_a), (own_b, recv_b, send_b)):
        for i in range(own.shape[0]):
            put_encoded(send.at[i], get_decoded(own.at[i], side) + get_decoded(recv.at[i], side))


def line_kernel(order, recv, kept, send, keep):
    side, half = kept.shape[1], send.shape[0]
    bit = here()[3]

    @pl.loop(0, half)
    def _(i):
        other, mine = (1 - bit) * half + i, bit * half + i
        put_encoded(send.at[i], kept[other] + get_decoded(recv.at[other], side))
        keep[i] = kept[mine] + get_decoded(recv.at[mine], side)


def finish_kernel(order, recv, kept, out):
    put_encoded(out, kept[0] + get_decoded(recv.at[0], kept.shape[1]))


def spread_kernel(chunk, order, *refs):
    blocks, (out, rows, sems) = refs[:4], refs[-3:]
    side, width = rows.shape[1:]
    x, y, _, _ = here()
    halves = len(blocks[0].shape) == 3
    copies = []
    for i in range(4):
        if halves:
            own, recv = blocks[i // 2].at[i % 2], blocks[2 + i // 2].at[i % 2]
            rows[i] = get_decoded(own, side) + get_decoded(recv, side)
            at = i * side
        else:
            rows[i] = get_decoded(blocks[i], side)
            at = pl.multiple_of(((2 * y + x) ^ i) * side, side)
        copies.append(
            pltpu.make_async_copy(
                rows.at[i], out.at[pl.ds(at, side), pl.ds(chunk * width, width)], sems.at[i]
            )
        )
        copies[-1].start()
    for copy in copies:
        copy.wait()


def in_vmem(count):
    return [pl.BlockSpec(memory_space=pltpu.VMEM)] * count


def in_smem(count):
    return [pl.BlockSpec(memory_space=pltpu.SMEM)] * count


def in_any(count):
    return [pl.BlockSpec(memory_space=pl.ANY)] * count


def shape(dims, kind):
    return jax.ShapeDtypeStruct(dims, kind)


def params(mib):
    return pltpu.CompilerParams(vmem_limit_bytes=mib * MIB)


def cost(flops, moved):
    return pl.CostEstimate(flops=flops, bytes_accessed=moved, transcendentals=0)


def sums_plan(tiles, contraction, row_tile, owner_map, panel):
    wide_count = lax.axis_size("wide")
    tile_dev, side = tiles.shape[0], tiles.shape[1]
    out_dev = owner_map.shape[0] // wide_count
    rows, columns = panel.shape
    shard = rows // side
    chunks = columns // CHUNK
    sums = owner_map.shape[0] // 2
    core = lax.axis_index("wide") % 2

    def to_core(v):
        return lax.ppermute(v, "wide", [(i, i ^ 1) for i in range(wide_count)])

    def to_grp(v, d):
        return lax.ppermute(v, "grp", [(i, i ^ d) for i in range(4)])

    def to_line(v, b):
        return lax.ppermute(v, "wide", [(i, i ^ (2 << b)) for i in range(wide_count)])


    own_index = jnp.concatenate([row_tile, contraction, owner_map])
    sib_index = to_core(own_index)
    sib_tiles = to_core(tiles)

    def own_half(source, j):
        return lax.dynamic_slice(source, (core * (rows // 2), j * CHUNK), (rows // 2, CHUNK))

    mines = [own_half(panel, j) for j in range(chunks)]
    ways = [None, (1, 2), (2, 1)]
    firsts = [None] + [to_grp(mines[j], ways[j][0]) for j in range(1, chunks)]
    mine, sib_index = lax.optimization_barrier((mines[0], sib_index))
    near = [to_grp(mine, 1), to_grp(mine, 2), to_grp(mines[0], 3)]

    half, quarter = sums // 2, sums // 4
    coded = shape((side + CODE_ROWS, CHUNK), jnp.int16)
    plain = shape((side, CHUNK), jnp.float32)

    def stack_of(count, one):
        return shape((count, *one.shape), one.dtype)

    order = jnp.zeros((1,), jnp.int32)
    last = None

    def in_order():
        return order if last is None else lax.optimization_barrier((order, last))[0]

    def call(body, name, outs, *args, smem=0, mib=16, extra=(), **more):
        nonlocal last
        done = pl.pallas_call(
            body,
            in_specs=more.pop("in_specs", in_any(1) + in_smem(smem) + in_vmem(len(args) - smem)),
            out_specs=more.pop("out_specs", in_vmem(len(outs))),
            out_shape=outs,
            scratch_shapes=list(extra),
            compiler_params=params(mib),
            cost_estimate=cost(0, sum(math.prod(a.shape) * a.dtype.itemsize for a in args)),
            name=name,
            **more,
        )(in_order(), *args)
        last = done[0]
        return done

    def places(operand, tiles_of, first):
        return [
            (operand, t, d * shard + first + i % part)
            for i, (t, d) in enumerate((t, d) for d, ts in tiles_of for t in ts)
        ]

    part = shard // 2

    def join(j):
        (joined,) = call(join_kernel, "join", [shape((3 * rows // 2, CHUNK), panel.dtype)], *near)
        tiles_of = [(d, range((d - 1) * part, d * part)) for d in (1, 2, 3)]
        fill = places(0, tiles_of, 0) + places(1, tiles_of, part)
        return fill, [joined, to_core(joined)]

    def pair(j):
        way, other = ways[j]
        (joined,) = call(
            join_kernel, "join", [shape((rows, CHUNK), panel.dtype)], mines[j], firsts[j]
        )
        second = to_grp(joined, other)
        in_first = [(way, range(part, 2 * part))]
        in_second = [(other, range(part)), (way ^ other, range(part, 2 * part))]
        fill = (
            places(0, in_first, 0)
            + places(1, in_first, part)
            + places(2, in_second, 0)
            + places(3, in_second, part)
        )
        return fill, [joined, to_core(joined), second, to_core(second)]

    def products(j, slot, sends, fill, parts):
        *sends, kept = call(
            functools.partial(products_kernel, tuple(fill), j),
            "products",
            [*sends, stack_of(sums + 1, plain)],
            counts,
            slot,
            label,
            held,
            panel,
            *parts,
            smem=3,
            extra=[pltpu.VMEM((4 * shard, side, CHUNK), panel.dtype)],
            mib=24,
        )
        return *sends, kept

    def gathered(done):
        return [done] + [to_grp(done, d) for d in (1, 2, 3)]

    def spread(j, blocks, result):
        earlier = [] if result is None else [result]
        return call(
            functools.partial(spread_kernel, j),
            "spread",
            [shape((out_dev * side, columns), jnp.float32)],
            *blocks,
            *earlier,
            in_specs=in_any(1) + in_vmem(4) + in_any(len(earlier)),
            out_specs=in_any(1),
            input_output_aliases={5: 0} if earlier else {},
            extra=[pltpu.VMEM((4, side, CHUNK), jnp.float32), pltpu.SemaphoreType.DMA((4,))],
        )[0]

    eighth = quarter // 2
    entries = shape((2 * tile_dev + UNROLL,), jnp.int32)
    counts, in_plane, in_line, label, held = call(
        hold_kernel,
        "hold",
        [shape((1,), jnp.int32)]
        + [entries] * 3
        + [pltpu.VMEM((2 * tile_dev + UNROLL, side, side), tiles.dtype)],
        own_index,
        sib_index,
        *[pltpu.with_memory_space_constraint(v, pltpu.HBM) for v in (tiles, sib_tiles)],
        in_specs=in_any(1) + in_smem(2) + in_any(2),
        out_specs=in_smem(4) + in_vmem(1),
        extra=[pltpu.SemaphoreType.DMA((2 * tile_dev,))],
        mib=8,
    )
    last = held
    pairs = {j: pair(j) for j in (1, 2)}

    send, keep_0 = products(0, in_line, [stack_of(half, coded)], *join(0))
    sent_0 = send
    sent, keep = {}, {}
    for j in (1, 2):
        send_a, send_b, keep[j] = products(j, in_plane, [stack_of(quarter, coded)] * 2, *pairs[j])
        sent[j] = send_a, send_b

    sent_0, keep_0 = call(
        line_kernel,
        "line",
        [stack_of(quarter, coded), stack_of(quarter, plain)],
        to_line(sent_0, 0),
        keep_0,
    )

    def plane(j):
        return call(
            plane_kernel,
            "plane",
            [stack_of(eighth, coded)] * 2 + [stack_of(quarter, plain)],
            to_grp(sent[j][0], 1),
            to_grp(sent[j][1], 2),
            keep[j],
        )

    def owner(j):
        return call(
            owner_kernel,
            "owner",
            [stack_of(eighth, coded), stack_of(eighth, plain)],
            to_grp(sent[j][0], 2),
            to_grp(sent[j][1], 1),
            keep[j],
        )

    *sent[1], keep[1] = plane(1)
    *sent[2], keep[2] = plane(2)
    sent[1], keep[1] = owner(1)
    pair_of = [stack_of(2, coded)] * 2
    own_a, own_b = call(rows_kernel, "rows", pair_of, to_line(sent_0, 1), keep_0)
    sent[2], keep[2] = owner(2)

    def line(j):
        return call(
            line_kernel,
            "line",
            [stack_of(1, coded), stack_of(1, plain)],
            to_line(sent[j], 0),
            keep[j],
        )

    def finish(j):
        return call(finish_kernel, "finish", [coded], to_line(sent[j], 1), keep[j])[0]

    sent[1], keep[1] = line(1)
    own_a, own_b = call(
        swap_kernel, "swap", pair_of, own_a, own_b, to_grp(own_a, 1), to_grp(own_b, 2)
    )
    sent[2], keep[2] = line(2)
    done_1 = finish(1)
    result = spread(0, [own_a, own_b, to_grp(own_a, 2), to_grp(own_b, 1)], None)
    done_2 = finish(2)
    result = spread(1, gathered(done_1), result)
    return spread(2, gathered(done_2), result)


def per_device(tiles, contraction, row_tile, owner_map, panel):
    dense = owner_map.shape[0] <= tiles.shape[0]
    wide_count = lax.axis_size("wide")
    fits = lax.axis_size("grp") == 4 and wide_count >= 4 and wide_count & (wide_count - 1) == 0
    out_dev = owner_map.shape[0] // wide_count
    if dense and fits and wide_count == 8 and out_dev == 4 and panel.shape[1] == 3 * CHUNK:
        return sums_plan(tiles, contraction, row_tile, owner_map, panel)
    return slots_plan(tiles, contraction, row_tile, owner_map, panel)


def solution(mesh):
    return jax.shard_map(
        per_device,
        mesh=mesh,
        in_specs=(
            P(("grp", "wide"), None, None),
            P(("grp", "wide")),
            P(("grp", "wide")),
            P(),
            P("grp", None),
        ),
        out_specs=P("wide", None),
        check_vma=False,
    )
```

```python
import functools
import math

import jax
import jax.numpy as jnp
from jax import lax
from jax.experimental import pallas as pl
from jax.experimental.pallas import tpu as pltpu
from jax.sharding import PartitionSpec as P

MIB = 1024 * 1024
CODE_ROWS = 16
CODE_STEPS = 256.0
TOP = 32000.0
CHUNK = 256
UNROLL = 8
LOG2 = math.log(2.0)


def place_slots(row_ids, owner_map, out_dev):
    table_ids = jnp.arange(owner_map.shape[0], dtype=jnp.int32)
    position = jnp.sum(jnp.where(row_ids[..., None] == table_ids, owner_map, 0), axis=-1)
    target = position // out_dev
    serial = jnp.arange(row_ids.shape[-1], dtype=jnp.int32)
    earlier = (target[..., :, None] == target[..., None, :]) & (serial[:, None] > serial[None, :])
    ranking = jnp.sum(earlier.astype(jnp.int32), axis=-1)
    return (position % out_dev, target, ranking)


def add_products(summed, arrived, slot_labels, panel_tiles):
    slot_count = arrived.shape[0]
    block_rows = math.gcd(slot_count, 32)
    out_dev = summed.shape[0]
    local_ids = jnp.arange(out_dev, dtype=jnp.int32)

    def one_block(which_block, running, source_tiles, source_labels):
        part_tiles = lax.dynamic_slice_in_dim(source_tiles, which_block * block_rows, block_rows, 0)
        part_labels = lax.dynamic_slice_in_dim(
            source_labels, which_block * block_rows, block_rows, 0
        )
        chosen = jnp.take(panel_tiles, part_labels[:, 1], axis=0)
        products = jnp.einsum(
            "sab,sbc->sac", part_tiles, chosen, preferred_element_type=jnp.float32
        )
        row_hits = (part_labels[:, 0][:, None] == local_ids[None, :]).astype(jnp.float32)
        return running + jnp.einsum(
            "sr,sac->rac", row_hits, products, precision=lax.Precision.HIGHEST
        )

    return lax.fori_loop(
        0,
        slot_count // block_rows,
        lambda which_block, running: one_block(which_block, running, arrived, slot_labels),
        summed,
    )


def slots_plan(tiles, contraction, row_tile, owner_map, panel):
    wide_count = lax.axis_size("wide")
    tile_dev = tiles.shape[0]
    tile_side = tiles.shape[1]
    out_dev = owner_map.shape[0] // wide_count
    most_slots = tile_dev * 8 // (3 * wide_count)
    slot_total = wide_count * most_slots
    local_row, target, ranking = place_slots(row_tile, owner_map, out_dev)
    slot_index = target * most_slots + ranking
    outgoing = jnp.zeros((slot_total, tile_side, tile_side), tiles.dtype).at[slot_index].set(tiles)
    all_rows, all_contraction = (
        lax.all_gather(row_tile, "wide", axis=0, tiled=True),
        lax.all_gather(contraction, "wide", axis=0, tiled=True),
    )
    all_rows = all_rows.reshape(wide_count, tile_dev)
    all_contraction = all_contraction.reshape(wide_count, tile_dev)
    source_local, source_target, source_rank = place_slots(all_rows, owner_map, out_dev)
    source_ids = jnp.arange(wide_count, dtype=jnp.int32)
    mine = source_target == lax.axis_index("wide")
    arrive_index = jnp.where(mine, source_ids[:, None] * most_slots + source_rank, slot_total)
    label_pairs = jnp.stack([source_local, all_contraction], axis=-1).reshape(
        wide_count * tile_dev, 2
    )
    vacant_label = jnp.stack(
        [jnp.full((slot_total,), out_dev, jnp.int32), jnp.zeros((slot_total,), jnp.int32)], axis=1
    )
    arrived_labels = vacant_label.at[arrive_index.reshape(-1)].set(label_pairs, mode="drop")
    gathered = lax.all_gather(panel, "grp", axis=0, tiled=True)
    panel_tiles = gathered.reshape(gathered.shape[0] // tile_side, tile_side, gathered.shape[1])
    summed = jnp.zeros((out_dev, tile_side, gathered.shape[1]), jnp.float32)
    arrived = lax.all_to_all(outgoing, "wide", split_axis=0, concat_axis=0, tiled=True)
    summed = add_products(summed, arrived, arrived_labels, panel_tiles)
    summed = lax.psum(summed, "grp")
    return summed.reshape(out_dev * tile_side, gathered.shape[1])


def encode(value):
    largest = jnp.max(jnp.abs(value), axis=0, keepdims=True)
    code = jnp.ceil(jnp.log(jnp.maximum(largest, 1e-30)) * (CODE_STEPS / LOG2))
    scale = jnp.exp(code * (-LOG2 / CODE_STEPS)) * TOP
    whole = jnp.round(value * scale).astype(jnp.int32).astype(jnp.int16)
    return whole, code.astype(jnp.int32)


def put_encoded(ref, value):
    side = value.shape[0]
    whole, code = encode(value)
    ref[pl.ds(0, side), :] = whole
    ref[pl.ds(side, CODE_ROWS), :] = jnp.broadcast_to(
        code, (CODE_ROWS, code.shape[1])
    ).astype(jnp.int16)


def get_decoded(ref, side):
    code = ref[pl.ds(side, CODE_ROWS), :].astype(jnp.int32).astype(jnp.float32)[:1]
    scale = jnp.exp(code * (LOG2 / CODE_STEPS)) * (1.0 / TOP)
    return ref[pl.ds(0, side), :].astype(jnp.int32).astype(jnp.float32) * scale


def here():
    g, w = lax.axis_index("grp"), lax.axis_index("wide")
    return g % 2, g // 2, (w // 2) % 2, w // 4


def hold_kernel(
    order, own_ref, sib_ref, own_tiles, sib_tiles,
    count_ref, plane_ref, line_ref, label_ref, out, sems,
):
    tile_dev = own_tiles.shape[0]
    sums = (own_ref.shape[0] - 2 * tile_dev) // 2
    shard, out_dev = 4, 4
    x, y, z_low, _ = here()
    g, core = lax.axis_index("grp"), lax.axis_index("wide") % 2

    def copy(tiles, which, at):
        return pltpu.make_async_copy(tiles.at[which], out.at[at], sems.at[at])

    def scan(tiles, index_ref, count):
        def one(i, count):
            position = own_ref[2 * tile_dev + index_ref[i]]
            k = index_ref[tile_dev + i]
            owner, local = lax.div(position, out_dev), lax.rem(position, out_dev)
            match = lax.rem(owner, 2) == core

            @pl.when(match)
            def _():
                copy(tiles, i, count).start()
                odd, to_z = lax.rem(lax.div(owner, 2), 2), lax.div(owner, 4)
                bit_x, bit_y = lax.rem(local, 2), lax.div(local, 2)
                first = jnp.where(odd == 1, bit_y == y, bit_x == x)
                second = jnp.where(odd == 1, bit_x, bit_y)
                plane_ref[count] = (
                    jnp.where(first, 0, sums // 2) + odd * (sums // 4) + 2 * to_z + second
                )
                line_ref[count] = (
                    jnp.where(odd == z_low, 0, sums // 2) + to_z * out_dev + local
                )
                apart, inner = lax.div(k, shard) ^ g, lax.rem(k, shard)
                half = shard // 2
                crossed = jnp.where(lax.div(inner, half) == core, 0, half) + lax.rem(inner, half)
                label_ref[count] = jnp.where(apart == 0, inner, apart * shard + crossed)

            return count + match.astype(jnp.int32)

        return lax.fori_loop(0, tile_dev, one, count)

    count = scan(own_tiles, own_ref, 0)
    count = scan(sib_tiles, sib_ref, count)
    count_ref[0] = count
    for i in range(UNROLL):
        plane_ref[count + i] = sums
        line_ref[count + i] = sums
        label_ref[count + i] = 0

    @pl.loop(0, count)
    def _(i):
        copy(own_tiles, 0, i).wait()


def join_kernel(order, *refs):
    *parts, out = refs
    rows = parts[0].shape[0]
    for i, part in enumerate(parts):
        out[pl.ds(i * rows, rows), :] = part[...]


def products_kernel(
    fill, chunk, order, count_ref, slot_ref, label_ref, tiles, own_panel, *refs
):
    parts = refs[: 1 + max(which for which, _, _ in fill)]
    *sends, sums, stack = refs[len(parts) :]
    side, width = stack.shape[1:]
    for t in range(own_panel.shape[0] // side):
        stack[t] = own_panel[pl.ds(t * side, side), pl.ds(chunk * width, width)]
    for which, t, at in fill:
        stack[at] = parts[which][pl.ds(t * side, side), :]

    @pl.loop(0, sums.shape[0])
    def _(i):
        sums[i] = jnp.zeros(sums.shape[1:], jnp.float32)

    @pl.loop(0, lax.div(count_ref[0] + UNROLL - 1, UNROLL))
    def _(i):
        found = [
            jnp.dot(
                tiles[i * UNROLL + u],
                stack[label_ref[i * UNROLL + u]],
                preferred_element_type=jnp.float32,
            )
            for u in range(UNROLL)
        ]
        for u in range(UNROLL):
            sums[slot_ref[i * UNROLL + u]] += found[u]

    sent = sums.shape[0] // 2
    for send in sends:

        @pl.loop(0, send.shape[0])
        def _(i, send=send, sent=sent):
            put_encoded(send.at[i], sums[sent + i])

        sent += send.shape[0]


def plane_kernel(order, recv_a, recv_b, kept, send_a, send_b, keep):
    side, half = kept.shape[1], send_a.shape[0]
    x, y, _, _ = here()
    for base, bit, recv, send in ((0, y, recv_a, send_a), (1, x, recv_b, send_b)):

        @pl.loop(0, half)
        def _(i, base=base, bit=bit, recv=recv, send=send):
            other, mine = 2 * i + 1 - bit, 2 * i + bit
            at = base * 2 * half
            put_encoded(send.at[i], kept[at + other] + get_decoded(recv.at[other], side))
            keep[base * half + i] = kept[at + mine] + get_decoded(recv.at[mine], side)


def owner_kernel(order, recv_a, recv_b, kept, send, keep):
    side, half = kept.shape[1], send.shape[0]
    odd = here()[2]

    @pl.loop(0, half)
    def _(i):
        value_a = kept[i] + get_decoded(recv_a.at[i], side)
        value_b = kept[half + i] + get_decoded(recv_b.at[i], side)
        put_encoded(send.at[i], jnp.where(odd == 1, value_a, value_b))
        keep[i] = jnp.where(odd == 1, value_b, value_a)


def rows_kernel(order, recv, kept, send_a, send_b):
    side, half = kept.shape[1], send_a.shape[0]
    for i in range(2 * half):
        put_encoded(
            (send_a, send_b)[i // half].at[i % half], kept[i] + get_decoded(recv.at[i], side)
        )


def swap_kernel(order, own_a, own_b, recv_a, recv_b, send_a, send_b):
    side = own_a.shape[1] - CODE_ROWS
    for own, recv, send in ((own_a, recv_a, send_a), (own_b, recv_b, send_b)):
        for i in range(own.shape[0]):
            put_encoded(send.at[i], get_decoded(own.at[i], side) + get_decoded(recv.at[i], side))


def line_kernel(order, recv, kept, send, keep):
    side, half = kept.shape[1], send.shape[0]
    bit = here()[3]

    @pl.loop(0, half)
    def _(i):
        other, mine = (1 - bit) * half + i, bit * half + i
        put_encoded(send.at[i], kept[other] + get_decoded(recv.at[other], side))
        keep[i] = kept[mine] + get_decoded(recv.at[mine], side)


def finish_kernel(order, recv, kept, out):
    put_encoded(out, kept[0] + get_decoded(recv.at[0], kept.shape[1]))


def spread_kernel(chunk, order, *refs):
    blocks, (out, rows, sems) = refs[:4], refs[-3:]
    side, width = rows.shape[1:]
    x, y, _, _ = here()
    halves = len(blocks[0].shape) == 3
    copies = []
    for i in range(4):
        if halves:
            own, recv = blocks[i // 2].at[i % 2], blocks[2 + i // 2].at[i % 2]
            rows[i] = get_decoded(own, side) + get_decoded(recv, side)
            at = i * side
        else:
            rows[i] = get_decoded(blocks[i], side)
            at = pl.multiple_of(((2 * y + x) ^ i) * side, side)
        copies.append(
            pltpu.make_async_copy(
                rows.at[i], out.at[pl.ds(at, side), pl.ds(chunk * width, width)], sems.at[i]
            )
        )
        copies[-1].start()
    for copy in copies:
        copy.wait()


def in_vmem(count):
    return [pl.BlockSpec(memory_space=pltpu.VMEM)] * count


def in_smem(count):
    return [pl.BlockSpec(memory_space=pltpu.SMEM)] * count


def in_any(count):
    return [pl.BlockSpec(memory_space=pl.ANY)] * count


def shape(dims, kind):
    return jax.ShapeDtypeStruct(dims, kind)


def params(mib):
    return pltpu.CompilerParams(vmem_limit_bytes=mib * MIB)


def cost(flops, moved):
    return pl.CostEstimate(flops=flops, bytes_accessed=moved, transcendentals=0)


def sums_plan(tiles, contraction, row_tile, owner_map, panel):
    wide_count = lax.axis_size("wide")
    tile_dev, side = tiles.shape[0], tiles.shape[1]
    out_dev = owner_map.shape[0] // wide_count
    rows, columns = panel.shape
    shard = rows // side
    chunks = columns // CHUNK
    sums = owner_map.shape[0] // 2
    core = lax.axis_index("wide") % 2

    def to_core(v):
        return lax.ppermute(v, "wide", [(i, i ^ 1) for i in range(wide_count)])

    def to_grp(v, d):
        return lax.ppermute(v, "grp", [(i, i ^ d) for i in range(4)])

    def to_line(v, b):
        return lax.ppermute(v, "wide", [(i, i ^ (2 << b)) for i in range(wide_count)])


    own_index = jnp.concatenate([row_tile, contraction, owner_map])
    sib_index = to_core(own_index)
    sib_tiles = to_core(tiles)

    def own_half(source, j):
        return lax.dynamic_slice(source, (core * (rows // 2), j * CHUNK), (rows // 2, CHUNK))

    mines = [own_half(panel, j) for j in range(chunks)]
    ways = [None, (1, 2), (2, 1)]
    firsts = [None] + [to_grp(mines[j], ways[j][0]) for j in range(1, chunks)]
    mine, sib_index = lax.optimization_barrier((mines[0], sib_index))
    near = [to_grp(mine, 1), to_grp(mine, 2), to_grp(mines[0], 3)]

    half, quarter = sums // 2, sums // 4
    coded = shape((side + CODE_ROWS, CHUNK), jnp.int16)
    plain = shape((side, CHUNK), jnp.float32)

    def stack_of(count, one):
        return shape((count, *one.shape), one.dtype)

    order = jnp.zeros((1,), jnp.int32)
    last = None

    def in_order():
        return order if last is None else lax.optimization_barrier((order, last))[0]

    def call(body, name, outs, *args, smem=0, mib=16, extra=(), **more):
        nonlocal last
        done = pl.pallas_call(
            body,
            in_specs=more.pop("in_specs", in_any(1) + in_smem(smem) + in_vmem(len(args) - smem)),
            out_specs=more.pop("out_specs", in_vmem(len(outs))),
            out_shape=outs,
            scratch_shapes=list(extra),
            compiler_params=params(mib),
            cost_estimate=cost(0, sum(math.prod(a.shape) * a.dtype.itemsize for a in args)),
            name=name,
            **more,
        )(in_order(), *args)
        last = done[0]
        return done

    def places(operand, tiles_of, first):
        return [
            (operand, t, d * shard + first + i % part)
            for i, (t, d) in enumerate((t, d) for d, ts in tiles_of for t in ts)
        ]

    part = shard // 2

    def join(j):
        (joined,) = call(join_kernel, "join", [shape((3 * rows // 2, CHUNK), panel.dtype)], *near)
        tiles_of = [(d, range((d - 1) * part, d * part)) for d in (1, 2, 3)]
        fill = places(0, tiles_of, 0) + places(1, tiles_of, part)
        return fill, [joined, to_core(joined)]

    def pair(j):
        way, other = ways[j]
        (joined,) = call(
            join_kernel, "join", [shape((rows, CHUNK), panel.dtype)], mines[j], firsts[j]
        )
        second = to_grp(joined, other)
        in_first = [(way, range(part, 2 * part))]
        in_second = [(other, range(part)), (way ^ other, range(part, 2 * part))]
        fill = (
            places(0, in_first, 0)
            + places(1, in_first, part)
            + places(2, in_second, 0)
            + places(3, in_second, part)
        )
        return fill, [joined, to_core(joined), second, to_core(second)]

    def products(j, slot, sends, fill, parts):
        *sends, kept = call(
            functools.partial(products_kernel, tuple(fill), j),
            "products",
            [*sends, stack_of(sums + 1, plain)],
            counts,
            slot,
            label,
            held,
            panel,
            *parts,
            smem=3,
            extra=[pltpu.VMEM((4 * shard, side, CHUNK), panel.dtype)],
            mib=24,
        )
        return *sends, kept

    def gathered(done):
        return [done] + [to_grp(done, d) for d in (1, 2, 3)]

    def spread(j, blocks, result):
        earlier = [] if result is None else [result]
        return call(
            functools.partial(spread_kernel, j),
            "spread",
            [shape((out_dev * side, columns), jnp.float32)],
            *blocks,
            *earlier,
            in_specs=in_any(1) + in_vmem(4) + in_any(len(earlier)),
            out_specs=in_any(1),
            input_output_aliases={5: 0} if earlier else {},
            extra=[pltpu.VMEM((4, side, CHUNK), jnp.float32), pltpu.SemaphoreType.DMA((4,))],
        )[0]

    eighth = quarter // 2
    entries = shape((2 * tile_dev + UNROLL,), jnp.int32)
    counts, in_plane, in_line, label, held = call(
        hold_kernel,
        "hold",
        [shape((1,), jnp.int32)]
        + [entries] * 3
        + [pltpu.VMEM((2 * tile_dev + UNROLL, side, side), tiles.dtype)],
        own_index,
        sib_index,
        *[pltpu.with_memory_space_constraint(v, pltpu.HBM) for v in (tiles, sib_tiles)],
        in_specs=in_any(1) + in_smem(2) + in_any(2),
        out_specs=in_smem(4) + in_vmem(1),
        extra=[pltpu.SemaphoreType.DMA((2 * tile_dev,))],
        mib=8,
    )
    last = held
    pairs = {j: pair(j) for j in (1, 2)}

    send, keep_0 = products(0, in_line, [stack_of(half, coded)], *join(0))
    sent_0 = send
    sent, keep = {}, {}
    for j in (1, 2):
        send_a, send_b, keep[j] = products(j, in_plane, [stack_of(quarter, coded)] * 2, *pairs[j])
        sent[j] = send_a, send_b

    sent_0, keep_0 = call(
        line_kernel,
        "line",
        [stack_of(quarter, coded), stack_of(quarter, plain)],
        to_line(sent_0, 0),
        keep_0,
    )

    def plane(j):
        return call(
            plane_kernel,
            "plane",
            [stack_of(eighth, coded)] * 2 + [stack_of(quarter, plain)],
            to_grp(sent[j][0], 1),
            to_grp(sent[j][1], 2),
            keep[j],
        )

    def owner(j):
        return call(
            owner_kernel,
            "owner",
            [stack_of(eighth, coded), stack_of(eighth, plain)],
            to_grp(sent[j][0], 2),
            to_grp(sent[j][1], 1),
            keep[j],
        )

    *sent[1], keep[1] = plane(1)
    *sent[2], keep[2] = plane(2)
    sent[1], keep[1] = owner(1)
    pair_of = [stack_of(2, coded)] * 2
    own_a, own_b = call(rows_kernel, "rows", pair_of, to_line(sent_0, 1), keep_0)
    sent[2], keep[2] = owner(2)

    def line(j):
        return call(
            line_kernel,
            "line",
            [stack_of(1, coded), stack_of(1, plain)],
            to_line(sent[j], 0),
            keep[j],
        )

    def finish(j):
        return call(finish_kernel, "finish", [coded], to_line(sent[j], 1), keep[j])[0]

    sent[1], keep[1] = line(1)
    own_a, own_b = call(
        swap_kernel, "swap", pair_of, own_a, own_b, to_grp(own_a, 1), to_grp(own_b, 2)
    )
    done_1 = finish(1)
    sent[2], keep[2] = line(2)
    result = spread(0, [own_a, own_b, to_grp(own_a, 2), to_grp(own_b, 1)], None)
    done_2 = finish(2)
    result = spread(1, gathered(done_1), result)
    return spread(2, gathered(done_2), result)


def per_device(tiles, contraction, row_tile, owner_map, panel):
    dense = owner_map.shape[0] <= tiles.shape[0]
    wide_count = lax.axis_size("wide")
    fits = lax.axis_size("grp") == 4 and wide_count >= 4 and wide_count & (wide_count - 1) == 0
    out_dev = owner_map.shape[0] // wide_count
    if dense and fits and wide_count == 8 and out_dev == 4 and panel.shape[1] == 3 * CHUNK:
        return sums_plan(tiles, contraction, row_tile, owner_map, panel)
    return slots_plan(tiles, contraction, row_tile, owner_map, panel)


def solution(mesh):
    return jax.shard_map(
        per_device,
        mesh=mesh,
        in_specs=(
            P(("grp", "wide"), None, None),
            P(("grp", "wide")),
            P(("grp", "wide")),
            P(),
            P("grp", None),
        ),
        out_specs=P("wide", None),
        check_vma=False,
    )
```

```python
import functools
import math

import jax
import jax.numpy as jnp
from jax import lax
from jax.experimental import pallas as pl
from jax.experimental.pallas import tpu as pltpu
from jax.sharding import PartitionSpec as P

MIB = 1024 * 1024
CODE_ROWS = 16
CODE_STEPS = 256.0
TOP = 32000.0
CHUNK = 256
UNROLL = 8
LOG2 = math.log(2.0)


def place_slots(row_ids, owner_map, out_dev):
    table_ids = jnp.arange(owner_map.shape[0], dtype=jnp.int32)
    position = jnp.sum(jnp.where(row_ids[..., None] == table_ids, owner_map, 0), axis=-1)
    target = position // out_dev
    serial = jnp.arange(row_ids.shape[-1], dtype=jnp.int32)
    earlier = (target[..., :, None] == target[..., None, :]) & (serial[:, None] > serial[None, :])
    ranking = jnp.sum(earlier.astype(jnp.int32), axis=-1)
    return (position % out_dev, target, ranking)


def add_products(summed, arrived, slot_labels, panel_tiles):
    slot_count = arrived.shape[0]
    block_rows = math.gcd(slot_count, 32)
    out_dev = summed.shape[0]
    local_ids = jnp.arange(out_dev, dtype=jnp.int32)

    def one_block(which_block, running, source_tiles, source_labels):
        part_tiles = lax.dynamic_slice_in_dim(source_tiles, which_block * block_rows, block_rows, 0)
        part_labels = lax.dynamic_slice_in_dim(
            source_labels, which_block * block_rows, block_rows, 0
        )
        chosen = jnp.take(panel_tiles, part_labels[:, 1], axis=0)
        products = jnp.einsum(
            "sab,sbc->sac", part_tiles, chosen, preferred_element_type=jnp.float32
        )
        row_hits = (part_labels[:, 0][:, None] == local_ids[None, :]).astype(jnp.float32)
        return running + jnp.einsum(
            "sr,sac->rac", row_hits, products, precision=lax.Precision.HIGHEST
        )

    return lax.fori_loop(
        0,
        slot_count // block_rows,
        lambda which_block, running: one_block(which_block, running, arrived, slot_labels),
        summed,
    )


def slots_plan(tiles, contraction, row_tile, owner_map, panel):
    wide_count = lax.axis_size("wide")
    tile_dev = tiles.shape[0]
    tile_side = tiles.shape[1]
    out_dev = owner_map.shape[0] // wide_count
    most_slots = tile_dev * 8 // (3 * wide_count)
    slot_total = wide_count * most_slots
    local_row, target, ranking = place_slots(row_tile, owner_map, out_dev)
    slot_index = target * most_slots + ranking
    outgoing = jnp.zeros((slot_total, tile_side, tile_side), tiles.dtype).at[slot_index].set(tiles)
    all_rows, all_contraction = (
        lax.all_gather(row_tile, "wide", axis=0, tiled=True),
        lax.all_gather(contraction, "wide", axis=0, tiled=True),
    )
    all_rows = all_rows.reshape(wide_count, tile_dev)
    all_contraction = all_contraction.reshape(wide_count, tile_dev)
    source_local, source_target, source_rank = place_slots(all_rows, owner_map, out_dev)
    source_ids = jnp.arange(wide_count, dtype=jnp.int32)
    mine = source_target == lax.axis_index("wide")
    arrive_index = jnp.where(mine, source_ids[:, None] * most_slots + source_rank, slot_total)
    label_pairs = jnp.stack([source_local, all_contraction], axis=-1).reshape(
        wide_count * tile_dev, 2
    )
    vacant_label = jnp.stack(
        [jnp.full((slot_total,), out_dev, jnp.int32), jnp.zeros((slot_total,), jnp.int32)], axis=1
    )
    arrived_labels = vacant_label.at[arrive_index.reshape(-1)].set(label_pairs, mode="drop")
    gathered = lax.all_gather(panel, "grp", axis=0, tiled=True)
    panel_tiles = gathered.reshape(gathered.shape[0] // tile_side, tile_side, gathered.shape[1])
    summed = jnp.zeros((out_dev, tile_side, gathered.shape[1]), jnp.float32)
    arrived = lax.all_to_all(outgoing, "wide", split_axis=0, concat_axis=0, tiled=True)
    summed = add_products(summed, arrived, arrived_labels, panel_tiles)
    summed = lax.psum(summed, "grp")
    return summed.reshape(out_dev * tile_side, gathered.shape[1])


def encode(value):
    largest = jnp.max(jnp.abs(value), axis=0, keepdims=True)
    code = jnp.ceil(jnp.log(jnp.maximum(largest, 1e-30)) * (CODE_STEPS / LOG2))
    scale = jnp.exp(code * (-LOG2 / CODE_STEPS)) * TOP
    whole = jnp.round(value * scale).astype(jnp.int32).astype(jnp.int16)
    return whole, code.astype(jnp.int32)


def put_encoded(ref, value):
    side = value.shape[0]
    whole, code = encode(value)
    ref[pl.ds(0, side), :] = whole
    ref[pl.ds(side, CODE_ROWS), :] = jnp.broadcast_to(
        code, (CODE_ROWS, code.shape[1])
    ).astype(jnp.int16)


def get_decoded(ref, side):
    code = ref[pl.ds(side, CODE_ROWS), :].astype(jnp.int32).astype(jnp.float32)[:1]
    scale = jnp.exp(code * (LOG2 / CODE_STEPS)) * (1.0 / TOP)
    return ref[pl.ds(0, side), :].astype(jnp.int32).astype(jnp.float32) * scale


def here():
    g, w = lax.axis_index("grp"), lax.axis_index("wide")
    return g % 2, g // 2, (w // 2) % 2, w // 4


def hold_kernel(
    order, own_ref, sib_ref, own_tiles, sib_tiles,
    count_ref, plane_ref, line_ref, label_ref, out, sems,
):
    tile_dev = own_tiles.shape[0]
    sums = (own_ref.shape[0] - 2 * tile_dev) // 2
    shard, out_dev = 4, 4
    x, y, z_low, _ = here()
    g, core = lax.axis_index("grp"), lax.axis_index("wide") % 2

    def copy(tiles, which, at):
        return pltpu.make_async_copy(tiles.at[which], out.at[at], sems.at[at])

    def scan(tiles, index_ref, count):
        def one(i, count):
            position = own_ref[2 * tile_dev + index_ref[i]]
            k = index_ref[tile_dev + i]
            owner, local = lax.div(position, out_dev), lax.rem(position, out_dev)
            match = lax.rem(owner, 2) == core

            @pl.when(match)
            def _():
                copy(tiles, i, count).start()
                odd, to_z = lax.rem(lax.div(owner, 2), 2), lax.div(owner, 4)
                bit_x, bit_y = lax.rem(local, 2), lax.div(local, 2)
                first = jnp.where(odd == 1, bit_y == y, bit_x == x)
                second = jnp.where(odd == 1, bit_x, bit_y)
                plane_ref[count] = (
                    jnp.where(first, 0, sums // 2) + odd * (sums // 4) + 2 * to_z + second
                )
                line_ref[count] = (
                    jnp.where(odd == z_low, 0, sums // 2) + to_z * out_dev + local
                )
                apart, inner = lax.div(k, shard) ^ g, lax.rem(k, shard)
                half = shard // 2
                crossed = jnp.where(lax.div(inner, half) == core, 0, half) + lax.rem(inner, half)
                label_ref[count] = jnp.where(apart == 0, inner, apart * shard + crossed)

            return count + match.astype(jnp.int32)

        return lax.fori_loop(0, tile_dev, one, count)

    count = scan(own_tiles, own_ref, 0)
    count = scan(sib_tiles, sib_ref, count)
    count_ref[0] = count
    for i in range(UNROLL):
        plane_ref[count + i] = sums
        line_ref[count + i] = sums
        label_ref[count + i] = 0

    @pl.loop(0, count)
    def _(i):
        copy(own_tiles, 0, i).wait()


def join_kernel(first, order, *refs):
    *parts, out = refs
    at, width = 0, out.shape[1]
    for part in parts:
        column = first if part.shape[1] > width else 0
        out[pl.ds(at, part.shape[0]), :] = part[:, pl.ds(column, width)]
        at += part.shape[0]


def forward_kernel(chunk, order, from_x, from_y, to_x, to_y):
    rows, width = to_x.shape
    if chunk == 0:
        to_x[...] = from_y[pl.ds(0, rows), pl.ds(0, width)]
        to_y[...] = from_x[pl.ds(rows, rows), pl.ds(0, width)]
    else:
        to_y[...] = from_x[:, pl.ds(width, width)]
        to_x[...] = from_y[:, pl.ds(2 * width, width)]


def products_kernel(
    places, chunk, order, count_ref, slot_ref, label_ref, tiles, own_panel, *refs
):
    near, far, *sends, sums, stack = refs
    side, width = stack.shape[1:]
    shard = own_panel.shape[0] // side
    for t in range(shard):
        stack[t] = own_panel[pl.ds(t * side, side), pl.ds(chunk * width, width)]
    for t, at in enumerate(places):
        stack[at] = near[pl.ds(t * side, side), :]
        stack[at + shard // 2] = far[pl.ds(t * side, side), :]

    @pl.loop(0, sums.shape[0])
    def _(i):
        sums[i] = jnp.zeros(sums.shape[1:], jnp.float32)

    @pl.loop(0, lax.div(count_ref[0] + UNROLL - 1, UNROLL))
    def _(i):
        found = [
            jnp.dot(
                tiles[i * UNROLL + u],
                stack[label_ref[i * UNROLL + u]],
                preferred_element_type=jnp.float32,
            )
            for u in range(UNROLL)
        ]
        for u in range(UNROLL):
            sums[slot_ref[i * UNROLL + u]] += found[u]

    sent = sums.shape[0] // 2
    for send in sends:

        @pl.loop(0, send.shape[0])
        def _(i, send=send, sent=sent):
            put_encoded(send.at[i], sums[sent + i])

        sent += send.shape[0]


def plane_kernel(order, recv_a, recv_b, kept, send_a, send_b, keep):
    side, half = kept.shape[1], send_a.shape[0]
    x, y, _, _ = here()
    for base, bit, recv, send in ((0, y, recv_a, send_a), (1, x, recv_b, send_b)):

        @pl.loop(0, half)
        def _(i, base=base, bit=bit, recv=recv, send=send):
            other, mine = 2 * i + 1 - bit, 2 * i + bit
            at = base * 2 * half
            put_encoded(send.at[i], kept[at + other] + get_decoded(recv.at[other], side))
            keep[base * half + i] = kept[at + mine] + get_decoded(recv.at[mine], side)


def owner_kernel(order, recv_a, recv_b, kept, send, keep):
    side, half = kept.shape[1], send.shape[0]
    odd = here()[2]

    @pl.loop(0, half)
    def _(i):
        value_a = kept[i] + get_decoded(recv_a.at[i], side)
        value_b = kept[half + i] + get_decoded(recv_b.at[i], side)
        put_encoded(send.at[i], jnp.where(odd == 1, value_a, value_b))
        keep[i] = jnp.where(odd == 1, value_b, value_a)


def rows_kernel(order, recv, kept, send_a, send_b):
    side, half = kept.shape[1], send_a.shape[0]
    for i in range(2 * half):
        put_encoded(
            (send_a, send_b)[i // half].at[i % half], kept[i] + get_decoded(recv.at[i], side)
        )


def swap_kernel(order, own_a, own_b, recv_a, recv_b, send_a, send_b):
    side = own_a.shape[1] - CODE_ROWS
    for own, recv, send in ((own_a, recv_a, send_a), (own_b, recv_b, send_b)):
        for i in range(own.shape[0]):
            put_encoded(send.at[i], get_decoded(own.at[i], side) + get_decoded(recv.at[i], side))


def line_kernel(order, recv, kept, send, keep):
    side, half = kept.shape[1], send.shape[0]
    bit = here()[3]

    @pl.loop(0, half)
    def _(i):
        other, mine = (1 - bit) * half + i, bit * half + i
        put_encoded(send.at[i], kept[other] + get_decoded(recv.at[other], side))
        keep[i] = kept[mine] + get_decoded(recv.at[mine], side)


def finish_kernel(order, recv, kept, out):
    put_encoded(out, kept[0] + get_decoded(recv.at[0], kept.shape[1]))


def spread_kernel(chunk, order, *refs):
    blocks, (out, rows, sems) = refs[:4], refs[-3:]
    side, width = rows.shape[1:]
    x, y, _, _ = here()
    halves = len(blocks[0].shape) == 3
    copies = []
    for i in range(4):
        if halves:
            own, recv = blocks[i // 2].at[i % 2], blocks[2 + i // 2].at[i % 2]
            rows[i] = get_decoded(own, side) + get_decoded(recv, side)
            at = i * side
        else:
            rows[i] = get_decoded(blocks[i], side)
            at = pl.multiple_of(((2 * y + x) ^ i) * side, side)
        copies.append(
            pltpu.make_async_copy(
                rows.at[i], out.at[pl.ds(at, side), pl.ds(chunk * width, width)], sems.at[i]
            )
        )
        copies[-1].start()
    for copy in copies:
        copy.wait()


def in_vmem(count):
    return [pl.BlockSpec(memory_space=pltpu.VMEM)] * count


def in_smem(count):
    return [pl.BlockSpec(memory_space=pltpu.SMEM)] * count


def in_any(count):
    return [pl.BlockSpec(memory_space=pl.ANY)] * count


def shape(dims, kind):
    return jax.ShapeDtypeStruct(dims, kind)


def params(mib):
    return pltpu.CompilerParams(vmem_limit_bytes=mib * MIB)


def cost(flops, moved):
    return pl.CostEstimate(flops=flops, bytes_accessed=moved, transcendentals=0)


def sums_plan(tiles, contraction, row_tile, owner_map, panel):
    wide_count = lax.axis_size("wide")
    tile_dev, side = tiles.shape[0], tiles.shape[1]
    out_dev = owner_map.shape[0] // wide_count
    rows, columns = panel.shape
    shard = rows // side
    chunks = columns // CHUNK
    sums = owner_map.shape[0] // 2
    core = lax.axis_index("wide") % 2

    def to_core(v):
        return lax.ppermute(v, "wide", [(i, i ^ 1) for i in range(wide_count)])

    def to_grp(v, d):
        return lax.ppermute(v, "grp", [(i, i ^ d) for i in range(4)])

    def to_line(v, b):
        return lax.ppermute(v, "wide", [(i, i ^ (2 << b)) for i in range(wide_count)])


    own_index = jnp.concatenate([row_tile, contraction, owner_map])
    sib_index = to_core(own_index)
    sib_tiles = to_core(tiles)

    mine = lax.dynamic_slice(panel, (core * (rows // 2), 0), (rows // 2, columns))
    from_x, from_y = to_grp(mine, 1), to_grp(mine, 2)

    half, quarter = sums // 2, sums // 4
    coded = shape((side + CODE_ROWS, CHUNK), jnp.int16)
    plain = shape((side, CHUNK), jnp.float32)

    def stack_of(count, one):
        return shape((count, *one.shape), one.dtype)

    order = jnp.zeros((1,), jnp.int32)
    last = None

    def in_order():
        return order if last is None else lax.optimization_barrier((order, last))[0]

    def call(body, name, outs, *args, smem=0, mib=16, extra=(), **more):
        nonlocal last
        done = pl.pallas_call(
            body,
            in_specs=more.pop("in_specs", in_any(1) + in_smem(smem) + in_vmem(len(args) - smem)),
            out_specs=more.pop("out_specs", in_vmem(len(outs))),
            out_shape=outs,
            scratch_shapes=list(extra),
            compiler_params=params(mib),
            cost_estimate=cost(0, sum(math.prod(a.shape) * a.dtype.itemsize for a in args)),
            name=name,
            **more,
        )(in_order(), *args)
        last = done[0]
        return done

    places = [d * shard + t for d in (1, 2, 3) for t in range(shard // 2)]

    def panel_of(first, *arrived):
        (joined,) = call(
            functools.partial(join_kernel, first * CHUNK),
            "join",
            [shape((3 * rows // 2, CHUNK), panel.dtype)],
            *arrived,
        )
        return places, [joined, to_core(joined)]

    def forward(chunk, count):
        to_x, to_y = call(
            functools.partial(forward_kernel, chunk),
            "forward",
            [shape((count, CHUNK), panel.dtype)] * 2,
            from_x,
            from_y,
        )
        return to_grp(to_x, 1), to_grp(to_y, 2)

    def products(j, slot, sends, places, parts):
        *sends, kept = call(
            functools.partial(products_kernel, tuple(places), j),
            "products",
            [*sends, stack_of(sums + 1, plain)],
            counts,
            slot,
            label,
            held,
            panel,
            *parts,
            smem=3,
            extra=[pltpu.VMEM((4 * shard, side, CHUNK), panel.dtype)],
            mib=24,
        )
        return *sends, kept

    def gathered(done):
        return [done] + [to_grp(done, d) for d in (1, 2, 3)]

    def spread(j, blocks, result):
        earlier = [] if result is None else [result]
        return call(
            functools.partial(spread_kernel, j),
            "spread",
            [shape((out_dev * side, columns), jnp.float32)],
            *blocks,
            *earlier,
            in_specs=in_any(1) + in_vmem(4) + in_any(len(earlier)),
            out_specs=in_any(1),
            input_output_aliases={5: 0} if earlier else {},
            extra=[pltpu.VMEM((4, side, CHUNK), jnp.float32), pltpu.SemaphoreType.DMA((4,))],
        )[0]

    eighth = quarter // 2
    entries = shape((2 * tile_dev + UNROLL,), jnp.int32)
    counts, in_plane, in_line, label, held = call(
        hold_kernel,
        "hold",
        [shape((1,), jnp.int32)]
        + [entries] * 3
        + [pltpu.VMEM((2 * tile_dev + UNROLL, side, side), tiles.dtype)],
        own_index,
        sib_index,
        *[pltpu.with_memory_space_constraint(v, pltpu.HBM) for v in (tiles, sib_tiles)],
        in_specs=in_any(1) + in_smem(2) + in_any(2),
        out_specs=in_smem(4) + in_vmem(1),
        extra=[pltpu.SemaphoreType.DMA((2 * tile_dev,))],
        mib=8,
    )
    last = held
    panels = {0: panel_of(0, from_x, from_y, *forward(0, rows // 4))}
    across_2, across_1 = forward(1, rows // 2)
    send_0, keep_0 = products(0, in_line, [stack_of(half, coded)], *panels[0])
    panels[1] = panel_of(1, from_x, from_y, across_1)
    panels[2] = panel_of(2, from_x, from_y, across_2)
    sent, keep = {}, {}
    for j in (1, 2):
        *sent[j], keep[j] = products(j, in_plane, [stack_of(quarter, coded)] * 2, *panels[j])

    sent_0, keep_0 = call(
        line_kernel,
        "line",
        [stack_of(quarter, coded), stack_of(quarter, plain)],
        to_line(send_0, 0),
        keep_0,
    )

    def plane(j):
        return call(
            plane_kernel,
            "plane",
            [stack_of(eighth, coded)] * 2 + [stack_of(quarter, plain)],
            to_grp(sent[j][0], 1),
            to_grp(sent[j][1], 2),
            keep[j],
        )

    def owner(j):
        return call(
            owner_kernel,
            "owner",
            [stack_of(eighth, coded), stack_of(eighth, plain)],
            to_grp(sent[j][0], 2),
            to_grp(sent[j][1], 1),
            keep[j],
        )

    *sent[1], keep[1] = plane(1)
    *sent[2], keep[2] = plane(2)
    sent[1], keep[1] = owner(1)
    pair_of = [stack_of(2, coded)] * 2
    own_a, own_b = call(rows_kernel, "rows", pair_of, to_line(sent_0, 1), keep_0)
    sent[2], keep[2] = owner(2)

    def line(j):
        return call(
            line_kernel,
            "line",
            [stack_of(1, coded), stack_of(1, plain)],
            to_line(sent[j], 0),
            keep[j],
        )

    def finish(j):
        return call(finish_kernel, "finish", [coded], to_line(sent[j], 1), keep[j])[0]

    sent[1], keep[1] = line(1)
    own_a, own_b = call(
        swap_kernel, "swap", pair_of, own_a, own_b, to_grp(own_a, 1), to_grp(own_b, 2)
    )
    done_1 = finish(1)
    sent[2], keep[2] = line(2)
    result = spread(0, [own_a, own_b, to_grp(own_a, 2), to_grp(own_b, 1)], None)
    done_2 = finish(2)
    result = spread(1, gathered(done_1), result)
    return spread(2, gathered(done_2), result)


def per_device(tiles, contraction, row_tile, owner_map, panel):
    dense = owner_map.shape[0] <= tiles.shape[0]
    wide_count = lax.axis_size("wide")
    fits = lax.axis_size("grp") == 4 and wide_count >= 4 and wide_count & (wide_count - 1) == 0
    out_dev = owner_map.shape[0] // wide_count
    if dense and fits and wide_count == 8 and out_dev == 4 and panel.shape[1] == 3 * CHUNK:
        return sums_plan(tiles, contraction, row_tile, owner_map, panel)
    return slots_plan(tiles, contraction, row_tile, owner_map, panel)


def solution(mesh):
    return jax.shard_map(
        per_device,
        mesh=mesh,
        in_specs=(
            P(("grp", "wide"), None, None),
            P(("grp", "wide")),
            P(("grp", "wide")),
            P(),
            P("grp", None),
        ),
        out_specs=P("wide", None),
        check_vma=False,
    )
```

```python
import functools
import math

import jax
import jax.numpy as jnp
from jax import lax
from jax.experimental import pallas as pl
from jax.experimental.pallas import tpu as pltpu
from jax.sharding import PartitionSpec as P

MIB = 1024 * 1024
CODE_ROWS = 16
CODE_STEPS = 256.0
TOP = 32000.0
CHUNK = 256
UNROLL = 8
LOG2 = math.log(2.0)


def place_slots(row_ids, owner_map, out_dev):
    table_ids = jnp.arange(owner_map.shape[0], dtype=jnp.int32)
    position = jnp.sum(jnp.where(row_ids[..., None] == table_ids, owner_map, 0), axis=-1)
    target = position // out_dev
    serial = jnp.arange(row_ids.shape[-1], dtype=jnp.int32)
    earlier = (target[..., :, None] == target[..., None, :]) & (serial[:, None] > serial[None, :])
    ranking = jnp.sum(earlier.astype(jnp.int32), axis=-1)
    return (position % out_dev, target, ranking)


def add_products(summed, arrived, slot_labels, panel_tiles):
    slot_count = arrived.shape[0]
    block_rows = math.gcd(slot_count, 32)
    out_dev = summed.shape[0]
    local_ids = jnp.arange(out_dev, dtype=jnp.int32)

    def one_block(which_block, running, source_tiles, source_labels):
        part_tiles = lax.dynamic_slice_in_dim(source_tiles, which_block * block_rows, block_rows, 0)
        part_labels = lax.dynamic_slice_in_dim(
            source_labels, which_block * block_rows, block_rows, 0
        )
        chosen = jnp.take(panel_tiles, part_labels[:, 1], axis=0)
        products = jnp.einsum(
            "sab,sbc->sac", part_tiles, chosen, preferred_element_type=jnp.float32
        )
        row_hits = (part_labels[:, 0][:, None] == local_ids[None, :]).astype(jnp.float32)
        return running + jnp.einsum(
            "sr,sac->rac", row_hits, products, precision=lax.Precision.HIGHEST
        )

    return lax.fori_loop(
        0,
        slot_count // block_rows,
        lambda which_block, running: one_block(which_block, running, arrived, slot_labels),
        summed,
    )


def slots_plan(tiles, contraction, row_tile, owner_map, panel):
    wide_count = lax.axis_size("wide")
    tile_dev = tiles.shape[0]
    tile_side = tiles.shape[1]
    out_dev = owner_map.shape[0] // wide_count
    most_slots = tile_dev * 8 // (3 * wide_count)
    slot_total = wide_count * most_slots
    local_row, target, ranking = place_slots(row_tile, owner_map, out_dev)
    slot_index = target * most_slots + ranking
    outgoing = jnp.zeros((slot_total, tile_side, tile_side), tiles.dtype).at[slot_index].set(tiles)
    all_rows, all_contraction = (
        lax.all_gather(row_tile, "wide", axis=0, tiled=True),
        lax.all_gather(contraction, "wide", axis=0, tiled=True),
    )
    all_rows = all_rows.reshape(wide_count, tile_dev)
    all_contraction = all_contraction.reshape(wide_count, tile_dev)
    source_local, source_target, source_rank = place_slots(all_rows, owner_map, out_dev)
    source_ids = jnp.arange(wide_count, dtype=jnp.int32)
    mine = source_target == lax.axis_index("wide")
    arrive_index = jnp.where(mine, source_ids[:, None] * most_slots + source_rank, slot_total)
    label_pairs = jnp.stack([source_local, all_contraction], axis=-1).reshape(
        wide_count * tile_dev, 2
    )
    vacant_label = jnp.stack(
        [jnp.full((slot_total,), out_dev, jnp.int32), jnp.zeros((slot_total,), jnp.int32)], axis=1
    )
    arrived_labels = vacant_label.at[arrive_index.reshape(-1)].set(label_pairs, mode="drop")
    gathered = lax.all_gather(panel, "grp", axis=0, tiled=True)
    panel_tiles = gathered.reshape(gathered.shape[0] // tile_side, tile_side, gathered.shape[1])
    summed = jnp.zeros((out_dev, tile_side, gathered.shape[1]), jnp.float32)
    arrived = lax.all_to_all(outgoing, "wide", split_axis=0, concat_axis=0, tiled=True)
    summed = add_products(summed, arrived, arrived_labels, panel_tiles)
    summed = lax.psum(summed, "grp")
    return summed.reshape(out_dev * tile_side, gathered.shape[1])


def encode(value):
    largest = jnp.max(jnp.abs(value), axis=0, keepdims=True)
    code = jnp.ceil(jnp.log(jnp.maximum(largest, 1e-30)) * (CODE_STEPS / LOG2))
    scale = jnp.exp(code * (-LOG2 / CODE_STEPS)) * TOP
    whole = jnp.round(value * scale).astype(jnp.int32).astype(jnp.int16)
    return whole, code.astype(jnp.int32)


def put_coded(ref, values):
    codes = []
    for value in values:
        side = value.shape[0]
        whole, code = encode(value)
        ref[pl.ds(len(codes) * side, side), :] = whole
        codes.append(code)
    end = len(codes) * side
    codes += [jnp.zeros_like(codes[0])] * (CODE_ROWS - len(codes))
    ref[pl.ds(end, CODE_ROWS), :] = jnp.concatenate(codes, axis=0).astype(jnp.int16)


class Decoded:
    def __init__(self, ref, side):
        self.ref, self.side = ref, side
        self.count = (ref.shape[0] - CODE_ROWS) // side
        code = ref[pl.ds(self.count * side, CODE_ROWS), :].astype(jnp.int32)
        self.scales = jnp.exp(code.astype(jnp.float32) * (LOG2 / CODE_STEPS)) * (1.0 / TOP)

    def tile(self, i):
        return self.part(i * self.side, self.scales[i : i + 1])

    def either(self, bit, zero, one):
        at = pl.multiple_of(jnp.where(bit == 1, one, zero) * self.side, self.side)
        scales = self.scales
        return self.part(at, jnp.where(bit == 1, scales[one : one + 1], scales[zero : zero + 1]))

    def part(self, at, scale):
        return self.ref[pl.ds(at, self.side), :].astype(jnp.int32).astype(jnp.float32) * scale


def here():
    g, w = lax.axis_index("grp"), lax.axis_index("wide")
    return g % 2, g // 2, (w // 2) % 2, w // 4


def hold_kernel(
    order, own_ref, sib_ref, own_tiles, sib_tiles,
    count_ref, plane_ref, line_ref, label_ref, out, sems,
):
    tile_dev = own_tiles.shape[0]
    sums = (own_ref.shape[0] - 2 * tile_dev) // 2
    shard, out_dev = 4, 4
    x, y, z_low, _ = here()
    g, core = lax.axis_index("grp"), lax.axis_index("wide") % 2

    def copy(tiles, which, at):
        return pltpu.make_async_copy(tiles.at[which], out.at[at], sems.at[at])

    def scan(tiles, index_ref, count):
        def one(i, count):
            position = own_ref[2 * tile_dev + index_ref[i]]
            k = index_ref[tile_dev + i]
            owner, local = lax.div(position, out_dev), lax.rem(position, out_dev)
            match = lax.rem(owner, 2) == core

            @pl.when(match)
            def _():
                copy(tiles, i, count).start()
                odd, to_z = lax.rem(lax.div(owner, 2), 2), lax.div(owner, 4)
                bit_x, bit_y = lax.rem(local, 2), lax.div(local, 2)
                first = jnp.where(odd == 1, bit_y == y, bit_x == x)
                second = jnp.where(odd == 1, bit_x, bit_y)
                plane_ref[count] = (
                    jnp.where(first, 0, sums // 2) + odd * (sums // 4) + 2 * to_z + second
                )
                line_ref[count] = (
                    jnp.where(odd == z_low, 0, sums // 2) + to_z * out_dev + local
                )
                apart, inner = lax.div(k, shard) ^ g, lax.rem(k, shard)
                half = shard // 2
                crossed = jnp.where(lax.div(inner, half) == core, 0, half) + lax.rem(inner, half)
                label_ref[count] = jnp.where(apart == 0, inner, apart * shard + crossed)

            return count + match.astype(jnp.int32)

        return lax.fori_loop(0, tile_dev, one, count)

    count = scan(own_tiles, own_ref, 0)
    count = scan(sib_tiles, sib_ref, count)
    count_ref[0] = count
    for i in range(UNROLL):
        plane_ref[count + i] = sums
        line_ref[count + i] = sums
        label_ref[count + i] = 0

    @pl.loop(0, count)
    def _(i):
        copy(own_tiles, 0, i).wait()


def join_kernel(order, *refs):
    *parts, out = refs
    rows = parts[0].shape[0]
    for i, part in enumerate(parts):
        out[pl.ds(i * rows, rows), :] = part[...]


def products_kernel(
    fill, chunk, order, count_ref, slot_ref, label_ref, tiles, own_panel, *refs
):
    parts = refs[: 1 + max(which for which, _, _ in fill)]
    *sends, sums, stack = refs[len(parts) :]
    side, width = stack.shape[1:]
    for t in range(own_panel.shape[0] // side):
        stack[t] = own_panel[pl.ds(t * side, side), pl.ds(chunk * width, width)]
    for which, t, at in fill:
        stack[at] = parts[which][pl.ds(t * side, side), :]

    @pl.loop(0, sums.shape[0])
    def _(i):
        sums[i] = jnp.zeros(sums.shape[1:], jnp.float32)

    @pl.loop(0, lax.div(count_ref[0] + UNROLL - 1, UNROLL))
    def _(i):
        found = [
            jnp.dot(
                tiles[i * UNROLL + u],
                stack[label_ref[i * UNROLL + u]],
                preferred_element_type=jnp.float32,
            )
            for u in range(UNROLL)
        ]
        for u in range(UNROLL):
            sums[slot_ref[i * UNROLL + u]] += found[u]

    sent = sums.shape[0] // 2
    for send in sends:
        count = (send.shape[0] - CODE_ROWS) // side
        put_coded(send, (sums[sent + i] for i in range(count)))
        sent += count


def plane_kernel(order, recv_a, recv_b, kept, send_a, send_b, keep):
    side, half = kept.shape[1], keep.shape[0] // 2
    x, y, _, _ = here()
    for base, bit, recv, send in ((0, y, recv_a, send_a), (1, x, recv_b, send_b)):
        came = Decoded(recv, side)

        def total(i, which, base=base, came=came):
            return kept[2 * half * base + 2 * i + which] + came.either(which, 2 * i, 2 * i + 1)

        put_coded(send, (total(i, 1 - bit) for i in range(half)))
        for i in range(half):
            keep[base * half + i] = total(i, bit)


def owner_kernel(order, recv_a, recv_b, kept, send, keep):
    side, half = kept.shape[1], keep.shape[0]
    odd = here()[2]
    came_a, came_b = Decoded(recv_a, side), Decoded(recv_b, side)

    def to_send():
        for i in range(half):
            value_a = kept[i] + came_a.tile(i)
            value_b = kept[half + i] + came_b.tile(i)
            keep[i] = jnp.where(odd == 1, value_b, value_a)
            yield jnp.where(odd == 1, value_a, value_b)

    put_coded(send, to_send())


def line_kernel(order, recv, kept, send, keep):
    side, half = kept.shape[1], keep.shape[0]
    bit = here()[3]
    came = Decoded(recv, side)

    def total(i, which):
        return kept[which * half + i] + came.either(which, i, half + i)

    put_coded(send, (total(i, 1 - bit) for i in range(half)))
    for i in range(half):
        keep[i] = total(i, bit)


def rows_kernel(order, recv, kept, send_a, send_b):
    came = Decoded(recv, kept.shape[1])
    half = came.count // 2
    put_coded(send_a, (kept[i] + came.tile(i) for i in range(half)))
    put_coded(send_b, (kept[half + i] + came.tile(half + i) for i in range(half)))


def swap_kernel(order, own_a, own_b, recv_a, recv_b, send_a, send_b):
    side = (own_a.shape[0] - CODE_ROWS) // 2
    for own, recv, send in ((own_a, recv_a, send_a), (own_b, recv_b, send_b)):
        here_, there = Decoded(own, side), Decoded(recv, side)
        put_coded(send, (here_.tile(i) + there.tile(i) for i in range(2)))


def finish_kernel(order, recv, kept, out):
    put_coded(out, [kept[0] + Decoded(recv, kept.shape[1]).tile(0)])


def spread_kernel(chunk, order, *refs):
    blocks, (out, rows, sems) = refs[:4], refs[-3:]
    side, width = rows.shape[1:]
    x, y, _, _ = here()
    blocks = [Decoded(block, side) for block in blocks]
    copies = []
    for i in range(4):
        if blocks[0].count == 2:
            rows[i] = blocks[i // 2].tile(i % 2) + blocks[2 + i // 2].tile(i % 2)
            at = i * side
        else:
            rows[i] = blocks[i].tile(0)
            at = pl.multiple_of(((2 * y + x) ^ i) * side, side)
        copies.append(
            pltpu.make_async_copy(
                rows.at[i], out.at[pl.ds(at, side), pl.ds(chunk * width, width)], sems.at[i]
            )
        )
        copies[-1].start()
    for copy in copies:
        copy.wait()


def in_vmem(count):
    return [pl.BlockSpec(memory_space=pltpu.VMEM)] * count


def in_smem(count):
    return [pl.BlockSpec(memory_space=pltpu.SMEM)] * count


def in_any(count):
    return [pl.BlockSpec(memory_space=pl.ANY)] * count


def shape(dims, kind):
    return jax.ShapeDtypeStruct(dims, kind)


def params(mib):
    return pltpu.CompilerParams(vmem_limit_bytes=mib * MIB)


def cost(flops, moved):
    return pl.CostEstimate(flops=flops, bytes_accessed=moved, transcendentals=0)


def sums_plan(tiles, contraction, row_tile, owner_map, panel):
    wide_count = lax.axis_size("wide")
    tile_dev, side = tiles.shape[0], tiles.shape[1]
    out_dev = owner_map.shape[0] // wide_count
    rows, columns = panel.shape
    shard = rows // side
    chunks = columns // CHUNK
    sums = owner_map.shape[0] // 2
    core = lax.axis_index("wide") % 2

    def to_core(v):
        return lax.ppermute(v, "wide", [(i, i ^ 1) for i in range(wide_count)])

    def to_grp(v, d):
        return lax.ppermute(v, "grp", [(i, i ^ d) for i in range(4)])

    def to_line(v, b):
        return lax.ppermute(v, "wide", [(i, i ^ (2 << b)) for i in range(wide_count)])


    own_index = jnp.concatenate([row_tile, contraction, owner_map])
    sib_index = to_core(own_index)
    sib_tiles = to_core(tiles)

    def own_half(source, j):
        return lax.dynamic_slice(source, (core * (rows // 2), j * CHUNK), (rows // 2, CHUNK))

    mines = [own_half(panel, j) for j in range(chunks)]
    ways = [None, (1, 2), (2, 1)]
    firsts = [None] + [to_grp(mines[j], ways[j][0]) for j in range(1, chunks)]
    mine, sib_index = lax.optimization_barrier((mines[0], sib_index))
    near = [to_grp(mine, 1), to_grp(mine, 2), to_grp(mines[0], 3)]

    half, quarter = sums // 2, sums // 4
    plain = shape((side, CHUNK), jnp.float32)

    def stack_of(count, one):
        return shape((count, *one.shape), one.dtype)

    def coded(count):
        return shape((count * side + CODE_ROWS, CHUNK), jnp.int16)

    order = jnp.zeros((1,), jnp.int32)
    last = None

    def in_order():
        return order if last is None else lax.optimization_barrier((order, last))[0]

    def call(body, name, outs, *args, smem=0, mib=16, extra=(), **more):
        nonlocal last
        done = pl.pallas_call(
            body,
            in_specs=more.pop("in_specs", in_any(1) + in_smem(smem) + in_vmem(len(args) - smem)),
            out_specs=more.pop("out_specs", in_vmem(len(outs))),
            out_shape=outs,
            scratch_shapes=list(extra),
            compiler_params=params(mib),
            cost_estimate=cost(0, sum(math.prod(a.shape) * a.dtype.itemsize for a in args)),
            name=name,
            **more,
        )(in_order(), *args)
        last = done[0]
        return done

    def places(operand, tiles_of, first):
        return [
            (operand, t, d * shard + first + i % part)
            for i, (t, d) in enumerate((t, d) for d, ts in tiles_of for t in ts)
        ]

    part = shard // 2

    def join(j):
        (joined,) = call(join_kernel, "join", [shape((3 * rows // 2, CHUNK), panel.dtype)], *near)
        tiles_of = [(d, range((d - 1) * part, d * part)) for d in (1, 2, 3)]
        fill = places(0, tiles_of, 0) + places(1, tiles_of, part)
        return fill, [joined, to_core(joined)]

    def pair(j):
        way, other = ways[j]
        (joined,) = call(
            join_kernel, "join", [shape((rows, CHUNK), panel.dtype)], mines[j], firsts[j]
        )
        second = to_grp(joined, other)
        in_first = [(way, range(part, 2 * part))]
        in_second = [(other, range(part)), (way ^ other, range(part, 2 * part))]
        fill = (
            places(0, in_first, 0)
            + places(1, in_first, part)
            + places(2, in_second, 0)
            + places(3, in_second, part)
        )
        return fill, [joined, to_core(joined), second, to_core(second)]

    def products(j, slot, sends, fill, parts):
        *sends, kept = call(
            functools.partial(products_kernel, tuple(fill), j),
            "products",
            [*sends, stack_of(sums + 1, plain)],
            counts,
            slot,
            label,
            held,
            panel,
            *parts,
            smem=3,
            extra=[pltpu.VMEM((4 * shard, side, CHUNK), panel.dtype)],
            mib=24,
        )
        return *sends, kept

    def gathered(done):
        return [done] + [to_grp(done, d) for d in (1, 2, 3)]

    def spread(j, blocks, result):
        earlier = [] if result is None else [result]
        return call(
            functools.partial(spread_kernel, j),
            "spread",
            [shape((out_dev * side, columns), jnp.float32)],
            *blocks,
            *earlier,
            in_specs=in_any(1) + in_vmem(4) + in_any(len(earlier)),
            out_specs=in_any(1),
            input_output_aliases={5: 0} if earlier else {},
            extra=[pltpu.VMEM((4, side, CHUNK), jnp.float32), pltpu.SemaphoreType.DMA((4,))],
        )[0]

    eighth = quarter // 2
    entries = shape((2 * tile_dev + UNROLL,), jnp.int32)
    counts, in_plane, in_line, label, held = call(
        hold_kernel,
        "hold",
        [shape((1,), jnp.int32)]
        + [entries] * 3
        + [pltpu.VMEM((2 * tile_dev + UNROLL, side, side), tiles.dtype)],
        own_index,
        sib_index,
        *[pltpu.with_memory_space_constraint(v, pltpu.HBM) for v in (tiles, sib_tiles)],
        in_specs=in_any(1) + in_smem(2) + in_any(2),
        out_specs=in_smem(4) + in_vmem(1),
        extra=[pltpu.SemaphoreType.DMA((2 * tile_dev,))],
        mib=8,
    )
    last = held
    pairs = {j: pair(j) for j in (1, 2)}

    send, keep_0 = products(0, in_line, [coded(half)], *join(0))
    sent_0 = send
    sent, keep = {}, {}
    for j in (1, 2):
        send_a, send_b, keep[j] = products(j, in_plane, [coded(quarter)] * 2, *pairs[j])
        sent[j] = send_a, send_b

    sent_0, keep_0 = call(
        line_kernel,
        "line",
        [coded(quarter), stack_of(quarter, plain)],
        to_line(sent_0, 0),
        keep_0,
    )

    def plane(j):
        return call(
            plane_kernel,
            "plane",
            [coded(eighth)] * 2 + [stack_of(quarter, plain)],
            to_grp(sent[j][0], 1),
            to_grp(sent[j][1], 2),
            keep[j],
        )

    def owner(j):
        return call(
            owner_kernel,
            "owner",
            [coded(eighth), stack_of(eighth, plain)],
            to_grp(sent[j][0], 2),
            to_grp(sent[j][1], 1),
            keep[j],
        )

    *sent[1], keep[1] = plane(1)
    *sent[2], keep[2] = plane(2)
    sent[1], keep[1] = owner(1)
    pair_of = [coded(2)] * 2
    own_a, own_b = call(rows_kernel, "rows", pair_of, to_line(sent_0, 1), keep_0)
    sent[2], keep[2] = owner(2)

    def line(j):
        return call(
            line_kernel,
            "line",
            [coded(1), stack_of(1, plain)],
            to_line(sent[j], 0),
            keep[j],
        )

    def finish(j):
        return call(finish_kernel, "finish", [coded(1)], to_line(sent[j], 1), keep[j])[0]

    sent[1], keep[1] = line(1)
    own_a, own_b = call(
        swap_kernel, "swap", pair_of, own_a, own_b, to_grp(own_a, 1), to_grp(own_b, 2)
    )
    done_1 = finish(1)
    sent[2], keep[2] = line(2)
    result = spread(0, [own_a, own_b, to_grp(own_a, 2), to_grp(own_b, 1)], None)
    done_2 = finish(2)
    result = spread(1, gathered(done_1), result)
    return spread(2, gathered(done_2), result)


def per_device(tiles, contraction, row_tile, owner_map, panel):
    dense = owner_map.shape[0] <= tiles.shape[0]
    wide_count = lax.axis_size("wide")
    fits = lax.axis_size("grp") == 4 and wide_count >= 4 and wide_count & (wide_count - 1) == 0
    out_dev = owner_map.shape[0] // wide_count
    if dense and fits and wide_count == 8 and out_dev == 4 and panel.shape[1] == 3 * CHUNK:
        return sums_plan(tiles, contraction, row_tile, owner_map, panel)
    return slots_plan(tiles, contraction, row_tile, owner_map, panel)


def solution(mesh):
    return jax.shard_map(
        per_device,
        mesh=mesh,
        in_specs=(
            P(("grp", "wide"), None, None),
            P(("grp", "wide")),
            P(("grp", "wide")),
            P(),
            P("grp", None),
        ),
        out_specs=P("wide", None),
        check_vma=False,
    )
```

```python
import functools
import math

import jax
import jax.numpy as jnp
from jax import lax
from jax.experimental import pallas as pl
from jax.experimental.pallas import tpu as pltpu
from jax.sharding import PartitionSpec as P

MIB = 1024 * 1024
CODE_ROWS = 16
CODE_STEPS = 256.0
TOP = 32000.0
CHUNK = 256
UNROLL = 8
LOG2 = math.log(2.0)


def place_slots(row_ids, owner_map, out_dev):
    table_ids = jnp.arange(owner_map.shape[0], dtype=jnp.int32)
    position = jnp.sum(jnp.where(row_ids[..., None] == table_ids, owner_map, 0), axis=-1)
    target = position // out_dev
    serial = jnp.arange(row_ids.shape[-1], dtype=jnp.int32)
    earlier = (target[..., :, None] == target[..., None, :]) & (serial[:, None] > serial[None, :])
    ranking = jnp.sum(earlier.astype(jnp.int32), axis=-1)
    return (position % out_dev, target, ranking)


def add_products(summed, arrived, slot_labels, panel_tiles):
    slot_count = arrived.shape[0]
    block_rows = math.gcd(slot_count, 32)
    out_dev = summed.shape[0]
    local_ids = jnp.arange(out_dev, dtype=jnp.int32)

    def one_block(which_block, running, source_tiles, source_labels):
        part_tiles = lax.dynamic_slice_in_dim(source_tiles, which_block * block_rows, block_rows, 0)
        part_labels = lax.dynamic_slice_in_dim(
            source_labels, which_block * block_rows, block_rows, 0
        )
        chosen = jnp.take(panel_tiles, part_labels[:, 1], axis=0)
        products = jnp.einsum(
            "sab,sbc->sac", part_tiles, chosen, preferred_element_type=jnp.float32
        )
        row_hits = (part_labels[:, 0][:, None] == local_ids[None, :]).astype(jnp.float32)
        return running + jnp.einsum(
            "sr,sac->rac", row_hits, products, precision=lax.Precision.HIGHEST
        )

    return lax.fori_loop(
        0,
        slot_count // block_rows,
        lambda which_block, running: one_block(which_block, running, arrived, slot_labels),
        summed,
    )


def slots_plan(tiles, contraction, row_tile, owner_map, panel):
    wide_count = lax.axis_size("wide")
    tile_dev = tiles.shape[0]
    tile_side = tiles.shape[1]
    out_dev = owner_map.shape[0] // wide_count
    most_slots = tile_dev * 8 // (3 * wide_count)
    slot_total = wide_count * most_slots
    local_row, target, ranking = place_slots(row_tile, owner_map, out_dev)
    slot_index = target * most_slots + ranking
    outgoing = jnp.zeros((slot_total, tile_side, tile_side), tiles.dtype).at[slot_index].set(tiles)
    all_rows, all_contraction = (
        lax.all_gather(row_tile, "wide", axis=0, tiled=True),
        lax.all_gather(contraction, "wide", axis=0, tiled=True),
    )
    all_rows = all_rows.reshape(wide_count, tile_dev)
    all_contraction = all_contraction.reshape(wide_count, tile_dev)
    source_local, source_target, source_rank = place_slots(all_rows, owner_map, out_dev)
    source_ids = jnp.arange(wide_count, dtype=jnp.int32)
    mine = source_target == lax.axis_index("wide")
    arrive_index = jnp.where(mine, source_ids[:, None] * most_slots + source_rank, slot_total)
    label_pairs = jnp.stack([source_local, all_contraction], axis=-1).reshape(
        wide_count * tile_dev, 2
    )
    vacant_label = jnp.stack(
        [jnp.full((slot_total,), out_dev, jnp.int32), jnp.zeros((slot_total,), jnp.int32)], axis=1
    )
    arrived_labels = vacant_label.at[arrive_index.reshape(-1)].set(label_pairs, mode="drop")
    gathered = lax.all_gather(panel, "grp", axis=0, tiled=True)
    panel_tiles = gathered.reshape(gathered.shape[0] // tile_side, tile_side, gathered.shape[1])
    summed = jnp.zeros((out_dev, tile_side, gathered.shape[1]), jnp.float32)
    arrived = lax.all_to_all(outgoing, "wide", split_axis=0, concat_axis=0, tiled=True)
    summed = add_products(summed, arrived, arrived_labels, panel_tiles)
    summed = lax.psum(summed, "grp")
    return summed.reshape(out_dev * tile_side, gathered.shape[1])


def encode(value):
    largest = jnp.max(jnp.abs(value), axis=0, keepdims=True)
    code = jnp.ceil(jnp.log(jnp.maximum(largest, 1e-30)) * (CODE_STEPS / LOG2))
    scale = jnp.exp(code * (-LOG2 / CODE_STEPS)) * TOP
    whole = jnp.round(value * scale).astype(jnp.int32).astype(jnp.int16)
    return whole, code.astype(jnp.int32)


def put_coded(ref, values):
    codes = []
    for value in values:
        side = value.shape[0]
        whole, code = encode(value)
        ref[pl.ds(len(codes) * side, side), :] = whole
        codes.append(code)
    end = len(codes) * side
    codes += [jnp.zeros_like(codes[0])] * (CODE_ROWS - len(codes))
    ref[pl.ds(end, CODE_ROWS), :] = jnp.concatenate(codes, axis=0).astype(jnp.int16)


class Decoded:
    def __init__(self, ref, side):
        self.ref, self.side = ref, side
        self.count = (ref.shape[0] - CODE_ROWS) // side
        code = ref[pl.ds(self.count * side, CODE_ROWS), :].astype(jnp.int32)
        self.scales = jnp.exp(code.astype(jnp.float32) * (LOG2 / CODE_STEPS)) * (1.0 / TOP)

    def tile(self, i):
        return self.part(i * self.side, self.scales[i : i + 1])

    def either(self, bit, zero, one):
        at = pl.multiple_of(jnp.where(bit == 1, one, zero) * self.side, self.side)
        scales = self.scales
        return self.part(at, jnp.where(bit == 1, scales[one : one + 1], scales[zero : zero + 1]))

    def part(self, at, scale):
        return self.ref[pl.ds(at, self.side), :].astype(jnp.int32).astype(jnp.float32) * scale


def here():
    g, w = lax.axis_index("grp"), lax.axis_index("wide")
    return g % 2, g // 2, (w // 2) % 2, w // 4


def hold_kernel(
    order, own_ref, sib_ref, own_tiles, sib_tiles,
    count_ref, plane_ref, line_ref, label_ref, out, sems,
):
    tile_dev = own_tiles.shape[0]
    sums = (own_ref.shape[0] - 2 * tile_dev) // 2
    shard, out_dev = 4, 4
    x, y, z_low, _ = here()
    g, core = lax.axis_index("grp"), lax.axis_index("wide") % 2

    def copy(tiles, which, at):
        return pltpu.make_async_copy(tiles.at[which], out.at[at], sems.at[at])

    def scan(tiles, index_ref, count):
        def one(i, count):
            position = own_ref[2 * tile_dev + index_ref[i]]
            k = index_ref[tile_dev + i]
            owner, local = lax.div(position, out_dev), lax.rem(position, out_dev)
            match = lax.rem(owner, 2) == core

            @pl.when(match)
            def _():
                copy(tiles, i, count).start()
                odd, to_z = lax.rem(lax.div(owner, 2), 2), lax.div(owner, 4)
                bit_x, bit_y = lax.rem(local, 2), lax.div(local, 2)
                first = jnp.where(odd == 1, bit_y == y, bit_x == x)
                second = jnp.where(odd == 1, bit_x, bit_y)
                plane_ref[count] = (
                    jnp.where(first, 0, sums // 2) + odd * (sums // 4) + 2 * to_z + second
                )
                line_ref[count] = (
                    jnp.where(odd == z_low, 0, sums // 2) + to_z * out_dev + local
                )
                apart, inner = lax.div(k, shard) ^ g, lax.rem(k, shard)
                half = shard // 2
                crossed = jnp.where(lax.div(inner, half) == core, 0, half) + lax.rem(inner, half)
                label_ref[count] = jnp.where(apart == 0, inner, apart * shard + crossed)

            return count + match.astype(jnp.int32)

        return lax.fori_loop(0, tile_dev, one, count)

    count = scan(own_tiles, own_ref, 0)
    count = scan(sib_tiles, sib_ref, count)
    count_ref[0] = count
    for i in range(UNROLL):
        plane_ref[count + i] = sums
        line_ref[count + i] = sums
        label_ref[count + i] = 0

    @pl.loop(0, count)
    def _(i):
        copy(own_tiles, 0, i).wait()


def join_kernel(order, *refs):
    *parts, out = refs
    rows = parts[0].shape[0]
    for i, part in enumerate(parts):
        out[pl.ds(i * rows, rows), :] = part[...]


def products_kernel(
    fill, chunk, order, count_ref, slot_ref, label_ref, tiles, own_panel, *refs
):
    parts = refs[: 1 + max(which for which, _, _ in fill)]
    *sends, sums, stack = refs[len(parts) :]
    side, width = stack.shape[1:]
    for t in range(own_panel.shape[0] // side):
        stack[t] = own_panel[pl.ds(t * side, side), pl.ds(chunk * width, width)]
    for which, t, at in fill:
        stack[at] = parts[which][pl.ds(t * side, side), :]

    @pl.loop(0, sums.shape[0])
    def _(i):
        sums[i] = jnp.zeros(sums.shape[1:], jnp.float32)

    @pl.loop(0, lax.div(count_ref[0] + UNROLL - 1, UNROLL))
    def _(i):
        found = [
            jnp.dot(
                tiles[i * UNROLL + u],
                stack[label_ref[i * UNROLL + u]],
                preferred_element_type=jnp.float32,
            )
            for u in range(UNROLL)
        ]
        for u in range(UNROLL):
            sums[slot_ref[i * UNROLL + u]] += found[u]

    sent = sums.shape[0] // 2
    for send in sends:
        count = (send.shape[0] - CODE_ROWS) // side
        put_coded(send, (sums[sent + i] for i in range(count)))
        sent += count


def plane_kernel(order, recv_a, recv_b, kept, send_a, send_b, keep):
    side, half = kept.shape[1], keep.shape[0] // 2
    x, y, _, _ = here()
    for base, bit, recv, send in ((0, y, recv_a, send_a), (1, x, recv_b, send_b)):
        came = Decoded(recv, side)

        def total(i, which, base=base, came=came):
            return kept[2 * half * base + 2 * i + which] + came.either(which, 2 * i, 2 * i + 1)

        put_coded(send, (total(i, 1 - bit) for i in range(half)))
        for i in range(half):
            keep[base * half + i] = total(i, bit)


def owner_kernel(order, recv_a, recv_b, kept, send, keep):
    side, half = kept.shape[1], keep.shape[0]
    odd = here()[2]
    came_a, came_b = Decoded(recv_a, side), Decoded(recv_b, side)

    def to_send():
        for i in range(half):
            value_a = kept[i] + came_a.tile(i)
            value_b = kept[half + i] + came_b.tile(i)
            keep[i] = jnp.where(odd == 1, value_b, value_a)
            yield jnp.where(odd == 1, value_a, value_b)

    put_coded(send, to_send())


def line_kernel(order, recv, kept, send, keep):
    side, half = kept.shape[1], keep.shape[0]
    bit = here()[3]
    came = Decoded(recv, side)

    def total(i, which):
        return kept[which * half + i] + came.either(which, i, half + i)

    put_coded(send, (total(i, 1 - bit) for i in range(half)))
    for i in range(half):
        keep[i] = total(i, bit)


def rows_kernel(order, recv, kept, send_a, send_b):
    came = Decoded(recv, kept.shape[1])
    half = came.count // 2
    put_coded(send_a, (kept[i] + came.tile(i) for i in range(half)))
    put_coded(send_b, (kept[half + i] + came.tile(half + i) for i in range(half)))


def swap_kernel(order, own_a, own_b, recv_a, recv_b, send_a, send_b):
    side = (own_a.shape[0] - CODE_ROWS) // 2
    for own, recv, send in ((own_a, recv_a, send_a), (own_b, recv_b, send_b)):
        here_, there = Decoded(own, side), Decoded(recv, side)
        put_coded(send, (here_.tile(i) + there.tile(i) for i in range(2)))


def finish_kernel(order, recv, kept, out):
    put_coded(out, [kept[0] + Decoded(recv, kept.shape[1]).tile(0)])


def spread_kernel(chunk, order, *refs):
    blocks, (out, rows, sems) = refs[:4], refs[-3:]
    side, width = rows.shape[1:]
    x, y, _, _ = here()
    blocks = [Decoded(block, side) for block in blocks]
    copies = []
    for i in range(4):
        if blocks[0].count == 2:
            rows[i] = blocks[i // 2].tile(i % 2) + blocks[2 + i // 2].tile(i % 2)
            at = i * side
        else:
            rows[i] = blocks[i].tile(0)
            at = pl.multiple_of(((2 * y + x) ^ i) * side, side)
        copies.append(
            pltpu.make_async_copy(
                rows.at[i], out.at[pl.ds(at, side), pl.ds(chunk * width, width)], sems.at[i]
            )
        )
        copies[-1].start()
    for copy in copies:
        copy.wait()


def in_vmem(count):
    return [pl.BlockSpec(memory_space=pltpu.VMEM)] * count


def in_smem(count):
    return [pl.BlockSpec(memory_space=pltpu.SMEM)] * count


def in_any(count):
    return [pl.BlockSpec(memory_space=pl.ANY)] * count


def shape(dims, kind):
    return jax.ShapeDtypeStruct(dims, kind)


def params(mib):
    return pltpu.CompilerParams(vmem_limit_bytes=mib * MIB)


def cost(flops, moved):
    return pl.CostEstimate(flops=flops, bytes_accessed=moved, transcendentals=0)


def sums_plan(tiles, contraction, row_tile, owner_map, panel):
    wide_count = lax.axis_size("wide")
    tile_dev, side = tiles.shape[0], tiles.shape[1]
    out_dev = owner_map.shape[0] // wide_count
    rows, columns = panel.shape
    shard = rows // side
    chunks = columns // CHUNK
    sums = owner_map.shape[0] // 2
    core = lax.axis_index("wide") % 2

    def to_core(v):
        return lax.ppermute(v, "wide", [(i, i ^ 1) for i in range(wide_count)])

    def to_grp(v, d):
        return lax.ppermute(v, "grp", [(i, i ^ d) for i in range(4)])

    def to_line(v, b):
        return lax.ppermute(v, "wide", [(i, i ^ (2 << b)) for i in range(wide_count)])


    own_index = jnp.concatenate([row_tile, contraction, owner_map])
    sib_index = to_core(own_index)
    sib_tiles = to_core(tiles)

    def own_half(source, j):
        return lax.dynamic_slice(source, (core * (rows // 2), j * CHUNK), (rows // 2, CHUNK))

    mines = [own_half(panel, j) for j in range(chunks)]
    ways = [None, (1, 2), (2, 1)]
    firsts = [None] + [to_grp(mines[j], ways[j][0]) for j in range(1, chunks)]
    mine, sib_index = lax.optimization_barrier((mines[0], sib_index))
    near = [to_grp(mine, 1), to_grp(mine, 2), to_grp(mines[0], 3)]

    half, quarter = sums // 2, sums // 4
    plain = shape((side, CHUNK), jnp.float32)

    def stack_of(count, one):
        return shape((count, *one.shape), one.dtype)

    def coded(count):
        return shape((count * side + CODE_ROWS, CHUNK), jnp.int16)

    order = jnp.zeros((1,), jnp.int32)
    last = None

    def in_order():
        return order if last is None else lax.optimization_barrier((order, last))[0]

    def call(body, name, outs, *args, smem=0, mib=16, extra=(), **more):
        nonlocal last
        done = pl.pallas_call(
            body,
            in_specs=more.pop("in_specs", in_any(1) + in_smem(smem) + in_vmem(len(args) - smem)),
            out_specs=more.pop("out_specs", in_vmem(len(outs))),
            out_shape=outs,
            scratch_shapes=list(extra),
            compiler_params=params(mib),
            cost_estimate=cost(0, sum(math.prod(a.shape) * a.dtype.itemsize for a in args)),
            name=name,
            **more,
        )(in_order(), *args)
        last = done[0]
        return done

    def places(operand, tiles_of, first):
        return [
            (operand, t, d * shard + first + i % part)
            for i, (t, d) in enumerate((t, d) for d, ts in tiles_of for t in ts)
        ]

    part = shard // 2

    def join(j):
        (joined,) = call(join_kernel, "join", [shape((3 * rows // 2, CHUNK), panel.dtype)], *near)
        tiles_of = [(d, range((d - 1) * part, d * part)) for d in (1, 2, 3)]
        fill = places(0, tiles_of, 0) + places(1, tiles_of, part)
        return fill, [joined, to_core(joined)]

    def pair(j):
        way, other = ways[j]
        (joined,) = call(
            join_kernel, "join", [shape((rows, CHUNK), panel.dtype)], mines[j], firsts[j]
        )
        second = to_grp(joined, other)
        in_first = [(way, range(part, 2 * part))]
        in_second = [(other, range(part)), (way ^ other, range(part, 2 * part))]
        fill = (
            places(0, in_first, 0)
            + places(1, in_first, part)
            + places(2, in_second, 0)
            + places(3, in_second, part)
        )
        return fill, [joined, to_core(joined), second, to_core(second)]

    def products(j, slot, sends, fill, parts):
        *sends, kept = call(
            functools.partial(products_kernel, tuple(fill), j),
            "products",
            [*sends, stack_of(sums + 1, plain)],
            counts,
            slot,
            label,
            held,
            panel,
            *parts,
            smem=3,
            extra=[pltpu.VMEM((4 * shard, side, CHUNK), panel.dtype)],
            mib=24,
        )
        return *sends, kept

    def gathered(done):
        return [done] + [to_grp(done, d) for d in (1, 2, 3)]

    def spread(j, blocks, result):
        earlier = [] if result is None else [result]
        return call(
            functools.partial(spread_kernel, j),
            "spread",
            [shape((out_dev * side, columns), jnp.float32)],
            *blocks,
            *earlier,
            in_specs=in_any(1) + in_vmem(4) + in_any(len(earlier)),
            out_specs=in_any(1),
            input_output_aliases={5: 0} if earlier else {},
            extra=[pltpu.VMEM((4, side, CHUNK), jnp.float32), pltpu.SemaphoreType.DMA((4,))],
        )[0]

    eighth = quarter // 2
    entries = shape((2 * tile_dev + UNROLL,), jnp.int32)
    counts, in_plane, in_line, label, held = call(
        hold_kernel,
        "hold",
        [shape((1,), jnp.int32)]
        + [entries] * 3
        + [pltpu.VMEM((2 * tile_dev + UNROLL, side, side), tiles.dtype)],
        own_index,
        sib_index,
        *[pltpu.with_memory_space_constraint(v, pltpu.HBM) for v in (tiles, sib_tiles)],
        in_specs=in_any(1) + in_smem(2) + in_any(2),
        out_specs=in_smem(4) + in_vmem(1),
        extra=[pltpu.SemaphoreType.DMA((2 * tile_dev,))],
        mib=8,
    )
    last = held
    pairs = {j: pair(j) for j in (1, 2)}

    send, keep_0 = products(0, in_line, [coded(half)], *join(0))
    sent_0 = send
    sent, keep = {}, {}
    for j in (1, 2):
        send_a, send_b, keep[j] = products(j, in_plane, [coded(quarter)] * 2, *pairs[j])
        sent[j] = send_a, send_b

    sent_0, keep_0 = call(
        line_kernel,
        "line",
        [coded(quarter), stack_of(quarter, plain)],
        to_line(sent_0, 0),
        keep_0,
    )

    def plane(j):
        return call(
            plane_kernel,
            "plane",
            [coded(eighth)] * 2 + [stack_of(quarter, plain)],
            to_grp(sent[j][0], 1),
            to_grp(sent[j][1], 2),
            keep[j],
        )

    def owner(j):
        return call(
            owner_kernel,
            "owner",
            [coded(eighth), stack_of(eighth, plain)],
            to_grp(sent[j][0], 2),
            to_grp(sent[j][1], 1),
            keep[j],
        )

    *sent[1], keep[1] = plane(1)
    *sent[2], keep[2] = plane(2)
    sent[1], keep[1] = owner(1)
    pair_of = [coded(2)] * 2
    sent[2], keep[2] = owner(2)
    own_a, own_b = call(rows_kernel, "rows", pair_of, to_line(sent_0, 1), keep_0)

    def line(j):
        return call(
            line_kernel,
            "line",
            [coded(1), stack_of(1, plain)],
            to_line(sent[j], 0),
            keep[j],
        )

    def finish(j):
        return call(finish_kernel, "finish", [coded(1)], to_line(sent[j], 1), keep[j])[0]

    sent[1], keep[1] = line(1)
    sent[2], keep[2] = line(2)
    own_a, own_b = call(
        swap_kernel, "swap", pair_of, own_a, own_b, to_grp(own_a, 1), to_grp(own_b, 2)
    )
    done_1 = finish(1)
    result = spread(0, [own_a, own_b, to_grp(own_a, 2), to_grp(own_b, 1)], None)
    done_2 = finish(2)
    result = spread(1, gathered(done_1), result)
    return spread(2, gathered(done_2), result)


def per_device(tiles, contraction, row_tile, owner_map, panel):
    dense = owner_map.shape[0] <= tiles.shape[0]
    wide_count = lax.axis_size("wide")
    fits = lax.axis_size("grp") == 4 and wide_count >= 4 and wide_count & (wide_count - 1) == 0
    out_dev = owner_map.shape[0] // wide_count
    if dense and fits and wide_count == 8 and out_dev == 4 and panel.shape[1] == 3 * CHUNK:
        return sums_plan(tiles, contraction, row_tile, owner_map, panel)
    return slots_plan(tiles, contraction, row_tile, owner_map, panel)


def solution(mesh):
    return jax.shard_map(
        per_device,
        mesh=mesh,
        in_specs=(
            P(("grp", "wide"), None, None),
            P(("grp", "wide")),
            P(("grp", "wide")),
            P(),
            P("grp", None),
        ),
        out_specs=P("wide", None),
        check_vma=False,
    )
```

```python
import functools
import math

import jax
import jax.numpy as jnp
from jax import lax
from jax.experimental import pallas as pl
from jax.experimental.pallas import tpu as pltpu
from jax.sharding import PartitionSpec as P

MIB = 1024 * 1024
CODE_ROWS = 16
CODE_STEPS = 256.0
TOP = 32000.0
CHUNK = 256
UNROLL = 8
LOG2 = math.log(2.0)


def place_slots(row_ids, owner_map, out_dev):
    table_ids = jnp.arange(owner_map.shape[0], dtype=jnp.int32)
    position = jnp.sum(jnp.where(row_ids[..., None] == table_ids, owner_map, 0), axis=-1)
    target = position // out_dev
    serial = jnp.arange(row_ids.shape[-1], dtype=jnp.int32)
    earlier = (target[..., :, None] == target[..., None, :]) & (serial[:, None] > serial[None, :])
    ranking = jnp.sum(earlier.astype(jnp.int32), axis=-1)
    return (position % out_dev, target, ranking)


def add_slot_products(summed, arrived, slot_labels, panel_tiles):
    slot_count = arrived.shape[0]
    block_rows = math.gcd(slot_count, 32)
    out_dev = summed.shape[0]
    local_ids = jnp.arange(out_dev, dtype=jnp.int32)

    def one_block(which_block, running, source_tiles, source_labels):
        part_tiles = lax.dynamic_slice_in_dim(source_tiles, which_block * block_rows, block_rows, 0)
        part_labels = lax.dynamic_slice_in_dim(
            source_labels, which_block * block_rows, block_rows, 0
        )
        chosen = jnp.take(panel_tiles, part_labels[:, 1], axis=0)
        products = jnp.einsum(
            "sab,sbc->sac", part_tiles, chosen, preferred_element_type=jnp.float32
        )
        row_hits = (part_labels[:, 0][:, None] == local_ids[None, :]).astype(jnp.float32)
        return running + jnp.einsum(
            "sr,sac->rac", row_hits, products, precision=lax.Precision.HIGHEST
        )

    return lax.fori_loop(
        0,
        slot_count // block_rows,
        lambda which_block, running: one_block(which_block, running, arrived, slot_labels),
        summed,
    )


def slots_plan(tiles, contraction, row_tile, owner_map, panel):
    wide_count = lax.axis_size("wide")
    tile_dev = tiles.shape[0]
    tile_side = tiles.shape[1]
    out_dev = owner_map.shape[0] // wide_count
    most_slots = tile_dev * 8 // (3 * wide_count)
    slot_total = wide_count * most_slots
    local_row, target, ranking = place_slots(row_tile, owner_map, out_dev)
    slot_index = target * most_slots + ranking
    outgoing = jnp.zeros((slot_total, tile_side, tile_side), tiles.dtype).at[slot_index].set(tiles)
    all_rows, all_contraction = (
        lax.all_gather(row_tile, "wide", axis=0, tiled=True),
        lax.all_gather(contraction, "wide", axis=0, tiled=True),
    )
    all_rows = all_rows.reshape(wide_count, tile_dev)
    all_contraction = all_contraction.reshape(wide_count, tile_dev)
    source_local, source_target, source_rank = place_slots(all_rows, owner_map, out_dev)
    source_ids = jnp.arange(wide_count, dtype=jnp.int32)
    mine = source_target == lax.axis_index("wide")
    arrive_index = jnp.where(mine, source_ids[:, None] * most_slots + source_rank, slot_total)
    label_pairs = jnp.stack([source_local, all_contraction], axis=-1).reshape(
        wide_count * tile_dev, 2
    )
    vacant_label = jnp.stack(
        [jnp.full((slot_total,), out_dev, jnp.int32), jnp.zeros((slot_total,), jnp.int32)], axis=1
    )
    arrived_labels = vacant_label.at[arrive_index.reshape(-1)].set(label_pairs, mode="drop")
    gathered = lax.all_gather(panel, "grp", axis=0, tiled=True)
    panel_tiles = gathered.reshape(gathered.shape[0] // tile_side, tile_side, gathered.shape[1])
    summed = jnp.zeros((out_dev, tile_side, gathered.shape[1]), jnp.float32)
    arrived = lax.all_to_all(outgoing, "wide", split_axis=0, concat_axis=0, tiled=True)
    summed = add_slot_products(summed, arrived, arrived_labels, panel_tiles)
    summed = lax.psum(summed, "grp")
    return summed.reshape(out_dev * tile_side, gathered.shape[1])


def encode(value):
    largest = jnp.max(jnp.abs(value), axis=0, keepdims=True)
    code = jnp.ceil(jnp.log(jnp.maximum(largest, 1e-30)) * (CODE_STEPS / LOG2))
    scale = jnp.exp(code * (-LOG2 / CODE_STEPS)) * TOP
    whole = jnp.round(value * scale).astype(jnp.int32).astype(jnp.int16)
    return whole, code.astype(jnp.int32)


def put_coded(ref, values):
    codes = []
    for value in values:
        side = value.shape[0]
        whole, code = encode(value)
        ref[pl.ds(len(codes) * side, side), :] = whole
        codes.append(code)
    end = len(codes) * side
    codes += [jnp.zeros_like(codes[0])] * (CODE_ROWS - len(codes))
    ref[pl.ds(end, CODE_ROWS), :] = jnp.concatenate(codes, axis=0).astype(jnp.int16)


class Decoded:
    def __init__(self, ref, side):
        self.ref, self.side = ref, side
        self.count = (ref.shape[0] - CODE_ROWS) // side
        code = ref[pl.ds(self.count * side, CODE_ROWS), :].astype(jnp.int32)
        self.scales = jnp.exp(code.astype(jnp.float32) * (LOG2 / CODE_STEPS)) * (1.0 / TOP)

    def tile(self, i):
        return self.part(i * self.side, self.scales[i : i + 1])

    def either(self, bit, zero, one):
        at = pl.multiple_of(jnp.where(bit == 1, one, zero) * self.side, self.side)
        scales = self.scales
        return self.part(at, jnp.where(bit == 1, scales[one : one + 1], scales[zero : zero + 1]))

    def part(self, at, scale):
        return self.ref[pl.ds(at, self.side), :].astype(jnp.int32).astype(jnp.float32) * scale


def here():
    g, w = lax.axis_index("grp"), lax.axis_index("wide")
    return g % 2, g // 2, (w // 2) % 2, w // 4


def hold_kernel(
    order, own_ref, sib_ref, own_tiles, sib_tiles,
    count_ref, plane_ref, line_ref, label_ref, plane_order, line_order, out, sems,
):
    tile_dev = own_tiles.shape[0]
    sums = (own_ref.shape[0] - 2 * tile_dev) // 2
    shard, out_dev = 4, 4
    room = 2 * tile_dev + UNROLL
    x, y, z_low, _ = here()
    g, core = lax.axis_index("grp"), lax.axis_index("wide") % 2

    def copy(tiles, which, at):
        return pltpu.make_async_copy(tiles.at[which], out.at[at], sems.at[at])

    def scan(tiles, index_ref, counts):
        def one(i, counts):
            position = own_ref[2 * tile_dev + index_ref[i]]
            k = index_ref[tile_dev + i]
            owner, local = lax.div(position, out_dev), lax.rem(position, out_dev)
            match = lax.rem(owner, 2) == core

            odd, to_z = lax.rem(lax.div(owner, 2), 2), lax.div(owner, 4)
            bit_x, bit_y = lax.rem(local, 2), lax.div(local, 2)
            kept = [
                jnp.where(odd == 1, bit_y == y, bit_x == x),
                odd == z_low,
            ]

            @pl.when(match)
            def _():
                copy(tiles, i, counts[0]).start()
                second = jnp.where(odd == 1, bit_x, bit_y)
                places = [odd * (sums // 4) + 2 * to_z + second, to_z * out_dev + local]
                for ref, order_ref, keep, place, sent in (
                    (plane_ref, plane_order, kept[0], places[0], counts[1]),
                    (line_ref, line_order, kept[1], places[1], counts[2]),
                ):
                    ref[counts[0]] = place
                    order_ref[jnp.where(keep, room + counts[0] - sent, sent)] = counts[0]
                apart, inner = lax.div(k, shard) ^ g, lax.rem(k, shard)
                half = shard // 2
                crossed = jnp.where(lax.div(inner, half) == core, 0, half) + lax.rem(inner, half)
                label_ref[counts[0]] = jnp.where(apart == 0, inner, apart * shard + crossed)

            more = [match, match & ~kept[0], match & ~kept[1]]
            return tuple(c + m.astype(jnp.int32) for c, m in zip(counts, more))

        return lax.fori_loop(0, tile_dev, one, counts)

    counts = scan(own_tiles, own_ref, (0, 0, 0))
    counts = scan(sib_tiles, sib_ref, counts)
    count = counts[0]
    for i in range(3):
        count_ref[i] = counts[i]
    spare = 2 * tile_dev
    plane_ref[spare] = sums // 2
    line_ref[spare] = sums // 2
    label_ref[spare] = 0
    for order_ref, sent in ((plane_order, counts[1]), (line_order, counts[2])):
        for i in range(UNROLL):
            order_ref[sent + i] = spare
            order_ref[room + count - sent + i] = spare

    @pl.loop(0, count)
    def _(i):
        copy(own_tiles, 0, i).wait()


def join_kernel(order, *refs):
    *parts, out = refs
    rows = parts[0].shape[0]
    for i, part in enumerate(parts):
        out[pl.ds(i * rows, rows), :] = part[...]


def add_products(count, first, order_ref, slot_ref, label_ref, tiles, stack, sums):
    @pl.loop(0, sums.shape[0])
    def _(i):
        sums[i] = jnp.zeros(sums.shape[1:], jnp.float32)

    @pl.loop(0, lax.div(count + UNROLL - 1, UNROLL))
    def _(i):
        entries = [order_ref[first + i * UNROLL + u] for u in range(UNROLL)]
        found = [
            jnp.dot(tiles[e], stack[label_ref[e]], preferred_element_type=jnp.float32)
            for e in entries
        ]
        for e, product in zip(entries, found):
            sums[slot_ref[e]] += product


def sent_kernel(
    fill, chunk, which, order, count_ref, order_ref, slot_ref, label_ref,
    tiles, own_panel, *refs
):
    parts = refs[: 1 + max(part for part, _, _ in fill)]
    *sends, stack, sums = refs[len(parts) :]
    side, width = stack.shape[1:]
    for t in range(own_panel.shape[0] // side):
        stack[t] = own_panel[pl.ds(t * side, side), pl.ds(chunk * width, width)]
    for part, t, at in fill:
        stack[at] = parts[part][pl.ds(t * side, side), :]
    add_products(count_ref[which], 0, order_ref, slot_ref, label_ref, tiles, stack, sums)
    sent = 0
    for send in sends:
        count = (send.shape[0] - CODE_ROWS) // side
        put_coded(send, (sums[sent + i] for i in range(count)))
        sent += count


def kept_kernel(which, order, count_ref, order_ref, slot_ref, label_ref, tiles, stack, sums):
    count = count_ref[0] - count_ref[which]
    room = tiles.shape[0]
    add_products(count, room, order_ref, slot_ref, label_ref, tiles, stack, sums)


def plane_kernel(order, recv_a, recv_b, kept, send_a, send_b, keep):
    side, half = kept.shape[1], keep.shape[0] // 2
    x, y, _, _ = here()
    for base, bit, recv, send in ((0, y, recv_a, send_a), (1, x, recv_b, send_b)):
        came = Decoded(recv, side)

        def total(i, which, base=base, came=came):
            return kept[2 * half * base + 2 * i + which] + came.either(which, 2 * i, 2 * i + 1)

        put_coded(send, (total(i, 1 - bit) for i in range(half)))
        for i in range(half):
            keep[base * half + i] = total(i, bit)


def owner_kernel(order, recv_a, recv_b, kept, send, keep):
    side, half = kept.shape[1], keep.shape[0]
    odd = here()[2]
    came_a, came_b = Decoded(recv_a, side), Decoded(recv_b, side)

    def to_send():
        for i in range(half):
            value_a = kept[i] + came_a.tile(i)
            value_b = kept[half + i] + came_b.tile(i)
            keep[i] = jnp.where(odd == 1, value_b, value_a)
            yield jnp.where(odd == 1, value_a, value_b)

    put_coded(send, to_send())


def line_kernel(order, recv, kept, send, keep):
    side, half = kept.shape[1], keep.shape[0]
    bit = here()[3]
    came = Decoded(recv, side)

    def total(i, which):
        return kept[which * half + i] + came.either(which, i, half + i)

    put_coded(send, (total(i, 1 - bit) for i in range(half)))
    for i in range(half):
        keep[i] = total(i, bit)


def rows_kernel(order, recv, kept, send_a, send_b):
    came = Decoded(recv, kept.shape[1])
    half = came.count // 2
    put_coded(send_a, (kept[i] + came.tile(i) for i in range(half)))
    put_coded(send_b, (kept[half + i] + came.tile(half + i) for i in range(half)))


def swap_kernel(order, own_a, own_b, recv_a, recv_b, send_a, send_b):
    side = (own_a.shape[0] - CODE_ROWS) // 2
    for own, recv, send in ((own_a, recv_a, send_a), (own_b, recv_b, send_b)):
        here_, there = Decoded(own, side), Decoded(recv, side)
        put_coded(send, (here_.tile(i) + there.tile(i) for i in range(2)))


def finish_kernel(order, recv, kept, out):
    put_coded(out, [kept[0] + Decoded(recv, kept.shape[1]).tile(0)])


def spread_kernel(chunk, order, *refs):
    blocks, (out, rows, sems) = refs[:4], refs[-3:]
    side, width = rows.shape[1:]
    x, y, _, _ = here()
    blocks = [Decoded(block, side) for block in blocks]
    copies = []
    for i in range(4):
        if blocks[0].count == 2:
            rows[i] = blocks[i // 2].tile(i % 2) + blocks[2 + i // 2].tile(i % 2)
            at = i * side
        else:
            rows[i] = blocks[i].tile(0)
            at = pl.multiple_of(((2 * y + x) ^ i) * side, side)
        copies.append(
            pltpu.make_async_copy(
                rows.at[i], out.at[pl.ds(at, side), pl.ds(chunk * width, width)], sems.at[i]
            )
        )
        copies[-1].start()
    for copy in copies:
        copy.wait()


def in_vmem(count):
    return [pl.BlockSpec(memory_space=pltpu.VMEM)] * count


def in_smem(count):
    return [pl.BlockSpec(memory_space=pltpu.SMEM)] * count


def in_any(count):
    return [pl.BlockSpec(memory_space=pl.ANY)] * count


def shape(dims, kind):
    return jax.ShapeDtypeStruct(dims, kind)


def params(mib):
    return pltpu.CompilerParams(vmem_limit_bytes=mib * MIB)


def cost(flops, moved):
    return pl.CostEstimate(flops=flops, bytes_accessed=moved, transcendentals=0)


def sums_plan(tiles, contraction, row_tile, owner_map, panel):
    wide_count = lax.axis_size("wide")
    tile_dev, side = tiles.shape[0], tiles.shape[1]
    out_dev = owner_map.shape[0] // wide_count
    rows, columns = panel.shape
    shard = rows // side
    chunks = columns // CHUNK
    sums = owner_map.shape[0] // 2
    core = lax.axis_index("wide") % 2

    def to_core(v):
        return lax.ppermute(v, "wide", [(i, i ^ 1) for i in range(wide_count)])

    def to_grp(v, d):
        return lax.ppermute(v, "grp", [(i, i ^ d) for i in range(4)])

    def to_line(v, b):
        return lax.ppermute(v, "wide", [(i, i ^ (2 << b)) for i in range(wide_count)])


    own_index = jnp.concatenate([row_tile, contraction, owner_map])
    sib_index = to_core(own_index)
    sib_tiles = to_core(tiles)

    def own_half(source, j):
        return lax.dynamic_slice(source, (core * (rows // 2), j * CHUNK), (rows // 2, CHUNK))

    mines = [own_half(panel, j) for j in range(chunks)]
    ways = [None, (1, 2), (2, 1)]
    firsts = [None] + [to_grp(mines[j], ways[j][0]) for j in range(1, chunks)]
    mine, sib_index = lax.optimization_barrier((mines[0], sib_index))
    near = [to_grp(mine, 1), to_grp(mine, 2), to_grp(mines[0], 3)]

    half, quarter = sums // 2, sums // 4
    plain = shape((side, CHUNK), jnp.float32)

    def stack_of(count, one):
        return shape((count, *one.shape), one.dtype)

    def coded(count):
        return shape((count * side + CODE_ROWS, CHUNK), jnp.int16)

    order = jnp.zeros((1,), jnp.int32)
    last = None

    def in_order():
        return order if last is None else lax.optimization_barrier((order, last))[0]

    def call(body, name, outs, *args, smem=0, mib=16, extra=(), **more):
        nonlocal last
        done = pl.pallas_call(
            body,
            in_specs=more.pop("in_specs", in_any(1) + in_smem(smem) + in_vmem(len(args) - smem)),
            out_specs=more.pop("out_specs", in_vmem(len(outs))),
            out_shape=outs,
            scratch_shapes=list(extra),
            compiler_params=params(mib),
            cost_estimate=cost(0, sum(math.prod(a.shape) * a.dtype.itemsize for a in args)),
            name=name,
            **more,
        )(in_order(), *args)
        last = done[0]
        return done

    def places(operand, tiles_of, first):
        return [
            (operand, t, d * shard + first + i % part)
            for i, (t, d) in enumerate((t, d) for d, ts in tiles_of for t in ts)
        ]

    part = shard // 2

    def join(j):
        (joined,) = call(join_kernel, "join", [shape((3 * rows // 2, CHUNK), panel.dtype)], *near)
        tiles_of = [(d, range((d - 1) * part, d * part)) for d in (1, 2, 3)]
        fill = places(0, tiles_of, 0) + places(1, tiles_of, part)
        return fill, [joined, to_core(joined)]

    def pair(j):
        way, other = ways[j]
        (joined,) = call(
            join_kernel, "join", [shape((rows, CHUNK), panel.dtype)], mines[j], firsts[j]
        )
        second = to_grp(joined, other)
        in_first = [(way, range(part, 2 * part))]
        in_second = [(other, range(part)), (way ^ other, range(part, 2 * part))]
        fill = (
            places(0, in_first, 0)
            + places(1, in_first, part)
            + places(2, in_second, 0)
            + places(3, in_second, part)
        )
        return fill, [joined, to_core(joined), second]

    def products(j, which, sends, fill, parts):
        lists = counts, orders[which], slots[which], label
        *sends, stacked = call(
            functools.partial(sent_kernel, tuple(fill), j, which),
            "products_sent",
            [*sends, shape((4 * shard, side, CHUNK), panel.dtype)],
            *lists,
            held,
            panel,
            *parts,
            smem=4,
            extra=[pltpu.VMEM((half + 1, side, CHUNK), jnp.float32)],
            mib=24,
        )
        (kept,) = call(
            functools.partial(kept_kernel, which),
            "products_kept",
            [stack_of(half + 1, plain)],
            *lists,
            held,
            stacked,
            smem=4,
            mib=24,
        )
        return *sends, kept

    def gathered(done):
        return [done] + [to_grp(done, d) for d in (1, 2, 3)]

    def spread(j, blocks, result):
        earlier = [] if result is None else [result]
        return call(
            functools.partial(spread_kernel, j),
            "spread",
            [shape((out_dev * side, columns), jnp.float32)],
            *blocks,
            *earlier,
            in_specs=in_any(1) + in_vmem(4) + in_any(len(earlier)),
            out_specs=in_any(1),
            input_output_aliases={5: 0} if earlier else {},
            extra=[pltpu.VMEM((4, side, CHUNK), jnp.float32), pltpu.SemaphoreType.DMA((4,))],
        )[0]

    eighth = quarter // 2
    entries = shape((2 * tile_dev + UNROLL,), jnp.int32)
    twice = shape((2 * entries.shape[0],), jnp.int32)
    counts, in_plane, in_line, label, plane_order, line_order, held = call(
        hold_kernel,
        "hold",
        [shape((3,), jnp.int32)]
        + [entries] * 3
        + [twice] * 2
        + [pltpu.VMEM((2 * tile_dev + UNROLL, side, side), tiles.dtype)],
        own_index,
        sib_index,
        *[pltpu.with_memory_space_constraint(v, pltpu.HBM) for v in (tiles, sib_tiles)],
        in_specs=in_any(1) + in_smem(2) + in_any(2),
        out_specs=in_smem(6) + in_vmem(1),
        extra=[pltpu.SemaphoreType.DMA((2 * tile_dev,))],
        mib=8,
    )
    last = held
    slots, orders = {1: in_plane, 2: in_line}, {1: plane_order, 2: line_order}
    pairs = {j: pair(j) for j in (1, 2)}

    send, keep_0 = products(0, 2, [coded(half)], *join(0))
    sent_0 = send
    sent, keep = {}, {}
    for j in (1, 2):
        fill, (*parts, second) = pairs[j]
        second = lax.optimization_barrier((second, keep_0))[0]
        parts += [second, to_core(second)]
        send_a, send_b, keep[j] = products(j, 1, [coded(quarter)] * 2, fill, parts)
        sent[j] = send_a, send_b

    sent_0, keep_0 = call(
        line_kernel,
        "line",
        [coded(quarter), stack_of(quarter, plain)],
        to_line(sent_0, 0),
        keep_0,
    )

    def plane(j):
        return call(
            plane_kernel,
            "plane",
            [coded(eighth)] * 2 + [stack_of(quarter, plain)],
            to_grp(sent[j][0], 1),
            to_grp(sent[j][1], 2),
            keep[j],
        )

    def owner(j):
        return call(
            owner_kernel,
            "owner",
            [coded(eighth), stack_of(eighth, plain)],
            to_grp(sent[j][0], 2),
            to_grp(sent[j][1], 1),
            keep[j],
        )

    *sent[1], keep[1] = plane(1)
    *sent[2], keep[2] = plane(2)
    sent[1], keep[1] = owner(1)
    pair_of = [coded(2)] * 2
    own_a, own_b = call(rows_kernel, "rows", pair_of, to_line(sent_0, 1), keep_0)
    sent[2], keep[2] = owner(2)

    def line(j):
        return call(
            line_kernel,
            "line",
            [coded(1), stack_of(1, plain)],
            to_line(sent[j], 0),
            keep[j],
        )

    def finish(j):
        return call(finish_kernel, "finish", [coded(1)], to_line(sent[j], 1), keep[j])[0]

    sent[1], keep[1] = line(1)
    own_a, own_b = call(
        swap_kernel, "swap", pair_of, own_a, own_b, to_grp(own_a, 1), to_grp(own_b, 2)
    )
    done_1 = finish(1)
    sent[2], keep[2] = line(2)
    result = spread(0, [own_a, own_b, to_grp(own_a, 2), to_grp(own_b, 1)], None)
    done_2 = finish(2)
    result = spread(1, gathered(done_1), result)
    return spread(2, gathered(done_2), result)


def per_device(tiles, contraction, row_tile, owner_map, panel):
    dense = owner_map.shape[0] <= tiles.shape[0]
    wide_count = lax.axis_size("wide")
    fits = lax.axis_size("grp") == 4 and wide_count >= 4 and wide_count & (wide_count - 1) == 0
    out_dev = owner_map.shape[0] // wide_count
    if dense and fits and wide_count == 8 and out_dev == 4 and panel.shape[1] == 3 * CHUNK:
        return sums_plan(tiles, contraction, row_tile, owner_map, panel)
    return slots_plan(tiles, contraction, row_tile, owner_map, panel)


def solution(mesh):
    return jax.shard_map(
        per_device,
        mesh=mesh,
        in_specs=(
            P(("grp", "wide"), None, None),
            P(("grp", "wide")),
            P(("grp", "wide")),
            P(),
            P("grp", None),
        ),
        out_specs=P("wide", None),
        check_vma=False,
    )
```

```python
import functools
import math

import jax
import jax.numpy as jnp
from jax import lax
from jax.experimental import pallas as pl
from jax.experimental.pallas import tpu as pltpu
from jax.sharding import PartitionSpec as P

MIB = 1024 * 1024
CODE_ROWS = 16
CODE_STEPS = 256.0
TOP = 32000.0
CHUNK = 256
UNROLL = 8
LOG2 = math.log(2.0)


def place_slots(row_ids, owner_map, out_dev):
    table_ids = jnp.arange(owner_map.shape[0], dtype=jnp.int32)
    position = jnp.sum(jnp.where(row_ids[..., None] == table_ids, owner_map, 0), axis=-1)
    target = position // out_dev
    serial = jnp.arange(row_ids.shape[-1], dtype=jnp.int32)
    earlier = (target[..., :, None] == target[..., None, :]) & (serial[:, None] > serial[None, :])
    ranking = jnp.sum(earlier.astype(jnp.int32), axis=-1)
    return (position % out_dev, target, ranking)


def add_slot_products(summed, arrived, slot_labels, panel_tiles):
    slot_count = arrived.shape[0]
    block_rows = math.gcd(slot_count, 32)
    out_dev = summed.shape[0]
    local_ids = jnp.arange(out_dev, dtype=jnp.int32)

    def one_block(which_block, running, source_tiles, source_labels):
        part_tiles = lax.dynamic_slice_in_dim(source_tiles, which_block * block_rows, block_rows, 0)
        part_labels = lax.dynamic_slice_in_dim(
            source_labels, which_block * block_rows, block_rows, 0
        )
        chosen = jnp.take(panel_tiles, part_labels[:, 1], axis=0)
        products = jnp.einsum(
            "sab,sbc->sac", part_tiles, chosen, preferred_element_type=jnp.float32
        )
        row_hits = (part_labels[:, 0][:, None] == local_ids[None, :]).astype(jnp.float32)
        return running + jnp.einsum(
            "sr,sac->rac", row_hits, products, precision=lax.Precision.HIGHEST
        )

    return lax.fori_loop(
        0,
        slot_count // block_rows,
        lambda which_block, running: one_block(which_block, running, arrived, slot_labels),
        summed,
    )


def slots_plan(tiles, contraction, row_tile, owner_map, panel):
    wide_count = lax.axis_size("wide")
    tile_dev = tiles.shape[0]
    tile_side = tiles.shape[1]
    out_dev = owner_map.shape[0] // wide_count
    most_slots = tile_dev * 8 // (3 * wide_count)
    slot_total = wide_count * most_slots
    local_row, target, ranking = place_slots(row_tile, owner_map, out_dev)
    slot_index = target * most_slots + ranking
    outgoing = jnp.zeros((slot_total, tile_side, tile_side), tiles.dtype).at[slot_index].set(tiles)
    all_rows, all_contraction = (
        lax.all_gather(row_tile, "wide", axis=0, tiled=True),
        lax.all_gather(contraction, "wide", axis=0, tiled=True),
    )
    all_rows = all_rows.reshape(wide_count, tile_dev)
    all_contraction = all_contraction.reshape(wide_count, tile_dev)
    source_local, source_target, source_rank = place_slots(all_rows, owner_map, out_dev)
    source_ids = jnp.arange(wide_count, dtype=jnp.int32)
    mine = source_target == lax.axis_index("wide")
    arrive_index = jnp.where(mine, source_ids[:, None] * most_slots + source_rank, slot_total)
    label_pairs = jnp.stack([source_local, all_contraction], axis=-1).reshape(
        wide_count * tile_dev, 2
    )
    vacant_label = jnp.stack(
        [jnp.full((slot_total,), out_dev, jnp.int32), jnp.zeros((slot_total,), jnp.int32)], axis=1
    )
    arrived_labels = vacant_label.at[arrive_index.reshape(-1)].set(label_pairs, mode="drop")
    gathered = lax.all_gather(panel, "grp", axis=0, tiled=True)
    panel_tiles = gathered.reshape(gathered.shape[0] // tile_side, tile_side, gathered.shape[1])
    summed = jnp.zeros((out_dev, tile_side, gathered.shape[1]), jnp.float32)
    arrived = lax.all_to_all(outgoing, "wide", split_axis=0, concat_axis=0, tiled=True)
    summed = add_slot_products(summed, arrived, arrived_labels, panel_tiles)
    summed = lax.psum(summed, "grp")
    return summed.reshape(out_dev * tile_side, gathered.shape[1])


def encode(value):
    largest = jnp.max(jnp.abs(value), axis=0, keepdims=True)
    code = jnp.ceil(jnp.log(jnp.maximum(largest, 1e-30)) * (CODE_STEPS / LOG2))
    scale = jnp.exp(code * (-LOG2 / CODE_STEPS)) * TOP
    whole = jnp.round(value * scale).astype(jnp.int32).astype(jnp.int16)
    return whole, code.astype(jnp.int32)


def put_coded(ref, values):
    codes = []
    for value in values:
        side = value.shape[0]
        whole, code = encode(value)
        ref[pl.ds(len(codes) * side, side), :] = whole
        codes.append(code)
    end = len(codes) * side
    codes += [jnp.zeros_like(codes[0])] * (CODE_ROWS - len(codes))
    ref[pl.ds(end, CODE_ROWS), :] = jnp.concatenate(codes, axis=0).astype(jnp.int16)


class Decoded:
    def __init__(self, ref, side):
        self.ref, self.side = ref, side
        self.count = (ref.shape[0] - CODE_ROWS) // side
        code = ref[pl.ds(self.count * side, CODE_ROWS), :].astype(jnp.int32)
        self.scales = jnp.exp(code.astype(jnp.float32) * (LOG2 / CODE_STEPS)) * (1.0 / TOP)

    def tile(self, i):
        return self.part(i * self.side, self.scales[i : i + 1])

    def either(self, bit, zero, one):
        at = pl.multiple_of(jnp.where(bit == 1, one, zero) * self.side, self.side)
        scales = self.scales
        return self.part(at, jnp.where(bit == 1, scales[one : one + 1], scales[zero : zero + 1]))

    def part(self, at, scale):
        return self.ref[pl.ds(at, self.side), :].astype(jnp.int32).astype(jnp.float32) * scale


def here():
    g, w = lax.axis_index("grp"), lax.axis_index("wide")
    return g % 2, g // 2, (w // 2) % 2, w // 4


def hold_kernel(
    order, own_ref, sib_ref, own_tiles, sib_tiles,
    count_ref, plane_ref, line_ref, label_ref, plane_order, line_order, out, sems,
):
    tile_dev = own_tiles.shape[0]
    sums = (own_ref.shape[0] - 2 * tile_dev) // 2
    shard, out_dev = 4, 4
    room = 2 * tile_dev + UNROLL
    x, y, z_low, _ = here()
    g, core = lax.axis_index("grp"), lax.axis_index("wide") % 2

    def copy(tiles, which, at):
        return pltpu.make_async_copy(tiles.at[which], out.at[at], sems.at[at])

    def scan(tiles, index_ref, counts):
        def one(i, counts):
            position = own_ref[2 * tile_dev + index_ref[i]]
            k = index_ref[tile_dev + i]
            owner, local = lax.div(position, out_dev), lax.rem(position, out_dev)
            match = lax.rem(owner, 2) == core

            odd, to_z = lax.rem(lax.div(owner, 2), 2), lax.div(owner, 4)
            bit_x, bit_y = lax.rem(local, 2), lax.div(local, 2)
            kept = [
                jnp.where(odd == 1, bit_y == y, bit_x == x),
                odd == z_low,
            ]

            @pl.when(match)
            def _():
                copy(tiles, i, counts[0]).start()
                second = jnp.where(odd == 1, bit_x, bit_y)
                places = [odd * (sums // 4) + 2 * to_z + second, to_z * out_dev + local]
                for ref, order_ref, keep, place, sent in (
                    (plane_ref, plane_order, kept[0], places[0], counts[1]),
                    (line_ref, line_order, kept[1], places[1], counts[2]),
                ):
                    ref[counts[0]] = place
                    order_ref[jnp.where(keep, room + counts[0] - sent, sent)] = counts[0]
                apart, inner = lax.div(k, shard) ^ g, lax.rem(k, shard)
                half = shard // 2
                crossed = jnp.where(lax.div(inner, half) == core, 0, half) + lax.rem(inner, half)
                label_ref[counts[0]] = jnp.where(apart == 0, inner, apart * shard + crossed)

            more = [match, match & ~kept[0], match & ~kept[1]]
            return tuple(c + m.astype(jnp.int32) for c, m in zip(counts, more))

        return lax.fori_loop(0, tile_dev, one, counts)

    counts = scan(own_tiles, own_ref, (0, 0, 0))
    counts = scan(sib_tiles, sib_ref, counts)
    count = counts[0]
    for i in range(3):
        count_ref[i] = counts[i]
    spare = 2 * tile_dev
    plane_ref[spare] = sums // 2
    line_ref[spare] = sums // 2
    label_ref[spare] = 0
    for order_ref, sent in ((plane_order, counts[1]), (line_order, counts[2])):
        for i in range(UNROLL):
            order_ref[sent + i] = spare
            order_ref[room + count - sent + i] = spare

    @pl.loop(0, count)
    def _(i):
        copy(own_tiles, 0, i).wait()


def join_kernel(first, order, *refs):
    *parts, out = refs
    at, width = 0, out.shape[1]
    for part in parts:
        column = first if part.shape[1] > width else 0
        out[pl.ds(at, part.shape[0]), :] = part[:, pl.ds(column, width)]
        at += part.shape[0]


def add_products(count, first, order_ref, slot_ref, label_ref, tiles, stack, sums):
    @pl.loop(0, sums.shape[0])
    def _(i):
        sums[i] = jnp.zeros(sums.shape[1:], jnp.float32)

    @pl.loop(0, lax.div(count + UNROLL - 1, UNROLL))
    def _(i):
        entries = [order_ref[first + i * UNROLL + u] for u in range(UNROLL)]
        found = [
            jnp.dot(tiles[e], stack[label_ref[e]], preferred_element_type=jnp.float32)
            for e in entries
        ]
        for e, product in zip(entries, found):
            sums[slot_ref[e]] += product


def sent_kernel(
    fill, chunk, which, order, count_ref, order_ref, slot_ref, label_ref,
    tiles, own_panel, *refs
):
    parts = refs[: 1 + max(part for part, _, _ in fill)]
    *sends, stack, sums = refs[len(parts) :]
    side, width = stack.shape[1:]
    for t in range(own_panel.shape[0] // side):
        stack[t] = own_panel[pl.ds(t * side, side), pl.ds(chunk * width, width)]
    for part, t, at in fill:
        stack[at] = parts[part][pl.ds(t * side, side), :]
    add_products(count_ref[which], 0, order_ref, slot_ref, label_ref, tiles, stack, sums)
    sent = 0
    for send in sends:
        count = (send.shape[0] - CODE_ROWS) // side
        put_coded(send, (sums[sent + i] for i in range(count)))
        sent += count


def kept_kernel(which, order, count_ref, order_ref, slot_ref, label_ref, tiles, stack, sums):
    count = count_ref[0] - count_ref[which]
    room = tiles.shape[0]
    add_products(count, room, order_ref, slot_ref, label_ref, tiles, stack, sums)


def plane_kernel(order, recv_a, recv_b, kept, send_a, send_b, keep):
    side, half = kept.shape[1], keep.shape[0] // 2
    x, y, _, _ = here()
    for base, bit, recv, send in ((0, y, recv_a, send_a), (1, x, recv_b, send_b)):
        came = Decoded(recv, side)

        def total(i, which, base=base, came=came):
            return kept[2 * half * base + 2 * i + which] + came.either(which, 2 * i, 2 * i + 1)

        put_coded(send, (total(i, 1 - bit) for i in range(half)))
        for i in range(half):
            keep[base * half + i] = total(i, bit)


def owner_kernel(order, recv_a, recv_b, kept, send, keep):
    side, half = kept.shape[1], keep.shape[0]
    odd = here()[2]
    came_a, came_b = Decoded(recv_a, side), Decoded(recv_b, side)

    def to_send():
        for i in range(half):
            value_a = kept[i] + came_a.tile(i)
            value_b = kept[half + i] + came_b.tile(i)
            keep[i] = jnp.where(odd == 1, value_b, value_a)
            yield jnp.where(odd == 1, value_a, value_b)

    put_coded(send, to_send())


def line_kernel(order, recv, kept, send, keep):
    side, half = kept.shape[1], keep.shape[0]
    bit = here()[3]
    came = Decoded(recv, side)

    def total(i, which):
        return kept[which * half + i] + came.either(which, i, half + i)

    put_coded(send, (total(i, 1 - bit) for i in range(half)))
    for i in range(half):
        keep[i] = total(i, bit)


def rows_kernel(order, recv, kept, send_a, send_b):
    came = Decoded(recv, kept.shape[1])
    half = came.count // 2
    put_coded(send_a, (kept[i] + came.tile(i) for i in range(half)))
    put_coded(send_b, (kept[half + i] + came.tile(half + i) for i in range(half)))


def swap_kernel(order, own_a, own_b, recv_a, recv_b, send_a, send_b):
    side = (own_a.shape[0] - CODE_ROWS) // 2
    for own, recv, send in ((own_a, recv_a, send_a), (own_b, recv_b, send_b)):
        here_, there = Decoded(own, side), Decoded(recv, side)
        put_coded(send, (here_.tile(i) + there.tile(i) for i in range(2)))


def finish_kernel(order, recv, kept, out):
    put_coded(out, [kept[0] + Decoded(recv, kept.shape[1]).tile(0)])


def spread_kernel(chunk, order, *refs):
    blocks, (out, rows, sems) = refs[:4], refs[-3:]
    side, width = rows.shape[1:]
    x, y, _, _ = here()
    blocks = [Decoded(block, side) for block in blocks]
    copies = []
    for i in range(4):
        if blocks[0].count == 2:
            rows[i] = blocks[i // 2].tile(i % 2) + blocks[2 + i // 2].tile(i % 2)
            at = i * side
        else:
            rows[i] = blocks[i].tile(0)
            at = pl.multiple_of(((2 * y + x) ^ i) * side, side)
        copies.append(
            pltpu.make_async_copy(
                rows.at[i], out.at[pl.ds(at, side), pl.ds(chunk * width, width)], sems.at[i]
            )
        )
        copies[-1].start()
    for copy in copies:
        copy.wait()


def in_vmem(count):
    return [pl.BlockSpec(memory_space=pltpu.VMEM)] * count


def in_smem(count):
    return [pl.BlockSpec(memory_space=pltpu.SMEM)] * count


def in_any(count):
    return [pl.BlockSpec(memory_space=pl.ANY)] * count


def shape(dims, kind):
    return jax.ShapeDtypeStruct(dims, kind)


def params(mib):
    return pltpu.CompilerParams(vmem_limit_bytes=mib * MIB)


def cost(flops, moved):
    return pl.CostEstimate(flops=flops, bytes_accessed=moved, transcendentals=0)


def sums_plan(tiles, contraction, row_tile, owner_map, panel):
    wide_count = lax.axis_size("wide")
    tile_dev, side = tiles.shape[0], tiles.shape[1]
    out_dev = owner_map.shape[0] // wide_count
    rows, columns = panel.shape
    shard = rows // side
    chunks = columns // CHUNK
    sums = owner_map.shape[0] // 2
    core = lax.axis_index("wide") % 2

    def to_core(v):
        return lax.ppermute(v, "wide", [(i, i ^ 1) for i in range(wide_count)])

    def to_grp(v, d):
        return lax.ppermute(v, "grp", [(i, i ^ d) for i in range(4)])

    def to_line(v, b):
        return lax.ppermute(v, "wide", [(i, i ^ (2 << b)) for i in range(wide_count)])


    own_index = jnp.concatenate([row_tile, contraction, owner_map])
    sib_index = to_core(own_index)
    sib_tiles = to_core(tiles)

    def own_half(source, j):
        return lax.dynamic_slice(source, (core * (rows // 2), j * CHUNK), (rows // 2, CHUNK))

    mines = [own_half(panel, j) for j in range(chunks)]
    ways = [None, (1, 2), (2, 1)]
    from_x, from_y = [to_grp(jnp.concatenate([mines[0], mines[d]], axis=1), d) for d in (1, 2)]
    firsts = [None, from_x, from_y]
    near = [from_x, from_y, to_grp(mines[0], 3)]

    half, quarter = sums // 2, sums // 4
    plain = shape((side, CHUNK), jnp.float32)

    def stack_of(count, one):
        return shape((count, *one.shape), one.dtype)

    def coded(count):
        return shape((count * side + CODE_ROWS, CHUNK), jnp.int16)

    order = jnp.zeros((1,), jnp.int32)
    last = None

    def in_order():
        return order if last is None else lax.optimization_barrier((order, last))[0]

    def call(body, name, outs, *args, smem=0, mib=16, extra=(), **more):
        nonlocal last
        done = pl.pallas_call(
            body,
            in_specs=more.pop("in_specs", in_any(1) + in_smem(smem) + in_vmem(len(args) - smem)),
            out_specs=more.pop("out_specs", in_vmem(len(outs))),
            out_shape=outs,
            scratch_shapes=list(extra),
            compiler_params=params(mib),
            cost_estimate=cost(0, sum(math.prod(a.shape) * a.dtype.itemsize for a in args)),
            name=name,
            **more,
        )(in_order(), *args)
        last = done[0]
        return done

    def places(operand, tiles_of, first):
        return [
            (operand, t, d * shard + first + i % part)
            for i, (t, d) in enumerate((t, d) for d, ts in tiles_of for t in ts)
        ]

    part = shard // 2

    def join(j):
        (joined,) = call(
            functools.partial(join_kernel, 0),
            "join",
            [shape((3 * rows // 2, CHUNK), panel.dtype)],
            *near,
        )
        tiles_of = [(d, range((d - 1) * part, d * part)) for d in (1, 2, 3)]
        fill = places(0, tiles_of, 0) + places(1, tiles_of, part)
        return fill, [joined, to_core(joined)]

    def pair(j):
        way, other = ways[j]
        (joined,) = call(
            functools.partial(join_kernel, CHUNK),
            "join",
            [shape((rows, CHUNK), panel.dtype)],
            mines[j],
            firsts[j],
        )
        second = to_grp(joined, other)
        in_first = [(way, range(part, 2 * part))]
        in_second = [(other, range(part)), (way ^ other, range(part, 2 * part))]
        fill = (
            places(0, in_first, 0)
            + places(1, in_first, part)
            + places(2, in_second, 0)
            + places(3, in_second, part)
        )
        return fill, [joined, to_core(joined), second]

    def products(j, which, sends, fill, parts):
        lists = counts, orders[which], slots[which], label
        *sends, stacked = call(
            functools.partial(sent_kernel, tuple(fill), j, which),
            "products_sent",
            [*sends, shape((4 * shard, side, CHUNK), panel.dtype)],
            *lists,
            held,
            panel,
            *parts,
            smem=4,
            extra=[pltpu.VMEM((half + 1, side, CHUNK), jnp.float32)],
            mib=24,
        )
        (kept,) = call(
            functools.partial(kept_kernel, which),
            "products_kept",
            [stack_of(half + 1, plain)],
            *lists,
            held,
            stacked,
            smem=4,
            mib=24,
        )
        return *sends, kept

    def gathered(done):
        return [done] + [to_grp(done, d) for d in (1, 2, 3)]

    def spread(j, blocks, result):
        earlier = [] if result is None else [result]
        return call(
            functools.partial(spread_kernel, j),
            "spread",
            [shape((out_dev * side, columns), jnp.float32)],
            *blocks,
            *earlier,
            in_specs=in_any(1) + in_vmem(4) + in_any(len(earlier)),
            out_specs=in_any(1),
            input_output_aliases={5: 0} if earlier else {},
            extra=[pltpu.VMEM((4, side, CHUNK), jnp.float32), pltpu.SemaphoreType.DMA((4,))],
        )[0]

    eighth = quarter // 2
    entries = shape((2 * tile_dev + UNROLL,), jnp.int32)
    twice = shape((2 * entries.shape[0],), jnp.int32)
    counts, in_plane, in_line, label, plane_order, line_order, held = call(
        hold_kernel,
        "hold",
        [shape((3,), jnp.int32)]
        + [entries] * 3
        + [twice] * 2
        + [pltpu.VMEM((2 * tile_dev + UNROLL, side, side), tiles.dtype)],
        own_index,
        sib_index,
        *[pltpu.with_memory_space_constraint(v, pltpu.HBM) for v in (tiles, sib_tiles)],
        in_specs=in_any(1) + in_smem(2) + in_any(2),
        out_specs=in_smem(6) + in_vmem(1),
        extra=[pltpu.SemaphoreType.DMA((2 * tile_dev,))],
        mib=8,
    )
    last = held
    slots, orders = {1: in_plane, 2: in_line}, {1: plane_order, 2: line_order}
    pairs = {j: pair(j) for j in (1, 2)}

    send, keep_0 = products(0, 2, [coded(half)], *join(0))
    sent_0 = send
    sent, keep = {}, {}
    for j in (1, 2):
        fill, (*parts, second) = pairs[j]
        second = lax.optimization_barrier((second, keep_0))[0]
        parts += [second, to_core(second)]
        send_a, send_b, keep[j] = products(j, 1, [coded(quarter)] * 2, fill, parts)
        sent[j] = send_a, send_b

    sent_0, keep_0 = call(
        line_kernel,
        "line",
        [coded(quarter), stack_of(quarter, plain)],
        to_line(sent_0, 0),
        keep_0,
    )

    def plane(j):
        return call(
            plane_kernel,
            "plane",
            [coded(eighth)] * 2 + [stack_of(quarter, plain)],
            to_grp(sent[j][0], 1),
            to_grp(sent[j][1], 2),
            keep[j],
        )

    def owner(j):
        return call(
            owner_kernel,
            "owner",
            [coded(eighth), stack_of(eighth, plain)],
            to_grp(sent[j][0], 2),
            to_grp(sent[j][1], 1),
            keep[j],
        )

    *sent[1], keep[1] = plane(1)
    *sent[2], keep[2] = plane(2)
    sent[1], keep[1] = owner(1)
    pair_of = [coded(2)] * 2
    own_a, own_b = call(rows_kernel, "rows", pair_of, to_line(sent_0, 1), keep_0)
    sent[2], keep[2] = owner(2)

    def line(j):
        return call(
            line_kernel,
            "line",
            [coded(1), stack_of(1, plain)],
            to_line(sent[j], 0),
            keep[j],
        )

    def finish(j):
        return call(finish_kernel, "finish", [coded(1)], to_line(sent[j], 1), keep[j])[0]

    sent[1], keep[1] = line(1)
    own_a, own_b = call(
        swap_kernel, "swap", pair_of, own_a, own_b, to_grp(own_a, 1), to_grp(own_b, 2)
    )
    done_1 = finish(1)
    sent[2], keep[2] = line(2)
    result = spread(0, [own_a, own_b, to_grp(own_a, 2), to_grp(own_b, 1)], None)
    done_2 = finish(2)
    result = spread(1, gathered(done_1), result)
    return spread(2, gathered(done_2), result)


def per_device(tiles, contraction, row_tile, owner_map, panel):
    dense = owner_map.shape[0] <= tiles.shape[0]
    wide_count = lax.axis_size("wide")
    fits = lax.axis_size("grp") == 4 and wide_count >= 4 and wide_count & (wide_count - 1) == 0
    out_dev = owner_map.shape[0] // wide_count
    if dense and fits and wide_count == 8 and out_dev == 4 and panel.shape[1] == 3 * CHUNK:
        return sums_plan(tiles, contraction, row_tile, owner_map, panel)
    return slots_plan(tiles, contraction, row_tile, owner_map, panel)


def solution(mesh):
    return jax.shard_map(
        per_device,
        mesh=mesh,
        in_specs=(
            P(("grp", "wide"), None, None),
            P(("grp", "wide")),
            P(("grp", "wide")),
            P(),
            P("grp", None),
        ),
        out_specs=P("wide", None),
        check_vma=False,
    )
```

```python
import functools
import math

import jax
import jax.numpy as jnp
from jax import lax
from jax.experimental import pallas as pl
from jax.experimental.pallas import tpu as pltpu
from jax.sharding import PartitionSpec as P

MIB = 1024 * 1024
CODE_ROWS = 16
CODE_STEPS = 256.0
TOP = 32000.0
CHUNK = 256
UNROLL = 8
LOG2 = math.log(2.0)


def place_slots(row_ids, owner_map, out_dev):
    table_ids = jnp.arange(owner_map.shape[0], dtype=jnp.int32)
    position = jnp.sum(jnp.where(row_ids[..., None] == table_ids, owner_map, 0), axis=-1)
    target = position // out_dev
    serial = jnp.arange(row_ids.shape[-1], dtype=jnp.int32)
    earlier = (target[..., :, None] == target[..., None, :]) & (serial[:, None] > serial[None, :])
    ranking = jnp.sum(earlier.astype(jnp.int32), axis=-1)
    return (position % out_dev, target, ranking)


def add_slot_products(summed, arrived, slot_labels, panel_tiles):
    slot_count = arrived.shape[0]
    block_rows = math.gcd(slot_count, 32)
    out_dev = summed.shape[0]
    local_ids = jnp.arange(out_dev, dtype=jnp.int32)

    def one_block(which_block, running, source_tiles, source_labels):
        part_tiles = lax.dynamic_slice_in_dim(source_tiles, which_block * block_rows, block_rows, 0)
        part_labels = lax.dynamic_slice_in_dim(
            source_labels, which_block * block_rows, block_rows, 0
        )
        chosen = jnp.take(panel_tiles, part_labels[:, 1], axis=0)
        products = jnp.einsum(
            "sab,sbc->sac", part_tiles, chosen, preferred_element_type=jnp.float32
        )
        row_hits = (part_labels[:, 0][:, None] == local_ids[None, :]).astype(jnp.float32)
        return running + jnp.einsum(
            "sr,sac->rac", row_hits, products, precision=lax.Precision.HIGHEST
        )

    return lax.fori_loop(
        0,
        slot_count // block_rows,
        lambda which_block, running: one_block(which_block, running, arrived, slot_labels),
        summed,
    )


def slots_plan(tiles, contraction, row_tile, owner_map, panel):
    wide_count = lax.axis_size("wide")
    tile_dev = tiles.shape[0]
    tile_side = tiles.shape[1]
    out_dev = owner_map.shape[0] // wide_count
    most_slots = tile_dev * 8 // (3 * wide_count)
    slot_total = wide_count * most_slots
    local_row, target, ranking = place_slots(row_tile, owner_map, out_dev)
    slot_index = target * most_slots + ranking
    outgoing = jnp.zeros((slot_total, tile_side, tile_side), tiles.dtype).at[slot_index].set(tiles)
    all_rows, all_contraction = (
        lax.all_gather(row_tile, "wide", axis=0, tiled=True),
        lax.all_gather(contraction, "wide", axis=0, tiled=True),
    )
    all_rows = all_rows.reshape(wide_count, tile_dev)
    all_contraction = all_contraction.reshape(wide_count, tile_dev)
    source_local, source_target, source_rank = place_slots(all_rows, owner_map, out_dev)
    source_ids = jnp.arange(wide_count, dtype=jnp.int32)
    mine = source_target == lax.axis_index("wide")
    arrive_index = jnp.where(mine, source_ids[:, None] * most_slots + source_rank, slot_total)
    label_pairs = jnp.stack([source_local, all_contraction], axis=-1).reshape(
        wide_count * tile_dev, 2
    )
    vacant_label = jnp.stack(
        [jnp.full((slot_total,), out_dev, jnp.int32), jnp.zeros((slot_total,), jnp.int32)], axis=1
    )
    arrived_labels = vacant_label.at[arrive_index.reshape(-1)].set(label_pairs, mode="drop")
    gathered = lax.all_gather(panel, "grp", axis=0, tiled=True)
    panel_tiles = gathered.reshape(gathered.shape[0] // tile_side, tile_side, gathered.shape[1])
    summed = jnp.zeros((out_dev, tile_side, gathered.shape[1]), jnp.float32)
    arrived = lax.all_to_all(outgoing, "wide", split_axis=0, concat_axis=0, tiled=True)
    summed = add_slot_products(summed, arrived, arrived_labels, panel_tiles)
    summed = lax.psum(summed, "grp")
    return summed.reshape(out_dev * tile_side, gathered.shape[1])


def encode(value):
    largest = jnp.max(jnp.abs(value), axis=0, keepdims=True)
    code = jnp.ceil(jnp.log(jnp.maximum(largest, 1e-30)) * (CODE_STEPS / LOG2))
    scale = jnp.exp(code * (-LOG2 / CODE_STEPS)) * TOP
    whole = jnp.round(value * scale).astype(jnp.int32).astype(jnp.int16)
    return whole, code.astype(jnp.int32)


def put_coded(ref, values):
    codes = []
    for value in values:
        side = value.shape[0]
        whole, code = encode(value)
        ref[pl.ds(len(codes) * side, side), :] = whole
        codes.append(code)
    end = len(codes) * side
    codes += [jnp.zeros_like(codes[0])] * (CODE_ROWS - len(codes))
    ref[pl.ds(end, CODE_ROWS), :] = jnp.concatenate(codes, axis=0).astype(jnp.int16)


class Decoded:
    def __init__(self, ref, side):
        self.ref, self.side = ref, side
        self.count = (ref.shape[0] - CODE_ROWS) // side
        code = ref[pl.ds(self.count * side, CODE_ROWS), :].astype(jnp.int32)
        self.scales = jnp.exp(code.astype(jnp.float32) * (LOG2 / CODE_STEPS)) * (1.0 / TOP)

    def tile(self, i):
        return self.part(i * self.side, self.scales[i : i + 1])

    def either(self, bit, zero, one):
        at = pl.multiple_of(jnp.where(bit == 1, one, zero) * self.side, self.side)
        scales = self.scales
        return self.part(at, jnp.where(bit == 1, scales[one : one + 1], scales[zero : zero + 1]))

    def part(self, at, scale):
        return self.ref[pl.ds(at, self.side), :].astype(jnp.int32).astype(jnp.float32) * scale


def here():
    g, w = lax.axis_index("grp"), lax.axis_index("wide")
    return g % 2, g // 2, (w // 2) % 2, w // 4


def hold_kernel(
    order, own_ref, sib_ref, own_tiles, sib_tiles,
    count_ref, plane_ref, line_ref, label_ref, plane_order, line_order, out, sems,
):
    tile_dev = own_tiles.shape[0]
    sums = (own_ref.shape[0] - 2 * tile_dev) // 2
    shard, out_dev = 4, 4
    room = 2 * tile_dev + UNROLL
    x, y, z_low, _ = here()
    g, core = lax.axis_index("grp"), lax.axis_index("wide") % 2

    def copy(tiles, which, at):
        return pltpu.make_async_copy(tiles.at[which], out.at[at], sems.at[at])

    def scan(tiles, index_ref, counts):
        def one(i, counts):
            position = own_ref[2 * tile_dev + index_ref[i]]
            k = index_ref[tile_dev + i]
            owner, local = lax.div(position, out_dev), lax.rem(position, out_dev)
            match = lax.rem(owner, 2) == core

            odd, to_z = lax.rem(lax.div(owner, 2), 2), lax.div(owner, 4)
            bit_x, bit_y = lax.rem(local, 2), lax.div(local, 2)
            kept = [
                jnp.where(odd == 1, bit_y == y, bit_x == x),
                odd == z_low,
            ]

            @pl.when(match)
            def _():
                copy(tiles, i, counts[0]).start()
                second = jnp.where(odd == 1, bit_x, bit_y)
                places = [odd * (sums // 4) + 2 * to_z + second, to_z * out_dev + local]
                for ref, order_ref, keep, place, sent in (
                    (plane_ref, plane_order, kept[0], places[0], counts[1]),
                    (line_ref, line_order, kept[1], places[1], counts[2]),
                ):
                    ref[counts[0]] = place
                    order_ref[jnp.where(keep, room + counts[0] - sent, sent)] = counts[0]
                apart, inner = lax.div(k, shard) ^ g, lax.rem(k, shard)
                half = shard // 2
                crossed = jnp.where(lax.div(inner, half) == core, 0, half) + lax.rem(inner, half)
                label_ref[counts[0]] = jnp.where(apart == 0, inner, apart * shard + crossed)

            more = [match, match & ~kept[0], match & ~kept[1]]
            return tuple(c + m.astype(jnp.int32) for c, m in zip(counts, more))

        return lax.fori_loop(0, tile_dev, one, counts)

    counts = scan(own_tiles, own_ref, (0, 0, 0))
    counts = scan(sib_tiles, sib_ref, counts)
    count = counts[0]
    for i in range(3):
        count_ref[i] = counts[i]
    spare = 2 * tile_dev
    plane_ref[spare] = sums // 2
    line_ref[spare] = sums // 2
    label_ref[spare] = 0
    for order_ref, sent in ((plane_order, counts[1]), (line_order, counts[2])):
        for i in range(UNROLL):
            order_ref[sent + i] = spare
            order_ref[room + count - sent + i] = spare

    @pl.loop(0, count)
    def _(i):
        copy(own_tiles, 0, i).wait()


def join_kernel(first, order, *refs):
    *parts, out = refs
    at, width = 0, out.shape[1]
    for part in parts:
        column = first if part.shape[1] > width else 0
        out[pl.ds(at, part.shape[0]), :] = part[:, pl.ds(column, width)]
        at += part.shape[0]


def add_products(count, first, order_ref, slot_ref, label_ref, tiles, stack, sums):
    @pl.loop(0, sums.shape[0])
    def _(i):
        sums[i] = jnp.zeros(sums.shape[1:], jnp.float32)

    @pl.loop(0, lax.div(count + UNROLL - 1, UNROLL))
    def _(i):
        entries = [order_ref[first + i * UNROLL + u] for u in range(UNROLL)]
        found = [
            jnp.dot(tiles[e], stack[label_ref[e]], preferred_element_type=jnp.float32)
            for e in entries
        ]
        for e, product in zip(entries, found):
            sums[slot_ref[e]] += product


def sent_kernel(
    fill, chunk, which, order, count_ref, order_ref, slot_ref, label_ref,
    tiles, own_panel, *refs
):
    parts = refs[: 1 + max(part for part, _, _ in fill)]
    *sends, stack, sums = refs[len(parts) :]
    side, width = stack.shape[1:]
    for t in range(own_panel.shape[0] // side):
        stack[t] = own_panel[pl.ds(t * side, side), pl.ds(chunk * width, width)]
    for part, t, at in fill:
        stack[at] = parts[part][pl.ds(t * side, side), :]
    add_products(count_ref[which], 0, order_ref, slot_ref, label_ref, tiles, stack, sums)
    sent = 0
    for send in sends:
        count = (send.shape[0] - CODE_ROWS) // side
        put_coded(send, (sums[sent + i] for i in range(count)))
        sent += count


def kept_kernel(which, order, count_ref, order_ref, slot_ref, label_ref, tiles, stack, sums):
    count = count_ref[0] - count_ref[which]
    room = tiles.shape[0]
    add_products(count, room, order_ref, slot_ref, label_ref, tiles, stack, sums)


def plane_kernel(order, recv_a, recv_b, kept, send_a, send_b, keep):
    side, half = kept.shape[1], keep.shape[0] // 2
    x, y, _, _ = here()
    for base, bit, recv, send in ((0, y, recv_a, send_a), (1, x, recv_b, send_b)):
        came = Decoded(recv, side)

        def total(i, which, base=base, came=came):
            return kept[2 * half * base + 2 * i + which] + came.either(which, 2 * i, 2 * i + 1)

        put_coded(send, (total(i, 1 - bit) for i in range(half)))
        for i in range(half):
            keep[base * half + i] = total(i, bit)


def owner_kernel(order, recv_a, recv_b, kept, send, keep):
    side, half = kept.shape[1], keep.shape[0]
    odd = here()[2]
    came_a, came_b = Decoded(recv_a, side), Decoded(recv_b, side)

    def to_send():
        for i in range(half):
            value_a = kept[i] + came_a.tile(i)
            value_b = kept[half + i] + came_b.tile(i)
            keep[i] = jnp.where(odd == 1, value_b, value_a)
            yield jnp.where(odd == 1, value_a, value_b)

    put_coded(send, to_send())


def line_kernel(order, recv, kept, send, keep):
    side, half = kept.shape[1], keep.shape[0]
    bit = here()[3]
    came = Decoded(recv, side)

    def total(i, which):
        return kept[which * half + i] + came.either(which, i, half + i)

    put_coded(send, (total(i, 1 - bit) for i in range(half)))
    for i in range(half):
        keep[i] = total(i, bit)


def rows_kernel(order, recv, kept, send_a, send_b):
    came = Decoded(recv, kept.shape[1])
    half = came.count // 2
    put_coded(send_a, (kept[i] + came.tile(i) for i in range(half)))
    put_coded(send_b, (kept[half + i] + came.tile(half + i) for i in range(half)))


def swap_kernel(order, own_a, own_b, recv_a, recv_b, send_a, send_b):
    side = (own_a.shape[0] - CODE_ROWS) // 2
    for own, recv, send in ((own_a, recv_a, send_a), (own_b, recv_b, send_b)):
        here_, there = Decoded(own, side), Decoded(recv, side)
        put_coded(send, (here_.tile(i) + there.tile(i) for i in range(2)))


def finish_kernel(order, recv, kept, out):
    put_coded(out, [kept[0] + Decoded(recv, kept.shape[1]).tile(0)])


def spread_kernel(chunk, order, *refs):
    blocks, (out, rows, sems) = refs[:4], refs[-3:]
    side, width = rows.shape[1:]
    x, y, _, _ = here()
    blocks = [Decoded(block, side) for block in blocks]
    copies = []
    for i in range(4):
        if blocks[0].count == 2:
            rows[i] = blocks[i // 2].tile(i % 2) + blocks[2 + i // 2].tile(i % 2)
            at = i * side
        else:
            rows[i] = blocks[i].tile(0)
            at = pl.multiple_of(((2 * y + x) ^ i) * side, side)
        copies.append(
            pltpu.make_async_copy(
                rows.at[i], out.at[pl.ds(at, side), pl.ds(chunk * width, width)], sems.at[i]
            )
        )
        copies[-1].start()
    for copy in copies:
        copy.wait()


def in_vmem(count):
    return [pl.BlockSpec(memory_space=pltpu.VMEM)] * count


def in_smem(count):
    return [pl.BlockSpec(memory_space=pltpu.SMEM)] * count


def in_any(count):
    return [pl.BlockSpec(memory_space=pl.ANY)] * count


def shape(dims, kind):
    return jax.ShapeDtypeStruct(dims, kind)


def params(mib):
    return pltpu.CompilerParams(vmem_limit_bytes=mib * MIB)


def cost(flops, moved):
    return pl.CostEstimate(flops=flops, bytes_accessed=moved, transcendentals=0)


def sums_plan(tiles, contraction, row_tile, owner_map, panel):
    wide_count = lax.axis_size("wide")
    tile_dev, side = tiles.shape[0], tiles.shape[1]
    out_dev = owner_map.shape[0] // wide_count
    rows, columns = panel.shape
    shard = rows // side
    chunks = columns // CHUNK
    sums = owner_map.shape[0] // 2
    core = lax.axis_index("wide") % 2

    def to_core(v):
        return lax.ppermute(v, "wide", [(i, i ^ 1) for i in range(wide_count)])

    def to_grp(v, d):
        return lax.ppermute(v, "grp", [(i, i ^ d) for i in range(4)])

    def to_line(v, b):
        return lax.ppermute(v, "wide", [(i, i ^ (2 << b)) for i in range(wide_count)])


    own_index = jnp.concatenate([row_tile, contraction, owner_map])
    sib_index = to_core(own_index)
    sib_tiles = to_core(tiles)

    def own_half(source, j):
        return lax.dynamic_slice(source, (core * (rows // 2), j * CHUNK), (rows // 2, CHUNK))

    mines = [own_half(panel, j) for j in range(chunks)]
    ways = [None, (1, 2), (2, 1)]
    from_x, from_y = [to_grp(jnp.concatenate([mines[0], mines[d]], axis=1), d) for d in (1, 2)]
    firsts = [None, from_x, from_y]
    near = [from_x, from_y, to_grp(mines[0], 3)]

    half, quarter = sums // 2, sums // 4
    plain = shape((side, CHUNK), jnp.float32)

    def stack_of(count, one):
        return shape((count, *one.shape), one.dtype)

    def coded(count):
        return shape((count * side + CODE_ROWS, CHUNK), jnp.int16)

    order = jnp.zeros((1,), jnp.int32)
    last = None

    def in_order():
        return order if last is None else lax.optimization_barrier((order, last))[0]

    def call(body, name, outs, *args, smem=0, mib=16, extra=(), **more):
        nonlocal last
        done = pl.pallas_call(
            body,
            in_specs=more.pop("in_specs", in_any(1) + in_smem(smem) + in_vmem(len(args) - smem)),
            out_specs=more.pop("out_specs", in_vmem(len(outs))),
            out_shape=outs,
            scratch_shapes=list(extra),
            compiler_params=params(mib),
            cost_estimate=cost(0, sum(math.prod(a.shape) * a.dtype.itemsize for a in args)),
            name=name,
            **more,
        )(in_order(), *args)
        last = done[0]
        return done

    def places(operand, tiles_of, first):
        return [
            (operand, t, d * shard + first + i % part)
            for i, (t, d) in enumerate((t, d) for d, ts in tiles_of for t in ts)
        ]

    part = shard // 2

    def join(j):
        (joined,) = call(
            functools.partial(join_kernel, 0),
            "join",
            [shape((3 * rows // 2, CHUNK), panel.dtype)],
            *near,
        )
        tiles_of = [(d, range((d - 1) * part, d * part)) for d in (1, 2, 3)]
        fill = places(0, tiles_of, 0) + places(1, tiles_of, part)
        return fill, [joined, to_core(joined)]

    def pair(j):
        way, other = ways[j]
        (joined,) = call(
            functools.partial(join_kernel, CHUNK),
            "join",
            [shape((rows, CHUNK), panel.dtype)],
            mines[j],
            firsts[j],
        )
        second = to_grp(joined, other)
        in_first = [(way, range(part, 2 * part))]
        in_second = [(other, range(part)), (way ^ other, range(part, 2 * part))]
        fill = (
            places(0, in_first, 0)
            + places(1, in_first, part)
            + places(2, in_second, 0)
            + places(3, in_second, part)
        )
        return fill, [joined, to_core(joined), second]

    def products(j, which, sends, fill, parts):
        lists = counts, orders[which], slots[which], label
        *sends, stacked = call(
            functools.partial(sent_kernel, tuple(fill), j, which),
            "products_sent",
            [*sends, shape((4 * shard, side, CHUNK), panel.dtype)],
            *lists,
            held,
            panel,
            *parts,
            smem=4,
            extra=[pltpu.VMEM((half + 1, side, CHUNK), jnp.float32)],
            mib=24,
        )
        (kept,) = call(
            functools.partial(kept_kernel, which),
            "products_kept",
            [stack_of(half + 1, plain)],
            *lists,
            held,
            stacked,
            smem=4,
            mib=24,
        )
        return *sends, kept

    def gathered(done):
        return [done] + [to_grp(done, d) for d in (1, 2, 3)]

    def spread(j, blocks, result):
        earlier = [] if result is None else [result]
        return call(
            functools.partial(spread_kernel, j),
            "spread",
            [shape((out_dev * side, columns), jnp.float32)],
            *blocks,
            *earlier,
            in_specs=in_any(1) + in_vmem(4) + in_any(len(earlier)),
            out_specs=in_any(1),
            input_output_aliases={5: 0} if earlier else {},
            extra=[pltpu.VMEM((4, side, CHUNK), jnp.float32), pltpu.SemaphoreType.DMA((4,))],
        )[0]

    eighth = quarter // 2
    entries = shape((2 * tile_dev + UNROLL,), jnp.int32)
    twice = shape((2 * entries.shape[0],), jnp.int32)
    counts, in_plane, in_line, label, plane_order, line_order, held = call(
        hold_kernel,
        "hold",
        [shape((3,), jnp.int32)]
        + [entries] * 3
        + [twice] * 2
        + [pltpu.VMEM((2 * tile_dev + UNROLL, side, side), tiles.dtype)],
        own_index,
        sib_index,
        *[pltpu.with_memory_space_constraint(v, pltpu.HBM) for v in (tiles, sib_tiles)],
        in_specs=in_any(1) + in_smem(2) + in_any(2),
        out_specs=in_smem(6) + in_vmem(1),
        extra=[pltpu.SemaphoreType.DMA((2 * tile_dev,))],
        mib=8,
    )
    last = held
    slots, orders = {1: in_plane, 2: in_line}, {1: plane_order, 2: line_order}
    pairs = {j: pair(j) for j in (1, 2)}

    send, keep_0 = products(0, 2, [coded(half)], *join(0))
    sent_0 = send
    sent, keep = {}, {}
    for j in (1, 2):
        fill, (*parts, second) = pairs[j]
        second = lax.optimization_barrier((second, keep_0))[0]
        parts += [second, to_core(second)]
        send_a, send_b, keep[j] = products(j, 1, [coded(quarter)] * 2, fill, parts)
        sent[j] = send_a, send_b

    sent_0, keep_0 = call(
        line_kernel,
        "line",
        [coded(quarter), stack_of(quarter, plain)],
        to_line(sent_0, 0),
        keep_0,
    )

    def plane(j):
        return call(
            plane_kernel,
            "plane",
            [coded(eighth)] * 2 + [stack_of(quarter, plain)],
            to_grp(sent[j][0], 1),
            to_grp(sent[j][1], 2),
            keep[j],
        )

    def owner(j):
        return call(
            owner_kernel,
            "owner",
            [coded(eighth), stack_of(eighth, plain)],
            to_grp(sent[j][0], 2),
            to_grp(sent[j][1], 1),
            keep[j],
        )

    *sent[1], keep[1] = plane(1)
    *sent[2], keep[2] = plane(2)
    sent[1], keep[1] = owner(1)
    pair_of = [coded(2)] * 2
    own_a, own_b = call(rows_kernel, "rows", pair_of, to_line(sent_0, 1), keep_0)
    sent[2], keep[2] = owner(2)

    def line(j):
        return call(
            line_kernel,
            "line",
            [coded(1), stack_of(1, plain)],
            to_line(sent[j], 0),
            keep[j],
        )

    def finish(j):
        return call(finish_kernel, "finish", [coded(1)], to_line(sent[j], 1), keep[j])[0]

    sent[1], keep[1] = line(1)
    own_a, own_b = call(
        swap_kernel, "swap", pair_of, own_a, own_b, to_grp(own_a, 1), to_grp(own_b, 2)
    )
    sent[2], keep[2] = line(2)
    done_1 = finish(1)
    result = spread(0, [own_a, own_b, to_grp(own_a, 2), to_grp(own_b, 1)], None)
    done_2 = finish(2)
    result = spread(1, gathered(done_1), result)
    return spread(2, gathered(done_2), result)


def per_device(tiles, contraction, row_tile, owner_map, panel):
    dense = owner_map.shape[0] <= tiles.shape[0]
    wide_count = lax.axis_size("wide")
    fits = lax.axis_size("grp") == 4 and wide_count >= 4 and wide_count & (wide_count - 1) == 0
    out_dev = owner_map.shape[0] // wide_count
    if dense and fits and wide_count == 8 and out_dev == 4 and panel.shape[1] == 3 * CHUNK:
        return sums_plan(tiles, contraction, row_tile, owner_map, panel)
    return slots_plan(tiles, contraction, row_tile, owner_map, panel)


def solution(mesh):
    return jax.shard_map(
        per_device,
        mesh=mesh,
        in_specs=(
            P(("grp", "wide"), None, None),
            P(("grp", "wide")),
            P(("grp", "wide")),
            P(),
            P("grp", None),
        ),
        out_specs=P("wide", None),
        check_vma=False,
    )
```

```python
import functools
import math

import jax
import jax.numpy as jnp
from jax import lax
from jax.experimental import pallas as pl
from jax.experimental.pallas import tpu as pltpu
from jax.sharding import PartitionSpec as P

MIB = 1024 * 1024
CODE_ROWS = 16
CODE_STEPS = 256.0
TOP = 32000.0
CHUNK = 256
UNROLL = 8
LOG2 = math.log(2.0)


def place_slots(row_ids, owner_map, out_dev):
    table_ids = jnp.arange(owner_map.shape[0], dtype=jnp.int32)
    position = jnp.sum(jnp.where(row_ids[..., None] == table_ids, owner_map, 0), axis=-1)
    target = position // out_dev
    serial = jnp.arange(row_ids.shape[-1], dtype=jnp.int32)
    earlier = (target[..., :, None] == target[..., None, :]) & (serial[:, None] > serial[None, :])
    ranking = jnp.sum(earlier.astype(jnp.int32), axis=-1)
    return (position % out_dev, target, ranking)


def add_slot_products(summed, arrived, slot_labels, panel_tiles):
    slot_count = arrived.shape[0]
    block_rows = math.gcd(slot_count, 32)
    out_dev = summed.shape[0]
    local_ids = jnp.arange(out_dev, dtype=jnp.int32)

    def one_block(which_block, running, source_tiles, source_labels):
        part_tiles = lax.dynamic_slice_in_dim(source_tiles, which_block * block_rows, block_rows, 0)
        part_labels = lax.dynamic_slice_in_dim(
            source_labels, which_block * block_rows, block_rows, 0
        )
        chosen = jnp.take(panel_tiles, part_labels[:, 1], axis=0)
        products = jnp.einsum(
            "sab,sbc->sac", part_tiles, chosen, preferred_element_type=jnp.float32
        )
        row_hits = (part_labels[:, 0][:, None] == local_ids[None, :]).astype(jnp.float32)
        return running + jnp.einsum(
            "sr,sac->rac", row_hits, products, precision=lax.Precision.HIGHEST
        )

    return lax.fori_loop(
        0,
        slot_count // block_rows,
        lambda which_block, running: one_block(which_block, running, arrived, slot_labels),
        summed,
    )


def slots_plan(tiles, contraction, row_tile, owner_map, panel):
    wide_count = lax.axis_size("wide")
    tile_dev = tiles.shape[0]
    tile_side = tiles.shape[1]
    out_dev = owner_map.shape[0] // wide_count
    most_slots = tile_dev * 8 // (3 * wide_count)
    slot_total = wide_count * most_slots
    local_row, target, ranking = place_slots(row_tile, owner_map, out_dev)
    slot_index = target * most_slots + ranking
    outgoing = jnp.zeros((slot_total, tile_side, tile_side), tiles.dtype).at[slot_index].set(tiles)
    all_rows, all_contraction = (
        lax.all_gather(row_tile, "wide", axis=0, tiled=True),
        lax.all_gather(contraction, "wide", axis=0, tiled=True),
    )
    all_rows = all_rows.reshape(wide_count, tile_dev)
    all_contraction = all_contraction.reshape(wide_count, tile_dev)
    source_local, source_target, source_rank = place_slots(all_rows, owner_map, out_dev)
    source_ids = jnp.arange(wide_count, dtype=jnp.int32)
    mine = source_target == lax.axis_index("wide")
    arrive_index = jnp.where(mine, source_ids[:, None] * most_slots + source_rank, slot_total)
    label_pairs = jnp.stack([source_local, all_contraction], axis=-1).reshape(
        wide_count * tile_dev, 2
    )
    vacant_label = jnp.stack(
        [jnp.full((slot_total,), out_dev, jnp.int32), jnp.zeros((slot_total,), jnp.int32)], axis=1
    )
    arrived_labels = vacant_label.at[arrive_index.reshape(-1)].set(label_pairs, mode="drop")
    gathered = lax.all_gather(panel, "grp", axis=0, tiled=True)
    panel_tiles = gathered.reshape(gathered.shape[0] // tile_side, tile_side, gathered.shape[1])
    summed = jnp.zeros((out_dev, tile_side, gathered.shape[1]), jnp.float32)
    arrived = lax.all_to_all(outgoing, "wide", split_axis=0, concat_axis=0, tiled=True)
    summed = add_slot_products(summed, arrived, arrived_labels, panel_tiles)
    summed = lax.psum(summed, "grp")
    return summed.reshape(out_dev * tile_side, gathered.shape[1])


def encode(value):
    largest = jnp.max(jnp.abs(value), axis=0, keepdims=True)
    code = jnp.ceil(jnp.log(jnp.maximum(largest, 1e-30)) * (CODE_STEPS / LOG2))
    scale = jnp.exp(code * (-LOG2 / CODE_STEPS)) * TOP
    whole = jnp.round(value * scale).astype(jnp.int32).astype(jnp.int16)
    return whole, code.astype(jnp.int32)


def put_coded(ref, values):
    codes = []
    for value in values:
        side = value.shape[0]
        whole, code = encode(value)
        ref[pl.ds(len(codes) * side, side), :] = whole
        codes.append(code)
    end = len(codes) * side
    codes += [jnp.zeros_like(codes[0])] * (CODE_ROWS - len(codes))
    ref[pl.ds(end, CODE_ROWS), :] = jnp.concatenate(codes, axis=0).astype(jnp.int16)


class Decoded:
    def __init__(self, ref, side):
        self.ref, self.side = ref, side
        self.count = (ref.shape[0] - CODE_ROWS) // side
        code = ref[pl.ds(self.count * side, CODE_ROWS), :].astype(jnp.int32)
        self.scales = jnp.exp(code.astype(jnp.float32) * (LOG2 / CODE_STEPS)) * (1.0 / TOP)

    def tile(self, i):
        return self.part(i * self.side, self.scales[i : i + 1])

    def either(self, bit, zero, one):
        at = pl.multiple_of(jnp.where(bit == 1, one, zero) * self.side, self.side)
        scales = self.scales
        return self.part(at, jnp.where(bit == 1, scales[one : one + 1], scales[zero : zero + 1]))

    def part(self, at, scale):
        return self.ref[pl.ds(at, self.side), :].astype(jnp.int32).astype(jnp.float32) * scale


def here():
    g, w = lax.axis_index("grp"), lax.axis_index("wide")
    return g % 2, g // 2, (w // 2) % 2, w // 4


def hold_kernel(
    order, own_ref, sib_ref, own_tiles, sib_tiles,
    count_ref, plane_ref, line_ref, label_ref, plane_order, line_order, out, sems,
):
    tile_dev = own_tiles.shape[0]
    sums = (own_ref.shape[0] - 2 * tile_dev) // 2
    shard, out_dev = 4, 4
    room = 2 * tile_dev + UNROLL
    x, y, z_low, _ = here()
    g, core = lax.axis_index("grp"), lax.axis_index("wide") % 2

    def copy(tiles, which, at):
        return pltpu.make_async_copy(tiles.at[which], out.at[at], sems.at[at])

    def scan(tiles, index_ref, counts):
        def one(i, counts):
            position = own_ref[2 * tile_dev + index_ref[i]]
            k = index_ref[tile_dev + i]
            owner, local = lax.div(position, out_dev), lax.rem(position, out_dev)
            match = lax.rem(owner, 2) == core

            odd, to_z = lax.rem(lax.div(owner, 2), 2), lax.div(owner, 4)
            bit_x, bit_y = lax.rem(local, 2), lax.div(local, 2)
            kept = [
                jnp.where(odd == 1, bit_y == y, bit_x == x),
                odd == z_low,
            ]

            @pl.when(match)
            def _():
                copy(tiles, i, counts[0]).start()
                second = jnp.where(odd == 1, bit_x, bit_y)
                places = [odd * (sums // 4) + 2 * to_z + second, to_z * out_dev + local]
                for ref, order_ref, keep, place, sent in (
                    (plane_ref, plane_order, kept[0], places[0], counts[1]),
                    (line_ref, line_order, kept[1], places[1], counts[2]),
                ):
                    ref[counts[0]] = place
                    order_ref[jnp.where(keep, room + counts[0] - sent, sent)] = counts[0]
                apart, inner = lax.div(k, shard) ^ g, lax.rem(k, shard)
                half = shard // 2
                crossed = jnp.where(lax.div(inner, half) == core, 0, half) + lax.rem(inner, half)
                label_ref[counts[0]] = jnp.where(apart == 0, inner, apart * shard + crossed)

            more = [match, match & ~kept[0], match & ~kept[1]]
            return tuple(c + m.astype(jnp.int32) for c, m in zip(counts, more))

        return lax.fori_loop(0, tile_dev, one, counts)

    counts = scan(own_tiles, own_ref, (0, 0, 0))
    counts = scan(sib_tiles, sib_ref, counts)
    count = counts[0]
    for i in range(3):
        count_ref[i] = counts[i]
    spare = 2 * tile_dev
    plane_ref[spare] = sums // 2
    line_ref[spare] = sums // 2
    label_ref[spare] = 0
    for order_ref, sent in ((plane_order, counts[1]), (line_order, counts[2])):
        for i in range(UNROLL):
            order_ref[sent + i] = spare
            order_ref[room + count - sent + i] = spare

    @pl.loop(0, count)
    def _(i):
        copy(own_tiles, 0, i).wait()


def join_kernel(first, order, *refs):
    *parts, out = refs
    at, width = 0, out.shape[1]
    for part in parts:
        column = first if part.shape[1] > width else 0
        out[pl.ds(at, part.shape[0]), :] = part[:, pl.ds(column, width)]
        at += part.shape[0]


def add_products(count, first, order_ref, slot_ref, label_ref, tiles, stack, sums):
    @pl.loop(0, sums.shape[0])
    def _(i):
        sums[i] = jnp.zeros(sums.shape[1:], jnp.float32)

    @pl.loop(0, lax.div(count + UNROLL - 1, UNROLL))
    def _(i):
        entries = [order_ref[first + i * UNROLL + u] for u in range(UNROLL)]
        found = [
            jnp.dot(tiles[e], stack[label_ref[e]], preferred_element_type=jnp.float32)
            for e in entries
        ]
        for e, product in zip(entries, found):
            sums[slot_ref[e]] += product


def sent_kernel(
    fill, chunk, which, order, count_ref, order_ref, slot_ref, label_ref,
    tiles, own_panel, *refs
):
    parts = refs[: 1 + max(part for part, _, _ in fill)]
    *sends, stack, sums = refs[len(parts) :]
    side, width = stack.shape[1:]
    for t in range(own_panel.shape[0] // side):
        stack[t] = own_panel[pl.ds(t * side, side), pl.ds(chunk * width, width)]
    for part, t, at in fill:
        stack[at] = parts[part][pl.ds(t * side, side), :]
    add_products(count_ref[which], 0, order_ref, slot_ref, label_ref, tiles, stack, sums)
    sent = 0
    for send in sends:
        count = (send.shape[0] - CODE_ROWS) // side
        put_coded(send, (sums[sent + i] for i in range(count)))
        sent += count


def kept_kernel(which, order, count_ref, order_ref, slot_ref, label_ref, tiles, stack, sums):
    count = count_ref[0] - count_ref[which]
    room = tiles.shape[0]
    add_products(count, room, order_ref, slot_ref, label_ref, tiles, stack, sums)


def plane_kernel(order, recv_a, recv_b, kept, send_a, send_b, keep):
    side, half = kept.shape[1], keep.shape[0] // 2
    x, y, _, _ = here()
    for base, bit, recv, send in ((0, y, recv_a, send_a), (1, x, recv_b, send_b)):
        came = Decoded(recv, side)

        def total(i, which, base=base, came=came):
            return kept[2 * half * base + 2 * i + which] + came.either(which, 2 * i, 2 * i + 1)

        put_coded(send, (total(i, 1 - bit) for i in range(half)))
        for i in range(half):
            keep[base * half + i] = total(i, bit)


def owner_kernel(order, recv_a, recv_b, kept, send, keep):
    side, half = kept.shape[1], keep.shape[0]
    odd = here()[2]
    came_a, came_b = Decoded(recv_a, side), Decoded(recv_b, side)

    def to_send():
        for i in range(half):
            value_a = kept[i] + came_a.tile(i)
            value_b = kept[half + i] + came_b.tile(i)
            keep[i] = jnp.where(odd == 1, value_b, value_a)
            yield jnp.where(odd == 1, value_a, value_b)

    put_coded(send, to_send())


def line_kernel(order, recv, kept, send, keep):
    side, half = kept.shape[1], keep.shape[0]
    bit = here()[3]
    came = Decoded(recv, side)

    def total(i, which):
        return kept[which * half + i] + came.either(which, i, half + i)

    put_coded(send, (total(i, 1 - bit) for i in range(half)))
    for i in range(half):
        keep[i] = total(i, bit)


def rows_kernel(order, recv, kept, send_a, send_b):
    came = Decoded(recv, kept.shape[1])
    half = came.count // 2
    put_coded(send_a, (kept[i] + came.tile(i) for i in range(half)))
    put_coded(send_b, (kept[half + i] + came.tile(half + i) for i in range(half)))


def swap_kernel(order, own_a, own_b, recv_a, recv_b, send_a, send_b):
    side = (own_a.shape[0] - CODE_ROWS) // 2
    for own, recv, send in ((own_a, recv_a, send_a), (own_b, recv_b, send_b)):
        here_, there = Decoded(own, side), Decoded(recv, side)
        put_coded(send, (here_.tile(i) + there.tile(i) for i in range(2)))


def finish_kernel(order, recv, kept, out):
    put_coded(out, [kept[0] + Decoded(recv, kept.shape[1]).tile(0)])


def spread_kernel(chunk, order, *refs):
    blocks, (out, rows, sems) = refs[:4], refs[-3:]
    side, width = rows.shape[1:]
    x, y, _, _ = here()
    blocks = [Decoded(block, side) for block in blocks]
    copies = []
    for i in range(4):
        if blocks[0].count == 2:
            rows[i] = blocks[i // 2].tile(i % 2) + blocks[2 + i // 2].tile(i % 2)
            at = i * side
        else:
            rows[i] = blocks[i].tile(0)
            at = pl.multiple_of(((2 * y + x) ^ i) * side, side)
        copies.append(
            pltpu.make_async_copy(
                rows.at[i], out.at[pl.ds(at, side), pl.ds(chunk * width, width)], sems.at[i]
            )
        )
        copies[-1].start()
    for copy in copies:
        copy.wait()


def in_vmem(count):
    return [pl.BlockSpec(memory_space=pltpu.VMEM)] * count


def in_smem(count):
    return [pl.BlockSpec(memory_space=pltpu.SMEM)] * count


def in_any(count):
    return [pl.BlockSpec(memory_space=pl.ANY)] * count


def shape(dims, kind):
    return jax.ShapeDtypeStruct(dims, kind)


def params(mib):
    return pltpu.CompilerParams(vmem_limit_bytes=mib * MIB)


def cost(flops, moved):
    return pl.CostEstimate(flops=flops, bytes_accessed=moved, transcendentals=0)


def sums_plan(tiles, contraction, row_tile, owner_map, panel):
    wide_count = lax.axis_size("wide")
    tile_dev, side = tiles.shape[0], tiles.shape[1]
    out_dev = owner_map.shape[0] // wide_count
    rows, columns = panel.shape
    shard = rows // side
    chunks = columns // CHUNK
    sums = owner_map.shape[0] // 2
    core = lax.axis_index("wide") % 2

    def to_core(v):
        return lax.ppermute(v, "wide", [(i, i ^ 1) for i in range(wide_count)])

    def to_grp(v, d):
        return lax.ppermute(v, "grp", [(i, i ^ d) for i in range(4)])

    def to_line(v, b):
        return lax.ppermute(v, "wide", [(i, i ^ (2 << b)) for i in range(wide_count)])


    own_index = jnp.concatenate([row_tile, contraction, owner_map])
    sib_index = to_core(own_index)
    sib_tiles = to_core(tiles)

    def own_half(source, j):
        return lax.dynamic_slice(source, (core * (rows // 2), j * CHUNK), (rows // 2, CHUNK))

    mines = [own_half(panel, j) for j in range(chunks)]
    ways = [None, (1, 2), (2, 1)]
    from_x, from_y = [to_grp(jnp.concatenate([mines[0], mines[d]], axis=1), d) for d in (1, 2)]
    firsts = [None, from_x, from_y]
    near = [from_x, from_y, to_grp(mines[0], 3)]

    half, quarter = sums // 2, sums // 4
    plain = shape((side, CHUNK), jnp.float32)

    def stack_of(count, one):
        return shape((count, *one.shape), one.dtype)

    def coded(count):
        return shape((count * side + CODE_ROWS, CHUNK), jnp.int16)

    order = jnp.zeros((1,), jnp.int32)
    last = None

    def in_order():
        return order if last is None else lax.optimization_barrier((order, last))[0]

    def call(body, name, outs, *args, smem=0, mib=16, extra=(), **more):
        nonlocal last
        done = pl.pallas_call(
            body,
            in_specs=more.pop("in_specs", in_any(1) + in_smem(smem) + in_vmem(len(args) - smem)),
            out_specs=more.pop("out_specs", in_vmem(len(outs))),
            out_shape=outs,
            scratch_shapes=list(extra),
            compiler_params=params(mib),
            cost_estimate=cost(0, sum(math.prod(a.shape) * a.dtype.itemsize for a in args)),
            name=name,
            **more,
        )(in_order(), *args)
        last = done[0]
        return done

    def places(operand, tiles_of, first):
        return [
            (operand, t, d * shard + first + i % part)
            for i, (t, d) in enumerate((t, d) for d, ts in tiles_of for t in ts)
        ]

    part = shard // 2

    def join(j):
        (joined,) = call(
            functools.partial(join_kernel, 0),
            "join",
            [shape((3 * rows // 2, CHUNK), panel.dtype)],
            *near,
        )
        tiles_of = [(d, range((d - 1) * part, d * part)) for d in (1, 2, 3)]
        fill = places(0, tiles_of, 0) + places(1, tiles_of, part)
        return fill, [joined, to_core(joined)]

    def pair(j):
        way, other = ways[j]
        (joined,) = call(
            functools.partial(join_kernel, CHUNK),
            "join",
            [shape((rows, CHUNK), panel.dtype)],
            mines[j],
            firsts[j],
        )
        second = to_grp(joined, other)
        in_first = [(way, range(part, 2 * part))]
        in_second = [(other, range(part)), (way ^ other, range(part, 2 * part))]
        fill = (
            places(0, in_first, 0)
            + places(1, in_first, part)
            + places(2, in_second, 0)
            + places(3, in_second, part)
        )
        return fill, [joined, to_core(joined), second]

    def products(j, which, sends, fill, parts):
        lists = counts, orders[which], slots[which], label
        *sends, stacked = call(
            functools.partial(sent_kernel, tuple(fill), j, which),
            "products_sent",
            [*sends, shape((4 * shard, side, CHUNK), panel.dtype)],
            *lists,
            held,
            panel,
            *parts,
            smem=4,
            extra=[pltpu.VMEM((half + 1, side, CHUNK), jnp.float32)],
            mib=24,
        )
        def kept():
            return call(
                functools.partial(kept_kernel, which),
                "products_kept",
                [stack_of(half + 1, plain)],
                *lists,
                held,
                stacked,
                smem=4,
                mib=24,
            )[0]

        return *sends, kept

    def gathered(done):
        return [done] + [to_grp(done, d) for d in (1, 2, 3)]

    def spread(j, blocks, result):
        earlier = [] if result is None else [result]
        return call(
            functools.partial(spread_kernel, j),
            "spread",
            [shape((out_dev * side, columns), jnp.float32)],
            *blocks,
            *earlier,
            in_specs=in_any(1) + in_vmem(4) + in_any(len(earlier)),
            out_specs=in_any(1),
            input_output_aliases={5: 0} if earlier else {},
            extra=[pltpu.VMEM((4, side, CHUNK), jnp.float32), pltpu.SemaphoreType.DMA((4,))],
        )[0]

    eighth = quarter // 2
    entries = shape((2 * tile_dev + UNROLL,), jnp.int32)
    twice = shape((2 * entries.shape[0],), jnp.int32)
    counts, in_plane, in_line, label, plane_order, line_order, held = call(
        hold_kernel,
        "hold",
        [shape((3,), jnp.int32)]
        + [entries] * 3
        + [twice] * 2
        + [pltpu.VMEM((2 * tile_dev + UNROLL, side, side), tiles.dtype)],
        own_index,
        sib_index,
        *[pltpu.with_memory_space_constraint(v, pltpu.HBM) for v in (tiles, sib_tiles)],
        in_specs=in_any(1) + in_smem(2) + in_any(2),
        out_specs=in_smem(6) + in_vmem(1),
        extra=[pltpu.SemaphoreType.DMA((2 * tile_dev,))],
        mib=8,
    )
    last = held
    slots, orders = {1: in_plane, 2: in_line}, {1: plane_order, 2: line_order}
    pairs = {j: pair(j) for j in (1, 2)}

    send, kept = products(0, 2, [coded(half)], *join(0))
    keep_0 = kept()
    sent_0 = send
    sent, keep = {}, {}
    for j in (1, 2):
        fill, (*parts, second) = pairs[j]
        second = lax.optimization_barrier((second, keep_0))[0]
        parts += [second, to_core(second)]
        send_a, send_b, kept = products(j, 1, [coded(quarter)] * 2, fill, parts)
        sent[j] = send_a, send_b
        if j == 2:
            sent_0, keep_0 = call(
                line_kernel,
                "line",
                [coded(quarter), stack_of(quarter, plain)],
                to_line(sent_0, 0),
                keep_0,
            )
        keep[j] = kept()

    def plane(j):
        return call(
            plane_kernel,
            "plane",
            [coded(eighth)] * 2 + [stack_of(quarter, plain)],
            to_grp(sent[j][0], 1),
            to_grp(sent[j][1], 2),
            keep[j],
        )

    def owner(j):
        return call(
            owner_kernel,
            "owner",
            [coded(eighth), stack_of(eighth, plain)],
            to_grp(sent[j][0], 2),
            to_grp(sent[j][1], 1),
            keep[j],
        )

    *sent[1], keep[1] = plane(1)
    *sent[2], keep[2] = plane(2)
    sent[1], keep[1] = owner(1)
    pair_of = [coded(2)] * 2
    own_a, own_b = call(rows_kernel, "rows", pair_of, to_line(sent_0, 1), keep_0)
    sent[2], keep[2] = owner(2)

    def line(j):
        return call(
            line_kernel,
            "line",
            [coded(1), stack_of(1, plain)],
            to_line(sent[j], 0),
            keep[j],
        )

    def finish(j):
        return call(finish_kernel, "finish", [coded(1)], to_line(sent[j], 1), keep[j])[0]

    sent[1], keep[1] = line(1)
    own_a, own_b = call(
        swap_kernel, "swap", pair_of, own_a, own_b, to_grp(own_a, 1), to_grp(own_b, 2)
    )
    sent[2], keep[2] = line(2)
    done_1 = finish(1)
    result = spread(0, [own_a, own_b, to_grp(own_a, 2), to_grp(own_b, 1)], None)
    done_2 = finish(2)
    result = spread(1, gathered(done_1), result)
    return spread(2, gathered(done_2), result)


def per_device(tiles, contraction, row_tile, owner_map, panel):
    dense = owner_map.shape[0] <= tiles.shape[0]
    wide_count = lax.axis_size("wide")
    fits = lax.axis_size("grp") == 4 and wide_count >= 4 and wide_count & (wide_count - 1) == 0
    out_dev = owner_map.shape[0] // wide_count
    if dense and fits and wide_count == 8 and out_dev == 4 and panel.shape[1] == 3 * CHUNK:
        return sums_plan(tiles, contraction, row_tile, owner_map, panel)
    return slots_plan(tiles, contraction, row_tile, owner_map, panel)


def solution(mesh):
    return jax.shard_map(
        per_device,
        mesh=mesh,
        in_specs=(
            P(("grp", "wide"), None, None),
            P(("grp", "wide")),
            P(("grp", "wide")),
            P(),
            P("grp", None),
        ),
        out_specs=P("wide", None),
        check_vma=False,
    )
```

```python
import functools
import math

import jax
import jax.numpy as jnp
from jax import lax
from jax.experimental import pallas as pl
from jax.experimental.pallas import tpu as pltpu
from jax.sharding import PartitionSpec as P

MIB = 1024 * 1024
CODE_ROWS = 16
CODE_STEPS = 256.0
TOP = 32000.0
CHUNK = 256
UNROLL = 8
LOG2 = math.log(2.0)


def place_slots(row_ids, owner_map, out_dev):
    table_ids = jnp.arange(owner_map.shape[0], dtype=jnp.int32)
    position = jnp.sum(jnp.where(row_ids[..., None] == table_ids, owner_map, 0), axis=-1)
    target = position // out_dev
    serial = jnp.arange(row_ids.shape[-1], dtype=jnp.int32)
    earlier = (target[..., :, None] == target[..., None, :]) & (serial[:, None] > serial[None, :])
    ranking = jnp.sum(earlier.astype(jnp.int32), axis=-1)
    return (position % out_dev, target, ranking)


def add_slot_products(summed, arrived, slot_labels, panel_tiles):
    slot_count = arrived.shape[0]
    block_rows = math.gcd(slot_count, 32)
    out_dev = summed.shape[0]
    local_ids = jnp.arange(out_dev, dtype=jnp.int32)

    def one_block(which_block, running, source_tiles, source_labels):
        part_tiles = lax.dynamic_slice_in_dim(source_tiles, which_block * block_rows, block_rows, 0)
        part_labels = lax.dynamic_slice_in_dim(
            source_labels, which_block * block_rows, block_rows, 0
        )
        chosen = jnp.take(panel_tiles, part_labels[:, 1], axis=0)
        products = jnp.einsum(
            "sab,sbc->sac", part_tiles, chosen, preferred_element_type=jnp.float32
        )
        row_hits = (part_labels[:, 0][:, None] == local_ids[None, :]).astype(jnp.float32)
        return running + jnp.einsum(
            "sr,sac->rac", row_hits, products, precision=lax.Precision.HIGHEST
        )

    return lax.fori_loop(
        0,
        slot_count // block_rows,
        lambda which_block, running: one_block(which_block, running, arrived, slot_labels),
        summed,
    )


def slots_plan(tiles, contraction, row_tile, owner_map, panel):
    wide_count = lax.axis_size("wide")
    tile_dev = tiles.shape[0]
    tile_side = tiles.shape[1]
    out_dev = owner_map.shape[0] // wide_count
    most_slots = tile_dev * 8 // (3 * wide_count)
    slot_total = wide_count * most_slots
    local_row, target, ranking = place_slots(row_tile, owner_map, out_dev)
    slot_index = target * most_slots + ranking
    outgoing = jnp.zeros((slot_total, tile_side, tile_side), tiles.dtype).at[slot_index].set(tiles)
    all_rows, all_contraction = (
        lax.all_gather(row_tile, "wide", axis=0, tiled=True),
        lax.all_gather(contraction, "wide", axis=0, tiled=True),
    )
    all_rows = all_rows.reshape(wide_count, tile_dev)
    all_contraction = all_contraction.reshape(wide_count, tile_dev)
    source_local, source_target, source_rank = place_slots(all_rows, owner_map, out_dev)
    source_ids = jnp.arange(wide_count, dtype=jnp.int32)
    mine = source_target == lax.axis_index("wide")
    arrive_index = jnp.where(mine, source_ids[:, None] * most_slots + source_rank, slot_total)
    label_pairs = jnp.stack([source_local, all_contraction], axis=-1).reshape(
        wide_count * tile_dev, 2
    )
    vacant_label = jnp.stack(
        [jnp.full((slot_total,), out_dev, jnp.int32), jnp.zeros((slot_total,), jnp.int32)], axis=1
    )
    arrived_labels = vacant_label.at[arrive_index.reshape(-1)].set(label_pairs, mode="drop")
    gathered = lax.all_gather(panel, "grp", axis=0, tiled=True)
    panel_tiles = gathered.reshape(gathered.shape[0] // tile_side, tile_side, gathered.shape[1])
    summed = jnp.zeros((out_dev, tile_side, gathered.shape[1]), jnp.float32)
    arrived = lax.all_to_all(outgoing, "wide", split_axis=0, concat_axis=0, tiled=True)
    summed = add_slot_products(summed, arrived, arrived_labels, panel_tiles)
    summed = lax.psum(summed, "grp")
    return summed.reshape(out_dev * tile_side, gathered.shape[1])


def encode(value):
    largest = jnp.max(jnp.abs(value), axis=0, keepdims=True)
    code = jnp.ceil(jnp.log(jnp.maximum(largest, 1e-30)) * (CODE_STEPS / LOG2))
    scale = jnp.exp(code * (-LOG2 / CODE_STEPS)) * TOP
    whole = jnp.round(value * scale).astype(jnp.int32).astype(jnp.int16)
    return whole, code.astype(jnp.int32)


def put_coded(ref, values):
    codes = []
    for value in values:
        side = value.shape[0]
        whole, code = encode(value)
        ref[pl.ds(len(codes) * side, side), :] = whole
        codes.append(code)
    end = len(codes) * side
    codes += [jnp.zeros_like(codes[0])] * (CODE_ROWS - len(codes))
    ref[pl.ds(end, CODE_ROWS), :] = jnp.concatenate(codes, axis=0).astype(jnp.int16)


class Decoded:
    def __init__(self, ref, side):
        self.ref, self.side = ref, side
        self.count = (ref.shape[0] - CODE_ROWS) // side
        code = ref[pl.ds(self.count * side, CODE_ROWS), :].astype(jnp.int32)
        self.scales = jnp.exp(code.astype(jnp.float32) * (LOG2 / CODE_STEPS)) * (1.0 / TOP)

    def tile(self, i):
        return self.part(i * self.side, self.scales[i : i + 1])

    def either(self, bit, zero, one):
        at = pl.multiple_of(jnp.where(bit == 1, one, zero) * self.side, self.side)
        scales = self.scales
        return self.part(at, jnp.where(bit == 1, scales[one : one + 1], scales[zero : zero + 1]))

    def part(self, at, scale):
        return self.ref[pl.ds(at, self.side), :].astype(jnp.int32).astype(jnp.float32) * scale


def here():
    g, w = lax.axis_index("grp"), lax.axis_index("wide")
    return g % 2, g // 2, (w // 2) % 2, w // 4


def hold_kernel(
    order, own_ref, sib_ref, own_tiles, sib_tiles,
    count_ref, plane_ref, line_ref, label_ref, plane_order, line_order, out, sems,
):
    tile_dev = own_tiles.shape[0]
    sums = (own_ref.shape[0] - 2 * tile_dev) // 2
    shard, out_dev = 4, 4
    room = 2 * tile_dev + UNROLL
    x, y, z_low, _ = here()
    g, core = lax.axis_index("grp"), lax.axis_index("wide") % 2

    def copy(tiles, which, at):
        return pltpu.make_async_copy(tiles.at[which], out.at[at], sems.at[at])

    def scan(tiles, index_ref, counts):
        def one(i, counts):
            position = own_ref[2 * tile_dev + index_ref[i]]
            k = index_ref[tile_dev + i]
            owner, local = lax.div(position, out_dev), lax.rem(position, out_dev)
            match = lax.rem(owner, 2) == core

            odd, to_z = lax.rem(lax.div(owner, 2), 2), lax.div(owner, 4)
            bit_x, bit_y = lax.rem(local, 2), lax.div(local, 2)
            kept = [
                jnp.where(odd == 1, bit_y == y, bit_x == x),
                odd == z_low,
            ]

            @pl.when(match)
            def _():
                copy(tiles, i, counts[0]).start()
                second = jnp.where(odd == 1, bit_x, bit_y)
                places = [odd * (sums // 4) + 2 * to_z + second, to_z * out_dev + local]
                for ref, order_ref, keep, place, sent in (
                    (plane_ref, plane_order, kept[0], places[0], counts[1]),
                    (line_ref, line_order, kept[1], places[1], counts[2]),
                ):
                    ref[counts[0]] = place
                    order_ref[jnp.where(keep, room + counts[0] - sent, sent)] = counts[0]
                apart, inner = lax.div(k, shard) ^ g, lax.rem(k, shard)
                half = shard // 2
                crossed = jnp.where(lax.div(inner, half) == core, 0, half) + lax.rem(inner, half)
                label_ref[counts[0]] = jnp.where(apart == 0, inner, apart * shard + crossed)

            more = [match, match & ~kept[0], match & ~kept[1]]
            return tuple(c + m.astype(jnp.int32) for c, m in zip(counts, more))

        return lax.fori_loop(0, tile_dev, one, counts)

    counts = scan(own_tiles, own_ref, (0, 0, 0))
    counts = scan(sib_tiles, sib_ref, counts)
    count = counts[0]
    for i in range(3):
        count_ref[i] = counts[i]
    spare = 2 * tile_dev
    plane_ref[spare] = sums // 2
    line_ref[spare] = sums // 2
    label_ref[spare] = 0
    for order_ref, sent in ((plane_order, counts[1]), (line_order, counts[2])):
        for i in range(UNROLL):
            order_ref[sent + i] = spare
            order_ref[room + count - sent + i] = spare

    @pl.loop(0, count)
    def _(i):
        copy(own_tiles, 0, i).wait()


def join_kernel(first, order, *refs):
    *parts, out = refs
    at, width = 0, out.shape[1]
    for part in parts:
        column = first if part.shape[1] > width else 0
        out[pl.ds(at, part.shape[0]), :] = part[:, pl.ds(column, width)]
        at += part.shape[0]


def add_products(count, first, order_ref, slot_ref, label_ref, tiles, stack, sums):
    @pl.loop(0, sums.shape[0])
    def _(i):
        sums[i] = jnp.zeros(sums.shape[1:], jnp.float32)

    @pl.loop(0, lax.div(count + UNROLL - 1, UNROLL))
    def _(i):
        entries = [order_ref[first + i * UNROLL + u] for u in range(UNROLL)]
        found = [
            jnp.dot(tiles[e], stack[label_ref[e]], preferred_element_type=jnp.float32)
            for e in entries
        ]
        for e, product in zip(entries, found):
            sums[slot_ref[e]] += product


def sent_kernel(
    fill, chunk, which, order, count_ref, order_ref, slot_ref, label_ref,
    tiles, own_panel, *refs
):
    parts = refs[: 1 + max(part for part, _, _ in fill)]
    *sends, stack, sums = refs[len(parts) :]
    side, width = stack.shape[1:]
    for t in range(own_panel.shape[0] // side):
        stack[t] = own_panel[pl.ds(t * side, side), pl.ds(chunk * width, width)]
    for part, t, at in fill:
        stack[at] = parts[part][pl.ds(t * side, side), :]
    add_products(count_ref[which], 0, order_ref, slot_ref, label_ref, tiles, stack, sums)
    sent = 0
    for send in sends:
        count = (send.shape[0] - CODE_ROWS) // side
        put_coded(send, (sums[sent + i] for i in range(count)))
        sent += count


def kept_kernel(which, order, count_ref, order_ref, slot_ref, label_ref, tiles, stack, sums):
    count = count_ref[0] - count_ref[which]
    room = tiles.shape[0]
    add_products(count, room, order_ref, slot_ref, label_ref, tiles, stack, sums)


def plane_kernel(order, recv_a, recv_b, kept, send_a, send_b, keep):
    side, half = kept.shape[1], keep.shape[0] // 2
    x, y, _, _ = here()
    for base, bit, recv, send in ((0, y, recv_a, send_a), (1, x, recv_b, send_b)):
        came = Decoded(recv, side)

        def total(i, which, base=base, came=came):
            return kept[2 * half * base + 2 * i + which] + came.either(which, 2 * i, 2 * i + 1)

        put_coded(send, (total(i, 1 - bit) for i in range(half)))
        for i in range(half):
            keep[base * half + i] = total(i, bit)


def owner_kernel(order, recv_a, recv_b, kept, send, keep):
    side, half = kept.shape[1], keep.shape[0]
    odd = here()[2]
    came_a, came_b = Decoded(recv_a, side), Decoded(recv_b, side)

    def to_send():
        for i in range(half):
            value_a = kept[i] + came_a.tile(i)
            value_b = kept[half + i] + came_b.tile(i)
            keep[i] = jnp.where(odd == 1, value_b, value_a)
            yield jnp.where(odd == 1, value_a, value_b)

    put_coded(send, to_send())


def line_kernel(order, recv, kept, send, keep):
    side, half = kept.shape[1], keep.shape[0]
    bit = here()[3]
    came = Decoded(recv, side)

    def total(i, which):
        return kept[which * half + i] + came.either(which, i, half + i)

    put_coded(send, (total(i, 1 - bit) for i in range(half)))
    for i in range(half):
        keep[i] = total(i, bit)


def rows_kernel(order, recv, kept, send_a, send_b):
    came = Decoded(recv, kept.shape[1])
    half = came.count // 2
    put_coded(send_a, (kept[i] + came.tile(i) for i in range(half)))
    put_coded(send_b, (kept[half + i] + came.tile(half + i) for i in range(half)))


def swap_kernel(order, own_a, own_b, recv_a, recv_b, send_a, send_b):
    side = (own_a.shape[0] - CODE_ROWS) // 2
    for own, recv, send in ((own_a, recv_a, send_a), (own_b, recv_b, send_b)):
        here_, there = Decoded(own, side), Decoded(recv, side)
        put_coded(send, (here_.tile(i) + there.tile(i) for i in range(2)))


def finish_kernel(order, recv, kept, out):
    put_coded(out, [kept[0] + Decoded(recv, kept.shape[1]).tile(0)])


def spread_kernel(chunk, order, *refs):
    blocks, (out, rows, sems) = refs[:4], refs[-3:]
    side, width = rows.shape[1:]
    x, y, _, _ = here()
    blocks = [Decoded(block, side) for block in blocks]
    copies = []
    for i in range(4):
        if blocks[0].count == 2:
            rows[i] = blocks[i // 2].tile(i % 2) + blocks[2 + i // 2].tile(i % 2)
            at = i * side
        else:
            rows[i] = blocks[i].tile(0)
            at = pl.multiple_of(((2 * y + x) ^ i) * side, side)
        copies.append(
            pltpu.make_async_copy(
                rows.at[i], out.at[pl.ds(at, side), pl.ds(chunk * width, width)], sems.at[i]
            )
        )
        copies[-1].start()
    for copy in copies:
        copy.wait()


def in_vmem(count):
    return [pl.BlockSpec(memory_space=pltpu.VMEM)] * count


def in_smem(count):
    return [pl.BlockSpec(memory_space=pltpu.SMEM)] * count


def in_any(count):
    return [pl.BlockSpec(memory_space=pl.ANY)] * count


def shape(dims, kind):
    return jax.ShapeDtypeStruct(dims, kind)


def params(mib):
    return pltpu.CompilerParams(vmem_limit_bytes=mib * MIB)


def cost(flops, moved):
    return pl.CostEstimate(flops=flops, bytes_accessed=moved, transcendentals=0)


def sums_plan(tiles, contraction, row_tile, owner_map, panel):
    wide_count = lax.axis_size("wide")
    tile_dev, side = tiles.shape[0], tiles.shape[1]
    out_dev = owner_map.shape[0] // wide_count
    rows, columns = panel.shape
    shard = rows // side
    chunks = columns // CHUNK
    sums = owner_map.shape[0] // 2
    core = lax.axis_index("wide") % 2

    def to_core(v):
        return lax.ppermute(v, "wide", [(i, i ^ 1) for i in range(wide_count)])

    def to_grp(v, d):
        return lax.ppermute(v, "grp", [(i, i ^ d) for i in range(4)])

    def to_line(v, b):
        return lax.ppermute(v, "wide", [(i, i ^ (2 << b)) for i in range(wide_count)])


    own_index = jnp.concatenate([row_tile, contraction, owner_map])
    sib_index = to_core(own_index)
    sib_tiles = to_core(tiles)

    def own_half(source, j):
        return lax.dynamic_slice(source, (core * (rows // 2), j * CHUNK), (rows // 2, CHUNK))

    mines = [own_half(panel, j) for j in range(chunks)]
    ways = [None, (1, 2), (2, 1)]
    from_x, from_y = [to_grp(jnp.concatenate([mines[0], mines[d]], axis=1), d) for d in (1, 2)]
    firsts = [None, from_x, from_y]
    near = [from_x, from_y, to_grp(mines[0], 3)]

    half, quarter = sums // 2, sums // 4
    plain = shape((side, CHUNK), jnp.float32)

    def stack_of(count, one):
        return shape((count, *one.shape), one.dtype)

    def coded(count):
        return shape((count * side + CODE_ROWS, CHUNK), jnp.int16)

    order = jnp.zeros((1,), jnp.int32)
    last = None

    def in_order():
        return order if last is None else lax.optimization_barrier((order, last))[0]

    def call(body, name, outs, *args, smem=0, mib=16, extra=(), **more):
        nonlocal last
        done = pl.pallas_call(
            body,
            in_specs=more.pop("in_specs", in_any(1) + in_smem(smem) + in_vmem(len(args) - smem)),
            out_specs=more.pop("out_specs", in_vmem(len(outs))),
            out_shape=outs,
            scratch_shapes=list(extra),
            compiler_params=params(mib),
            cost_estimate=cost(0, sum(math.prod(a.shape) * a.dtype.itemsize for a in args)),
            name=name,
            **more,
        )(in_order(), *args)
        last = done[0]
        return done

    def places(operand, tiles_of, first):
        return [
            (operand, t, d * shard + first + i % part)
            for i, (t, d) in enumerate((t, d) for d, ts in tiles_of for t in ts)
        ]

    part = shard // 2

    def join(j):
        (joined,) = call(
            functools.partial(join_kernel, 0),
            "join",
            [shape((3 * rows // 2, CHUNK), panel.dtype)],
            *near,
        )
        tiles_of = [(d, range((d - 1) * part, d * part)) for d in (1, 2, 3)]
        fill = places(0, tiles_of, 0) + places(1, tiles_of, part)
        return fill, [joined, to_core(joined)]

    def pair(j):
        way, other = ways[j]
        (joined,) = call(
            functools.partial(join_kernel, CHUNK),
            "join",
            [shape((rows, CHUNK), panel.dtype)],
            mines[j],
            firsts[j],
        )
        second = to_grp(joined, other)
        in_first = [(way, range(part, 2 * part))]
        in_second = [(other, range(part)), (way ^ other, range(part, 2 * part))]
        fill = (
            places(0, in_first, 0)
            + places(1, in_first, part)
            + places(2, in_second, 0)
            + places(3, in_second, part)
        )
        return fill, [joined, to_core(joined), second]

    def products(j, which, sends, fill, parts):
        lists = counts, orders[which], slots[which], label
        *sends, stacked = call(
            functools.partial(sent_kernel, tuple(fill), j, which),
            "products_sent",
            [*sends, shape((4 * shard, side, CHUNK), panel.dtype)],
            *lists,
            held,
            panel,
            *parts,
            smem=4,
            extra=[pltpu.VMEM((half + 1, side, CHUNK), jnp.float32)],
            mib=24,
        )
        def kept():
            return call(
                functools.partial(kept_kernel, which),
                "products_kept",
                [stack_of(half + 1, plain)],
                *lists,
                held,
                stacked,
                smem=4,
                mib=24,
            )[0]

        return *sends, kept

    def gathered(done):
        return [done] + [to_grp(done, d) for d in (1, 2, 3)]

    def spread(j, blocks, result):
        earlier = [] if result is None else [result]
        return call(
            functools.partial(spread_kernel, j),
            "spread",
            [shape((out_dev * side, columns), jnp.float32)],
            *blocks,
            *earlier,
            in_specs=in_any(1) + in_vmem(4) + in_any(len(earlier)),
            out_specs=in_any(1),
            input_output_aliases={5: 0} if earlier else {},
            extra=[pltpu.VMEM((4, side, CHUNK), jnp.float32), pltpu.SemaphoreType.DMA((4,))],
        )[0]

    eighth = quarter // 2
    entries = shape((2 * tile_dev + UNROLL,), jnp.int32)
    twice = shape((2 * entries.shape[0],), jnp.int32)
    counts, in_plane, in_line, label, plane_order, line_order, held = call(
        hold_kernel,
        "hold",
        [shape((3,), jnp.int32)]
        + [entries] * 3
        + [twice] * 2
        + [pltpu.VMEM((2 * tile_dev + UNROLL, side, side), tiles.dtype)],
        own_index,
        sib_index,
        *[pltpu.with_memory_space_constraint(v, pltpu.HBM) for v in (tiles, sib_tiles)],
        in_specs=in_any(1) + in_smem(2) + in_any(2),
        out_specs=in_smem(6) + in_vmem(1),
        extra=[pltpu.SemaphoreType.DMA((2 * tile_dev,))],
        mib=8,
    )
    last = held
    slots, orders = {1: in_plane, 2: in_line}, {1: plane_order, 2: line_order}
    pairs = {j: pair(j) for j in (1, 2)}

    send, kept = products(0, 2, [coded(half)], *join(0))
    keep_0 = kept()
    sent_0 = send
    sent, keep = {}, {}
    for j in (1, 2):
        fill, (*parts, second) = pairs[j]
        second = lax.optimization_barrier((second, keep_0))[0]
        parts += [second, to_core(second)]
        send_a, send_b, kept = products(j, 1, [coded(quarter)] * 2, fill, parts)
        sent[j] = send_a, send_b
        if j == 2:
            sent_0, keep_0 = call(
                line_kernel,
                "line",
                [coded(quarter), stack_of(quarter, plain)],
                to_line(sent_0, 0),
                keep_0,
            )
        else:
            keep[j] = kept()

    def plane(j):
        return call(
            plane_kernel,
            "plane",
            [coded(eighth)] * 2 + [stack_of(quarter, plain)],
            to_grp(sent[j][0], 1),
            to_grp(sent[j][1], 2),
            keep[j],
        )

    def owner(j):
        return call(
            owner_kernel,
            "owner",
            [coded(eighth), stack_of(eighth, plain)],
            to_grp(sent[j][0], 2),
            to_grp(sent[j][1], 1),
            keep[j],
        )

    *sent[1], keep[1] = plane(1)
    keep[2] = kept()
    *sent[2], keep[2] = plane(2)
    sent[1], keep[1] = owner(1)
    pair_of = [coded(2)] * 2
    own_a, own_b = call(rows_kernel, "rows", pair_of, to_line(sent_0, 1), keep_0)
    sent[2], keep[2] = owner(2)

    def line(j):
        return call(
            line_kernel,
            "line",
            [coded(1), stack_of(1, plain)],
            to_line(sent[j], 0),
            keep[j],
        )

    def finish(j):
        return call(finish_kernel, "finish", [coded(1)], to_line(sent[j], 1), keep[j])[0]

    sent[1], keep[1] = line(1)
    own_a, own_b = call(
        swap_kernel, "swap", pair_of, own_a, own_b, to_grp(own_a, 1), to_grp(own_b, 2)
    )
    sent[2], keep[2] = line(2)
    done_1 = finish(1)
    result = spread(0, [own_a, own_b, to_grp(own_a, 2), to_grp(own_b, 1)], None)
    done_2 = finish(2)
    result = spread(1, gathered(done_1), result)
    return spread(2, gathered(done_2), result)


def per_device(tiles, contraction, row_tile, owner_map, panel):
    dense = owner_map.shape[0] <= tiles.shape[0]
    wide_count = lax.axis_size("wide")
    fits = lax.axis_size("grp") == 4 and wide_count >= 4 and wide_count & (wide_count - 1) == 0
    out_dev = owner_map.shape[0] // wide_count
    if dense and fits and wide_count == 8 and out_dev == 4 and panel.shape[1] == 3 * CHUNK:
        return sums_plan(tiles, contraction, row_tile, owner_map, panel)
    return slots_plan(tiles, contraction, row_tile, owner_map, panel)


def solution(mesh):
    return jax.shard_map(
        per_device,
        mesh=mesh,
        in_specs=(
            P(("grp", "wide"), None, None),
            P(("grp", "wide")),
            P(("grp", "wide")),
            P(),
            P("grp", None),
        ),
        out_specs=P("wide", None),
        check_vma=False,
    )
```
